128 devices in a mesh: space: 8 (over z, core), dp: 16 (over x, y).
Axes of the slice: x: 4, y: 4, z: 4, core: 2. Of those that a mesh axis runs over, the one named last changes fastest.
Arguments:
- features: bfloat16 [32, 96, 100, 176], P('dp', 'space'), may hold values from -15 to 15
- w_expand: bfloat16 [176, 1056], P(None, 'dp'), may hold values from -0.4375 to 0.4375
- w_depth: bfloat16 [5, 5, 1056], P(None, None, 'dp'), may hold values from -1.25 to 1.25
- w_reduce: bfloat16 [1056, 44], P('dp'), may hold values from -0.375 to 0.375
- b_reduce: bfloat16 [44], replicated, may hold values from -4 to 4
- w_excite: bfloat16 [44, 1056], P(None, 'dp'), may hold values from -1.75 to 1.75
- b_excite: bfloat16 [1056], P('dp'), may hold values from -4 to 4
- w_project: bfloat16 [1056, 176], P('dp'), may hold values from -0.375 to 0.375
- cotangent: bfloat16 [32, 96, 100, 176], P('dp', 'space'), may hold values from -6 to 6
Outputs:
- output: bfloat16 [32, 96, 100, 176], P('dp', 'space')
- grad_features: bfloat16 [32, 96, 100, 176], P('dp', 'space')
- grad_expand: float32 [176, 1056], P(None, 'dp')
- grad_depth: float32 [5, 5, 1056], P(None, None, 'dp')
- grad_reduce: float32 [1056, 44], P('dp')
- grad_excite: float32 [44, 1056], P(None, 'dp')
- grad_bexcite: float32 [1056], P('dp')
- grad_project: float32 [1056, 176], P('dp')
- grad_breduce: float32 [44], replicated
The draws below stay inside these ranges and needn't reach their ends.
All inputs are finite; a program needn't handle non-finite values.
Results may differ from the reference program's by a relative error of at most 0.0062.
Values may be sent and summed in bfloat16 or wider, within the bound.
A program may use at most 128 MiB of HBM per device.

```python
import jax
import jax.numpy as jnp
from jax import lax

C = 176
CE = 1056
SE = 44
KS = 5
W = 100
IMAGES = 32
H = 96


def draw_features(key, part):
    key = jax.random.fold_in(key, 11)
    rows = jnp.arange(H, dtype=jnp.float32) / max(H - 1, 1)
    row_scale = jnp.exp(jnp.log(3.0) * rows)[None, :, None, None]
    base = jnp.clip(jax.random.normal(key, (IMAGES, H, W, C), jnp.float32), -4.0, 4.0)
    return (base * row_scale).astype(jnp.bfloat16)


def levels(own_key, dims, split, low, high):
    level = 1.0
    for dim, shards_of in split:
        draws = jax.random.uniform(jax.random.fold_in(jax.random.fold_in(own_key, 6), dim), (shards_of,), jnp.float32, low / len(split), high / len(split))
        level = level * jnp.repeat(jnp.exp(draws), dims[dim] // shards_of).reshape((-1,) + (1,) * (len(dims) - 1 - dim))
    return level


def gaussian(key, extent, spread, limit, pieces=(), kind=jnp.bfloat16):
    loudness = levels(key, extent, pieces, -0.22, 0.18) if pieces else 1.0
    drawn = jax.random.normal(key, extent, jnp.float32) * spread * loudness
    return jnp.minimum(jnp.maximum(drawn, -limit), limit).astype(kind)


def setup_inputs(seed: int = 0) -> dict:
    streams_of = jax.random.split(jax.random.key(seed), 10)
    features = draw_features(jax.random.fold_in(streams_of[9], 71), 0)
    w_expand = gaussian(streams_of[1], (C, CE), C ** -0.5, 0.4375, ((1, 16),))
    w_depth = gaussian(streams_of[2], (KS, KS, CE), (KS * KS) ** -0.5, 1.25, ((2, 16),))
    w_reduce = gaussian(streams_of[3], (CE, SE), (CE // 4) ** -0.5, 0.375, ((0, 16),))
    b_reduce = gaussian(streams_of[4], (SE,), 1.0, 4.0)
    w_excite = gaussian(streams_of[5], (SE, CE), (SE // 4) ** -0.5, 1.75, ((1, 16),))
    b_excite = gaussian(streams_of[6], (CE,), 1.0, 4.0, ((0, 16),))
    w_project = gaussian(streams_of[7], (CE, C), (CE // 4) ** -0.5, 0.375, ((0, 16),))
    cotangent = gaussian(streams_of[8], (IMAGES, H, W, C), 1.0, 6.0, ((0, 16), (1, 8)))
    return dict(features=features, w_expand=w_expand, w_depth=w_depth, w_reduce=w_reduce, b_reduce=b_reduce, w_excite=w_excite, b_excite=b_excite, w_project=w_project, cotangent=cotangent)


def swish(value):
    return value * jax.nn.sigmoid(value)

def swish_grad(value):
    sig = jax.nn.sigmoid(value)
    return sig * (1.0 + value * (1.0 - sig))

def depthwise(padded, kernel, rows, cols):
    total = jnp.zeros((padded.shape[0], rows, cols, padded.shape[3]), jnp.float32)
    for i in range(KS):
        for j in range(KS):
            total = total + padded[:, i:i + rows, j:j + cols, :].astype(jnp.float32) * kernel[i, j].astype(jnp.float32)
    return total

def depthwise_back(padded, kernel, rows, cols):
    total = jnp.zeros((padded.shape[0], rows, cols, padded.shape[3]), jnp.float32)
    for i in range(KS):
        for j in range(KS):
            total = total + padded[:, 4 - i:4 - i + rows, 4 - j:4 - j + cols, :].astype(jnp.float32) * kernel[i, j].astype(jnp.float32)
    return total

def kernel_grad(ddepth, padded, rows, cols):
    parts = []
    for i in range(KS):
        row_parts = []
        for j in range(KS):
            row_parts.append(lax.optimization_barrier(jnp.sum(ddepth.astype(jnp.float32) * padded[:, i:i + rows, j:j + cols, :].astype(jnp.float32), axis=(0, 1, 2))))
        parts.append(jnp.stack(row_parts))
    return jnp.stack(parts)

def hdot(left, right):
    return jnp.dot(left, right, precision=lax.Precision.HIGHEST)

def one_image(args, w_expand, w_depth, w_reduce, b_reduce, w_excite, b_excite, w_project):
    features, cotangent = args
    chans = features.shape[-1]
    wide = w_expand.shape[1]
    flat = features.reshape(-1, chans)
    pre = jnp.dot(flat, w_expand, preferred_element_type=jnp.float32).reshape(1, H, W, wide)
    expanded = swish(pre).astype(jnp.bfloat16)
    padded = jnp.pad(expanded, ((0, 0), (2, 2), (2, 2), (0, 0)))
    depth = depthwise(padded, w_depth, H, W)
    act = swish(depth)
    pooled = lax.optimization_barrier(jnp.sum(act, axis=(1, 2))) / (H * W)
    wr = w_reduce.astype(jnp.float32)
    wx = w_excite.astype(jnp.float32)
    squeeze_pre = hdot(pooled, wr) + b_reduce.astype(jnp.float32)
    squeeze = swish(squeeze_pre)
    gate = jax.nn.sigmoid(hdot(squeeze, wx) + b_excite.astype(jnp.float32))
    gated = (act * gate[:, None, None, :]).astype(jnp.bfloat16)
    gflat = gated.reshape(-1, wide)
    output = (features.astype(jnp.float32) + jnp.dot(gflat, w_project, preferred_element_type=jnp.float32).reshape(features.shape)).astype(jnp.bfloat16)
    dflat = cotangent.reshape(-1, chans)
    dgated = jnp.dot(dflat, w_project.T, preferred_element_type=jnp.float32).reshape(1, H, W, wide)
    g_project = jnp.dot(gflat.T, dflat, preferred_element_type=jnp.float32)
    dgate = lax.optimization_barrier(jnp.sum(dgated * act, axis=(1, 2)))
    dlogit = dgate * gate * (1.0 - gate)
    g_excite = hdot(squeeze.T, dlogit)
    g_bexcite = lax.optimization_barrier(jnp.sum(dlogit, axis=0))
    dsq_pre = hdot(dlogit, wx.T) * swish_grad(squeeze_pre)
    g_reduce = hdot(pooled.T, dsq_pre)
    g_breduce = lax.optimization_barrier(jnp.sum(dsq_pre, axis=0))
    dpooled = hdot(dsq_pre, wr.T)
    ddepth = ((dgated * gate[:, None, None, :] + dpooled[:, None, None, :] / (H * W)) * swish_grad(depth)).astype(jnp.bfloat16)
    g_depth = kernel_grad(ddepth, padded, H, W)
    dpadded = jnp.pad(ddepth, ((0, 0), (2, 2), (2, 2), (0, 0)))
    dexp = depthwise_back(dpadded, w_depth, H, W)
    dpre = (dexp * swish_grad(pre)).astype(jnp.bfloat16)
    pflat = dpre.reshape(-1, wide)
    grad_features = (cotangent.astype(jnp.float32) + jnp.dot(pflat, w_expand.T, preferred_element_type=jnp.float32).reshape(features.shape)).astype(jnp.bfloat16)
    g_expand = jnp.dot(flat.T, pflat, preferred_element_type=jnp.float32)
    return (output[0], grad_features[0], (g_expand, g_depth, g_reduce, g_excite, g_bexcite, g_project, g_breduce))

def reference(features, w_expand, w_depth, w_reduce, b_reduce, w_excite, b_excite, w_project, cotangent):

    def step(carry, args):
        out_img, grad_img, grads = one_image((args[0][None], args[1][None]), w_expand, w_depth, w_reduce, b_reduce, w_excite, b_excite, w_project)
        carry = jax.tree.map(lambda left, right: left + right, carry, grads)
        return (carry, (out_img, grad_img))
    chans = features.shape[-1]
    wide = w_expand.shape[1]
    start = (jnp.zeros((chans, wide), jnp.float32), jnp.zeros((KS, KS, wide), jnp.float32), jnp.zeros((wide, SE), jnp.float32), jnp.zeros((SE, wide), jnp.float32), jnp.zeros((wide,), jnp.float32), jnp.zeros((wide, chans), jnp.float32), jnp.zeros((SE,), jnp.float32))
    grads, outs = lax.scan(step, start, (features, cotangent))
    return (outs[0], outs[1], grads[0], grads[1], grads[2], grads[3], grads[4], grads[5], grads[6])
```

```python
import functools

import jax
import jax.numpy as jnp
from jax import lax
from jax.experimental import pallas as pl
from jax.experimental.pallas import tpu as pltpu
from jax.sharding import PartitionSpec as P

F32 = jnp.float32
BF16 = jnp.bfloat16
MESH = pl.DeviceIdType.MESH
HIGH = lax.Precision.HIGHEST

IMGS, ROWS, COLS, C, SE = 2, 12, 100, 176, 44
BLOCK, SUB = 13, 16
PIX = BLOCK * SUB
WIDE = BLOCK + 4
HROWS = ROWS + 4
PART, SLOT = 66, 72
CP = 16 * SLOT
TILES = CP // 128
AREA = 9600.0
NS, ND = 8, 16

VMEM = pl.BlockSpec(memory_space=pltpu.VMEM)
ANY = pl.BlockSpec(memory_space=pl.ANY)


def sigmoid(value):
    return 0.5 * jnp.tanh(0.5 * value) + 0.5


def swish(value):
    return value * sigmoid(value)


def swish_grad(value):
    sig = sigmoid(value)
    act = value * sig
    return sig + act - act * sig


def dot_nt(left, right, precision=None):
    return lax.dot_general(
        left, right, (((1,), (1,)), ((), ())), precision=precision, preferred_element_type=F32
    )


def dot_tn(left, right, precision=None):
    return lax.dot_general(
        left, right, (((0,), (0,)), ((), ())), precision=precision, preferred_element_type=F32
    )


def dot_nn(left, right, precision=None):
    return lax.dot_general(
        left, right, (((1,), (0,)), ((), ())), precision=precision, preferred_element_type=F32
    )


def greet(space_peers, dp_peers):
    me_s, me_d = lax.axis_index("space"), lax.axis_index("dp")
    barrier = pltpu.get_barrier_semaphore()
    for k in space_peers:
        pl.semaphore_signal(
            barrier, inc=1, device_id=(lax.rem(me_s + k, NS), me_d), device_id_type=MESH
        )
    for k in dp_peers:
        pl.semaphore_signal(
            barrier, inc=1, device_id=(me_s, lax.rem(me_d + k, ND)), device_id_type=MESH
        )
    pl.semaphore_wait(barrier, len(space_peers) + len(dp_peers))


def gather_kernel(
    pack, feats, full, top, bottom, send, recv, halo_send, halo_recv, mate_send, mate_recv, own
):
    me_s, me_d = lax.axis_index("space"), lax.axis_index("dp")
    core = lax.rem(me_s, 2)
    mate = me_s + 1 - 2 * core
    barrier = pltpu.get_barrier_semaphore()
    for k in (1, NS - 1):
        pl.semaphore_signal(
            barrier, inc=1, device_id=(lax.rem(me_s + k, NS), me_d), device_id_type=MESH
        )
    for k in range(1, ND):
        pl.semaphore_signal(
            barrier, inc=1, device_id=(me_s, lax.rem(me_d + k, ND)), device_id_type=MESH
        )
    pl.semaphore_wait(barrier, ND + 1)
    copies = []
    for k in range(1, ND):
        copy = pltpu.make_async_remote_copy(
            src_ref=pack.at[core],
            dst_ref=full.at[core, me_d],
            send_sem=send.at[k],
            recv_sem=recv.at[k],
            device_id=(me_s, lax.rem(me_d + k, ND)),
            device_id_type=MESH,
        )
        copy.start()
        copies.append(copy)
    down = pltpu.make_async_remote_copy(
        src_ref=feats.at[:, pl.ds(ROWS - 2, 2)],
        dst_ref=top,
        send_sem=halo_send.at[0],
        recv_sem=halo_recv.at[0],
        device_id=(lax.rem(me_s + 1, NS), me_d),
        device_id_type=MESH,
    )
    up = pltpu.make_async_remote_copy(
        src_ref=feats.at[:, pl.ds(0, 2)],
        dst_ref=bottom,
        send_sem=halo_send.at[1],
        recv_sem=halo_recv.at[1],
        device_id=(lax.rem(me_s + NS - 1, NS), me_d),
        device_id_type=MESH,
    )
    down.start()
    up.start()
    mine = pltpu.make_async_copy(pack.at[core], full.at[core, me_d], own)
    mine.start()
    mine.wait()
    for copy in copies:
        copy.wait()
    share = pltpu.make_async_remote_copy(
        src_ref=full.at[core],
        dst_ref=full.at[core],
        send_sem=mate_send,
        recv_sem=mate_recv,
        device_id=(mate, me_d),
        device_id_type=MESH,
    )
    share.start()
    down.wait()
    up.wait()
    share.wait()


def gather(pack, features):
    return pl.pallas_call(
        gather_kernel,
        out_shape=(
            jax.ShapeDtypeStruct((2, ND, 80, 256), BF16),
            jax.ShapeDtypeStruct((IMGS, 2, COLS, C), BF16),
            jax.ShapeDtypeStruct((IMGS, 2, COLS, C), BF16),
        ),
        in_specs=[ANY, ANY],
        out_specs=(ANY, ANY, ANY),
        scratch_shapes=[
            pltpu.SemaphoreType.DMA((ND,)),
            pltpu.SemaphoreType.DMA((ND,)),
            pltpu.SemaphoreType.DMA((2,)),
            pltpu.SemaphoreType.DMA((2,)),
            pltpu.SemaphoreType.DMA,
            pltpu.SemaphoreType.DMA,
            pltpu.SemaphoreType.DMA,
        ],
        compiler_params=pltpu.CompilerParams(collective_id=0, has_side_effects=True),
        name="gather_weights",
    )(pack, features)


def one_hot(img, transposed):
    shape = (COLS, PIX) if transposed else (PIX, COLS)
    place = lax.broadcasted_iota(jnp.int32, shape, 1 if transposed else 0)
    col = lax.broadcasted_iota(jnp.int32, shape, 0 if transposed else 1)
    wanted = (col % BLOCK) * SUB + img * 8 + col // BLOCK
    return jnp.where(place == wanted, 1.0, 0.0).astype(BF16)


def prep_kernel(
    full, top, bottom, feats, cot, fp, cp, fpt, cpt, we, wp, misc, flat
):
    me_s = lax.axis_index("space")
    for half, out in ((0, we), (1, wp)):
        for d in range(ND):
            flat[d * SLOT : (d + 1) * SLOT, :] = full[half, d, 0:SLOT, :].astype(F32)
        valid = lax.broadcasted_iota(jnp.int32, (CP, 256), 0) % SLOT < PART
        whole = jnp.where(valid, flat[...], 0.0)
        out[...] = whole[:, 0:C].astype(BF16)
        turned = whole[:, 128:256].T
        if half == 0:
            misc[0:32, :] = turned[48:80, :]
            misc[32:80, :] = turned[80:128, :]
        else:
            misc[80:128, :] = turned[48:96, :]
            misc[128:136, :] = turned[96:104, :]
    spread = (one_hot(0, False), one_hot(1, False))
    gather_t = (one_hot(0, True), one_hot(1, True))
    has_top = jnp.where(me_s > 0, 1.0, 0.0)
    has_bottom = jnp.where(me_s < NS - 1, 1.0, 0.0)
    for r in range(2):
        value = dot_nn(spread[0], top[0, r]) + dot_nn(spread[1], top[1, r])
        fp[r] = (value * has_top).astype(BF16)
        value = dot_nn(spread[0], bottom[0, r]) + dot_nn(spread[1], bottom[1, r])
        fp[ROWS + 2 + r] = (value * has_bottom).astype(BF16)

    def row(r, carry):
        for src, dst, shift, dst_t in ((feats, fp, 2, fpt), (cot, cp, 0, cpt)):
            a, b = src[0, r], src[1, r]
            dst[r + shift] = (dot_nn(spread[0], a) + dot_nn(spread[1], b)).astype(BF16)
            dst_t[r] = (dot_tn(a, gather_t[0]) + dot_tn(b, gather_t[1])).astype(BF16)
        return carry

    lax.fori_loop(0, ROWS, row, 0)


def prep(full, top, bottom, features, cotangent):
    return pl.pallas_call(
        prep_kernel,
        out_shape=(
            jax.ShapeDtypeStruct((HROWS, PIX, C), BF16),
            jax.ShapeDtypeStruct((ROWS, PIX, C), BF16),
            jax.ShapeDtypeStruct((ROWS, C, PIX), BF16),
            jax.ShapeDtypeStruct((ROWS, C, PIX), BF16),
            jax.ShapeDtypeStruct((CP, C), BF16),
            jax.ShapeDtypeStruct((CP, C), BF16),
            jax.ShapeDtypeStruct((136, CP), F32),
        ),
        in_specs=[VMEM] * 5,
        out_specs=(VMEM,) * 7,
        scratch_shapes=[pltpu.VMEM((CP, 256), F32)],
        compiler_params=pltpu.CompilerParams(vmem_limit_bytes=56 * 2**20),
        name="prep",
    )(full, top, bottom, features, cotangent)


def spread_taps(taps, wide_taps):
    for k in range(25):
        wide_taps[k] = jnp.broadcast_to(taps[k : k + 1, :], (8, 128))


def edge_columns(value):
    split = value.reshape(BLOCK, 2, 8, 128)
    block = lax.broadcasted_iota(jnp.int32, (2, 2, 8, 128), 2)
    left = jnp.where(block > 0, pltpu.roll(split[BLOCK - 2 :], 1, 2), 0.0)
    right = jnp.where(block < 7, pltpu.roll(split[:2], 7, 2), 0.0)
    return left.reshape(2, SUB, 128), right.reshape(2, SUB, 128)


def store_row(ref, r, value):
    left, right = edge_columns(value)
    ref[r, 0:2] = left
    ref[r, 2 : 2 + BLOCK] = value
    ref[r, 2 + BLOCK :] = right


def conv_row(ref, r, h, wide_taps, flip):
    total = jnp.zeros((BLOCK, 8, 128), F32)
    for i in range(5):
        source = ref[r + i, :, 8 * h : 8 * h + 8, :]
        for j in range(5):
            k = (4 - i) * 5 + 4 - j if flip else i * 5 + j
            total = total + source[j : j + BLOCK] * wide_taps[k][None]
    return total


def pad_mask():
    block = lax.broadcasted_iota(jnp.int32, (4, 8, 128), 1)
    return jnp.where(block < 7, 1.0, 0.0)


def first_kernel(fp, cp, we, wp, misc, ex, depth, sums, wide_taps):
    spread_taps(misc, wide_taps)
    keep = pad_mask()

    def expand(r, carry):
        pre = dot_nt(fp[r], we[...])
        store_row(ex.at[0], r, swish(pre).astype(BF16).astype(F32).reshape(BLOCK, SUB, 128))
        return carry

    lax.fori_loop(0, HROWS, expand, 0)

    def conv(r, carry):
        pools, grads = list(carry[:2]), list(carry[2:])
        dgated = dot_nt(cp[r], wp[...]).reshape(BLOCK, SUB, 128)
        for h in range(2):
            total = conv_row(ex.at[0], r, h, wide_taps, False)
            depth[0, r, :, 8 * h : 8 * h + 8, :] = total
            act = swish(total)
            grads[h] = grads[h] + jnp.sum(act * dgated[:, 8 * h : 8 * h + 8, :], axis=0)
            pools[h] = pools[h] + jnp.sum(act[:9], axis=0) + jnp.sum(act[9:] * keep, axis=0)
        return (*pools, *grads)

    zero = jnp.zeros((8, 128), F32)
    parts = lax.fori_loop(0, ROWS, conv, (zero,) * 4)
    for k in range(4):
        sums[0, k : k + 1, :] = jnp.sum(parts[k], axis=0, keepdims=True)
    sums[0, 4:8, :] = jnp.zeros((4, 128), F32)


def tile_spec(*shape):
    zeros = (0,) * len(shape)
    return pl.BlockSpec((1, *shape), lambda t: (t, *zeros))


def whole_spec(*shape):
    zeros = (0,) * len(shape)
    return pl.BlockSpec(shape, lambda t: zeros)


def first(fp, cp, we, wp, misc):
    return pl.pallas_call(
        first_kernel,
        grid=(TILES,),
        out_shape=(
            jax.ShapeDtypeStruct((TILES, HROWS, WIDE, SUB, 128), F32),
            jax.ShapeDtypeStruct((TILES, ROWS, BLOCK, SUB, 128), F32),
            jax.ShapeDtypeStruct((TILES, 8, 128), F32),
        ),
        in_specs=[
            whole_spec(HROWS, PIX, C),
            whole_spec(ROWS, PIX, C),
            pl.BlockSpec((128, C), lambda t: (t, 0)),
            pl.BlockSpec((128, C), lambda t: (t, 0)),
            pl.BlockSpec((32, 128), lambda t: (0, t)),
        ],
        out_specs=(
            tile_spec(HROWS, WIDE, SUB, 128),
            tile_spec(ROWS, BLOCK, SUB, 128),
            tile_spec(8, 128),
        ),
        scratch_shapes=[pltpu.VMEM((25, 8, 128), F32)],
        compiler_params=pltpu.CompilerParams(vmem_limit_bytes=56 * 2**20),
        name="phase_a",
    )(fp, cp, we, wp, misc)


def mid_kernel(
    sums, misc, breduce, gates, greduce, gexcite, gbias, landed, msgs, got, lanes, vecs,
    send, recv, msend, mrecv,
):
    me_s, me_d = lax.axis_index("space"), lax.axis_index("dp")
    greet(range(1, NS), range(1, ND))
    copies = []
    for k in range(1, NS):
        copy = pltpu.make_async_remote_copy(
            src_ref=sums,
            dst_ref=landed.at[k],
            send_sem=send.at[k],
            recv_sem=recv.at[k],
            device_id=(lax.rem(me_s + k, NS), me_d),
            device_id_type=MESH,
        )
        copy.start()
        copies.append(copy)
    landed[0] = sums[...]
    for copy in copies:
        copy.wait()
    total = landed[lax.rem(me_s, NS)]
    for s in range(1, NS):
        total = total + landed[lax.rem(me_s + NS - s, NS)]
    for t in range(TILES):
        lanes[0:8, 128 * t : 128 * (t + 1)] = total[t]
    lanes[:, CP:] = jnp.zeros((8, 128), F32)
    allsum = lanes[:, 0:CP]
    wr = misc[32 : 32 + SE, :]
    wx = misc[80 : 80 + SE, :]
    bexcite = misc[128:129, :]
    pooled = allsum[0:2] / AREA
    dgate = allsum[2:4]
    squeeze_pre = dot_nt(pooled, wr, HIGH) + breduce[...].astype(F32)
    squeeze = swish(squeeze_pre)
    gate = sigmoid(dot_nn(squeeze, wx, HIGH) + bexcite)
    dlogit = dgate * gate * (1.0 - gate)
    dsq = dot_nt(dlogit, wx, HIGH) * swish_grad(squeeze_pre)
    dpooled = dot_nn(dsq, wr, HIGH)
    gates[0:2, :] = gate
    gates[2:4, :] = dpooled / AREA
    gates[4:8, :] = jnp.zeros((4, CP), F32)
    lanes[0:2, 0:CP] = pooled
    lanes[2:4, 0:CP] = dlogit
    vecs[...] = jnp.zeros((8, 128), F32)
    vecs[4:6, 0:SE] = squeeze
    vecs[6:8, 0:SE] = dsq
    for d in range(ND):
        msgs[d, 0:4, :] = lanes[0:4, SLOT * d : SLOT * d + 128]
        msgs[d, 4:8, :] = vecs[4:8, :]
    copies = []
    for k in range(1, ND):
        target = lax.rem(me_d + k, ND)
        copy = pltpu.make_async_remote_copy(
            src_ref=msgs.at[target],
            dst_ref=got.at[k],
            send_sem=msend.at[k],
            recv_sem=mrecv.at[k],
            device_id=(me_s, target),
            device_id_type=MESH,
        )
        copy.start()
        copies.append(copy)
    got[0] = msgs[me_d]
    for copy in copies:
        copy.wait()
    rows = [got[lax.rem(me_d + ND - d, ND)] for d in range(ND)]
    pool_all = jnp.concatenate([row[0:2] for row in rows], axis=0)
    dlog_all = jnp.concatenate([row[2:4] for row in rows], axis=0)
    sq_all = jnp.concatenate([row[4:6] for row in rows], axis=0)
    dsq_all = jnp.concatenate([row[6:8] for row in rows], axis=0)
    greduce[...] = dot_tn(pool_all, dsq_all, HIGH)
    gexcite[...] = dot_tn(sq_all, dlog_all, HIGH)
    gbias[0:1, :] = jnp.sum(dlog_all, axis=0, keepdims=True)
    gbias[1:2, :] = jnp.sum(dsq_all, axis=0, keepdims=True)
    gbias[2:8, :] = jnp.zeros((6, 128), F32)


def mid(sums, misc, breduce):
    return pl.pallas_call(
        mid_kernel,
        out_shape=(
            jax.ShapeDtypeStruct((8, CP), F32),
            jax.ShapeDtypeStruct((128, 128), F32),
            jax.ShapeDtypeStruct((128, 128), F32),
            jax.ShapeDtypeStruct((8, 128), F32),
        ),
        in_specs=[VMEM] * 3,
        out_specs=(VMEM,) * 4,
        scratch_shapes=[
            pltpu.VMEM((NS, TILES, 8, 128), F32),
            pltpu.VMEM((ND, 8, 128), F32),
            pltpu.VMEM((ND, 8, 128), F32),
            pltpu.VMEM((8, CP + 128), F32),
            pltpu.VMEM((8, 128), F32),
            pltpu.SemaphoreType.DMA((NS,)),
            pltpu.SemaphoreType.DMA((NS,)),
            pltpu.SemaphoreType.DMA((ND,)),
            pltpu.SemaphoreType.DMA((ND,)),
        ],
        compiler_params=pltpu.CompilerParams(
            collective_id=1, has_side_effects=True, vmem_limit_bytes=56 * 2**20
        ),
        name="squeeze_excite",
    )(sums, misc, breduce)


def gate_row(depth, dgated, gates, h, keep):
    gate = gates[h : h + 1, :][None]
    pull = gates[2 + h : 3 + h, :][None]
    sig = sigmoid(depth)
    act = depth * sig
    gated = act * gate
    ddepth = (dgated * gate + pull) * (sig + act - act * sig)
    ddepth = jnp.concatenate([ddepth[:9], ddepth[9:] * keep], axis=0)
    return gated, ddepth


def edge_kernel(depth, cp, wp, gates, edge):
    keep = pad_mask()
    for n, r in enumerate((0, 1, ROWS - 2, ROWS - 1)):
        dgated = dot_nt(cp[r], wp[...]).reshape(BLOCK, SUB, 128)
        both = []
        for h in range(2):
            rows = slice(8 * h, 8 * h + 8)
            _, ddepth = gate_row(depth[0, r, :, rows, :], dgated[:, rows, :], gates, h, keep)
            both.append(ddepth)
        edge[0, n] = jnp.concatenate(both, axis=1).astype(BF16)


def edges(depth, cp, wp, gates):
    return pl.pallas_call(
        edge_kernel,
        grid=(TILES,),
        out_shape=jax.ShapeDtypeStruct((TILES, 4, BLOCK, SUB, 128), BF16),
        in_specs=[
            tile_spec(ROWS, BLOCK, SUB, 128),
            whole_spec(ROWS, PIX, C),
            pl.BlockSpec((128, C), lambda t: (t, 0)),
            pl.BlockSpec((8, 128), lambda t: (0, t)),
        ],
        out_specs=tile_spec(4, BLOCK, SUB, 128),
        compiler_params=pltpu.CompilerParams(vmem_limit_bytes=56 * 2**20),
        name="edge_rows",
    )(depth, cp, wp, gates)


def unpermute(value, out, r, back):
    for img in range(2):
        out[img, r] = dot_nn(back[img], value).astype(BF16)


def second_kernel(
    ex, depth, fp, cp, cpt, wp, gates, dd, out, gproj, gdepth, gated_rows, total, acc
):
    keep = pad_mask()
    t = pl.program_id(0)

    def pointwise(r, carry):
        dgated = dot_nt(cp[r], wp[...]).reshape(BLOCK, SUB, 128)
        both, gates_both = [], []
        for h in range(2):
            rows = slice(8 * h, 8 * h + 8)
            gated, ddepth = gate_row(depth[0, r, :, rows, :], dgated[:, rows, :], gates, h, keep)
            both.append(ddepth)
            gates_both.append(gated)
        value = jnp.concatenate(both, axis=1).astype(BF16).astype(F32)
        store_row(dd.at[0], r, value)
        gated_rows[r] = jnp.concatenate(gates_both, axis=1).reshape(PIX, 128).astype(BF16)
        return carry

    lax.fori_loop(0, ROWS, pointwise, 0)

    @pl.when(t == 0)
    def _():
        total[...] = jnp.zeros_like(total)

    def matmuls(r, grad):
        total[r] = total[r] + dot_nn(gated_rows[r], wp[...])
        return grad + dot_nn(cpt[r], gated_rows[r])

    gproj[0] = lax.fori_loop(0, ROWS, matmuls, jnp.zeros((C, 128), F32))

    acc[...] = jnp.zeros_like(acc)

    def taps(r, carry):
        for h in range(2):
            rows = slice(8 * h, 8 * h + 8)
            mine = dd[0, r, 2 : 2 + BLOCK, rows, :]
            for i in range(5):
                source = ex[0, r + i, :, rows, :]
                for j in range(5):
                    k = 5 * i + j
                    acc[k] = acc[k] + jnp.sum(mine * source[j : j + BLOCK], axis=0)
        return carry

    lax.fori_loop(0, ROWS, taps, 0)
    for k in range(25):
        gdepth[0, k : k + 1, :] = jnp.sum(acc[k], axis=0, keepdims=True)
    gdepth[0, 25:32, :] = jnp.zeros((7, 128), F32)

    @pl.when(t == TILES - 1)
    def _():
        back = (one_hot(0, True), one_hot(1, True))

        def finish(r, carry):
            value = (total[r] + fp[r + 2].astype(F32)).astype(BF16)
            unpermute(value, out, r, back)
            return carry

        lax.fori_loop(0, ROWS, finish, 0)


def second(ex, depth, fp, cp, cpt, wp, gates):
    return pl.pallas_call(
        second_kernel,
        grid=(TILES,),
        out_shape=(
            jax.ShapeDtypeStruct((TILES, ROWS, WIDE, SUB, 128), F32),
            jax.ShapeDtypeStruct((IMGS, ROWS, COLS, C), BF16),
            jax.ShapeDtypeStruct((TILES, C, 128), F32),
            jax.ShapeDtypeStruct((TILES, 32, 128), F32),
        ),
        in_specs=[
            tile_spec(HROWS, WIDE, SUB, 128),
            tile_spec(ROWS, BLOCK, SUB, 128),
            whole_spec(HROWS, PIX, C),
            whole_spec(ROWS, PIX, C),
            whole_spec(ROWS, C, PIX),
            pl.BlockSpec((128, C), lambda t: (t, 0)),
            pl.BlockSpec((8, 128), lambda t: (0, t)),
        ],
        out_specs=(
            tile_spec(ROWS, WIDE, SUB, 128),
            whole_spec(IMGS, ROWS, COLS, C),
            tile_spec(C, 128),
            tile_spec(32, 128),
        ),
        scratch_shapes=[
            pltpu.VMEM((ROWS, PIX, 128), BF16),
            pltpu.VMEM((ROWS, PIX, C), F32),
            pltpu.VMEM((25, 8, 128), F32),
        ],
        compiler_params=pltpu.CompilerParams(vmem_limit_bytes=56 * 2**20),
        cost_estimate=pl.CostEstimate(
            flops=4 * 10**9, bytes_accessed=50 * 10**6, transcendentals=3 * 10**6
        ),
        name="phase_b",
    )(ex, depth, fp, cp, cpt, wp, gates)


def third_kernel(dd, above, below, fp, cp, fpt, we, misc, out, gexp, wide_taps, rows_in, dpre, total):
    t = pl.program_id(0)
    spread_taps(misc, wide_taps)
    for n in range(2):
        store_row(rows_in, n, above[0, n].astype(F32))
        store_row(rows_in, ROWS + 2 + n, below[0, n].astype(F32))

    def move(r, carry):
        rows_in[r + 2] = dd[0, r]
        return carry

    lax.fori_loop(0, ROWS, move, 0)

    @pl.when(t == 0)
    def _():
        total[...] = jnp.zeros_like(total)

    def conv(r, carry):
        slope = swish_grad(dot_nt(fp[r + 2], we[...])).reshape(BLOCK, SUB, 128)
        both = []
        for h in range(2):
            both.append(conv_row(rows_in, r, h, wide_taps, True) * slope[:, 8 * h : 8 * h + 8, :])
        dpre[r] = jnp.concatenate(both, axis=1).reshape(PIX, 128).astype(BF16)
        return carry

    lax.fori_loop(0, ROWS, conv, 0)

    def matmuls(r, grad):
        total[r] = total[r] + dot_nn(dpre[r], we[...])
        return grad + dot_nn(fpt[r], dpre[r])

    gexp[0] = lax.fori_loop(0, ROWS, matmuls, jnp.zeros((C, 128), F32))

    @pl.when(t == TILES - 1)
    def _():
        back = (one_hot(0, True), one_hot(1, True))

        def finish(r, carry):
            value = (total[r] + cp[r].astype(F32)).astype(BF16)
            unpermute(value, out, r, back)
            return carry

        lax.fori_loop(0, ROWS, finish, 0)


def third(dd, above, below, fp, cp, fpt, we, misc):
    return pl.pallas_call(
        third_kernel,
        grid=(TILES,),
        out_shape=(
            jax.ShapeDtypeStruct((IMGS, ROWS, COLS, C), BF16),
            jax.ShapeDtypeStruct((TILES, C, 128), F32),
        ),
        in_specs=[
            tile_spec(ROWS, WIDE, SUB, 128),
            tile_spec(2, BLOCK, SUB, 128),
            tile_spec(2, BLOCK, SUB, 128),
            whole_spec(HROWS, PIX, C),
            whole_spec(ROWS, PIX, C),
            whole_spec(ROWS, C, PIX),
            pl.BlockSpec((128, C), lambda t: (t, 0)),
            pl.BlockSpec((32, 128), lambda t: (0, t)),
        ],
        out_specs=(whole_spec(IMGS, ROWS, COLS, C), tile_spec(C, 128)),
        scratch_shapes=[
            pltpu.VMEM((25, 8, 128), F32),
            pltpu.VMEM((HROWS, WIDE, SUB, 128), F32),
            pltpu.VMEM((ROWS, PIX, 128), BF16),
            pltpu.VMEM((ROWS, PIX, C), F32),
        ],
        compiler_params=pltpu.CompilerParams(vmem_limit_bytes=56 * 2**20),
        name="phase_c",
    )(dd, above, below, fp, cp, fpt, we, misc)


CHUNK = 48


def reduce_kernel(
    gexp, gproj, gdepth, out, stack, packed, landed, part, pieces, got, final,
    send, recv, dsend, drecv, fsend, frecv,
):
    me_s, me_d = lax.axis_index("space"), lax.axis_index("dp")
    greet(range(1, NS), range(1, ND))
    for t in range(TILES):
        lanes = slice(128 * t, 128 * (t + 1))
        stack[0:C, lanes] = gexp[t]
        stack[C : 2 * C, lanes] = gproj[t]
        stack[2 * C :, lanes] = gdepth[t]
    packed[...] = stack[...].reshape(NS, CHUNK, CP).astype(BF16)
    copies = []
    for k in range(1, NS):
        target = lax.rem(me_s + k, NS)
        copy = pltpu.make_async_remote_copy(
            src_ref=packed.at[target],
            dst_ref=landed.at[k],
            send_sem=send.at[k],
            recv_sem=recv.at[k],
            device_id=(target, me_d),
            device_id_type=MESH,
        )
        copy.start()
        copies.append(copy)
    start = pl.multiple_of(me_s * CHUNK, CHUNK)
    part[:, 0:CP] = stack[pl.ds(start, CHUNK), :]
    part[:, CP:] = jnp.zeros((CHUNK, 128), F32)
    for k, copy in enumerate(copies):
        copy.wait()
        part[:, 0:CP] = part[:, 0:CP] + landed[k + 1].astype(F32)
    for d in range(ND):
        pieces[d] = part[:, SLOT * d : SLOT * d + 128].astype(BF16)
    copies = []
    for k in range(1, ND):
        target = lax.rem(me_d + k, ND)
        copy = pltpu.make_async_remote_copy(
            src_ref=pieces.at[target],
            dst_ref=got.at[k],
            send_sem=dsend.at[k],
            recv_sem=drecv.at[k],
            device_id=(me_s, target),
            device_id_type=MESH,
        )
        copy.start()
        copies.append(copy)
    total = pieces[me_d].astype(F32)
    for k, copy in enumerate(copies):
        copy.wait()
        total = total + got[k + 1].astype(F32)
    final[me_s] = total
    copies = []
    for k in range(1, NS):
        copy = pltpu.make_async_remote_copy(
            src_ref=final.at[me_s],
            dst_ref=final.at[me_s],
            send_sem=fsend.at[k],
            recv_sem=frecv.at[k],
            device_id=(lax.rem(me_s + k, NS), me_d),
            device_id_type=MESH,
        )
        copy.start()
        copies.append(copy)
    for copy in copies:
        copy.wait()
    out[...] = final[...]


def reduce_grads(gexp, gproj, gdepth):
    return pl.pallas_call(
        reduce_kernel,
        out_shape=jax.ShapeDtypeStruct((NS, CHUNK, 128), F32),
        in_specs=[VMEM] * 3,
        out_specs=VMEM,
        scratch_shapes=[
            pltpu.VMEM((NS * CHUNK, CP), F32),
            pltpu.VMEM((NS, CHUNK, CP), BF16),
            pltpu.VMEM((NS, CHUNK, CP), BF16),
            pltpu.VMEM((CHUNK, CP + 128), F32),
            pltpu.VMEM((ND, CHUNK, 128), BF16),
            pltpu.VMEM((ND, CHUNK, 128), BF16),
            pltpu.VMEM((NS, CHUNK, 128), F32),
            pltpu.SemaphoreType.DMA((NS,)),
            pltpu.SemaphoreType.DMA((NS,)),
            pltpu.SemaphoreType.DMA((ND,)),
            pltpu.SemaphoreType.DMA((ND,)),
            pltpu.SemaphoreType.DMA((NS,)),
            pltpu.SemaphoreType.DMA((NS,)),
        ],
        compiler_params=pltpu.CompilerParams(
            collective_id=2, has_side_effects=True, vmem_limit_bytes=56 * 2**20
        ),
        name="reduce_grads",
    )(gexp, gproj, gdepth)


def on_device(
    features, w_expand, w_depth, w_reduce, b_reduce, w_excite, b_excite, w_project, cotangent
):
    def blank(count):
        return jnp.zeros((PART, count), BF16)

    first_half = jnp.concatenate(
        [w_expand.T, w_depth.reshape(25, PART).T, blank(7), w_reduce, blank(4)], axis=1
    )
    second_half = jnp.concatenate(
        [w_project, w_excite.T, blank(4), b_excite[:, None], blank(31)], axis=1
    )
    pack = jnp.pad(jnp.stack([first_half, second_half]), ((0, 0), (0, 80 - PART), (0, 0)))
    full, top, bottom = gather(pack, features)
    fp, cp, fpt, cpt, we, wp, misc = prep(full, top, bottom, features, cotangent)
    ex, depth, sums = first(fp, cp, we, wp, misc)
    gates, greduce, gexcite, gbias = mid(sums, misc, b_reduce[None, :])
    edge = edges(depth, cp, wp, gates)
    above = lax.ppermute(edge[:, 2:4], "space", [(i, i + 1) for i in range(NS - 1)])
    below = lax.ppermute(edge[:, 0:2], "space", [(i + 1, i) for i in range(NS - 1)])
    dd, output, gproj, gdepth = second(ex, depth, fp, cp, cpt, wp, gates)
    grad_features, gexp = third(dd, above, below, fp, cp, fpt, we, misc)
    grads = reduce_grads(gexp, gproj, gdepth).reshape(NS * CHUNK, 128)
    return (
        output,
        grad_features,
        grads[0:C, 0:PART],
        grads[2 * C : 2 * C + 25, 0:PART].reshape(5, 5, PART),
        greduce[0:PART, 0:SE],
        gexcite[0:SE, 0:PART],
        gbias[0, 0:PART],
        grads[C : 2 * C, 0:PART].T,
        gbias[1, 0:SE],
    )


def solution(mesh):
    return jax.shard_map(
        on_device,
        mesh=mesh,
        in_specs=(
            P("dp", "space", None, None),
            P(None, "dp"),
            P(None, None, "dp"),
            P("dp", None),
            P(),
            P(None, "dp"),
            P("dp"),
            P("dp", None),
            P("dp", "space", None, None),
        ),
        out_specs=(
            P("dp", "space", None, None),
            P("dp", "space", None, None),
            P(None, "dp"),
            P(None, None, "dp"),
            P("dp", None),
            P(None, "dp"),
            P("dp"),
            P("dp", None),
            P(),
        ),
        check_vma=False,
    )
```

```python
import functools

import jax
import jax.numpy as jnp
from jax import lax
from jax.experimental import pallas as pl
from jax.experimental.pallas import tpu as pltpu
from jax.sharding import PartitionSpec as P

F32 = jnp.float32
BF16 = jnp.bfloat16
MESH = pl.DeviceIdType.MESH
HIGH = lax.Precision.HIGHEST

IMGS, ROWS, COLS, C, SE = 2, 12, 100, 176, 44
BLOCK, SUB = 13, 16
PIX = BLOCK * SUB
WIDE = BLOCK + 4
HROWS = ROWS + 4
PART, SLOT = 66, 72
CP = 16 * SLOT
TILES = CP // 128
AREA = 9600.0
NS, ND = 8, 16

VMEM = pl.BlockSpec(memory_space=pltpu.VMEM)
ANY = pl.BlockSpec(memory_space=pl.ANY)


def sigmoid(value):
    return 0.5 * jnp.tanh(0.5 * value) + 0.5


def swish(value):
    return value * sigmoid(value)


def swish_grad(value):
    sig = sigmoid(value)
    act = value * sig
    return sig + act - act * sig


def dot_nt(left, right, precision=None):
    return lax.dot_general(
        left, right, (((1,), (1,)), ((), ())), precision=precision, preferred_element_type=F32
    )


def dot_tn(left, right, precision=None):
    return lax.dot_general(
        left, right, (((0,), (0,)), ((), ())), precision=precision, preferred_element_type=F32
    )


def dot_nn(left, right, precision=None):
    return lax.dot_general(
        left, right, (((1,), (0,)), ((), ())), precision=precision, preferred_element_type=F32
    )


def greet(space_peers, dp_peers):
    me_s, me_d = lax.axis_index("space"), lax.axis_index("dp")
    barrier = pltpu.get_barrier_semaphore()
    for k in space_peers:
        pl.semaphore_signal(
            barrier, inc=1, device_id=(lax.rem(me_s + k, NS), me_d), device_id_type=MESH
        )
    for k in dp_peers:
        pl.semaphore_signal(
            barrier, inc=1, device_id=(me_s, lax.rem(me_d + k, ND)), device_id_type=MESH
        )
    pl.semaphore_wait(barrier, len(space_peers) + len(dp_peers))


def gather_kernel(
    pack, feats, full, top, bottom, send, recv, halo_send, halo_recv, mate_send, mate_recv, own
):
    me_s, me_d = lax.axis_index("space"), lax.axis_index("dp")
    core = lax.rem(me_s, 2)
    mate = me_s + 1 - 2 * core
    barrier = pltpu.get_barrier_semaphore()
    for k in (1, NS - 1):
        pl.semaphore_signal(
            barrier, inc=1, device_id=(lax.rem(me_s + k, NS), me_d), device_id_type=MESH
        )
    for k in range(1, ND):
        pl.semaphore_signal(
            barrier, inc=1, device_id=(me_s, lax.rem(me_d + k, ND)), device_id_type=MESH
        )
    pl.semaphore_wait(barrier, ND + 1)
    copies = []
    for k in range(1, ND):
        copy = pltpu.make_async_remote_copy(
            src_ref=pack.at[core],
            dst_ref=full.at[core, me_d],
            send_sem=send.at[k],
            recv_sem=recv.at[k],
            device_id=(me_s, lax.rem(me_d + k, ND)),
            device_id_type=MESH,
        )
        copy.start()
        copies.append(copy)
    down = pltpu.make_async_remote_copy(
        src_ref=feats.at[:, pl.ds(ROWS - 2, 2)],
        dst_ref=top,
        send_sem=halo_send.at[0],
        recv_sem=halo_recv.at[0],
        device_id=(lax.rem(me_s + 1, NS), me_d),
        device_id_type=MESH,
    )
    up = pltpu.make_async_remote_copy(
        src_ref=feats.at[:, pl.ds(0, 2)],
        dst_ref=bottom,
        send_sem=halo_send.at[1],
        recv_sem=halo_recv.at[1],
        device_id=(lax.rem(me_s + NS - 1, NS), me_d),
        device_id_type=MESH,
    )
    down.start()
    up.start()
    mine = pltpu.make_async_copy(pack.at[core], full.at[core, me_d], own)
    mine.start()
    mine.wait()
    for copy in copies:
        copy.wait()
    share = pltpu.make_async_remote_copy(
        src_ref=full.at[core],
        dst_ref=full.at[core],
        send_sem=mate_send,
        recv_sem=mate_recv,
        device_id=(mate, me_d),
        device_id_type=MESH,
    )
    share.start()
    down.wait()
    up.wait()
    share.wait()


def gather(pack, features):
    return pl.pallas_call(
        gather_kernel,
        out_shape=(
            jax.ShapeDtypeStruct((2, ND, 80, 256), BF16),
            jax.ShapeDtypeStruct((IMGS, 2, COLS, C), BF16),
            jax.ShapeDtypeStruct((IMGS, 2, COLS, C), BF16),
        ),
        in_specs=[ANY, ANY],
        out_specs=(ANY, ANY, ANY),
        scratch_shapes=[
            pltpu.SemaphoreType.DMA((ND,)),
            pltpu.SemaphoreType.DMA((ND,)),
            pltpu.SemaphoreType.DMA((2,)),
            pltpu.SemaphoreType.DMA((2,)),
            pltpu.SemaphoreType.DMA,
            pltpu.SemaphoreType.DMA,
            pltpu.SemaphoreType.DMA,
        ],
        compiler_params=pltpu.CompilerParams(collective_id=0, has_side_effects=True),
        name="gather_weights",
    )(pack, features)


def one_hot(img, transposed):
    shape = (COLS, PIX) if transposed else (PIX, COLS)
    place = lax.broadcasted_iota(jnp.int32, shape, 1 if transposed else 0)
    col = lax.broadcasted_iota(jnp.int32, shape, 0 if transposed else 1)
    wanted = (col % BLOCK) * SUB + img * 8 + col // BLOCK
    return jnp.where(place == wanted, 1.0, 0.0).astype(BF16)


def prep_kernel(
    full, top, bottom, feats, cot, fp, cp, fpt, cpt, we, wp, misc, flat
):
    me_s = lax.axis_index("space")
    for half, out in ((0, we), (1, wp)):
        for d in range(ND):
            flat[d * SLOT : (d + 1) * SLOT, :] = full[half, d, 0:SLOT, :].astype(F32)
        valid = lax.broadcasted_iota(jnp.int32, (CP, 256), 0) % SLOT < PART
        whole = jnp.where(valid, flat[...], 0.0)
        out[...] = whole[:, 0:C].astype(BF16)
        turned = whole[:, 128:256].T
        if half == 0:
            misc[0:32, :] = turned[48:80, :]
            misc[32:80, :] = turned[80:128, :]
        else:
            misc[80:128, :] = turned[48:96, :]
            misc[128:136, :] = turned[96:104, :]
    spread = (one_hot(0, False), one_hot(1, False))
    gather_t = (one_hot(0, True), one_hot(1, True))
    has_top = jnp.where(me_s > 0, 1.0, 0.0)
    has_bottom = jnp.where(me_s < NS - 1, 1.0, 0.0)
    for r in range(2):
        value = dot_nn(spread[0], top[0, r]) + dot_nn(spread[1], top[1, r])
        fp[r] = (value * has_top).astype(BF16)
        value = dot_nn(spread[0], bottom[0, r]) + dot_nn(spread[1], bottom[1, r])
        fp[ROWS + 2 + r] = (value * has_bottom).astype(BF16)

    def row(r, carry):
        for src, dst, shift, dst_t in ((feats, fp, 2, fpt), (cot, cp, 0, cpt)):
            a, b = src[0, r], src[1, r]
            dst[r + shift] = (dot_nn(spread[0], a) + dot_nn(spread[1], b)).astype(BF16)
            dst_t[r] = (dot_tn(a, gather_t[0]) + dot_tn(b, gather_t[1])).astype(BF16)
        return carry

    lax.fori_loop(0, ROWS, row, 0)


def prep(full, top, bottom, features, cotangent):
    return pl.pallas_call(
        prep_kernel,
        out_shape=(
            jax.ShapeDtypeStruct((HROWS, PIX, C), BF16),
            jax.ShapeDtypeStruct((ROWS, PIX, C), BF16),
            jax.ShapeDtypeStruct((ROWS, C, PIX), BF16),
            jax.ShapeDtypeStruct((ROWS, C, PIX), BF16),
            jax.ShapeDtypeStruct((CP, C), BF16),
            jax.ShapeDtypeStruct((CP, C), BF16),
            jax.ShapeDtypeStruct((136, CP), F32),
        ),
        in_specs=[VMEM] * 5,
        out_specs=(VMEM,) * 7,
        scratch_shapes=[pltpu.VMEM((CP, 256), F32)],
        compiler_params=pltpu.CompilerParams(vmem_limit_bytes=56 * 2**20),
        name="prep",
    )(full, top, bottom, features, cotangent)


def spread_taps(taps, wide_taps):
    for k in range(25):
        wide_taps[k] = jnp.broadcast_to(taps[k : k + 1, :], (8, 128))


def edge_columns(value):
    split = value.reshape(BLOCK, 2, 8, 128)
    block = lax.broadcasted_iota(jnp.int32, (2, 2, 8, 128), 2)
    left = jnp.where(block > 0, pltpu.roll(split[BLOCK - 2 :], 1, 2), 0.0)
    right = jnp.where(block < 7, pltpu.roll(split[:2], 7, 2), 0.0)
    return left.reshape(2, SUB, 128), right.reshape(2, SUB, 128)


def store_row(ref, r, value):
    left, right = edge_columns(value)
    ref[r, 0:2] = left
    ref[r, 2 : 2 + BLOCK] = value
    ref[r, 2 + BLOCK :] = right


def conv_row(ref, r, h, wide_taps, flip):
    total = jnp.zeros((BLOCK, 8, 128), F32)
    for i in range(5):
        source = ref[r + i, :, 8 * h : 8 * h + 8, :]
        for j in range(5):
            k = (4 - i) * 5 + 4 - j if flip else i * 5 + j
            total = total + source[j : j + BLOCK] * wide_taps[k][None]
    return total


def pad_mask():
    block = lax.broadcasted_iota(jnp.int32, (4, 8, 128), 1)
    return jnp.where(block < 7, 1.0, 0.0)


def first_kernel(fp, cp, we, wp, misc, ex, depth, sums, wide_taps, pres, dgs):
    spread_taps(misc, wide_taps)
    keep = pad_mask()

    def expand(slot, r):
        store_row(ex.at[0], r, swish(pres[slot]).astype(BF16).astype(F32).reshape(BLOCK, SUB, 128))

    head = fp[0:6].reshape(6 * PIX, C)
    pres[...] = dot_nt(head, we[...]).reshape(6, PIX, 128)
    dgs[0] = dot_nt(cp[0], wp[...])

    def start(r, carry):
        expand(r, r)
        return carry

    lax.fori_loop(0, 5, start, 0)
    pres[1] = pres[5]

    def conv(r, carry):
        pools, grads = list(carry[:2]), list(carry[2:])
        later = lax.rem(r + 1, 2)
        for h in range(2):
            total = conv_row(ex.at[0], r, h, wide_taps, False)
            depth[0, r, :, 8 * h : 8 * h + 8, :] = total
            act = swish(total)
            dgated = dgs[lax.rem(r, 2)].reshape(BLOCK, SUB, 128)[:, 8 * h : 8 * h + 8, :]
            grads[h] = grads[h] + jnp.sum(act * dgated, axis=0)
            pools[h] = pools[h] + jnp.sum(act[:9], axis=0) + jnp.sum(act[9:] * keep, axis=0)
        expand(later, jnp.minimum(r + 5, HROWS - 1))
        pres[lax.rem(r, 2)] = dot_nt(fp[jnp.minimum(r + 6, HROWS - 1)], we[...])
        dgs[later] = dot_nt(cp[jnp.minimum(r + 1, ROWS - 1)], wp[...])
        return (*pools, *grads)

    zero = jnp.zeros((8, 128), F32)
    parts = lax.fori_loop(0, ROWS, conv, (zero,) * 4)
    for k in range(4):
        sums[0, k : k + 1, :] = jnp.sum(parts[k], axis=0, keepdims=True)
    sums[0, 4:8, :] = jnp.zeros((4, 128), F32)


def tile_spec(*shape):
    zeros = (0,) * len(shape)
    return pl.BlockSpec((1, *shape), lambda t: (t, *zeros))


def whole_spec(*shape):
    zeros = (0,) * len(shape)
    return pl.BlockSpec(shape, lambda t: zeros)


def first(fp, cp, we, wp, misc):
    return pl.pallas_call(
        first_kernel,
        grid=(TILES,),
        out_shape=(
            jax.ShapeDtypeStruct((TILES, HROWS, WIDE, SUB, 128), F32),
            jax.ShapeDtypeStruct((TILES, ROWS, BLOCK, SUB, 128), F32),
            jax.ShapeDtypeStruct((TILES, 8, 128), F32),
        ),
        in_specs=[
            whole_spec(HROWS, PIX, C),
            whole_spec(ROWS, PIX, C),
            pl.BlockSpec((128, C), lambda t: (t, 0)),
            pl.BlockSpec((128, C), lambda t: (t, 0)),
            pl.BlockSpec((32, 128), lambda t: (0, t)),
        ],
        out_specs=(
            tile_spec(HROWS, WIDE, SUB, 128),
            tile_spec(ROWS, BLOCK, SUB, 128),
            tile_spec(8, 128),
        ),
        scratch_shapes=[
            pltpu.VMEM((25, 8, 128), F32),
            pltpu.VMEM((6, PIX, 128), F32),
            pltpu.VMEM((2, PIX, 128), F32),
        ],
        compiler_params=pltpu.CompilerParams(vmem_limit_bytes=56 * 2**20),
        name="phase_a",
    )(fp, cp, we, wp, misc)


def mid_kernel(
    sums, misc, breduce, gates, greduce, gexcite, gbias, landed, msgs, got, lanes, vecs,
    send, recv, msend, mrecv,
):
    me_s, me_d = lax.axis_index("space"), lax.axis_index("dp")
    greet(range(1, NS), range(1, ND))
    copies = []
    for k in range(1, NS):
        copy = pltpu.make_async_remote_copy(
            src_ref=sums,
            dst_ref=landed.at[k],
            send_sem=send.at[k],
            recv_sem=recv.at[k],
            device_id=(lax.rem(me_s + k, NS), me_d),
            device_id_type=MESH,
        )
        copy.start()
        copies.append(copy)
    landed[0] = sums[...]
    for copy in copies:
        copy.wait()
    total = landed[lax.rem(me_s, NS)]
    for s in range(1, NS):
        total = total + landed[lax.rem(me_s + NS - s, NS)]
    for t in range(TILES):
        lanes[0:8, 128 * t : 128 * (t + 1)] = total[t]
    lanes[:, CP:] = jnp.zeros((8, 128), F32)
    allsum = lanes[:, 0:CP]
    wr = misc[32 : 32 + SE, :]
    wx = misc[80 : 80 + SE, :]
    bexcite = misc[128:129, :]
    pooled = allsum[0:2] / AREA
    dgate = allsum[2:4]
    squeeze_pre = dot_nt(pooled, wr, HIGH) + breduce[...].astype(F32)
    squeeze = swish(squeeze_pre)
    gate = sigmoid(dot_nn(squeeze, wx, HIGH) + bexcite)
    dlogit = dgate * gate * (1.0 - gate)
    dsq = dot_nt(dlogit, wx, HIGH) * swish_grad(squeeze_pre)
    dpooled = dot_nn(dsq, wr, HIGH)
    gates[0:2, :] = gate
    gates[2:4, :] = dpooled / AREA
    gates[4:8, :] = jnp.zeros((4, CP), F32)
    lanes[0:2, 0:CP] = pooled
    lanes[2:4, 0:CP] = dlogit
    vecs[...] = jnp.zeros((8, 128), F32)
    vecs[4:6, 0:SE] = squeeze
    vecs[6:8, 0:SE] = dsq
    for d in range(ND):
        msgs[d, 0:4, :] = lanes[0:4, SLOT * d : SLOT * d + 128]
        msgs[d, 4:8, :] = vecs[4:8, :]
    copies = []
    for k in range(1, ND):
        target = lax.rem(me_d + k, ND)
        copy = pltpu.make_async_remote_copy(
            src_ref=msgs.at[target],
            dst_ref=got.at[k],
            send_sem=msend.at[k],
            recv_sem=mrecv.at[k],
            device_id=(me_s, target),
            device_id_type=MESH,
        )
        copy.start()
        copies.append(copy)
    got[0] = msgs[me_d]
    for copy in copies:
        copy.wait()
    rows = [got[lax.rem(me_d + ND - d, ND)] for d in range(ND)]
    pool_all = jnp.concatenate([row[0:2] for row in rows], axis=0)
    dlog_all = jnp.concatenate([row[2:4] for row in rows], axis=0)
    sq_all = jnp.concatenate([row[4:6] for row in rows], axis=0)
    dsq_all = jnp.concatenate([row[6:8] for row in rows], axis=0)
    greduce[...] = dot_tn(pool_all, dsq_all, HIGH)
    gexcite[...] = dot_tn(sq_all, dlog_all, HIGH)
    gbias[0:1, :] = jnp.sum(dlog_all, axis=0, keepdims=True)
    gbias[1:2, :] = jnp.sum(dsq_all, axis=0, keepdims=True)
    gbias[2:8, :] = jnp.zeros((6, 128), F32)


def mid(sums, misc, breduce):
    return pl.pallas_call(
        mid_kernel,
        out_shape=(
            jax.ShapeDtypeStruct((8, CP), F32),
            jax.ShapeDtypeStruct((128, 128), F32),
            jax.ShapeDtypeStruct((128, 128), F32),
            jax.ShapeDtypeStruct((8, 128), F32),
        ),
        in_specs=[VMEM] * 3,
        out_specs=(VMEM,) * 4,
        scratch_shapes=[
            pltpu.VMEM((NS, TILES, 8, 128), F32),
            pltpu.VMEM((ND, 8, 128), F32),
            pltpu.VMEM((ND, 8, 128), F32),
            pltpu.VMEM((8, CP + 128), F32),
            pltpu.VMEM((8, 128), F32),
            pltpu.SemaphoreType.DMA((NS,)),
            pltpu.SemaphoreType.DMA((NS,)),
            pltpu.SemaphoreType.DMA((ND,)),
            pltpu.SemaphoreType.DMA((ND,)),
        ],
        compiler_params=pltpu.CompilerParams(
            collective_id=1, has_side_effects=True, vmem_limit_bytes=56 * 2**20
        ),
        name="squeeze_excite",
    )(sums, misc, breduce)


def gate_row(depth, dgated, gates, h, keep):
    gate = gates[h : h + 1, :][None]
    pull = gates[2 + h : 3 + h, :][None]
    sig = sigmoid(depth)
    act = depth * sig
    gated = act * gate
    ddepth = (dgated * gate + pull) * (sig + act - act * sig)
    ddepth = jnp.concatenate([ddepth[:9], ddepth[9:] * keep], axis=0)
    return gated, ddepth


def edge_kernel(depth, cp, wp, gates, edge):
    keep = pad_mask()
    for n, r in enumerate((0, 1, ROWS - 2, ROWS - 1)):
        dgated = dot_nt(cp[r], wp[...]).reshape(BLOCK, SUB, 128)
        both = []
        for h in range(2):
            rows = slice(8 * h, 8 * h + 8)
            _, ddepth = gate_row(depth[0, r, :, rows, :], dgated[:, rows, :], gates, h, keep)
            both.append(ddepth)
        edge[0, n] = jnp.concatenate(both, axis=1).astype(BF16)


def edges(depth, cp, wp, gates):
    return pl.pallas_call(
        edge_kernel,
        grid=(TILES,),
        out_shape=jax.ShapeDtypeStruct((TILES, 4, BLOCK, SUB, 128), BF16),
        in_specs=[
            tile_spec(ROWS, BLOCK, SUB, 128),
            whole_spec(ROWS, PIX, C),
            pl.BlockSpec((128, C), lambda t: (t, 0)),
            pl.BlockSpec((8, 128), lambda t: (0, t)),
        ],
        out_specs=tile_spec(4, BLOCK, SUB, 128),
        compiler_params=pltpu.CompilerParams(vmem_limit_bytes=56 * 2**20),
        name="edge_rows",
    )(depth, cp, wp, gates)


def unpermute(value, out, r, back):
    for img in range(2):
        out[img, r] = dot_nn(back[img], value).astype(BF16)


def second_kernel(
    ex, depth, fp, cp, cpt, wp, gates, dd, out, gproj, gdepth, gated_rows, total, acc, dgs
):
    keep = pad_mask()
    t = pl.program_id(0)

    def pointwise(slot, r):
        dgated = dgs[slot].reshape(BLOCK, SUB, 128)
        both, gates_both = [], []
        for h in range(2):
            rows = slice(8 * h, 8 * h + 8)
            gated, ddepth = gate_row(depth[0, r, :, rows, :], dgated[:, rows, :], gates, h, keep)
            both.append(ddepth)
            gates_both.append(gated)
        value = jnp.concatenate(both, axis=1).astype(BF16).astype(F32)
        store_row(dd.at[0], r, value)
        gated_rows[r] = jnp.concatenate(gates_both, axis=1).reshape(PIX, 128).astype(BF16)

    @pl.when(t == 0)
    def _():
        total[...] = jnp.zeros_like(total)

    acc[...] = jnp.zeros_like(acc)
    gproj[...] = jnp.zeros_like(gproj)
    dgs[...] = dot_nt(cp[0:2].reshape(2 * PIX, C), wp[...]).reshape(2, PIX, 128)
    pointwise(0, 0)

    def taps(r, carry):
        for h in range(2):
            rows = slice(8 * h, 8 * h + 8)
            mine = dd[0, r, 2 : 2 + BLOCK, rows, :]
            for i in range(5):
                source = ex[0, r + i, :, rows, :]
                for j in range(5):
                    k = 5 * i + j
                    acc[k] = acc[k] + jnp.sum(mine * source[j : j + BLOCK], axis=0)
        total[r] = total[r] + dot_nn(gated_rows[r], wp[...])
        gproj[0] = gproj[0] + dot_nn(cpt[r], gated_rows[r])
        pointwise(lax.rem(r + 1, 2), jnp.minimum(r + 1, ROWS - 1))
        dgs[lax.rem(r, 2)] = dot_nt(cp[jnp.minimum(r + 2, ROWS - 1)], wp[...])
        return carry

    lax.fori_loop(0, ROWS, taps, 0)
    for k in range(25):
        gdepth[0, k : k + 1, :] = jnp.sum(acc[k], axis=0, keepdims=True)
    gdepth[0, 25:32, :] = jnp.zeros((7, 128), F32)

    @pl.when(t == TILES - 1)
    def _():
        back = (one_hot(0, True), one_hot(1, True))

        def finish(r, carry):
            value = (total[r] + fp[r + 2].astype(F32)).astype(BF16)
            unpermute(value, out, r, back)
            return carry

        lax.fori_loop(0, ROWS, finish, 0)


def second(ex, depth, fp, cp, cpt, wp, gates):
    return pl.pallas_call(
        second_kernel,
        grid=(TILES,),
        out_shape=(
            jax.ShapeDtypeStruct((TILES, ROWS, WIDE, SUB, 128), F32),
            jax.ShapeDtypeStruct((IMGS, ROWS, COLS, C), BF16),
            jax.ShapeDtypeStruct((TILES, C, 128), F32),
            jax.ShapeDtypeStruct((TILES, 32, 128), F32),
        ),
        in_specs=[
            tile_spec(HROWS, WIDE, SUB, 128),
            tile_spec(ROWS, BLOCK, SUB, 128),
            whole_spec(HROWS, PIX, C),
            whole_spec(ROWS, PIX, C),
            whole_spec(ROWS, C, PIX),
            pl.BlockSpec((128, C), lambda t: (t, 0)),
            pl.BlockSpec((8, 128), lambda t: (0, t)),
        ],
        out_specs=(
            tile_spec(ROWS, WIDE, SUB, 128),
            whole_spec(IMGS, ROWS, COLS, C),
            tile_spec(C, 128),
            tile_spec(32, 128),
        ),
        scratch_shapes=[
            pltpu.VMEM((ROWS, PIX, 128), BF16),
            pltpu.VMEM((ROWS, PIX, C), F32),
            pltpu.VMEM((25, 8, 128), F32),
            pltpu.VMEM((2, PIX, 128), F32),
        ],
        compiler_params=pltpu.CompilerParams(vmem_limit_bytes=56 * 2**20),
        cost_estimate=pl.CostEstimate(
            flops=4 * 10**9, bytes_accessed=50 * 10**6, transcendentals=3 * 10**6
        ),
        name="phase_b",
    )(ex, depth, fp, cp, cpt, wp, gates)


def third_kernel(
    dd, above, below, fp, cp, fpt, we, misc, out, gexp, wide_taps, rows_in, dpre, total, pres
):
    t = pl.program_id(0)
    spread_taps(misc, wide_taps)
    for n in range(2):
        store_row(rows_in, n, above[0, n].astype(F32))
        store_row(rows_in, ROWS + 2 + n, below[0, n].astype(F32))
    for n in range(3):
        rows_in[n + 2] = dd[0, n]

    @pl.when(t == 0)
    def _():
        total[...] = jnp.zeros_like(total)

    gexp[...] = jnp.zeros_like(gexp)
    dpre[0] = jnp.zeros((PIX, 128), BF16)
    pres[0] = dot_nt(fp[2], we[...])

    def matmuls(n, r):
        total[r] = total[r] + dot_nn(dpre[n], we[...])
        gexp[0] = gexp[0] + dot_nn(fpt[r], dpre[n])

    def conv(r, carry):
        both = []
        for h in range(2):
            rows = slice(8 * h, 8 * h + 8)
            slope = swish_grad(pres[lax.rem(r, 2)].reshape(BLOCK, SUB, 128)[:, rows, :])
            both.append(conv_row(rows_in, r, h, wide_taps, True) * slope)
        matmuls(r, jnp.maximum(r - 1, 0))
        dpre[r + 1] = jnp.concatenate(both, axis=1).reshape(PIX, 128).astype(BF16)
        pres[lax.rem(r + 1, 2)] = dot_nt(fp[jnp.minimum(r + 3, ROWS + 1)], we[...])
        later = jnp.minimum(r + 3, ROWS - 1)
        rows_in[later + 2] = dd[0, later]
        return carry

    lax.fori_loop(0, ROWS, conv, 0)
    matmuls(ROWS, ROWS - 1)

    @pl.when(t == TILES - 1)
    def _():
        back = (one_hot(0, True), one_hot(1, True))

        def finish(r, carry):
            value = (total[r] + cp[r].astype(F32)).astype(BF16)
            unpermute(value, out, r, back)
            return carry

        lax.fori_loop(0, ROWS, finish, 0)


def third(dd, above, below, fp, cp, fpt, we, misc):
    return pl.pallas_call(
        third_kernel,
        grid=(TILES,),
        out_shape=(
            jax.ShapeDtypeStruct((IMGS, ROWS, COLS, C), BF16),
            jax.ShapeDtypeStruct((TILES, C, 128), F32),
        ),
        in_specs=[
            tile_spec(ROWS, WIDE, SUB, 128),
            tile_spec(2, BLOCK, SUB, 128),
            tile_spec(2, BLOCK, SUB, 128),
            whole_spec(HROWS, PIX, C),
            whole_spec(ROWS, PIX, C),
            whole_spec(ROWS, C, PIX),
            pl.BlockSpec((128, C), lambda t: (t, 0)),
            pl.BlockSpec((32, 128), lambda t: (0, t)),
        ],
        out_specs=(whole_spec(IMGS, ROWS, COLS, C), tile_spec(C, 128)),
        scratch_shapes=[
            pltpu.VMEM((25, 8, 128), F32),
            pltpu.VMEM((HROWS, WIDE, SUB, 128), F32),
            pltpu.VMEM((ROWS + 1, PIX, 128), BF16),
            pltpu.VMEM((ROWS, PIX, C), F32),
            pltpu.VMEM((2, PIX, 128), F32),
        ],
        compiler_params=pltpu.CompilerParams(vmem_limit_bytes=56 * 2**20),
        name="phase_c",
    )(dd, above, below, fp, cp, fpt, we, misc)


CHUNK = 48


def reduce_kernel(
    gexp, gproj, gdepth, out, stack, packed, landed, part, pieces, got, final,
    send, recv, dsend, drecv, fsend, frecv,
):
    me_s, me_d = lax.axis_index("space"), lax.axis_index("dp")
    greet(range(1, NS), range(1, ND))
    for t in range(TILES):
        lanes = slice(128 * t, 128 * (t + 1))
        stack[0:C, lanes] = gexp[t]
        stack[C : 2 * C, lanes] = gproj[t]
        stack[2 * C :, lanes] = gdepth[t]
    packed[...] = stack[...].reshape(NS, CHUNK, CP).astype(BF16)
    copies = []
    for k in range(1, NS):
        target = lax.rem(me_s + k, NS)
        copy = pltpu.make_async_remote_copy(
            src_ref=packed.at[target],
            dst_ref=landed.at[k],
            send_sem=send.at[k],
            recv_sem=recv.at[k],
            device_id=(target, me_d),
            device_id_type=MESH,
        )
        copy.start()
        copies.append(copy)
    start = pl.multiple_of(me_s * CHUNK, CHUNK)
    part[:, 0:CP] = stack[pl.ds(start, CHUNK), :]
    part[:, CP:] = jnp.zeros((CHUNK, 128), F32)
    for k, copy in enumerate(copies):
        copy.wait()
        part[:, 0:CP] = part[:, 0:CP] + landed[k + 1].astype(F32)
    for d in range(ND):
        pieces[d] = part[:, SLOT * d : SLOT * d + 128].astype(BF16)
    copies = []
    for k in range(1, ND):
        target = lax.rem(me_d + k, ND)
        copy = pltpu.make_async_remote_copy(
            src_ref=pieces.at[target],
            dst_ref=got.at[k],
            send_sem=dsend.at[k],
            recv_sem=drecv.at[k],
            device_id=(me_s, target),
            device_id_type=MESH,
        )
        copy.start()
        copies.append(copy)
    total = pieces[me_d].astype(F32)
    for k, copy in enumerate(copies):
        copy.wait()
        total = total + got[k + 1].astype(F32)
    final[me_s] = total
    copies = []
    for k in range(1, NS):
        copy = pltpu.make_async_remote_copy(
            src_ref=final.at[me_s],
            dst_ref=final.at[me_s],
            send_sem=fsend.at[k],
            recv_sem=frecv.at[k],
            device_id=(lax.rem(me_s + k, NS), me_d),
            device_id_type=MESH,
        )
        copy.start()
        copies.append(copy)
    for copy in copies:
        copy.wait()
    out[...] = final[...]


def reduce_grads(gexp, gproj, gdepth):
    return pl.pallas_call(
        reduce_kernel,
        out_shape=jax.ShapeDtypeStruct((NS, CHUNK, 128), F32),
        in_specs=[VMEM] * 3,
        out_specs=VMEM,
        scratch_shapes=[
            pltpu.VMEM((NS * CHUNK, CP), F32),
            pltpu.VMEM((NS, CHUNK, CP), BF16),
            pltpu.VMEM((NS, CHUNK, CP), BF16),
            pltpu.VMEM((CHUNK, CP + 128), F32),
            pltpu.VMEM((ND, CHUNK, 128), BF16),
            pltpu.VMEM((ND, CHUNK, 128), BF16),
            pltpu.VMEM((NS, CHUNK, 128), F32),
            pltpu.SemaphoreType.DMA((NS,)),
            pltpu.SemaphoreType.DMA((NS,)),
            pltpu.SemaphoreType.DMA((ND,)),
            pltpu.SemaphoreType.DMA((ND,)),
            pltpu.SemaphoreType.DMA((NS,)),
            pltpu.SemaphoreType.DMA((NS,)),
        ],
        compiler_params=pltpu.CompilerParams(
            collective_id=2, has_side_effects=True, vmem_limit_bytes=56 * 2**20
        ),
        name="reduce_grads",
    )(gexp, gproj, gdepth)


def on_device(
    features, w_expand, w_depth, w_reduce, b_reduce, w_excite, b_excite, w_project, cotangent
):
    def blank(count):
        return jnp.zeros((PART, count), BF16)

    first_half = jnp.concatenate(
        [w_expand.T, w_depth.reshape(25, PART).T, blank(7), w_reduce, blank(4)], axis=1
    )
    second_half = jnp.concatenate(
        [w_project, w_excite.T, blank(4), b_excite[:, None], blank(31)], axis=1
    )
    pack = jnp.pad(jnp.stack([first_half, second_half]), ((0, 0), (0, 80 - PART), (0, 0)))
    full, top, bottom = gather(pack, features)
    fp, cp, fpt, cpt, we, wp, misc = prep(full, top, bottom, features, cotangent)
    ex, depth, sums = first(fp, cp, we, wp, misc)
    gates, greduce, gexcite, gbias = mid(sums, misc, b_reduce[None, :])
    edge = edges(depth, cp, wp, gates)
    above = lax.ppermute(edge[:, 2:4], "space", [(i, i + 1) for i in range(NS - 1)])
    below = lax.ppermute(edge[:, 0:2], "space", [(i + 1, i) for i in range(NS - 1)])
    dd, output, gproj, gdepth = second(ex, depth, fp, cp, cpt, wp, gates)
    grad_features, gexp = third(dd, above, below, fp, cp, fpt, we, misc)
    grads = reduce_grads(gexp, gproj, gdepth).reshape(NS * CHUNK, 128)
    return (
        output,
        grad_features,
        grads[0:C, 0:PART],
        grads[2 * C : 2 * C + 25, 0:PART].reshape(5, 5, PART),
        greduce[0:PART, 0:SE],
        gexcite[0:SE, 0:PART],
        gbias[0, 0:PART],
        grads[C : 2 * C, 0:PART].T,
        gbias[1, 0:SE],
    )


def solution(mesh):
    return jax.shard_map(
        on_device,
        mesh=mesh,
        in_specs=(
            P("dp", "space", None, None),
            P(None, "dp"),
            P(None, None, "dp"),
            P("dp", None),
            P(),
            P(None, "dp"),
            P("dp"),
            P("dp", None),
            P("dp", "space", None, None),
        ),
        out_specs=(
            P("dp", "space", None, None),
            P("dp", "space", None, None),
            P(None, "dp"),
            P(None, None, "dp"),
            P("dp", None),
            P(None, "dp"),
            P("dp"),
            P("dp", None),
            P(),
        ),
        check_vma=False,
    )
```

```python
import functools

import jax
import jax.numpy as jnp
from jax import lax
from jax.experimental import pallas as pl
from jax.experimental.pallas import tpu as pltpu
from jax.sharding import PartitionSpec as P

F32 = jnp.float32
BF16 = jnp.bfloat16
MESH = pl.DeviceIdType.MESH
HIGH = lax.Precision.HIGHEST

IMGS, ROWS, COLS, C, SE = 2, 12, 100, 176, 44
BLOCK, SUB = 13, 16
PIX = BLOCK * SUB
WIDE = BLOCK + 4
HROWS = ROWS + 4
PART, SLOT = 66, 72
CP = 16 * SLOT
TILES = CP // 128
AREA = 9600.0
NS, ND = 8, 16

VMEM = pl.BlockSpec(memory_space=pltpu.VMEM)
ANY = pl.BlockSpec(memory_space=pl.ANY)


def sigmoid(value):
    return 0.5 * jnp.tanh(0.5 * value) + 0.5


def swish(value):
    return value * sigmoid(value)


def swish_grad(value):
    sig = sigmoid(value)
    act = value * sig
    return sig + act - act * sig


def dot_nt(left, right, precision=None):
    return lax.dot_general(
        left, right, (((1,), (1,)), ((), ())), precision=precision, preferred_element_type=F32
    )


def dot_tn(left, right, precision=None):
    return lax.dot_general(
        left, right, (((0,), (0,)), ((), ())), precision=precision, preferred_element_type=F32
    )


def dot_nn(left, right, precision=None):
    return lax.dot_general(
        left, right, (((1,), (0,)), ((), ())), precision=precision, preferred_element_type=F32
    )


def greet(space_peers, dp_peers):
    me_s, me_d = lax.axis_index("space"), lax.axis_index("dp")
    barrier = pltpu.get_barrier_semaphore()
    for k in space_peers:
        pl.semaphore_signal(
            barrier, inc=1, device_id=(lax.rem(me_s + k, NS), me_d), device_id_type=MESH
        )
    for k in dp_peers:
        pl.semaphore_signal(
            barrier, inc=1, device_id=(me_s, lax.rem(me_d + k, ND)), device_id_type=MESH
        )
    pl.semaphore_wait(barrier, len(space_peers) + len(dp_peers))


def one_hot(img, transposed):
    shape = (COLS, PIX) if transposed else (PIX, COLS)
    place = lax.broadcasted_iota(jnp.int32, shape, 1 if transposed else 0)
    col = lax.broadcasted_iota(jnp.int32, shape, 0 if transposed else 1)
    wanted = (col % BLOCK) * SUB + img * 8 + col // BLOCK
    return jnp.where(place == wanted, 1.0, 0.0).astype(BF16)


def gather_kernel(
    wet, wpr, taps, wrt, wx, bex, feats, cot,
    fp, cp, fpt, cpt, we, wp, misc,
    stage, pack, full, top, bottom, flat,
    send, recv, halo_send, halo_recv, mate_send, mate_recv,
):
    me_s, me_d = lax.axis_index("space"), lax.axis_index("dp")
    core = lax.rem(me_s, 2)
    mate = me_s + 1 - 2 * core
    barrier = pltpu.get_barrier_semaphore()
    for k in (1, NS - 1):
        pl.semaphore_signal(
            barrier, inc=1, device_id=(lax.rem(me_s + k, NS), me_d), device_id_type=MESH
        )
    for k in range(1, ND):
        pl.semaphore_signal(
            barrier, inc=1, device_id=(me_s, lax.rem(me_d + k, ND)), device_id_type=MESH
        )
    stage[...] = jnp.zeros_like(stage)
    stage[0, 0:PART, 0:C] = wet[...].astype(F32)
    stage[1, 0:PART, 0:C] = wpr[...].astype(F32)
    side = slice(C, C + PART)
    stage[0, 0:25, side] = taps[...].astype(F32)
    stage[0, 32 : 32 + SE, side] = wrt[...].astype(F32)
    stage[1, 0:SE, side] = wx[...].astype(F32)
    stage[1, 48:49, side] = bex[...].astype(F32)
    pack[...] = stage[...].astype(BF16)
    pl.semaphore_wait(barrier, ND + 1)
    copies = []
    for k in range(1, ND):
        copy = pltpu.make_async_remote_copy(
            src_ref=pack.at[core],
            dst_ref=full.at[core, me_d],
            send_sem=send.at[k],
            recv_sem=recv.at[k],
            device_id=(me_s, lax.rem(me_d + k, ND)),
            device_id_type=MESH,
        )
        copy.start()
        copies.append(copy)
    down = pltpu.make_async_remote_copy(
        src_ref=feats.at[:, pl.ds(ROWS - 2, 2)],
        dst_ref=top,
        send_sem=halo_send.at[0],
        recv_sem=halo_recv.at[0],
        device_id=(lax.rem(me_s + 1, NS), me_d),
        device_id_type=MESH,
    )
    up = pltpu.make_async_remote_copy(
        src_ref=feats.at[:, pl.ds(0, 2)],
        dst_ref=bottom,
        send_sem=halo_send.at[1],
        recv_sem=halo_recv.at[1],
        device_id=(lax.rem(me_s + NS - 1, NS), me_d),
        device_id_type=MESH,
    )
    down.start()
    up.start()
    full[core, me_d] = pack[core]
    spread = (one_hot(0, False), one_hot(1, False))
    gather_t = (one_hot(0, True), one_hot(1, True))

    def row(r, carry):
        for src, dst, shift in ((feats, fp, 2), (cot, cp, 0)):
            a, b = src[0, r], src[1, r]
            dst[r + shift] = (dot_nt(spread[0], a) + dot_nt(spread[1], b)).astype(BF16)
        return carry

    lax.fori_loop(0, ROWS, row, 0)
    for r in range(ROWS):
        for src, dst in ((feats, fpt), (cot, cpt)):
            value = dot_nn(src[0, r], gather_t[0]) + dot_nn(src[1, r], gather_t[1])
            dst[:, PIX * r : PIX * (r + 1)] = value.astype(BF16)
    for copy in copies:
        copy.wait()
    share = pltpu.make_async_remote_copy(
        src_ref=full.at[core],
        dst_ref=full.at[core],
        send_sem=mate_send,
        recv_sem=mate_recv,
        device_id=(mate, me_d),
        device_id_type=MESH,
    )
    share.start()
    down.wait()
    up.wait()
    has_top = jnp.where(me_s > 0, 1.0, 0.0)
    has_bottom = jnp.where(me_s < NS - 1, 1.0, 0.0)
    for r in range(2):
        value = dot_nt(spread[0], top[0, r]) + dot_nt(spread[1], top[1, r])
        fp[r] = (value * has_top).astype(BF16)
        value = dot_nt(spread[0], bottom[0, r]) + dot_nt(spread[1], bottom[1, r])
        fp[ROWS + 2 + r] = (value * has_bottom).astype(BF16)
    share.wait()
    for half, out in ((0, we), (1, wp)):
        for d in range(ND):
            part = full[half, d].astype(F32)
            flat[d * SLOT : (d + 1) * SLOT, :] = part[0:SLOT, 0:C]
            lanes = slice(d * SLOT, (d + 1) * SLOT)
            if half == 0:
                misc[0:80, lanes] = part[:, C : C + SLOT]
            else:
                misc[80:136, lanes] = part[0:56, C : C + SLOT]
        out[...] = flat[...].astype(BF16)


def gather(wet, wpr, taps, wrt, wx, bex, feats, cot):
    return pl.pallas_call(
        gather_kernel,
        out_shape=(
            jax.ShapeDtypeStruct((HROWS, PIX, C), BF16),
            jax.ShapeDtypeStruct((ROWS, PIX, C), BF16),
            jax.ShapeDtypeStruct((C, ROWS * PIX), BF16),
            jax.ShapeDtypeStruct((C, ROWS * PIX), BF16),
            jax.ShapeDtypeStruct((CP, C), BF16),
            jax.ShapeDtypeStruct((CP, C), BF16),
            jax.ShapeDtypeStruct((136, CP), F32),
        ),
        in_specs=[VMEM] * 8,
        out_specs=(VMEM,) * 7,
        scratch_shapes=[
            pltpu.VMEM((2, 80, 256), F32),
            pltpu.VMEM((2, 80, 256), BF16),
            pltpu.VMEM((2, ND, 80, 256), BF16),
            pltpu.VMEM((IMGS, 2, C, COLS), BF16),
            pltpu.VMEM((IMGS, 2, C, COLS), BF16),
            pltpu.VMEM((CP, C), F32),
            pltpu.SemaphoreType.DMA((ND,)),
            pltpu.SemaphoreType.DMA((ND,)),
            pltpu.SemaphoreType.DMA((2,)),
            pltpu.SemaphoreType.DMA((2,)),
            pltpu.SemaphoreType.DMA,
            pltpu.SemaphoreType.DMA,
        ],
        compiler_params=pltpu.CompilerParams(
            collective_id=0, has_side_effects=True, vmem_limit_bytes=56 * 2**20
        ),
        name="gather_weights",
    )(wet, wpr, taps, wrt, wx, bex, feats, cot)


def spread_taps(taps, wide_taps):
    for k in range(25):
        wide_taps[k] = jnp.broadcast_to(taps[k : k + 1, :], (8, 128))


def edge_columns(value):
    split = value.reshape(BLOCK, 2, 8, 128)
    block = lax.broadcasted_iota(jnp.int32, (2, 2, 8, 128), 2)
    left = jnp.where(block > 0, pltpu.roll(split[BLOCK - 2 :], 1, 2), 0.0)
    right = jnp.where(block < 7, pltpu.roll(split[:2], 7, 2), 0.0)
    return left.reshape(2, SUB, 128), right.reshape(2, SUB, 128)


def store_row(ref, r, value):
    left, right = edge_columns(value)
    ref[r, 0:2] = left
    ref[r, 2 : 2 + BLOCK] = value
    ref[r, 2 + BLOCK :] = right


def conv_row(ref, r, h, wide_taps, flip):
    total = jnp.zeros((BLOCK, 8, 128), F32)
    for i in range(5):
        source = ref[r + i, :, 8 * h : 8 * h + 8, :]
        for j in range(5):
            k = (4 - i) * 5 + 4 - j if flip else i * 5 + j
            total = total + source[j : j + BLOCK] * wide_taps[k][None]
    return total


def pad_mask():
    block = lax.broadcasted_iota(jnp.int32, (4, 8, 128), 1)
    return jnp.where(block < 7, 1.0, 0.0)


def first_kernel(fp, cp, we, wp, misc, saved, depth, sums, wide_taps, ex, dgs):
    spread_taps(misc, wide_taps)
    keep = pad_mask()

    def expand(q, carry):
        pre = dot_nt(fp[pl.ds(8 * q, 8)].reshape(8 * PIX, C), we[...])
        value = swish(pre).astype(BF16).astype(F32).reshape(8, BLOCK, SUB, 128)
        for n in range(8):
            store_row(ex, 8 * q + n, value[n])
        return carry

    lax.fori_loop(0, 2, expand, 0)
    cot_matmul(cp, wp, dgs)

    def conv(r, carry):
        pools, grads = list(carry[:2]), list(carry[2:])
        for h in range(2):
            total = conv_row(ex, r, h, wide_taps, False)
            depth[0, r, :, 8 * h : 8 * h + 8, :] = total
            act = swish(total)
            dgated = dgs[r, :, 8 * h : 8 * h + 8, :]
            grads[h] = grads[h] + jnp.sum(act * dgated, axis=0)
            pools[h] = pools[h] + jnp.sum(act[:9], axis=0) + jnp.sum(act[9:] * keep, axis=0)
        saved[0, r] = ex[r].astype(BF16)
        return (*pools, *grads)

    zero = jnp.zeros((8, 128), F32)
    parts = lax.fori_loop(0, ROWS, conv, (zero,) * 4)
    for r in range(ROWS, HROWS):
        saved[0, r] = ex[r].astype(BF16)
    for k in range(4):
        sums[0, k : k + 1, :] = jnp.sum(parts[k], axis=0, keepdims=True)
    sums[0, 4:8, :] = jnp.zeros((4, 128), F32)


def cot_matmul(cp, wp, dgs):
    def chunk(q, carry):
        rows = pl.ds(6 * q, 6)
        dgs[rows] = dot_nt(cp[rows].reshape(6 * PIX, C), wp[...]).reshape(6, BLOCK, SUB, 128)
        return carry

    lax.fori_loop(0, 2, chunk, 0)


def tile_spec(*shape):
    zeros = (0,) * len(shape)
    return pl.BlockSpec((1, *shape), lambda t: (t, *zeros))


def whole_spec(*shape):
    zeros = (0,) * len(shape)
    return pl.BlockSpec(shape, lambda t: zeros)


def first(fp, cp, we, wp, misc):
    return pl.pallas_call(
        first_kernel,
        grid=(TILES,),
        out_shape=(
            jax.ShapeDtypeStruct((TILES, HROWS, WIDE, SUB, 128), BF16),
            jax.ShapeDtypeStruct((TILES, ROWS, BLOCK, SUB, 128), F32),
            jax.ShapeDtypeStruct((TILES, 8, 128), F32),
        ),
        in_specs=[
            whole_spec(HROWS, PIX, C),
            whole_spec(ROWS, PIX, C),
            pl.BlockSpec((128, C), lambda t: (t, 0)),
            pl.BlockSpec((128, C), lambda t: (t, 0)),
            pl.BlockSpec((32, 128), lambda t: (0, t)),
        ],
        out_specs=(
            tile_spec(HROWS, WIDE, SUB, 128),
            tile_spec(ROWS, BLOCK, SUB, 128),
            tile_spec(8, 128),
        ),
        scratch_shapes=[
            pltpu.VMEM((25, 8, 128), F32),
            pltpu.VMEM((HROWS, WIDE, SUB, 128), F32),
            pltpu.VMEM((ROWS, BLOCK, SUB, 128), F32),
        ],
        compiler_params=pltpu.CompilerParams(vmem_limit_bytes=56 * 2**20),
        name="phase_a",
    )(fp, cp, we, wp, misc)


def mid_kernel(sums, misc, breduce, gates, msgs, packed, landed, lanes, vecs, send, recv):
    me_s, me_d = lax.axis_index("space"), lax.axis_index("dp")
    greet(range(1, NS), ())
    packed[...] = jnp.zeros_like(packed)
    for t in range(TILES):
        packed[t // 2, 4 * (t % 2) : 4 * (t % 2) + 4, :] = sums[t, 0:4, :]
    copies = []
    for k in range(1, NS):
        copy = pltpu.make_async_remote_copy(
            src_ref=packed,
            dst_ref=landed.at[k],
            send_sem=send.at[k],
            recv_sem=recv.at[k],
            device_id=(lax.rem(me_s + k, NS), me_d),
            device_id_type=MESH,
        )
        copy.start()
        copies.append(copy)
    landed[0] = packed[...]
    for copy in copies:
        copy.wait()
    total = landed[lax.rem(me_s, NS)]
    for s in range(1, NS):
        total = total + landed[lax.rem(me_s + NS - s, NS)]
    for t in range(TILES):
        lanes[0:4, 128 * t : 128 * (t + 1)] = total[t // 2, 4 * (t % 2) : 4 * (t % 2) + 4]
    lanes[:, CP:] = jnp.zeros((8, 128), F32)
    wr = misc[32 : 32 + SE, :]
    wx = misc[80 : 80 + SE, :]
    bexcite = misc[128:129, :]
    pooled = lanes[0:2, 0:CP] / AREA
    dgate = lanes[2:4, 0:CP]
    squeeze_pre = dot_nt(pooled, wr, HIGH) + breduce[...].astype(F32)
    squeeze = swish(squeeze_pre)
    gate = sigmoid(dot_nn(squeeze, wx, HIGH) + bexcite)
    dlogit = dgate * gate * (1.0 - gate)
    dsq = dot_nt(dlogit, wx, HIGH) * swish_grad(squeeze_pre)
    dpooled = dot_nn(dsq, wr, HIGH)
    gates[0:2, :] = gate
    gates[2:4, :] = dpooled / AREA
    gates[4:8, :] = jnp.zeros((4, CP), F32)
    lanes[0:2, 0:CP] = pooled
    lanes[2:4, 0:CP] = dlogit
    vecs[...] = jnp.zeros((8, 128), F32)
    vecs[4:6, 0:SE] = squeeze
    vecs[6:8, 0:SE] = dsq
    for d in range(ND):
        msgs[d, 0:4, :] = lanes[0:4, SLOT * d : SLOT * d + 128]
        msgs[d, 4:8, :] = vecs[4:8, :]


def mid(sums, misc, breduce):
    return pl.pallas_call(
        mid_kernel,
        out_shape=(
            jax.ShapeDtypeStruct((8, CP), F32),
            jax.ShapeDtypeStruct((ND, 8, 128), F32),
        ),
        in_specs=[VMEM] * 3,
        out_specs=(VMEM,) * 2,
        scratch_shapes=[
            pltpu.VMEM((5, 8, 128), F32),
            pltpu.VMEM((NS, 5, 8, 128), F32),
            pltpu.VMEM((8, CP + 128), F32),
            pltpu.VMEM((8, 128), F32),
            pltpu.SemaphoreType.DMA((NS,)),
            pltpu.SemaphoreType.DMA((NS,)),
        ],
        compiler_params=pltpu.CompilerParams(
            collective_id=1, has_side_effects=True, vmem_limit_bytes=56 * 2**20
        ),
        name="squeeze_excite",
    )(sums, misc, breduce)


def gate_row(depth, dgated, gates, h, keep):
    gate = gates[h : h + 1, :][None]
    pull = gates[2 + h : 3 + h, :][None]
    sig = sigmoid(depth)
    act = depth * sig
    gated = act * gate
    ddepth = (dgated * gate + pull) * (sig + act - act * sig)
    ddepth = jnp.concatenate([ddepth[:9], ddepth[9:] * keep], axis=0)
    return gated, ddepth


def unpermute(value, out, r):
    for img in range(2):
        out[img, r] = dot_tn(value, one_hot(img, False)).astype(BF16)


def all_channels(rows_in, weights, base, shift, turned, out, grad):
    def chunk(q, carry):
        block = rows_in[pl.ds(pl.multiple_of(4 * PIX * q, 4 * PIX), 4 * PIX), :]
        product = dot_nn(block, weights[...]).reshape(4, PIX, C)
        for n in range(4):
            value = product[n] + base[4 * q + n + shift].astype(F32)
            unpermute(value.astype(BF16), out, 4 * q + n)
        return carry

    lax.fori_loop(0, 3, chunk, 0)

    def lanes(q, carry):
        span = pl.ds(pl.multiple_of(384 * q, 128), 384)
        grad[:, span] = dot_nn(turned[...], rows_in[:, span])
        return carry

    lax.fori_loop(0, 3, lanes, 0)


def second_kernel(
    depth, fp, cp, cpt, wp, gates, dd, upper, lower, out, gproj, gated_rows, dgs
):
    keep = pad_mask()
    t = pl.program_id(0)
    lane = pl.ds(pl.multiple_of(128 * t, 128), 128)
    cot_matmul(cp, wp.at[lane], dgs)

    def pointwise(r, carry):
        both, gates_both = [], []
        for h in range(2):
            rows = slice(8 * h, 8 * h + 8)
            gated, ddepth = gate_row(depth[0, r, :, rows, :], dgs[r, :, rows, :], gates, h, keep)
            both.append(ddepth)
            gates_both.append(gated)
        dd[0, r] = jnp.concatenate(both, axis=1).astype(BF16)
        gated_rows[pl.ds(pl.multiple_of(r * PIX, PIX), PIX), lane] = (
            jnp.concatenate(gates_both, axis=1).reshape(PIX, 128).astype(BF16)
        )
        return carry

    lax.fori_loop(0, ROWS, pointwise, 0)
    upper[0] = dd[0, 0:2]
    lower[0] = dd[0, ROWS - 2 :]

    @pl.when(t == TILES - 1)
    def _():
        all_channels(gated_rows, wp, fp, 2, cpt, out, gproj)


def second(depth, fp, cp, cpt, wp, gates):
    return pl.pallas_call(
        second_kernel,
        grid=(TILES,),
        out_shape=(
            jax.ShapeDtypeStruct((TILES, ROWS, BLOCK, SUB, 128), BF16),
            jax.ShapeDtypeStruct((TILES, 2, BLOCK, SUB, 128), BF16),
            jax.ShapeDtypeStruct((TILES, 2, BLOCK, SUB, 128), BF16),
            jax.ShapeDtypeStruct((IMGS, ROWS, C, COLS), BF16),
            jax.ShapeDtypeStruct((C, CP), F32),
        ),
        in_specs=[
            tile_spec(ROWS, BLOCK, SUB, 128),
            whole_spec(HROWS, PIX, C),
            whole_spec(ROWS, PIX, C),
            whole_spec(C, ROWS * PIX),
            whole_spec(CP, C),
            pl.BlockSpec((8, 128), lambda t: (0, t)),
        ],
        out_specs=(
            tile_spec(ROWS, BLOCK, SUB, 128),
            tile_spec(2, BLOCK, SUB, 128),
            tile_spec(2, BLOCK, SUB, 128),
            whole_spec(IMGS, ROWS, C, COLS),
            whole_spec(C, CP),
        ),
        scratch_shapes=[
            pltpu.VMEM((ROWS * PIX, CP), BF16),
            pltpu.VMEM((ROWS, BLOCK, SUB, 128), F32),
        ],
        compiler_params=pltpu.CompilerParams(vmem_limit_bytes=56 * 2**20),
        name="phase_b",
    )(depth, fp, cp, cpt, wp, gates)


def tap_kernel(ex, dd, gdepth, acc):
    acc[...] = jnp.zeros_like(acc)

    def taps(r, carry):
        for h in range(2):
            rows = slice(8 * h, 8 * h + 8)
            mine = dd[0, r, :, :, :].astype(F32)[:, rows, :]
            for i in range(5):
                source = ex[0, r + i].astype(F32)[:, rows, :]
                for j in range(5):
                    k = 5 * i + j
                    acc[k] = acc[k] + jnp.sum(mine * source[j : j + BLOCK], axis=0)
        return carry

    lax.fori_loop(0, ROWS, taps, 0)
    for k in range(25):
        gdepth[0, k : k + 1, :] = jnp.sum(acc[k], axis=0, keepdims=True)
    gdepth[0, 25:32, :] = jnp.zeros((7, 128), F32)


def tap_grads(ex, dd):
    return pl.pallas_call(
        tap_kernel,
        grid=(TILES,),
        out_shape=jax.ShapeDtypeStruct((TILES, 32, 128), F32),
        in_specs=[tile_spec(HROWS, WIDE, SUB, 128), tile_spec(ROWS, BLOCK, SUB, 128)],
        out_specs=tile_spec(32, 128),
        scratch_shapes=[pltpu.VMEM((25, 8, 128), F32)],
        compiler_params=pltpu.CompilerParams(vmem_limit_bytes=56 * 2**20),
        cost_estimate=pl.CostEstimate(
            flops=4 * 10**9, bytes_accessed=50 * 10**6, transcendentals=3 * 10**6
        ),
        name="tap_grads",
    )(ex, dd)


def third_kernel(
    dd, above, below, fp, cp, fpt, we, misc, out, gexp, wide_taps, rows_in, dpre, pres
):
    t = pl.program_id(0)
    lane = pl.ds(pl.multiple_of(128 * t, 128), 128)
    spread_taps(misc, wide_taps)
    for n in range(2):
        store_row(rows_in, n, above[0, n].astype(F32))
        store_row(rows_in, ROWS + 2 + n, below[0, n].astype(F32))

    def spread(r, carry):
        store_row(rows_in, r + 2, dd[0, r].astype(F32))
        return carry

    lax.fori_loop(0, ROWS, spread, 0)

    def chunk(q, carry):
        pre = dot_nt(fp[pl.ds(6 * q + 2, 6)].reshape(6 * PIX, C), we[lane, :])
        pres[pl.ds(6 * q, 6)] = swish_grad(pre).reshape(6, BLOCK, SUB, 128)
        return carry

    lax.fori_loop(0, 2, chunk, 0)

    def conv(r, carry):
        both = []
        for h in range(2):
            slope = pres[r, :, 8 * h : 8 * h + 8, :]
            both.append(conv_row(rows_in, r, h, wide_taps, True) * slope)
        dpre[pl.ds(pl.multiple_of(r * PIX, PIX), PIX), lane] = (
            jnp.concatenate(both, axis=1).reshape(PIX, 128).astype(BF16)
        )
        return carry

    lax.fori_loop(0, ROWS, conv, 0)

    @pl.when(t == TILES - 1)
    def _():
        all_channels(dpre, we, cp, 0, fpt, out, gexp)


def third(dd, above, below, fp, cp, fpt, we, misc):
    return pl.pallas_call(
        third_kernel,
        grid=(TILES,),
        out_shape=(
            jax.ShapeDtypeStruct((IMGS, ROWS, C, COLS), BF16),
            jax.ShapeDtypeStruct((C, CP), F32),
        ),
        in_specs=[
            tile_spec(ROWS, BLOCK, SUB, 128),
            tile_spec(2, BLOCK, SUB, 128),
            tile_spec(2, BLOCK, SUB, 128),
            whole_spec(HROWS, PIX, C),
            whole_spec(ROWS, PIX, C),
            whole_spec(C, ROWS * PIX),
            whole_spec(CP, C),
            pl.BlockSpec((32, 128), lambda t: (0, t)),
        ],
        out_specs=(whole_spec(IMGS, ROWS, C, COLS), whole_spec(C, CP)),
        scratch_shapes=[
            pltpu.VMEM((25, 8, 128), F32),
            pltpu.VMEM((HROWS, WIDE, SUB, 128), F32),
            pltpu.VMEM((ROWS * PIX, CP), BF16),
            pltpu.VMEM((ROWS, BLOCK, SUB, 128), F32),
        ],
        compiler_params=pltpu.CompilerParams(vmem_limit_bytes=56 * 2**20),
        name="phase_c",
    )(dd, above, below, fp, cp, fpt, we, misc)


CHUNK = 48


def reduce_kernel(
    gexp, gproj, gdepth, msgs, final, mail, stack, packed, landed, part, pieces, got,
    send, recv, dsend, drecv, fsend, frecv, msend, mrecv,
):
    me_s, me_d = lax.axis_index("space"), lax.axis_index("dp")
    greet(range(1, NS), range(1, ND))
    small = []
    for k in range(1, ND):
        target = lax.rem(me_d + k, ND)
        copy = pltpu.make_async_remote_copy(
            src_ref=msgs.at[target],
            dst_ref=mail.at[me_d],
            send_sem=msend.at[k],
            recv_sem=mrecv.at[k],
            device_id=(me_s, target),
            device_id_type=MESH,
        )
        copy.start()
        small.append(copy)
    mail[me_d] = msgs[me_d]
    stack[0:C, :] = gexp[...]
    stack[C : 2 * C, :] = gproj[...]
    for t in range(TILES):
        stack[2 * C :, 128 * t : 128 * (t + 1)] = gdepth[t]
    packed[...] = stack[...].reshape(NS, CHUNK, CP).astype(BF16)
    copies = []
    for k in range(1, NS):
        target = lax.rem(me_s + k, NS)
        copy = pltpu.make_async_remote_copy(
            src_ref=packed.at[target],
            dst_ref=landed.at[k],
            send_sem=send.at[k],
            recv_sem=recv.at[k],
            device_id=(target, me_d),
            device_id_type=MESH,
        )
        copy.start()
        copies.append(copy)
    start = pl.multiple_of(me_s * CHUNK, CHUNK)
    part[:, 0:CP] = stack[pl.ds(start, CHUNK), :]
    part[:, CP:] = jnp.zeros((CHUNK, 128), F32)
    for k, copy in enumerate(copies):
        copy.wait()
        part[:, 0:CP] = part[:, 0:CP] + landed[k + 1].astype(F32)
    for d in range(ND):
        pieces[d] = part[:, SLOT * d : SLOT * d + 128].astype(BF16)
    copies = []
    for k in range(1, ND):
        target = lax.rem(me_d + k, ND)
        copy = pltpu.make_async_remote_copy(
            src_ref=pieces.at[target],
            dst_ref=got.at[k],
            send_sem=dsend.at[k],
            recv_sem=drecv.at[k],
            device_id=(me_s, target),
            device_id_type=MESH,
        )
        copy.start()
        copies.append(copy)
    total = pieces[me_d].astype(F32)
    for k, copy in enumerate(copies):
        copy.wait()
        total = total + got[k + 1].astype(F32)
    final[me_s] = total
    copies = []
    for k in range(1, NS):
        copy = pltpu.make_async_remote_copy(
            src_ref=final.at[me_s],
            dst_ref=final.at[me_s],
            send_sem=fsend.at[k],
            recv_sem=frecv.at[k],
            device_id=(lax.rem(me_s + k, NS), me_d),
            device_id_type=MESH,
        )
        copy.start()
        copies.append(copy)
    for copy in copies:
        copy.wait()
    for copy in small:
        copy.wait()


def reduce_grads(gexp, gproj, gdepth, msgs):
    return pl.pallas_call(
        reduce_kernel,
        out_shape=(
            jax.ShapeDtypeStruct((NS, CHUNK, 128), F32),
            jax.ShapeDtypeStruct((ND, 8, 128), F32),
        ),
        in_specs=[VMEM] * 4,
        out_specs=(VMEM, VMEM),
        scratch_shapes=[
            pltpu.VMEM((NS * CHUNK, CP), F32),
            pltpu.VMEM((NS, CHUNK, CP), BF16),
            pltpu.VMEM((NS, CHUNK, CP), BF16),
            pltpu.VMEM((CHUNK, CP + 128), F32),
            pltpu.VMEM((ND, CHUNK, 128), BF16),
            pltpu.VMEM((ND, CHUNK, 128), BF16),
            pltpu.SemaphoreType.DMA((NS,)),
            pltpu.SemaphoreType.DMA((NS,)),
            pltpu.SemaphoreType.DMA((ND,)),
            pltpu.SemaphoreType.DMA((ND,)),
            pltpu.SemaphoreType.DMA((NS,)),
            pltpu.SemaphoreType.DMA((NS,)),
            pltpu.SemaphoreType.DMA((ND,)),
            pltpu.SemaphoreType.DMA((ND,)),
        ],
        compiler_params=pltpu.CompilerParams(
            collective_id=2, has_side_effects=True, vmem_limit_bytes=56 * 2**20
        ),
        name="reduce_grads",
    )(gexp, gproj, gdepth, msgs)


def finish_kernel(final, mail, gexp, gdepth, greduce, gexcite, gbex, gproj, gbred):
    grads = final[...].reshape(NS * CHUNK, 128)
    gexp[...] = grads[0:C].T[0:PART]
    gproj[...] = grads[C : 2 * C].T[0:PART]
    gdepth[...] = grads[2 * C : 2 * C + 25, 0:PART]
    rows = [mail[d] for d in range(ND)]
    pool_all = jnp.concatenate([row[0:2] for row in rows], axis=0)
    dlog_all = jnp.concatenate([row[2:4] for row in rows], axis=0)
    sq_all = jnp.concatenate([row[4:6] for row in rows], axis=0)
    dsq_all = jnp.concatenate([row[6:8] for row in rows], axis=0)
    greduce[...] = dot_tn(dsq_all, pool_all, HIGH)[0:SE, 0:PART]
    gexcite[...] = dot_tn(sq_all, dlog_all, HIGH)[0:SE, 0:PART]
    gbex[...] = jnp.sum(dlog_all, axis=0, keepdims=True)[:, 0:PART]
    gbred[...] = jnp.sum(dsq_all, axis=0, keepdims=True)[:, 0:SE]


def finish(final, mail):
    return pl.pallas_call(
        finish_kernel,
        out_shape=(
            jax.ShapeDtypeStruct((PART, C), F32),
            jax.ShapeDtypeStruct((25, PART), F32),
            jax.ShapeDtypeStruct((SE, PART), F32),
            jax.ShapeDtypeStruct((SE, PART), F32),
            jax.ShapeDtypeStruct((1, PART), F32),
            jax.ShapeDtypeStruct((PART, C), F32),
            jax.ShapeDtypeStruct((1, SE), F32),
        ),
        in_specs=[VMEM] * 2,
        out_specs=(VMEM,) * 7,
        name="finish",
    )(final, mail)


def on_device(
    features, w_expand, w_depth, w_reduce, b_reduce, w_excite, b_excite, w_project, cotangent
):
    fp, cp, fpt, cpt, we, wp, misc = gather(
        w_expand.T,
        w_project,
        w_depth.reshape(25, PART),
        w_reduce.T,
        w_excite,
        b_excite[None, :],
        features.swapaxes(2, 3),
        cotangent.swapaxes(2, 3),
    )
    ex, depth, sums = first(fp, cp, we, wp, misc)
    gates, msgs = mid(sums, misc, b_reduce[None, :])
    dd, upper, lower, output, gproj = second(depth, fp, cp, cpt, wp, gates)
    above = lax.ppermute(lower, "space", [(i, i + 1) for i in range(NS - 1)])
    below = lax.ppermute(upper, "space", [(i + 1, i) for i in range(NS - 1)])
    gdepth = tap_grads(ex, dd)
    grad_features, gexp = third(dd, above, below, fp, cp, fpt, we, misc)
    final, mail = reduce_grads(gexp, gproj, gdepth, msgs)
    s_expand, s_depth, s_reduce, s_excite, s_bexcite, s_project, s_breduce = finish(final, mail)
    return (
        output.swapaxes(2, 3),
        grad_features.swapaxes(2, 3),
        s_expand.T,
        s_depth.reshape(5, 5, PART),
        s_reduce.T,
        s_excite,
        s_bexcite[0],
        s_project,
        s_breduce[0],
    )


def solution(mesh):
    return jax.shard_map(
        on_device,
        mesh=mesh,
        in_specs=(
            P("dp", "space", None, None),
            P(None, "dp"),
            P(None, None, "dp"),
            P("dp", None),
            P(),
            P(None, "dp"),
            P("dp"),
            P("dp", None),
            P("dp", "space", None, None),
        ),
        out_specs=(
            P("dp", "space", None, None),
            P("dp", "space", None, None),
            P(None, "dp"),
            P(None, None, "dp"),
            P("dp", None),
            P(None, "dp"),
            P("dp"),
            P("dp", None),
            P(),
        ),
        check_vma=False,
    )
```

```python
import functools

import jax
import jax.numpy as jnp
from jax import lax
from jax.experimental import pallas as pl
from jax.experimental.pallas import tpu as pltpu
from jax.sharding import PartitionSpec as P

F32 = jnp.float32
BF16 = jnp.bfloat16
MESH = pl.DeviceIdType.MESH
HIGH = lax.Precision.HIGHEST

IMGS, ROWS, COLS, C, SE = 2, 12, 100, 176, 44
BLOCK, SUB = 13, 16
PIX = BLOCK * SUB
WIDE = BLOCK + 4
HROWS = ROWS + 4
PART, SLOT = 66, 72
CP = 16 * SLOT
TILES = CP // 128
AREA = 9600.0
NS, ND = 8, 16

VMEM = pl.BlockSpec(memory_space=pltpu.VMEM)
ANY = pl.BlockSpec(memory_space=pl.ANY)


def sigmoid(value):
    return 0.5 * jnp.tanh(0.5 * value) + 0.5


def swish(value):
    return value * sigmoid(value)


def swish_grad(value):
    sig = sigmoid(value)
    act = value * sig
    return sig + act - act * sig


def dot_nt(left, right, precision=None):
    return lax.dot_general(
        left, right, (((1,), (1,)), ((), ())), precision=precision, preferred_element_type=F32
    )


def dot_tn(left, right, precision=None):
    return lax.dot_general(
        left, right, (((0,), (0,)), ((), ())), precision=precision, preferred_element_type=F32
    )


def dot_nn(left, right, precision=None):
    return lax.dot_general(
        left, right, (((1,), (0,)), ((), ())), precision=precision, preferred_element_type=F32
    )


def greet(space_peers, dp_peers):
    me_s, me_d = lax.axis_index("space"), lax.axis_index("dp")
    barrier = pltpu.get_barrier_semaphore()
    for k in space_peers:
        pl.semaphore_signal(
            barrier, inc=1, device_id=(lax.rem(me_s + k, NS), me_d), device_id_type=MESH
        )
    for k in dp_peers:
        pl.semaphore_signal(
            barrier, inc=1, device_id=(me_s, lax.rem(me_d + k, ND)), device_id_type=MESH
        )
    pl.semaphore_wait(barrier, len(space_peers) + len(dp_peers))


def one_hot(img, transposed):
    shape = (COLS, PIX) if transposed else (PIX, COLS)
    place = lax.broadcasted_iota(jnp.int32, shape, 1 if transposed else 0)
    col = lax.broadcasted_iota(jnp.int32, shape, 0 if transposed else 1)
    wanted = (col % BLOCK) * SUB + img * 8 + col // BLOCK
    return jnp.where(place == wanted, 1.0, 0.0).astype(BF16)


def gather_kernel(
    wet, wpr, taps, wrt, wx, bex, feats, cot,
    fp, cp, fpt, cpt, we, wp, misc,
    stage, pack, full, top, bottom, flat,
    send, recv, halo_send, halo_recv, mate_send, mate_recv,
):
    me_s, me_d = lax.axis_index("space"), lax.axis_index("dp")
    core = lax.rem(me_s, 2)
    mate = me_s + 1 - 2 * core
    barrier = pltpu.get_barrier_semaphore()
    for k in (1, NS - 1):
        pl.semaphore_signal(
            barrier, inc=1, device_id=(lax.rem(me_s + k, NS), me_d), device_id_type=MESH
        )
    for k in range(1, ND):
        pl.semaphore_signal(
            barrier, inc=1, device_id=(me_s, lax.rem(me_d + k, ND)), device_id_type=MESH
        )
    stage[...] = jnp.zeros_like(stage)
    stage[0, 0:PART, 0:C] = wet[...].astype(F32)
    stage[1, 0:PART, 0:C] = wpr[...].astype(F32)
    side = slice(C, C + PART)
    stage[0, 0:25, side] = taps[...].astype(F32)
    stage[0, 32 : 32 + SE, side] = wrt[...].astype(F32)
    stage[1, 0:SE, side] = wx[...].astype(F32)
    stage[1, 48:49, side] = bex[...].astype(F32)
    pack[...] = stage[...].astype(BF16)
    pl.semaphore_wait(barrier, ND + 1)
    copies = []
    for k in range(1, ND):
        copy = pltpu.make_async_remote_copy(
            src_ref=pack.at[core],
            dst_ref=full.at[core, me_d],
            send_sem=send.at[k],
            recv_sem=recv.at[k],
            device_id=(me_s, lax.rem(me_d + k, ND)),
            device_id_type=MESH,
        )
        copy.start()
        copies.append(copy)
    down = pltpu.make_async_remote_copy(
        src_ref=feats.at[:, pl.ds(ROWS - 2, 2)],
        dst_ref=top,
        send_sem=halo_send.at[0],
        recv_sem=halo_recv.at[0],
        device_id=(lax.rem(me_s + 1, NS), me_d),
        device_id_type=MESH,
    )
    up = pltpu.make_async_remote_copy(
        src_ref=feats.at[:, pl.ds(0, 2)],
        dst_ref=bottom,
        send_sem=halo_send.at[1],
        recv_sem=halo_recv.at[1],
        device_id=(lax.rem(me_s + NS - 1, NS), me_d),
        device_id_type=MESH,
    )
    down.start()
    up.start()
    full[core, me_d] = pack[core]
    spread = (one_hot(0, False), one_hot(1, False))
    gather_t = (one_hot(0, True), one_hot(1, True))

    def row(r, carry):
        for src, dst, shift in ((feats, fp, 2), (cot, cp, 0)):
            a, b = src[0, r], src[1, r]
            dst[r + shift] = (dot_nt(spread[0], a) + dot_nt(spread[1], b)).astype(BF16)
        return carry

    lax.fori_loop(0, ROWS, row, 0)
    for r in range(ROWS):
        for src, dst in ((feats, fpt), (cot, cpt)):
            value = dot_nn(src[0, r], gather_t[0]) + dot_nn(src[1, r], gather_t[1])
            dst[:, PIX * r : PIX * (r + 1)] = value.astype(BF16)
    for copy in copies:
        copy.wait()
    share = pltpu.make_async_remote_copy(
        src_ref=full.at[core],
        dst_ref=full.at[core],
        send_sem=mate_send,
        recv_sem=mate_recv,
        device_id=(mate, me_d),
        device_id_type=MESH,
    )
    share.start()
    down.wait()
    up.wait()
    has_top = jnp.where(me_s > 0, 1.0, 0.0)
    has_bottom = jnp.where(me_s < NS - 1, 1.0, 0.0)
    for r in range(2):
        value = dot_nt(spread[0], top[0, r]) + dot_nt(spread[1], top[1, r])
        fp[r] = (value * has_top).astype(BF16)
        value = dot_nt(spread[0], bottom[0, r]) + dot_nt(spread[1], bottom[1, r])
        fp[ROWS + 2 + r] = (value * has_bottom).astype(BF16)
    share.wait()
    for half, out in ((0, we), (1, wp)):
        for d in range(ND):
            part = full[half, d].astype(F32)
            flat[d * SLOT : (d + 1) * SLOT, :] = part[0:SLOT, 0:C]
            lanes = slice(d * SLOT, (d + 1) * SLOT)
            if half == 0:
                misc[0:80, lanes] = part[:, C : C + SLOT]
            else:
                misc[80:136, lanes] = part[0:56, C : C + SLOT]
        out[...] = flat[...].astype(BF16)


def gather(wet, wpr, taps, wrt, wx, bex, feats, cot):
    return pl.pallas_call(
        gather_kernel,
        out_shape=(
            jax.ShapeDtypeStruct((HROWS, PIX, C), BF16),
            jax.ShapeDtypeStruct((ROWS, PIX, C), BF16),
            jax.ShapeDtypeStruct((C, ROWS * PIX), BF16),
            jax.ShapeDtypeStruct((C, ROWS * PIX), BF16),
            jax.ShapeDtypeStruct((CP, C), BF16),
            jax.ShapeDtypeStruct((CP, C), BF16),
            jax.ShapeDtypeStruct((136, CP), F32),
        ),
        in_specs=[VMEM] * 8,
        out_specs=(VMEM,) * 7,
        scratch_shapes=[
            pltpu.VMEM((2, 80, 256), F32),
            pltpu.VMEM((2, 80, 256), BF16),
            pltpu.VMEM((2, ND, 80, 256), BF16),
            pltpu.VMEM((IMGS, 2, C, COLS), BF16),
            pltpu.VMEM((IMGS, 2, C, COLS), BF16),
            pltpu.VMEM((CP, C), F32),
            pltpu.SemaphoreType.DMA((ND,)),
            pltpu.SemaphoreType.DMA((ND,)),
            pltpu.SemaphoreType.DMA((2,)),
            pltpu.SemaphoreType.DMA((2,)),
            pltpu.SemaphoreType.DMA,
            pltpu.SemaphoreType.DMA,
        ],
        compiler_params=pltpu.CompilerParams(
            collective_id=0, has_side_effects=True, vmem_limit_bytes=56 * 2**20
        ),
        name="gather_weights",
    )(wet, wpr, taps, wrt, wx, bex, feats, cot)


def spread_taps(taps, wide_taps):
    for k in range(25):
        wide_taps[k] = jnp.broadcast_to(taps[k : k + 1, :], (8, 128))


def edge_columns(value):
    split = value.reshape(BLOCK, 2, 8, 128)
    block = lax.broadcasted_iota(jnp.int32, (2, 2, 8, 128), 2)
    left = jnp.where(block > 0, pltpu.roll(split[BLOCK - 2 :], 1, 2), 0.0)
    right = jnp.where(block < 7, pltpu.roll(split[:2], 7, 2), 0.0)
    return left.reshape(2, SUB, 128), right.reshape(2, SUB, 128)


def store_row(ref, r, value):
    left, right = edge_columns(value)
    ref[r, 0:2] = left
    ref[r, 2 : 2 + BLOCK] = value
    ref[r, 2 + BLOCK :] = right


def conv_row(ref, r, h, wide_taps, flip):
    total = jnp.zeros((BLOCK, 8, 128), F32)
    for i in range(5):
        source = ref[r + i, :, 8 * h : 8 * h + 8, :]
        for j in range(5):
            k = (4 - i) * 5 + 4 - j if flip else i * 5 + j
            total = total + source[j : j + BLOCK] * wide_taps[k][None]
    return total


def pad_mask():
    block = lax.broadcasted_iota(jnp.int32, (4, 8, 128), 1)
    return jnp.where(block < 7, 1.0, 0.0)


def first_kernel(fp, cp, we, wp, misc, saved, depth, sums, wide_taps, ex, dgs):
    spread_taps(misc, wide_taps)
    keep = pad_mask()

    def expand(q, carry):
        pre = dot_nt(fp[pl.ds(8 * q, 8)].reshape(8 * PIX, C), we[...])
        value = swish(pre).astype(BF16).astype(F32).reshape(8, BLOCK, SUB, 128)
        for n in range(8):
            store_row(ex, 8 * q + n, value[n])
        return carry

    lax.fori_loop(0, 2, expand, 0)
    cot_matmul(cp, wp, dgs)

    def conv(r, carry):
        pools, grads = list(carry[:2]), list(carry[2:])
        for h in range(2):
            total = conv_row(ex, r, h, wide_taps, False)
            depth[0, r, :, 8 * h : 8 * h + 8, :] = total
            act = swish(total)
            dgated = dgs[r, :, 8 * h : 8 * h + 8, :]
            grads[h] = grads[h] + jnp.sum(act * dgated, axis=0)
            pools[h] = pools[h] + jnp.sum(act[:9], axis=0) + jnp.sum(act[9:] * keep, axis=0)
        saved[0, r] = ex[r].astype(BF16)
        return (*pools, *grads)

    zero = jnp.zeros((8, 128), F32)
    parts = lax.fori_loop(0, ROWS, conv, (zero,) * 4)
    for r in range(ROWS, HROWS):
        saved[0, r] = ex[r].astype(BF16)
    for k in range(4):
        sums[0, k : k + 1, :] = jnp.sum(parts[k], axis=0, keepdims=True)
    sums[0, 4:8, :] = jnp.zeros((4, 128), F32)


def cot_matmul(cp, wp, dgs):
    def chunk(q, carry):
        rows = pl.ds(6 * q, 6)
        dgs[rows] = dot_nt(cp[rows].reshape(6 * PIX, C), wp[...]).reshape(6, BLOCK, SUB, 128)
        return carry

    lax.fori_loop(0, 2, chunk, 0)


def tile_spec(*shape):
    zeros = (0,) * len(shape)
    return pl.BlockSpec((1, *shape), lambda t: (t, *zeros))


def whole_spec(*shape):
    zeros = (0,) * len(shape)
    return pl.BlockSpec(shape, lambda t: zeros)


def first(fp, cp, we, wp, misc):
    return pl.pallas_call(
        first_kernel,
        grid=(TILES,),
        out_shape=(
            jax.ShapeDtypeStruct((TILES, HROWS, WIDE, SUB, 128), BF16),
            jax.ShapeDtypeStruct((TILES, ROWS, BLOCK, SUB, 128), F32),
            jax.ShapeDtypeStruct((TILES, 8, 128), F32),
        ),
        in_specs=[
            whole_spec(HROWS, PIX, C),
            whole_spec(ROWS, PIX, C),
            pl.BlockSpec((128, C), lambda t: (t, 0)),
            pl.BlockSpec((128, C), lambda t: (t, 0)),
            pl.BlockSpec((32, 128), lambda t: (0, t)),
        ],
        out_specs=(
            tile_spec(HROWS, WIDE, SUB, 128),
            tile_spec(ROWS, BLOCK, SUB, 128),
            tile_spec(8, 128),
        ),
        scratch_shapes=[
            pltpu.VMEM((25, 8, 128), F32),
            pltpu.VMEM((HROWS, WIDE, SUB, 128), F32),
            pltpu.VMEM((ROWS, BLOCK, SUB, 128), F32),
        ],
        compiler_params=pltpu.CompilerParams(vmem_limit_bytes=56 * 2**20),
        name="phase_a",
    )(fp, cp, we, wp, misc)


def mid_kernel(sums, misc, breduce, gates, msgs, packed, landed, lanes, vecs, send, recv):
    me_s, me_d = lax.axis_index("space"), lax.axis_index("dp")
    greet(range(1, NS), ())
    packed[...] = jnp.zeros_like(packed)
    for t in range(TILES):
        packed[t // 2, 4 * (t % 2) : 4 * (t % 2) + 4, :] = sums[t, 0:4, :]
    copies = []
    for k in range(1, NS):
        copy = pltpu.make_async_remote_copy(
            src_ref=packed,
            dst_ref=landed.at[k],
            send_sem=send.at[k],
            recv_sem=recv.at[k],
            device_id=(lax.rem(me_s + k, NS), me_d),
            device_id_type=MESH,
        )
        copy.start()
        copies.append(copy)
    landed[0] = packed[...]
    for copy in copies:
        copy.wait()
    total = landed[lax.rem(me_s, NS)]
    for s in range(1, NS):
        total = total + landed[lax.rem(me_s + NS - s, NS)]
    for t in range(TILES):
        lanes[0:4, 128 * t : 128 * (t + 1)] = total[t // 2, 4 * (t % 2) : 4 * (t % 2) + 4]
    lanes[:, CP:] = jnp.zeros((8, 128), F32)
    wr = misc[32 : 32 + SE, :]
    wx = misc[80 : 80 + SE, :]
    bexcite = misc[128:129, :]
    pooled = lanes[0:2, 0:CP] / AREA
    dgate = lanes[2:4, 0:CP]
    squeeze_pre = dot_nt(pooled, wr, HIGH) + breduce[...].astype(F32)
    squeeze = swish(squeeze_pre)
    gate = sigmoid(dot_nn(squeeze, wx, HIGH) + bexcite)
    dlogit = dgate * gate * (1.0 - gate)
    dsq = dot_nt(dlogit, wx, HIGH) * swish_grad(squeeze_pre)
    dpooled = dot_nn(dsq, wr, HIGH)
    gates[0:2, :] = gate
    gates[2:4, :] = dpooled / AREA
    gates[4:8, :] = jnp.zeros((4, CP), F32)
    lanes[0:2, 0:CP] = pooled
    lanes[2:4, 0:CP] = dlogit
    vecs[...] = jnp.zeros((8, 128), F32)
    vecs[4:6, 0:SE] = squeeze
    vecs[6:8, 0:SE] = dsq
    for d in range(ND):
        msgs[d, 0:4, :] = lanes[0:4, SLOT * d : SLOT * d + 128]
        msgs[d, 4:8, :] = vecs[4:8, :]


def mid(sums, misc, breduce):
    return pl.pallas_call(
        mid_kernel,
        out_shape=(
            jax.ShapeDtypeStruct((8, CP), F32),
            jax.ShapeDtypeStruct((ND, 8, 128), F32),
        ),
        in_specs=[VMEM] * 3,
        out_specs=(VMEM,) * 2,
        scratch_shapes=[
            pltpu.VMEM((5, 8, 128), F32),
            pltpu.VMEM((NS, 5, 8, 128), F32),
            pltpu.VMEM((8, CP + 128), F32),
            pltpu.VMEM((8, 128), F32),
            pltpu.SemaphoreType.DMA((NS,)),
            pltpu.SemaphoreType.DMA((NS,)),
        ],
        compiler_params=pltpu.CompilerParams(
            collective_id=1, has_side_effects=True, vmem_limit_bytes=56 * 2**20
        ),
        name="squeeze_excite",
    )(sums, misc, breduce)


def gate_row(depth, dgated, gates, h, keep):
    gate = gates[h : h + 1, :][None]
    pull = gates[2 + h : 3 + h, :][None]
    sig = sigmoid(depth)
    act = depth * sig
    gated = act * gate
    ddepth = (dgated * gate + pull) * (sig + act - act * sig)
    ddepth = jnp.concatenate([ddepth[:9], ddepth[9:] * keep], axis=0)
    return gated, ddepth


def unpermute(value, out, r):
    for img in range(2):
        out[img, r] = dot_tn(value, one_hot(img, False)).astype(BF16)


def all_channels_out(rows_in, weights, base, shift, out):
    def chunk(q, carry):
        block = rows_in[pl.ds(pl.multiple_of(4 * PIX * q, 4 * PIX), 4 * PIX), :]
        product = dot_nn(block, weights[...]).reshape(4, PIX, C)
        for n in range(4):
            value = product[n] + base[4 * q + n + shift].astype(F32)
            unpermute(value.astype(BF16), out, 4 * q + n)
        return carry

    lax.fori_loop(0, 3, chunk, 0)


def all_channels_grad(rows_in, turned, grad):
    def lanes(q, carry):
        span = pl.ds(pl.multiple_of(384 * q, 128), 384)
        grad[:, span] = dot_nn(turned[...], rows_in[:, span])
        return carry

    lax.fori_loop(0, 3, lanes, 0)


def second_kernel(
    depth, fp, cp, cpt, wp, gates, dd, upper, lower, out, gproj, gated_rows, dgs
):
    keep = pad_mask()
    t = pl.program_id(0)
    lane = pl.ds(pl.multiple_of(128 * t, 128), 128)
    cot_matmul(cp, wp.at[lane], dgs)

    def pointwise(r, carry):
        both, gates_both = [], []
        for h in range(2):
            rows = slice(8 * h, 8 * h + 8)
            gated, ddepth = gate_row(depth[0, r, :, rows, :], dgs[r, :, rows, :], gates, h, keep)
            both.append(ddepth)
            gates_both.append(gated)
        dd[0, r] = jnp.concatenate(both, axis=1).astype(BF16)
        gated_rows[pl.ds(pl.multiple_of(r * PIX, PIX), PIX), lane] = (
            jnp.concatenate(gates_both, axis=1).reshape(PIX, 128).astype(BF16)
        )
        return carry

    lax.fori_loop(0, ROWS, pointwise, 0)
    upper[0] = dd[0, 0:2]
    lower[0] = dd[0, ROWS - 2 :]

    @pl.when(t == TILES - 1)
    def _():
        all_channels_out(gated_rows, wp, fp, 2, out)
        all_channels_grad(gated_rows, cpt, gproj)


def second(depth, fp, cp, cpt, wp, gates):
    return pl.pallas_call(
        second_kernel,
        grid=(TILES,),
        out_shape=(
            jax.ShapeDtypeStruct((TILES, ROWS, BLOCK, SUB, 128), BF16),
            jax.ShapeDtypeStruct((TILES, 2, BLOCK, SUB, 128), BF16),
            jax.ShapeDtypeStruct((TILES, 2, BLOCK, SUB, 128), BF16),
            jax.ShapeDtypeStruct((IMGS, ROWS, C, COLS), BF16),
            jax.ShapeDtypeStruct((C, CP), F32),
        ),
        in_specs=[
            tile_spec(ROWS, BLOCK, SUB, 128),
            whole_spec(HROWS, PIX, C),
            whole_spec(ROWS, PIX, C),
            whole_spec(C, ROWS * PIX),
            whole_spec(CP, C),
            pl.BlockSpec((8, 128), lambda t: (0, t)),
        ],
        out_specs=(
            tile_spec(ROWS, BLOCK, SUB, 128),
            tile_spec(2, BLOCK, SUB, 128),
            tile_spec(2, BLOCK, SUB, 128),
            whole_spec(IMGS, ROWS, C, COLS),
            whole_spec(C, CP),
        ),
        scratch_shapes=[
            pltpu.VMEM((ROWS * PIX, CP), BF16),
            pltpu.VMEM((ROWS, BLOCK, SUB, 128), F32),
        ],
        compiler_params=pltpu.CompilerParams(vmem_limit_bytes=56 * 2**20),
        name="phase_b",
    )(depth, fp, cp, cpt, wp, gates)


def tap_kernel(ex, dd, gdepth, acc):
    acc[...] = jnp.zeros_like(acc)

    def taps(r, carry):
        for h in range(2):
            rows = slice(8 * h, 8 * h + 8)
            mine = dd[0, r, :, :, :].astype(F32)[:, rows, :]
            for i in range(5):
                source = ex[0, r + i].astype(F32)[:, rows, :]
                for j in range(5):
                    k = 5 * i + j
                    acc[k] = acc[k] + jnp.sum(mine * source[j : j + BLOCK], axis=0)
        return carry

    lax.fori_loop(0, ROWS, taps, 0)
    for k in range(25):
        gdepth[0, k : k + 1, :] = jnp.sum(acc[k], axis=0, keepdims=True)
    gdepth[0, 25:32, :] = jnp.zeros((7, 128), F32)


def tap_grads(ex, dd):
    return pl.pallas_call(
        tap_kernel,
        grid=(TILES,),
        out_shape=jax.ShapeDtypeStruct((TILES, 32, 128), F32),
        in_specs=[tile_spec(HROWS, WIDE, SUB, 128), tile_spec(ROWS, BLOCK, SUB, 128)],
        out_specs=tile_spec(32, 128),
        scratch_shapes=[pltpu.VMEM((25, 8, 128), F32)],
        compiler_params=pltpu.CompilerParams(vmem_limit_bytes=56 * 2**20),
        cost_estimate=pl.CostEstimate(
            flops=4 * 10**9, bytes_accessed=50 * 10**6, transcendentals=3 * 10**6
        ),
        name="tap_grads",
    )(ex, dd)


EARLY = C + 32


def third_kernel(
    dd, above, below, fp, cp, fpt, we, misc, gproj, gdepth, msgs,
    out, early, late, mail_out,
    mail, wide_taps, rows_in, dpre, pres, flat, epiece, egot, espace, lpiece, lgot, lspace,
    esend, erecv, fsend, frecv, lsend, lrecv, gsend, grecv, msend, mrecv,
):
    t = pl.program_id(0)
    me_s, me_d = lax.axis_index("space"), lax.axis_index("dp")
    lane = pl.ds(pl.multiple_of(128 * t, 128), 128)

    def to_dp(src, dst, send, recv, slotted):
        copies = []
        for k in range(1, ND):
            target = lax.rem(me_d + k, ND)
            copies.append(
                pltpu.make_async_remote_copy(
                    src_ref=src.at[target],
                    dst_ref=dst.at[me_d] if slotted else dst.at[k],
                    send_sem=send.at[k],
                    recv_sem=recv.at[k],
                    device_id=(me_s, target),
                    device_id_type=MESH,
                )
            )
        return copies

    def to_space(ref, send, recv):
        copies = []
        for k in range(1, NS):
            copies.append(
                pltpu.make_async_remote_copy(
                    src_ref=ref.at[me_s],
                    dst_ref=ref.at[me_s],
                    send_sem=send.at[k],
                    recv_sem=recv.at[k],
                    device_id=(lax.rem(me_s + k, NS), me_d),
                    device_id_type=MESH,
                )
            )
        return copies

    def dp_sum(copies, piece, got):
        total = piece[me_d].astype(F32)
        for k, copy in enumerate(copies):
            copy.wait()
            total = total + got[k + 1].astype(F32)
        return total

    def space_sum(copies, ref):
        for copy in copies:
            copy.wait()
        total = ref[0].astype(F32)
        for s in range(1, NS):
            total = total + ref[s].astype(F32)
        return total

    @pl.when(t == 0)
    def _():
        barrier = pltpu.get_barrier_semaphore()
        for k in range(1, NS):
            pl.semaphore_signal(
                barrier, inc=1, device_id=(lax.rem(me_s + k, NS), me_d), device_id_type=MESH
            )
        for k in range(1, ND):
            pl.semaphore_signal(
                barrier, inc=1, device_id=(me_s, lax.rem(me_d + k, ND)), device_id_type=MESH
            )

    spread_taps(misc, wide_taps)
    for n in range(2):
        store_row(rows_in, n, above[0, n].astype(F32))
        store_row(rows_in, ROWS + 2 + n, below[0, n].astype(F32))

    def spread(r, carry):
        store_row(rows_in, r + 2, dd[0, r].astype(F32))
        return carry

    lax.fori_loop(0, ROWS, spread, 0)

    def chunk(q, carry):
        pre = dot_nt(fp[pl.ds(6 * q + 2, 6)].reshape(6 * PIX, C), we[lane, :])
        pres[pl.ds(6 * q, 6)] = swish_grad(pre).reshape(6, BLOCK, SUB, 128)
        return carry

    lax.fori_loop(0, 2, chunk, 0)

    def conv(r, carry):
        both = []
        for h in range(2):
            slope = pres[r, :, 8 * h : 8 * h + 8, :]
            both.append(conv_row(rows_in, r, h, wide_taps, True) * slope)
        dpre[pl.ds(pl.multiple_of(r * PIX, PIX), PIX), lane] = (
            jnp.concatenate(both, axis=1).reshape(PIX, 128).astype(BF16)
        )
        return carry

    lax.fori_loop(0, ROWS, conv, 0)

    @pl.when(t == 0)
    def _():
        pl.semaphore_wait(pltpu.get_barrier_semaphore(), NS + ND - 2)
        flat[:, CP:] = jnp.zeros((EARLY, 128), F32)
        flat[0:C, 0:CP] = gproj[...]
        for n in range(TILES):
            flat[C:, 128 * n : 128 * (n + 1)] = gdepth[n]
        for d in range(ND):
            epiece[d] = flat[:, SLOT * d : SLOT * d + 128].astype(BF16)
        mail[me_d] = msgs[me_d]
        for copy in to_dp(epiece, egot, esend, erecv, False):
            copy.start()
        for copy in to_dp(msgs, mail, msend, mrecv, True):
            copy.start()

    @pl.when(t == TILES // 2)
    def _():
        total = dp_sum(to_dp(epiece, egot, esend, erecv, False), epiece, egot)
        espace[me_s] = total.astype(BF16)
        for copy in to_space(espace, fsend, frecv):
            copy.start()

    @pl.when(t == TILES - 1)
    def _():
        early[...] = space_sum(to_space(espace, fsend, frecv), espace)
        for copy in to_dp(msgs, mail, msend, mrecv, True):
            copy.wait()
        mail_out[...] = mail[...]
        all_channels_grad(dpre, fpt, flat.at[0:C])
        for d in range(ND):
            lpiece[d] = flat[0:C, SLOT * d : SLOT * d + 128].astype(BF16)
        copies = to_dp(lpiece, lgot, lsend, lrecv, False)
        for copy in copies:
            copy.start()
        all_channels_out(dpre, we, cp, 0, out)
        lspace[me_s] = dp_sum(copies, lpiece, lgot).astype(BF16)
        copies = to_space(lspace, gsend, grecv)
        for copy in copies:
            copy.start()
        late[...] = space_sum(copies, lspace)


def third(dd, above, below, fp, cp, fpt, we, misc, gproj, gdepth, msgs):
    return pl.pallas_call(
        third_kernel,
        grid=(TILES,),
        out_shape=(
            jax.ShapeDtypeStruct((IMGS, ROWS, C, COLS), BF16),
            jax.ShapeDtypeStruct((EARLY, 128), F32),
            jax.ShapeDtypeStruct((C, 128), F32),
            jax.ShapeDtypeStruct((ND, 8, 128), F32),
        ),
        in_specs=[
            tile_spec(ROWS, BLOCK, SUB, 128),
            tile_spec(2, BLOCK, SUB, 128),
            tile_spec(2, BLOCK, SUB, 128),
            whole_spec(HROWS, PIX, C),
            whole_spec(ROWS, PIX, C),
            whole_spec(C, ROWS * PIX),
            whole_spec(CP, C),
            pl.BlockSpec((32, 128), lambda t: (0, t)),
            VMEM,
            VMEM,
            VMEM,
        ],
        out_specs=(whole_spec(IMGS, ROWS, C, COLS), VMEM, VMEM, VMEM),
        scratch_shapes=[
            pltpu.VMEM((ND, 8, 128), F32),
            pltpu.VMEM((25, 8, 128), F32),
            pltpu.VMEM((HROWS, WIDE, SUB, 128), F32),
            pltpu.VMEM((ROWS * PIX, CP), BF16),
            pltpu.VMEM((ROWS, BLOCK, SUB, 128), F32),
            pltpu.VMEM((EARLY, CP + 128), F32),
            pltpu.VMEM((ND, EARLY, 128), BF16),
            pltpu.VMEM((ND, EARLY, 128), BF16),
            pltpu.VMEM((NS, EARLY, 128), BF16),
            pltpu.VMEM((ND, C, 128), BF16),
            pltpu.VMEM((ND, C, 128), BF16),
            pltpu.VMEM((NS, C, 128), BF16),
        ]
        + [pltpu.SemaphoreType.DMA((n,)) for n in (ND, ND, NS, NS, ND, ND, NS, NS, ND, ND)],
        compiler_params=pltpu.CompilerParams(
            collective_id=2, has_side_effects=True, vmem_limit_bytes=56 * 2**20
        ),
        name="phase_c",
    )(dd, above, below, fp, cp, fpt, we, misc, gproj, gdepth, msgs)


def finish_kernel(early, late, mail, gexp, gdepth, greduce, gexcite, gbex, gproj, gbred):
    gexp[...] = late[...].T[0:PART]
    gproj[...] = early[0:C].T[0:PART]
    gdepth[...] = early[C : C + 25, 0:PART]
    rows = [mail[d] for d in range(ND)]
    pool_all = jnp.concatenate([row[0:2] for row in rows], axis=0)
    dlog_all = jnp.concatenate([row[2:4] for row in rows], axis=0)
    sq_all = jnp.concatenate([row[4:6] for row in rows], axis=0)
    dsq_all = jnp.concatenate([row[6:8] for row in rows], axis=0)
    greduce[...] = dot_tn(dsq_all, pool_all, HIGH)[0:SE, 0:PART]
    gexcite[...] = dot_tn(sq_all, dlog_all, HIGH)[0:SE, 0:PART]
    gbex[...] = jnp.sum(dlog_all, axis=0, keepdims=True)[:, 0:PART]
    gbred[...] = jnp.sum(dsq_all, axis=0, keepdims=True)[:, 0:SE]


def finish(early, late, mail):
    return pl.pallas_call(
        finish_kernel,
        out_shape=(
            jax.ShapeDtypeStruct((PART, C), F32),
            jax.ShapeDtypeStruct((25, PART), F32),
            jax.ShapeDtypeStruct((SE, PART), F32),
            jax.ShapeDtypeStruct((SE, PART), F32),
            jax.ShapeDtypeStruct((1, PART), F32),
            jax.ShapeDtypeStruct((PART, C), F32),
            jax.ShapeDtypeStruct((1, SE), F32),
        ),
        in_specs=[VMEM] * 3,
        out_specs=(VMEM,) * 7,
        name="finish",
    )(early, late, mail)


def on_device(
    features, w_expand, w_depth, w_reduce, b_reduce, w_excite, b_excite, w_project, cotangent
):
    fp, cp, fpt, cpt, we, wp, misc = gather(
        w_expand.T,
        w_project,
        w_depth.reshape(25, PART),
        w_reduce.T,
        w_excite,
        b_excite[None, :],
        features.swapaxes(2, 3),
        cotangent.swapaxes(2, 3),
    )
    ex, depth, sums = first(fp, cp, we, wp, misc)
    gates, msgs = mid(sums, misc, b_reduce[None, :])
    dd, upper, lower, output, gproj = second(depth, fp, cp, cpt, wp, gates)
    above = lax.ppermute(lower, "space", [(i, i + 1) for i in range(NS - 1)])
    below = lax.ppermute(upper, "space", [(i + 1, i) for i in range(NS - 1)])
    gdepth = tap_grads(ex, dd)
    grad_features, early, late, mail = third(
        dd, above, below, fp, cp, fpt, we, misc, gproj, gdepth, msgs
    )
    s_expand, s_depth, s_reduce, s_excite, s_bexcite, s_project, s_breduce = finish(
        early, late, mail
    )
    return (
        output.swapaxes(2, 3),
        grad_features.swapaxes(2, 3),
        s_expand.T,
        s_depth.reshape(5, 5, PART),
        s_reduce.T,
        s_excite,
        s_bexcite[0],
        s_project,
        s_breduce[0],
    )


def solution(mesh):
    return jax.shard_map(
        on_device,
        mesh=mesh,
        in_specs=(
            P("dp", "space", None, None),
            P(None, "dp"),
            P(None, None, "dp"),
            P("dp", None),
            P(),
            P(None, "dp"),
            P("dp"),
            P("dp", None),
            P("dp", "space", None, None),
        ),
        out_specs=(
            P("dp", "space", None, None),
            P("dp", "space", None, None),
            P(None, "dp"),
            P(None, None, "dp"),
            P("dp", None),
            P(None, "dp"),
            P("dp"),
            P("dp", None),
            P(),
        ),
        check_vma=False,
    )
```

```python
import functools

import jax
import jax.numpy as jnp
from jax import lax
from jax.experimental import pallas as pl
from jax.experimental.pallas import tpu as pltpu
from jax.sharding import PartitionSpec as P

F32 = jnp.float32
BF16 = jnp.bfloat16
MESH = pl.DeviceIdType.MESH
HIGH = lax.Precision.HIGHEST

IMGS, ROWS, COLS, C, SE = 2, 12, 100, 176, 44
BLOCK, SUB = 13, 16
PIX = BLOCK * SUB
WIDE = BLOCK + 4
HROWS = ROWS + 4
PART, SLOT = 66, 72
CP = 16 * SLOT
TILES = CP // 128
AREA = 9600.0
NS, ND = 8, 16

VMEM = pl.BlockSpec(memory_space=pltpu.VMEM)
ANY = pl.BlockSpec(memory_space=pl.ANY)


def sigmoid(value):
    return 0.5 * jnp.tanh(0.5 * value) + 0.5


def swish(value):
    return value * sigmoid(value)


def swish_grad(value):
    sig = sigmoid(value)
    act = value * sig
    return sig + act - act * sig


def dot_nt(left, right, precision=None):
    return lax.dot_general(
        left, right, (((1,), (1,)), ((), ())), precision=precision, preferred_element_type=F32
    )


def dot_tn(left, right, precision=None):
    return lax.dot_general(
        left, right, (((0,), (0,)), ((), ())), precision=precision, preferred_element_type=F32
    )


def dot_nn(left, right, precision=None):
    return lax.dot_general(
        left, right, (((1,), (0,)), ((), ())), precision=precision, preferred_element_type=F32
    )


def one_hot(img, transposed):
    shape = (COLS, PIX) if transposed else (PIX, COLS)
    place = lax.broadcasted_iota(jnp.int32, shape, 1 if transposed else 0)
    col = lax.broadcasted_iota(jnp.int32, shape, 0 if transposed else 1)
    wanted = (col % BLOCK) * SUB + img * 8 + col // BLOCK
    return jnp.where(place == wanted, 1.0, 0.0).astype(BF16)


def spread_taps(taps, wide_taps):
    for k in range(25):
        wide_taps[k] = jnp.broadcast_to(taps[k : k + 1, :], (8, 128))


def edge_columns(value):
    split = value.reshape(BLOCK, 2, 8, 128)
    block = lax.broadcasted_iota(jnp.int32, (2, 2, 8, 128), 2)
    left = jnp.where(block > 0, pltpu.roll(split[BLOCK - 2 :], 1, 2), 0.0)
    right = jnp.where(block < 7, pltpu.roll(split[:2], 7, 2), 0.0)
    return left.reshape(2, SUB, 128), right.reshape(2, SUB, 128)


def store_row(ref, r, value):
    left, right = edge_columns(value)
    ref[r, 0:2] = left
    ref[r, 2 : 2 + BLOCK] = value
    ref[r, 2 + BLOCK :] = right


def conv_row(ref, r, h, wide_taps, flip):
    total = jnp.zeros((BLOCK, 8, 128), F32)
    for i in range(5):
        source = ref[r + i, :, 8 * h : 8 * h + 8, :]
        for j in range(5):
            k = (4 - i) * 5 + 4 - j if flip else i * 5 + j
            total = total + source[j : j + BLOCK] * wide_taps[k][None]
    return total


def pad_mask():
    block = lax.broadcasted_iota(jnp.int32, (4, 8, 128), 1)
    return jnp.where(block < 7, 1.0, 0.0)


def gate_row(depth, dgated, gates, h, keep):
    gate = gates[h : h + 1, :][None]
    pull = gates[2 + h : 3 + h, :][None]
    sig = sigmoid(depth)
    act = depth * sig
    gated = act * gate
    ddepth = (dgated * gate + pull) * (sig + act - act * sig)
    ddepth = jnp.concatenate([ddepth[:9], ddepth[9:] * keep], axis=0)
    return gated, ddepth


def unpermute(value, out, r):
    for img in range(2):
        out[img, r] = dot_tn(value, one_hot(img, False)).astype(BF16)


def all_channels_out(rows_in, weights, base, shift, out):
    def chunk(q, carry):
        block = rows_in[pl.ds(pl.multiple_of(4 * PIX * q, 4 * PIX), 4 * PIX), :]
        product = dot_nn(block, weights[...]).reshape(4, PIX, C)
        for n in range(4):
            value = product[n] + base[4 * q + n + shift].astype(F32)
            unpermute(value.astype(BF16), out, 4 * q + n)
        return carry

    lax.fori_loop(0, 3, chunk, 0)


def all_channels_grad(rows_in, turned, grad):
    def lanes(q, carry):
        span = pl.ds(pl.multiple_of(384 * q, 128), 384)
        grad[:, span] = dot_nn(turned[...], rows_in[:, span])
        return carry

    lax.fori_loop(0, 3, lanes, 0)


def to_dp(src, dst, send, recv, by_sender=False):
    me_s, me_d = lax.axis_index("space"), lax.axis_index("dp")
    copies = []
    for k in range(1, ND):
        target = lax.rem(me_d + k, ND)
        copies.append(
            pltpu.make_async_remote_copy(
                src_ref=src.at[target],
                dst_ref=dst.at[me_d] if by_sender else dst.at[k],
                send_sem=send.at[k],
                recv_sem=recv.at[k],
                device_id=(me_s, target),
                device_id_type=MESH,
            )
        )
    return copies


def to_space(ref, send, recv):
    me_s, me_d = lax.axis_index("space"), lax.axis_index("dp")
    copies = []
    for k in range(1, NS):
        copies.append(
            pltpu.make_async_remote_copy(
                src_ref=ref.at[me_s],
                dst_ref=ref.at[me_s],
                send_sem=send.at[k],
                recv_sem=recv.at[k],
                device_id=(lax.rem(me_s + k, NS), me_d),
                device_id_type=MESH,
            )
        )
    return copies


def to_neighbours(down_src, down_dst, up_src, up_dst, send, recv):
    me_s, me_d = lax.axis_index("space"), lax.axis_index("dp")
    down = pltpu.make_async_remote_copy(
        src_ref=down_src,
        dst_ref=down_dst,
        send_sem=send[0],
        recv_sem=recv[0],
        device_id=(lax.rem(me_s + 1, NS), me_d),
        device_id_type=MESH,
    )
    up = pltpu.make_async_remote_copy(
        src_ref=up_src,
        dst_ref=up_dst,
        send_sem=send[1],
        recv_sem=recv[1],
        device_id=(lax.rem(me_s + NS - 1, NS), me_d),
        device_id_type=MESH,
    )
    return down, up


def dp_sum(copies, piece, got):
    total = piece[lax.axis_index("dp")].astype(F32)
    for k, copy in enumerate(copies):
        copy.wait()
        total = total + got[k + 1].astype(F32)
    return total


def space_sum(copies, ref):
    for copy in copies:
        copy.wait()
    total = ref[0].astype(F32)
    for s in range(1, NS):
        total = total + ref[s].astype(F32)
    return total


EARLY = C + 32


def block_kernel(
    wet, wpr, taps, wrt, wx_own, bex, bred, feats, cot,
    out, out_grad, early, late, mail_out,
    stage, pack, full, top, bottom, flatw, fp, cp, fpt, cpt, we, wp, misc,
    wide_taps, ex, dgs, saved, depth, sums, packed, landed, lanes, vecs, gates, msgs, mail,
    edge, above, below, gated, dpre, acc, flat, epiece, egot, espace, lpiece, lgot, lspace,
    wsend, wrecv, hsend, hrecv, csend, crecv, ssend, srecv, msend, mrecv,
    dsend, drecv, esend, erecv, fsend, frecv, lsend, lrecv, gsend, grecv,
):
    me_s, me_d = lax.axis_index("space"), lax.axis_index("dp")
    core = lax.rem(me_s, 2)
    barrier = pltpu.get_barrier_semaphore()
    for k in range(1, ND):
        pl.semaphore_signal(
            barrier, inc=1, device_id=(me_s, lax.rem(me_d + k, ND)), device_id_type=MESH
        )
    for k in range(1, NS):
        pl.semaphore_signal(
            barrier, inc=1, device_id=(lax.rem(me_s + k, NS), me_d), device_id_type=MESH
        )

    stage[...] = jnp.zeros_like(stage)
    stage[0, 0:PART, 0:C] = wet[...].astype(F32)
    stage[1, 0:PART, 0:C] = wpr[...].astype(F32)
    side = slice(C, C + PART)
    stage[0, 0:25, side] = taps[...].astype(F32)
    stage[0, 32 : 32 + SE, side] = wrt[...].astype(F32)
    stage[1, 0:SE, side] = wx_own[...].astype(F32)
    stage[1, 48:49, side] = bex[...].astype(F32)
    pack[...] = stage[...].astype(BF16)
    pl.semaphore_wait(barrier, NS + ND - 2)
    copies = []
    for k in range(1, ND):
        copy = pltpu.make_async_remote_copy(
            src_ref=pack.at[core],
            dst_ref=full.at[core, me_d],
            send_sem=wsend.at[k],
            recv_sem=wrecv.at[k],
            device_id=(me_s, lax.rem(me_d + k, ND)),
            device_id_type=MESH,
        )
        copy.start()
        copies.append(copy)
    halo = to_neighbours(
        feats.at[:, pl.ds(ROWS - 2, 2)],
        top,
        feats.at[:, pl.ds(0, 2)],
        bottom,
        (hsend.at[0], hsend.at[1]),
        (hrecv.at[0], hrecv.at[1]),
    )
    for copy in halo:
        copy.start()
    full[core, me_d] = pack[core]
    spread = (one_hot(0, False), one_hot(1, False))
    gather_t = (one_hot(0, True), one_hot(1, True))

    def permute(r, carry):
        for src, dst, shift in ((feats, fp, 2), (cot, cp, 0)):
            a, b = src[0, r], src[1, r]
            dst[r + shift] = (dot_nt(spread[0], a) + dot_nt(spread[1], b)).astype(BF16)
        return carry

    lax.fori_loop(0, ROWS, permute, 0)
    for r in range(ROWS):
        for src, dst in ((feats, fpt), (cot, cpt)):
            value = dot_nn(src[0, r], gather_t[0]) + dot_nn(src[1, r], gather_t[1])
            dst[:, PIX * r : PIX * (r + 1)] = value.astype(BF16)
    for copy in copies:
        copy.wait()
    share = pltpu.make_async_remote_copy(
        src_ref=full.at[core],
        dst_ref=full.at[core],
        send_sem=csend,
        recv_sem=crecv,
        device_id=(me_s + 1 - 2 * core, me_d),
        device_id_type=MESH,
    )
    share.start()
    for copy in halo:
        copy.wait()
    has_top = jnp.where(me_s > 0, 1.0, 0.0)
    has_bottom = jnp.where(me_s < NS - 1, 1.0, 0.0)
    for r in range(2):
        value = dot_nt(spread[0], top[0, r]) + dot_nt(spread[1], top[1, r])
        fp[r] = (value * has_top).astype(BF16)
        value = dot_nt(spread[0], bottom[0, r]) + dot_nt(spread[1], bottom[1, r])
        fp[ROWS + 2 + r] = (value * has_bottom).astype(BF16)
    share.wait()
    for half, whole in ((0, we), (1, wp)):
        for d in range(ND):
            part = full[half, d].astype(F32)
            flatw[d * SLOT : (d + 1) * SLOT, :] = part[0:SLOT, 0:C]
            span = slice(d * SLOT, (d + 1) * SLOT)
            if half == 0:
                misc[0:80, span] = part[:, C : C + SLOT]
            else:
                misc[80:136, span] = part[0:56, C : C + SLOT]
        whole[...] = flatw[...].astype(BF16)

    keep = pad_mask()

    def lane_of(t):
        return pl.ds(pl.multiple_of(128 * t, 128), 128)

    def cot_matmul(t):
        def chunk(q, carry):
            rows = pl.ds(6 * q, 6)
            product = dot_nt(cp[rows].reshape(6 * PIX, C), wp[lane_of(t), :])
            dgs[rows] = product.reshape(6, BLOCK, SUB, 128)
            return carry

        lax.fori_loop(0, 2, chunk, 0)

    def first(t, carry):
        spread_taps(misc[0:32, lane_of(t)], wide_taps)

        def expand(q, carry):
            pre = dot_nt(fp[pl.ds(8 * q, 8)].reshape(8 * PIX, C), we[lane_of(t), :])
            value = swish(pre).astype(BF16).astype(F32).reshape(8, BLOCK, SUB, 128)
            for n in range(8):
                store_row(ex, 8 * q + n, value[n])
            return carry

        lax.fori_loop(0, 2, expand, 0)
        cot_matmul(t)

        def conv(r, carry):
            pools, grads = list(carry[:2]), list(carry[2:])
            for h in range(2):
                total = conv_row(ex, r, h, wide_taps, False)
                depth[t, r, :, 8 * h : 8 * h + 8, :] = total
                act = swish(total)
                dgated = dgs[r, :, 8 * h : 8 * h + 8, :]
                grads[h] = grads[h] + jnp.sum(act * dgated, axis=0)
                pools[h] = pools[h] + jnp.sum(act[:9], axis=0) + jnp.sum(act[9:] * keep, axis=0)
            saved[t, r] = ex[r].astype(BF16)
            return (*pools, *grads)

        zero = jnp.zeros((8, 128), F32)
        parts = lax.fori_loop(0, ROWS, conv, (zero,) * 4)
        for r in range(ROWS, HROWS):
            saved[t, r] = ex[r].astype(BF16)
        for k in range(4):
            sums[t, k : k + 1, :] = jnp.sum(parts[k], axis=0, keepdims=True)
        return carry

    lax.fori_loop(0, TILES, first, 0)

    packed[...] = jnp.zeros_like(packed)
    for t in range(TILES):
        packed[t // 2, 4 * (t % 2) : 4 * (t % 2) + 4, :] = sums[t, 0:4, :]
    landed[me_s] = packed[...]
    copies = to_space(landed, ssend, srecv)
    for copy in copies:
        copy.start()
    total = space_sum(copies, landed)
    for t in range(TILES):
        lanes[0:4, 128 * t : 128 * (t + 1)] = total[t // 2, 4 * (t % 2) : 4 * (t % 2) + 4]
    lanes[:, CP:] = jnp.zeros((8, 128), F32)
    wr = misc[32 : 32 + SE, :]
    wx = misc[80 : 80 + SE, :]
    pooled = lanes[0:2, 0:CP] / AREA
    dgate = lanes[2:4, 0:CP]
    squeeze_pre = dot_nt(pooled, wr, HIGH) + bred[...].astype(F32)
    squeeze = swish(squeeze_pre)
    gate = sigmoid(dot_nn(squeeze, wx, HIGH) + misc[128:129, :])
    dlogit = dgate * gate * (1.0 - gate)
    dsq = dot_nt(dlogit, wx, HIGH) * swish_grad(squeeze_pre)
    dpooled = dot_nn(dsq, wr, HIGH)
    gates[0:2, :] = gate
    gates[2:4, :] = dpooled / AREA
    gates[4:8, :] = jnp.zeros((4, CP), F32)
    lanes[0:2, 0:CP] = pooled
    lanes[2:4, 0:CP] = dlogit
    vecs[...] = jnp.zeros((8, 128), F32)
    vecs[4:6, 0:SE] = squeeze
    vecs[6:8, 0:SE] = dsq
    for d in range(ND):
        msgs[d, 0:4, :] = lanes[0:4, SLOT * d : SLOT * d + 128]
        msgs[d, 4:8, :] = vecs[4:8, :]
    mail[me_d] = msgs[me_d]
    small = to_dp(msgs, mail, msend, mrecv, True)
    for copy in small:
        copy.start()

    def edge_copies(t):
        return to_neighbours(
            edge.at[t, 1],
            above.at[t],
            edge.at[t, 0],
            below.at[t],
            (dsend.at[0, t], dsend.at[1, t]),
            (drecv.at[0, t], drecv.at[1, t]),
        )

    def second(t, carry):
        cot_matmul(t)

        def pointwise(r, carry):
            both = []
            for h in range(2):
                rows = slice(8 * h, 8 * h + 8)
                value, ddepth = gate_row(
                    depth[t, r, :, rows, :], dgs[r, :, rows, :], gates.at[:, lane_of(t)], h, keep
                )
                depth[t, r, :, rows, :] = ddepth.astype(BF16).astype(F32)
                both.append(value)
            gated[pl.ds(pl.multiple_of(r * PIX, PIX), PIX), lane_of(t)] = (
                jnp.concatenate(both, axis=1).reshape(PIX, 128).astype(BF16)
            )
            return carry

        lax.fori_loop(0, ROWS, pointwise, 0)
        for n in range(2):
            edge[t, 0, n] = depth[t, n].astype(BF16)
            edge[t, 1, n] = depth[t, ROWS - 2 + n].astype(BF16)
        for copy in edge_copies(t):
            copy.start()
        return carry

    lax.fori_loop(0, TILES, second, 0)

    def tap_grads(t, carry):
        acc[...] = jnp.zeros_like(acc)

        def row(r, carry):
            for h in range(2):
                rows = slice(8 * h, 8 * h + 8)
                mine = depth[t, r, :, rows, :]
                for i in range(5):
                    source = saved[t, r + i].astype(F32)[:, rows, :]
                    for j in range(5):
                        k = 5 * i + j
                        acc[k] = acc[k] + jnp.sum(mine * source[j : j + BLOCK], axis=0)
            return carry

        lax.fori_loop(0, ROWS, row, 0)
        for k in range(25):
            flat[C + k : C + k + 1, lane_of(t)] = jnp.sum(acc[k], axis=0, keepdims=True)
        return carry

    flat[...] = jnp.zeros_like(flat)
    lax.fori_loop(0, TILES, tap_grads, 0)
    all_channels_grad(gated, cpt, flat.at[0:C])
    for d in range(ND):
        epiece[d] = flat[:, SLOT * d : SLOT * d + 128].astype(BF16)
    for copy in to_dp(epiece, egot, esend, erecv):
        copy.start()

    def third(t, carry):
        spread_taps(misc[0:32, lane_of(t)], wide_taps)

        def middle(r, carry):
            store_row(ex, r + 2, depth[t, r])
            return carry

        lax.fori_loop(0, ROWS, middle, 0)

        def chunk(q, carry):
            pre = dot_nt(fp[pl.ds(6 * q + 2, 6)].reshape(6 * PIX, C), we[lane_of(t), :])
            dgs[pl.ds(6 * q, 6)] = swish_grad(pre).reshape(6, BLOCK, SUB, 128)
            return carry

        lax.fori_loop(0, 2, chunk, 0)
        for copy in edge_copies(t):
            copy.wait()
        for n in range(2):
            store_row(ex, n, above[t, n].astype(F32) * has_top)
            store_row(ex, ROWS + 2 + n, below[t, n].astype(F32) * has_bottom)

        def conv(r, carry):
            both = []
            for h in range(2):
                slope = dgs[r, :, 8 * h : 8 * h + 8, :]
                both.append(conv_row(ex, r, h, wide_taps, True) * slope)
            dpre[pl.ds(pl.multiple_of(r * PIX, PIX), PIX), lane_of(t)] = (
                jnp.concatenate(both, axis=1).reshape(PIX, 128).astype(BF16)
            )
            return carry

        lax.fori_loop(0, ROWS, conv, 0)

        @pl.when(t == TILES // 2)
        def _():
            total = dp_sum(to_dp(epiece, egot, esend, erecv), epiece, egot)
            espace[me_s] = total.astype(BF16)
            for copy in to_space(espace, fsend, frecv):
                copy.start()

        return carry

    lax.fori_loop(0, TILES, third, 0)

    all_channels_grad(dpre, fpt, flat.at[0:C])
    for d in range(ND):
        lpiece[d] = flat[0:C, SLOT * d : SLOT * d + 128].astype(BF16)
    copies = to_dp(lpiece, lgot, lsend, lrecv)
    for copy in copies:
        copy.start()
    all_channels_out(dpre, we, cp, 0, out_grad)
    early[...] = space_sum(to_space(espace, fsend, frecv), espace)
    for copy in small:
        copy.wait()
    mail_out[...] = mail[...]
    lspace[me_s] = dp_sum(copies, lpiece, lgot).astype(BF16)
    copies = to_space(lspace, gsend, grecv)
    for copy in copies:
        copy.start()
    all_channels_out(gated, wp, fp, 2, out)
    late[...] = space_sum(copies, lspace)


def block(*args):
    def bf16(*shape):
        return pltpu.VMEM(shape, BF16)

    def f32(*shape):
        return pltpu.VMEM(shape, F32)

    def sems(*shape):
        return pltpu.SemaphoreType.DMA(shape)

    one = pltpu.SemaphoreType.DMA
    return pl.pallas_call(
        block_kernel,
        out_shape=(
            jax.ShapeDtypeStruct((IMGS, ROWS, C, COLS), BF16),
            jax.ShapeDtypeStruct((IMGS, ROWS, C, COLS), BF16),
            jax.ShapeDtypeStruct((EARLY, 128), F32),
            jax.ShapeDtypeStruct((C, 128), F32),
            jax.ShapeDtypeStruct((ND, 8, 128), F32),
        ),
        in_specs=[VMEM] * 9,
        out_specs=(VMEM,) * 5,
        scratch_shapes=[
            f32(2, 80, 256),
            bf16(2, 80, 256),
            bf16(2, ND, 80, 256),
            bf16(IMGS, 2, C, COLS),
            bf16(IMGS, 2, C, COLS),
            f32(CP, C),
            bf16(HROWS, PIX, C),
            bf16(ROWS, PIX, C),
            bf16(C, ROWS * PIX),
            bf16(C, ROWS * PIX),
            bf16(CP, C),
            bf16(CP, C),
            f32(136, CP),
            f32(25, 8, 128),
            f32(HROWS, WIDE, SUB, 128),
            f32(ROWS, BLOCK, SUB, 128),
            bf16(TILES, HROWS, WIDE, SUB, 128),
            f32(TILES, ROWS, BLOCK, SUB, 128),
            f32(TILES, 8, 128),
            f32(5, 8, 128),
            f32(NS, 5, 8, 128),
            f32(8, CP + 128),
            f32(8, 128),
            f32(8, CP),
            f32(ND, 8, 128),
            f32(ND, 8, 128),
            bf16(TILES, 2, 2, BLOCK, SUB, 128),
            bf16(TILES, 2, BLOCK, SUB, 128),
            bf16(TILES, 2, BLOCK, SUB, 128),
            bf16(ROWS * PIX, CP),
            bf16(ROWS * PIX, CP),
            f32(25, 8, 128),
            f32(EARLY, CP + 128),
            bf16(ND, EARLY, 128),
            bf16(ND, EARLY, 128),
            bf16(NS, EARLY, 128),
            bf16(ND, C, 128),
            bf16(ND, C, 128),
            bf16(NS, C, 128),
            sems(ND),
            sems(ND),
            sems(2),
            sems(2),
            one,
            one,
            sems(NS),
            sems(NS),
            sems(ND),
            sems(ND),
            sems(2, TILES),
            sems(2, TILES),
            sems(ND),
            sems(ND),
            sems(NS),
            sems(NS),
            sems(ND),
            sems(ND),
            sems(NS),
            sems(NS),
        ],
        compiler_params=pltpu.CompilerParams(
            collective_id=0, has_side_effects=True, vmem_limit_bytes=63 * 2**20
        ),
        name="block",
    )(*args)


def finish_kernel(
    early, late, mail, raw, raw_grad,
    gexp, gdepth, greduce, gexcite, gbex, gproj, gbred, out, out_grad, sem,
):
    moves = [
        pltpu.make_async_copy(raw, out, sem.at[0]),
        pltpu.make_async_copy(raw_grad, out_grad, sem.at[1]),
    ]
    for move in moves:
        move.start()
    gexp[...] = late[...].T[0:PART]
    gproj[...] = early[0:C].T[0:PART]
    gdepth[...] = early[C : C + 25, 0:PART]
    rows = [mail[d] for d in range(ND)]
    pool_all = jnp.concatenate([row[0:2] for row in rows], axis=0)
    dlog_all = jnp.concatenate([row[2:4] for row in rows], axis=0)
    sq_all = jnp.concatenate([row[4:6] for row in rows], axis=0)
    dsq_all = jnp.concatenate([row[6:8] for row in rows], axis=0)
    greduce[...] = dot_tn(dsq_all, pool_all, HIGH)[0:SE, 0:PART]
    gexcite[...] = dot_tn(sq_all, dlog_all, HIGH)[0:SE, 0:PART]
    gbex[...] = jnp.sum(dlog_all, axis=0, keepdims=True)[:, 0:PART]
    gbred[...] = jnp.sum(dsq_all, axis=0, keepdims=True)[:, 0:SE]
    for move in moves:
        move.wait()


def finish(early, late, mail, raw, raw_grad):
    return pl.pallas_call(
        finish_kernel,
        out_shape=(
            jax.ShapeDtypeStruct((PART, C), F32),
            jax.ShapeDtypeStruct((25, PART), F32),
            jax.ShapeDtypeStruct((SE, PART), F32),
            jax.ShapeDtypeStruct((SE, PART), F32),
            jax.ShapeDtypeStruct((1, PART), F32),
            jax.ShapeDtypeStruct((PART, C), F32),
            jax.ShapeDtypeStruct((1, SE), F32),
            jax.ShapeDtypeStruct((IMGS, ROWS, C, COLS), BF16),
            jax.ShapeDtypeStruct((IMGS, ROWS, C, COLS), BF16),
        ),
        in_specs=[VMEM, VMEM, VMEM, ANY, ANY],
        out_specs=(VMEM,) * 7 + (ANY, ANY),
        scratch_shapes=[pltpu.SemaphoreType.DMA((2,))],
        name="finish",
    )(early, late, mail, raw, raw_grad)


def on_device(
    features, w_expand, w_depth, w_reduce, b_reduce, w_excite, b_excite, w_project, cotangent
):
    raw, raw_grad, early, late, mail = block(
        w_expand.T,
        w_project,
        w_depth.reshape(25, PART),
        w_reduce.T,
        w_excite,
        b_excite[None, :],
        b_reduce[None, :],
        features.swapaxes(2, 3),
        cotangent.swapaxes(2, 3),
    )
    (
        s_expand, s_depth, s_reduce, s_excite, s_bexcite, s_project, s_breduce, output, grad,
    ) = finish(early, late, mail, raw, raw_grad)
    return (
        output.swapaxes(2, 3),
        grad.swapaxes(2, 3),
        s_expand.T,
        s_depth.reshape(5, 5, PART),
        s_reduce.T,
        s_excite,
        s_bexcite[0],
        s_project,
        s_breduce[0],
    )


def solution(mesh):
    return jax.shard_map(
        on_device,
        mesh=mesh,
        in_specs=(
            P("dp", "space", None, None),
            P(None, "dp"),
            P(None, None, "dp"),
            P("dp", None),
            P(),
            P(None, "dp"),
            P("dp"),
            P("dp", None),
            P("dp", "space", None, None),
        ),
        out_specs=(
            P("dp", "space", None, None),
            P("dp", "space", None, None),
            P(None, "dp"),
            P(None, None, "dp"),
            P("dp", None),
            P(None, "dp"),
            P("dp"),
            P("dp", None),
            P(),
        ),
        check_vma=False,
    )
```

```python
import functools

import jax
import jax.numpy as jnp
from jax import lax
from jax.experimental import pallas as pl
from jax.experimental.pallas import tpu as pltpu
from jax.sharding import PartitionSpec as P

F32 = jnp.float32
BF16 = jnp.bfloat16
MESH = pl.DeviceIdType.MESH
HIGH = lax.Precision.HIGHEST

IMGS, ROWS, COLS, C, SE = 2, 12, 100, 176, 44
BLOCK, SUB = 13, 16
PIX = BLOCK * SUB
WIDE = BLOCK + 4
HROWS = ROWS + 4
PART, SLOT = 66, 72
CP = 16 * SLOT
TILES = CP // 128
AREA = 9600.0
NS, ND = 8, 16

VMEM = pl.BlockSpec(memory_space=pltpu.VMEM)
ANY = pl.BlockSpec(memory_space=pl.ANY)


def sigmoid(value):
    return 0.5 * jnp.tanh(0.5 * value) + 0.5


def swish(value):
    return value * sigmoid(value)


def swish_grad(value):
    sig = sigmoid(value)
    act = value * sig
    return sig + act - act * sig


def dot_nt(left, right, precision=None):
    return lax.dot_general(
        left, right, (((1,), (1,)), ((), ())), precision=precision, preferred_element_type=F32
    )


def dot_tn(left, right, precision=None):
    return lax.dot_general(
        left, right, (((0,), (0,)), ((), ())), precision=precision, preferred_element_type=F32
    )


def dot_nn(left, right, precision=None):
    return lax.dot_general(
        left, right, (((1,), (0,)), ((), ())), precision=precision, preferred_element_type=F32
    )


def one_hot(img, transposed):
    shape = (COLS, PIX) if transposed else (PIX, COLS)
    place = lax.broadcasted_iota(jnp.int32, shape, 1 if transposed else 0)
    col = lax.broadcasted_iota(jnp.int32, shape, 0 if transposed else 1)
    wanted = (col % BLOCK) * SUB + img * 8 + col // BLOCK
    return jnp.where(place == wanted, 1.0, 0.0).astype(BF16)


def spread_taps(taps, wide_taps):
    for k in range(25):
        wide_taps[k] = jnp.broadcast_to(taps[k : k + 1, :], (8, 128))


def edge_columns(value):
    split = value.reshape(BLOCK, 2, 8, 128)
    block = lax.broadcasted_iota(jnp.int32, (2, 2, 8, 128), 2)
    left = jnp.where(block > 0, pltpu.roll(split[BLOCK - 2 :], 1, 2), 0.0)
    right = jnp.where(block < 7, pltpu.roll(split[:2], 7, 2), 0.0)
    return left.reshape(2, SUB, 128), right.reshape(2, SUB, 128)


def store_row(ref, r, value):
    left, right = edge_columns(value)
    ref[r, 0:2] = left
    ref[r, 2 : 2 + BLOCK] = value
    ref[r, 2 + BLOCK :] = right


def conv_row(ref, r, h, wide_taps, flip):
    total = jnp.zeros((BLOCK, 8, 128), F32)
    for i in range(5):
        source = ref[r + i, :, 8 * h : 8 * h + 8, :]
        for j in range(5):
            k = (4 - i) * 5 + 4 - j if flip else i * 5 + j
            total = total + source[j : j + BLOCK] * wide_taps[k][None]
    return total


def pad_mask():
    block = lax.broadcasted_iota(jnp.int32, (4, 8, 128), 1)
    return jnp.where(block < 7, 1.0, 0.0)


def gate_row(depth, dgated, gates, h, keep):
    gate = gates[h : h + 1, :][None]
    pull = gates[2 + h : 3 + h, :][None]
    sig = sigmoid(depth)
    act = depth * sig
    gated = act * gate
    ddepth = (dgated * gate + pull) * (sig + act - act * sig)
    ddepth = jnp.concatenate([ddepth[:9], ddepth[9:] * keep], axis=0)
    return gated, ddepth


def unpermute(value, out, r):
    for img in range(2):
        out[img, r] = dot_tn(value, one_hot(img, False)).astype(BF16)


def all_channels_out(rows_in, weights, base, shift, out):
    def chunk(q, carry):
        block = rows_in[pl.ds(pl.multiple_of(4 * PIX * q, 4 * PIX), 4 * PIX), :]
        product = dot_nn(block, weights[...]).reshape(4, PIX, C)
        for n in range(4):
            value = product[n] + base[4 * q + n + shift].astype(F32)
            unpermute(value.astype(BF16), out, 4 * q + n)
        return carry

    lax.fori_loop(0, 3, chunk, 0)


def all_channels_grad(rows_in, turned, grad):
    def lanes(q, carry):
        span = pl.ds(pl.multiple_of(384 * q, 128), 384)
        grad[:, span] = dot_nn(turned[...], rows_in[:, span])
        return carry

    lax.fori_loop(0, 3, lanes, 0)


def to_dp(src, dst, send, recv, by_sender=False):
    me_s, me_d = lax.axis_index("space"), lax.axis_index("dp")
    copies = []
    for k in range(1, ND):
        target = lax.rem(me_d + k, ND)
        copies.append(
            pltpu.make_async_remote_copy(
                src_ref=src.at[target],
                dst_ref=dst.at[me_d] if by_sender else dst.at[k],
                send_sem=send.at[k],
                recv_sem=recv.at[k],
                device_id=(me_s, target),
                device_id_type=MESH,
            )
        )
    return copies


def to_space(ref, send, recv):
    me_s, me_d = lax.axis_index("space"), lax.axis_index("dp")
    copies = []
    for k in range(1, NS):
        copies.append(
            pltpu.make_async_remote_copy(
                src_ref=ref.at[me_s],
                dst_ref=ref.at[me_s],
                send_sem=send.at[k],
                recv_sem=recv.at[k],
                device_id=(lax.rem(me_s + k, NS), me_d),
                device_id_type=MESH,
            )
        )
    return copies


def to_neighbours(down_src, down_dst, up_src, up_dst, send, recv):
    me_s, me_d = lax.axis_index("space"), lax.axis_index("dp")
    down = pltpu.make_async_remote_copy(
        src_ref=down_src,
        dst_ref=down_dst,
        send_sem=send[0],
        recv_sem=recv[0],
        device_id=(lax.rem(me_s + 1, NS), me_d),
        device_id_type=MESH,
    )
    up = pltpu.make_async_remote_copy(
        src_ref=up_src,
        dst_ref=up_dst,
        send_sem=send[1],
        recv_sem=recv[1],
        device_id=(lax.rem(me_s + NS - 1, NS), me_d),
        device_id_type=MESH,
    )
    return down, up


def dp_sum(copies, piece, got):
    total = piece[lax.axis_index("dp")].astype(F32)
    for k, copy in enumerate(copies):
        copy.wait()
        total = total + got[k + 1].astype(F32)
    return total


def space_sum(copies, ref):
    for copy in copies:
        copy.wait()
    total = ref[0].astype(F32)
    for s in range(1, NS):
        total = total + ref[s].astype(F32)
    return total


EARLY = C + 32


def block_kernel(
    wet, wpr, taps, wrt, wx_own, bex, bred, feats, cot,
    out, out_grad, early, late, mail_out,
    stage, pack, full, top, bottom, flatw, fp, cp, fpt, cpt, we, wp, misc,
    wide_taps, ex, dgs, saved, depth, sums, packed, landed, lanes, vecs, gates, msgs, mail,
    edge, above, below, gated, dpre, acc, flat, epiece, egot, espace, lpiece, lgot, lspace,
    wsend, wrecv, hsend, hrecv, csend, crecv, ssend, srecv, msend, mrecv,
    dsend, drecv, esend, erecv, fsend, frecv, lsend, lrecv, gsend, grecv,
):
    me_s, me_d = lax.axis_index("space"), lax.axis_index("dp")
    core = lax.rem(me_s, 2)
    barrier = pltpu.get_barrier_semaphore()
    for k in range(1, ND):
        pl.semaphore_signal(
            barrier, inc=1, device_id=(me_s, lax.rem(me_d + k, ND)), device_id_type=MESH
        )
    for k in range(1, NS):
        pl.semaphore_signal(
            barrier, inc=1, device_id=(lax.rem(me_s + k, NS), me_d), device_id_type=MESH
        )

    stage[...] = jnp.zeros_like(stage)
    stage[0, 0:PART, 0:C] = wet[...].astype(F32)
    stage[1, 0:PART, 0:C] = wpr[...].astype(F32)
    side = slice(C, C + PART)
    stage[0, 0:25, side] = taps[...].astype(F32)
    stage[0, 32 : 32 + SE, side] = wrt[...].astype(F32)
    stage[1, 0:SE, side] = wx_own[...].astype(F32)
    stage[1, 48:49, side] = bex[...].astype(F32)
    pack[...] = stage[...].astype(BF16)
    pl.semaphore_wait(barrier, NS + ND - 2)
    copies = []
    for k in range(1, ND):
        copy = pltpu.make_async_remote_copy(
            src_ref=pack.at[core],
            dst_ref=full.at[core, me_d],
            send_sem=wsend.at[k],
            recv_sem=wrecv.at[k],
            device_id=(me_s, lax.rem(me_d + k, ND)),
            device_id_type=MESH,
        )
        copy.start()
        copies.append(copy)
    halo = to_neighbours(
        feats.at[:, pl.ds(ROWS - 2, 2)],
        top,
        feats.at[:, pl.ds(0, 2)],
        bottom,
        (hsend.at[0], hsend.at[1]),
        (hrecv.at[0], hrecv.at[1]),
    )
    for copy in halo:
        copy.start()
    full[core, me_d] = pack[core]
    spread = (one_hot(0, False), one_hot(1, False))
    gather_t = (one_hot(0, True), one_hot(1, True))

    def permute(r, carry):
        for src, dst, shift in ((feats, fp, 2), (cot, cp, 0)):
            a, b = src[0, r], src[1, r]
            dst[r + shift] = (dot_nt(spread[0], a) + dot_nt(spread[1], b)).astype(BF16)
        return carry

    lax.fori_loop(0, ROWS, permute, 0)
    for r in range(ROWS):
        for src, dst in ((feats, fpt), (cot, cpt)):
            value = dot_nn(src[0, r], gather_t[0]) + dot_nn(src[1, r], gather_t[1])
            dst[:, PIX * r : PIX * (r + 1)] = value.astype(BF16)
    for copy in copies:
        copy.wait()
    share = pltpu.make_async_remote_copy(
        src_ref=full.at[core],
        dst_ref=full.at[core],
        send_sem=csend,
        recv_sem=crecv,
        device_id=(me_s + 1 - 2 * core, me_d),
        device_id_type=MESH,
    )
    share.start()
    for copy in halo:
        copy.wait()
    has_top = jnp.where(me_s > 0, 1.0, 0.0)
    has_bottom = jnp.where(me_s < NS - 1, 1.0, 0.0)
    for r in range(2):
        value = dot_nt(spread[0], top[0, r]) + dot_nt(spread[1], top[1, r])
        fp[r] = (value * has_top).astype(BF16)
        value = dot_nt(spread[0], bottom[0, r]) + dot_nt(spread[1], bottom[1, r])
        fp[ROWS + 2 + r] = (value * has_bottom).astype(BF16)
    share.wait()
    for half, whole in ((0, we), (1, wp)):
        for d in range(ND):
            part = full[half, d].astype(F32)
            flatw[d * SLOT : (d + 1) * SLOT, :] = part[0:SLOT, 0:C]
            span = slice(d * SLOT, (d + 1) * SLOT)
            if half == 0:
                misc[0:80, span] = part[:, C : C + SLOT]
            else:
                misc[80:136, span] = part[0:56, C : C + SLOT]
        whole[...] = flatw[...].astype(BF16)

    keep = pad_mask()

    def lane_of(t):
        return pl.ds(pl.multiple_of(128 * t, 128), 128)

    def cot_matmul(t):
        def chunk(q, carry):
            rows = pl.ds(6 * q, 6)
            product = dot_nt(cp[rows].reshape(6 * PIX, C), wp[lane_of(t), :])
            dgs[rows] = product.reshape(6, BLOCK, SUB, 128)
            return carry

        lax.fori_loop(0, 2, chunk, 0)

    def first(t, carry):
        spread_taps(misc[0:32, lane_of(t)], wide_taps)

        def expand(q, carry):
            pre = dot_nt(fp[pl.ds(8 * q, 8)].reshape(8 * PIX, C), we[lane_of(t), :])
            value = swish(pre).astype(BF16).astype(F32).reshape(8, BLOCK, SUB, 128)
            for n in range(8):
                store_row(ex, 8 * q + n, value[n])
            return carry

        lax.fori_loop(0, 2, expand, 0)
        cot_matmul(t)

        def conv(r, carry):
            pools, grads = list(carry[:2]), list(carry[2:])
            for h in range(2):
                total = conv_row(ex, r, h, wide_taps, False)
                depth[t, r, :, 8 * h : 8 * h + 8, :] = total
                act = swish(total)
                dgated = dgs[r, :, 8 * h : 8 * h + 8, :]
                grads[h] = grads[h] + jnp.sum(act * dgated, axis=0)
                pools[h] = pools[h] + jnp.sum(act[:9], axis=0) + jnp.sum(act[9:] * keep, axis=0)
            saved[t, r] = ex[r].astype(BF16)
            return (*pools, *grads)

        zero = jnp.zeros((8, 128), F32)
        parts = lax.fori_loop(0, ROWS, conv, (zero,) * 4)
        for r in range(ROWS, HROWS):
            saved[t, r] = ex[r].astype(BF16)
        for k in range(4):
            sums[t, k : k + 1, :] = jnp.sum(parts[k], axis=0, keepdims=True)
        return carry

    lax.fori_loop(0, TILES, first, 0)

    packed[...] = jnp.zeros_like(packed)
    for t in range(TILES):
        packed[t // 2, 4 * (t % 2) : 4 * (t % 2) + 4, :] = sums[t, 0:4, :]
    landed[me_s] = packed[...]
    copies = to_space(landed, ssend, srecv)
    for copy in copies:
        copy.start()
    total = space_sum(copies, landed)
    for t in range(TILES):
        lanes[0:4, 128 * t : 128 * (t + 1)] = total[t // 2, 4 * (t % 2) : 4 * (t % 2) + 4]
    lanes[:, CP:] = jnp.zeros((8, 128), F32)
    wr = misc[32 : 32 + SE, :]
    wx = misc[80 : 80 + SE, :]
    pooled = lanes[0:2, 0:CP] / AREA
    dgate = lanes[2:4, 0:CP]
    squeeze_pre = dot_nt(pooled, wr, HIGH) + bred[...].astype(F32)
    squeeze = swish(squeeze_pre)
    gate = sigmoid(dot_nn(squeeze, wx, HIGH) + misc[128:129, :])
    dlogit = dgate * gate * (1.0 - gate)
    dsq = dot_nt(dlogit, wx, HIGH) * swish_grad(squeeze_pre)
    dpooled = dot_nn(dsq, wr, HIGH)
    gates[0:2, :] = gate
    gates[2:4, :] = dpooled / AREA
    gates[4:8, :] = jnp.zeros((4, CP), F32)
    lanes[0:2, 0:CP] = pooled
    lanes[2:4, 0:CP] = dlogit
    vecs[...] = jnp.zeros((8, 128), F32)
    vecs[4:6, 0:SE] = squeeze
    vecs[6:8, 0:SE] = dsq
    for d in range(ND):
        msgs[d, 0:4, :] = lanes[0:4, SLOT * d : SLOT * d + 128]
        msgs[d, 4:8, :] = vecs[4:8, :]
    mail[me_d] = msgs[me_d]
    small = to_dp(msgs, mail, msend, mrecv, True)
    for copy in small:
        copy.start()

    def edge_copies(t):
        return to_neighbours(
            edge.at[t, 1],
            above.at[t],
            edge.at[t, 0],
            below.at[t],
            (dsend.at[0, t], dsend.at[1, t]),
            (drecv.at[0, t], drecv.at[1, t]),
        )

    def second(t, carry):
        cot_matmul(t)

        def pointwise(r, carry):
            both = []
            for h in range(2):
                rows = slice(8 * h, 8 * h + 8)
                value, ddepth = gate_row(
                    depth[t, r, :, rows, :], dgs[r, :, rows, :], gates.at[:, lane_of(t)], h, keep
                )
                depth[t, r, :, rows, :] = ddepth.astype(BF16).astype(F32)
                both.append(value)
            gated[pl.ds(pl.multiple_of(r * PIX, PIX), PIX), lane_of(t)] = (
                jnp.concatenate(both, axis=1).reshape(PIX, 128).astype(BF16)
            )
            return carry

        lax.fori_loop(0, ROWS, pointwise, 0)
        for n in range(2):
            edge[t, 0, n] = depth[t, n].astype(BF16)
            edge[t, 1, n] = depth[t, ROWS - 2 + n].astype(BF16)
        for copy in edge_copies(t):
            copy.start()
        return carry

    lax.fori_loop(0, TILES, second, 0)

    def tap_grads(t, carry):
        acc[...] = jnp.zeros_like(acc)

        def row(r, carry):
            for h in range(2):
                rows = slice(8 * h, 8 * h + 8)
                mine = depth[t, r, :, rows, :]
                for i in range(5):
                    source = saved[t, r + i].astype(F32)[:, rows, :]
                    for j in range(5):
                        k = 5 * i + j
                        acc[k] = acc[k] + jnp.sum(mine * source[j : j + BLOCK], axis=0)
            return carry

        lax.fori_loop(0, ROWS, row, 0)
        for k in range(25):
            flat[C + k : C + k + 1, lane_of(t)] = jnp.sum(acc[k], axis=0, keepdims=True)
        return carry

    flat[...] = jnp.zeros_like(flat)
    lax.fori_loop(0, TILES, tap_grads, 0)
    all_channels_grad(gated, cpt, flat.at[0:C])
    for d in range(ND):
        epiece[d] = flat[:, SLOT * d : SLOT * d + 128].astype(BF16)
    for copy in to_dp(epiece, egot, esend, erecv):
        copy.start()

    def third(t, carry):
        spread_taps(misc[0:32, lane_of(t)], wide_taps)

        def middle(r, carry):
            store_row(ex, r + 2, depth[t, r])
            return carry

        lax.fori_loop(0, ROWS, middle, 0)

        def chunk(q, carry):
            pre = dot_nt(fp[pl.ds(6 * q + 2, 6)].reshape(6 * PIX, C), we[lane_of(t), :])
            dgs[pl.ds(6 * q, 6)] = swish_grad(pre).reshape(6, BLOCK, SUB, 128)
            return carry

        lax.fori_loop(0, 2, chunk, 0)
        for copy in edge_copies(t):
            copy.wait()
        for n in range(2):
            store_row(ex, n, above[t, n].astype(F32) * has_top)
            store_row(ex, ROWS + 2 + n, below[t, n].astype(F32) * has_bottom)

        def conv(r, carry):
            both = []
            for h in range(2):
                slope = dgs[r, :, 8 * h : 8 * h + 8, :]
                both.append(conv_row(ex, r, h, wide_taps, True) * slope)
            dpre[pl.ds(pl.multiple_of(r * PIX, PIX), PIX), lane_of(t)] = (
                jnp.concatenate(both, axis=1).reshape(PIX, 128).astype(BF16)
            )
            return carry

        lax.fori_loop(0, ROWS, conv, 0)

        @pl.when(t == TILES // 2)
        def _():
            total = dp_sum(to_dp(epiece, egot, esend, erecv), epiece, egot)
            espace[me_s] = total.astype(BF16)
            for copy in to_space(espace, fsend, frecv):
                copy.start()

        return carry

    lax.fori_loop(0, TILES, third, 0)

    all_channels_grad(dpre, fpt, flat.at[0:C])
    for d in range(ND):
        lpiece[d] = flat[0:C, SLOT * d : SLOT * d + 128].astype(BF16)
    copies = to_dp(lpiece, lgot, lsend, lrecv)
    for copy in copies:
        copy.start()
    all_channels_out(dpre, we, cp, 0, out_grad)
    early[...] = space_sum(to_space(espace, fsend, frecv), espace)
    for copy in small:
        copy.wait()
    mail_out[...] = mail[...]
    lspace[me_s] = dp_sum(copies, lpiece, lgot).astype(BF16)
    copies = to_space(lspace, gsend, grecv)
    for copy in copies:
        copy.start()
    all_channels_out(gated, wp, fp, 2, out)
    late[...] = space_sum(copies, lspace)


def block(*args):
    def bf16(*shape):
        return pltpu.VMEM(shape, BF16)

    def f32(*shape):
        return pltpu.VMEM(shape, F32)

    def sems(*shape):
        return pltpu.SemaphoreType.DMA(shape)

    one = pltpu.SemaphoreType.DMA
    return pl.pallas_call(
        block_kernel,
        out_shape=(
            jax.ShapeDtypeStruct((IMGS, ROWS, C, COLS), BF16),
            jax.ShapeDtypeStruct((IMGS, ROWS, C, COLS), BF16),
            jax.ShapeDtypeStruct((EARLY, 128), F32),
            jax.ShapeDtypeStruct((C, 128), F32),
            jax.ShapeDtypeStruct((ND, 8, 128), F32),
        ),
        in_specs=[VMEM] * 9,
        out_specs=(VMEM,) * 5,
        scratch_shapes=[
            f32(2, 80, 256),
            bf16(2, 80, 256),
            bf16(2, ND, 80, 256),
            bf16(IMGS, 2, C, COLS),
            bf16(IMGS, 2, C, COLS),
            f32(CP, C),
            bf16(HROWS, PIX, C),
            bf16(ROWS, PIX, C),
            bf16(C, ROWS * PIX),
            bf16(C, ROWS * PIX),
            bf16(CP, C),
            bf16(CP, C),
            f32(136, CP),
            f32(25, 8, 128),
            f32(HROWS, WIDE, SUB, 128),
            f32(ROWS, BLOCK, SUB, 128),
            bf16(TILES, HROWS, WIDE, SUB, 128),
            f32(TILES, ROWS, BLOCK, SUB, 128),
            f32(TILES, 8, 128),
            f32(5, 8, 128),
            f32(NS, 5, 8, 128),
            f32(8, CP + 128),
            f32(8, 128),
            f32(8, CP),
            f32(ND, 8, 128),
            f32(ND, 8, 128),
            bf16(TILES, 2, 2, BLOCK, SUB, 128),
            bf16(TILES, 2, BLOCK, SUB, 128),
            bf16(TILES, 2, BLOCK, SUB, 128),
            bf16(ROWS * PIX, CP),
            bf16(ROWS * PIX, CP),
            f32(25, 8, 128),
            f32(EARLY, CP + 128),
            bf16(ND, EARLY, 128),
            bf16(ND, EARLY, 128),
            bf16(NS, EARLY, 128),
            bf16(ND, C, 128),
            bf16(ND, C, 128),
            bf16(NS, C, 128),
            sems(ND),
            sems(ND),
            sems(2),
            sems(2),
            one,
            one,
            sems(NS),
            sems(NS),
            sems(ND),
            sems(ND),
            sems(2, TILES),
            sems(2, TILES),
            sems(ND),
            sems(ND),
            sems(NS),
            sems(NS),
            sems(ND),
            sems(ND),
            sems(NS),
            sems(NS),
        ],
        compiler_params=pltpu.CompilerParams(
            collective_id=0, has_side_effects=True, vmem_limit_bytes=63 * 2**20
        ),
        name="block",
    )(*args)


def finish_kernel(
    early, late, mail, raw, raw_grad,
    gexp, gdepth, greduce, gexcite, gbex, gproj, gbred, out, out_grad,
):
    out[...] = raw[...]
    out_grad[...] = raw_grad[...]

    @pl.when(pl.program_id(0) == 0)
    def _():
        gexp[...] = late[...].T[0:PART]
        gproj[...] = early[0:C].T[0:PART]
        gdepth[...] = early[C : C + 25, 0:PART]
        rows = [mail[d] for d in range(ND)]
        pool_all = jnp.concatenate([row[0:2] for row in rows], axis=0)
        dlog_all = jnp.concatenate([row[2:4] for row in rows], axis=0)
        sq_all = jnp.concatenate([row[4:6] for row in rows], axis=0)
        dsq_all = jnp.concatenate([row[6:8] for row in rows], axis=0)
        greduce[...] = dot_tn(dsq_all, pool_all, HIGH)[0:SE, 0:PART]
        gexcite[...] = dot_tn(sq_all, dlog_all, HIGH)[0:SE, 0:PART]
        gbex[...] = jnp.sum(dlog_all, axis=0, keepdims=True)[:, 0:PART]
        gbred[...] = jnp.sum(dsq_all, axis=0, keepdims=True)[:, 0:SE]


def finish(early, late, mail, raw, raw_grad):
    def whole(*shape):
        zeros = (0,) * len(shape)
        return pl.BlockSpec(shape, lambda n: zeros)

    part = pl.BlockSpec((IMGS, 3, C, COLS), lambda n: (0, n, 0, 0))
    shapes = ((PART, C), (25, PART), (SE, PART), (SE, PART), (1, PART), (PART, C), (1, SE))
    return pl.pallas_call(
        finish_kernel,
        grid=(ROWS // 3,),
        out_shape=tuple(jax.ShapeDtypeStruct(shape, F32) for shape in shapes)
        + (jax.ShapeDtypeStruct((IMGS, ROWS, C, COLS), BF16),) * 2,
        in_specs=[whole(EARLY, 128), whole(C, 128), whole(ND, 8, 128), part, part],
        out_specs=tuple(whole(*shape) for shape in shapes) + (part, part),
        name="finish",
    )(early, late, mail, raw, raw_grad)


def on_device(
    features, w_expand, w_depth, w_reduce, b_reduce, w_excite, b_excite, w_project, cotangent
):
    raw, raw_grad, early, late, mail = block(
        w_expand.T,
        w_project,
        w_depth.reshape(25, PART),
        w_reduce.T,
        w_excite,
        b_excite[None, :],
        b_reduce[None, :],
        features.swapaxes(2, 3),
        cotangent.swapaxes(2, 3),
    )
    (
        s_expand, s_depth, s_reduce, s_excite, s_bexcite, s_project, s_breduce, output, grad,
    ) = finish(early, late, mail, raw, raw_grad)
    return (
        output.swapaxes(2, 3),
        grad.swapaxes(2, 3),
        s_expand.T,
        s_depth.reshape(5, 5, PART),
        s_reduce.T,
        s_excite,
        s_bexcite[0],
        s_project,
        s_breduce[0],
    )


def solution(mesh):
    return jax.shard_map(
        on_device,
        mesh=mesh,
        in_specs=(
            P("dp", "space", None, None),
            P(None, "dp"),
            P(None, None, "dp"),
            P("dp", None),
            P(),
            P(None, "dp"),
            P("dp"),
            P("dp", None),
            P("dp", "space", None, None),
        ),
        out_specs=(
            P("dp", "space", None, None),
            P("dp", "space", None, None),
            P(None, "dp"),
            P(None, None, "dp"),
            P("dp", None),
            P(None, "dp"),
            P("dp"),
            P("dp", None),
            P(),
        ),
        check_vma=False,
    )
```

```python
import functools

import jax
import jax.numpy as jnp
from jax import lax
from jax.experimental import pallas as pl
from jax.experimental.pallas import tpu as pltpu
from jax.sharding import PartitionSpec as P

F32 = jnp.float32
BF16 = jnp.bfloat16
MESH = pl.DeviceIdType.MESH
HIGH = lax.Precision.HIGHEST

IMGS, ROWS, COLS, C, SE = 2, 12, 100, 176, 44
BLOCK, SUB = 13, 16
PIX = BLOCK * SUB
WIDE = BLOCK + 4
HROWS = ROWS + 4
PART, SLOT = 66, 72
CP = 16 * SLOT
TILES = CP // 128
AREA = 9600.0
NS, ND = 8, 16

VMEM = pl.BlockSpec(memory_space=pltpu.VMEM)
ANY = pl.BlockSpec(memory_space=pl.ANY)


def sigmoid(value):
    return 0.5 * jnp.tanh(0.5 * value) + 0.5


def swish(value):
    return value * sigmoid(value)


def swish_grad(value):
    sig = sigmoid(value)
    act = value * sig
    return sig + act - act * sig


def dot_nt(left, right, precision=None):
    return lax.dot_general(
        left, right, (((1,), (1,)), ((), ())), precision=precision, preferred_element_type=F32
    )


def dot_tn(left, right, precision=None):
    return lax.dot_general(
        left, right, (((0,), (0,)), ((), ())), precision=precision, preferred_element_type=F32
    )


def dot_nn(left, right, precision=None):
    return lax.dot_general(
        left, right, (((1,), (0,)), ((), ())), precision=precision, preferred_element_type=F32
    )


def one_hot(img, transposed):
    shape = (COLS, PIX) if transposed else (PIX, COLS)
    place = lax.broadcasted_iota(jnp.int32, shape, 1 if transposed else 0)
    col = lax.broadcasted_iota(jnp.int32, shape, 0 if transposed else 1)
    wanted = (col % BLOCK) * SUB + img * 8 + col // BLOCK
    return jnp.where(place == wanted, 1.0, 0.0).astype(BF16)


def point_taps(taps):
    w0, w1, w2, w3, w4 = taps
    even, odd = w0 + w2 + w4, w1 + w3
    even2, odd2 = w0 + 4.0 * w2 + 16.0 * w4, 2.0 * w1 + 8.0 * w3
    even3, odd3 = w0 + 0.25 * w2 + 0.0625 * w4, 0.5 * w1 + 0.125 * w3
    return [
        w0,
        (even + odd) * (-2.0 / 9.0),
        (even - odd) * (-2.0 / 9.0),
        (even2 + odd2) * (1.0 / 360.0),
        (even2 - odd2) * (1.0 / 360.0),
        (even3 + odd3) * (32.0 / 45.0),
        (even3 - odd3) * (32.0 / 45.0),
        w4,
    ]


def taps_from_points(g):
    s1, d1 = (g[1] + g[2]) * (-2.0 / 9.0), (g[1] - g[2]) * (-2.0 / 9.0)
    s2, d2 = (g[3] + g[4]) * (1.0 / 360.0), (g[3] - g[4]) * (1.0 / 360.0)
    s3, d3 = (g[5] + g[6]) * (32.0 / 45.0), (g[5] - g[6]) * (32.0 / 45.0)
    return [
        g[0] + s1 + s2 + s3,
        d1 + 2.0 * d2 + 0.5 * d3,
        s1 + 4.0 * s2 + 0.25 * s3,
        d1 + 8.0 * d2 + 0.125 * d3,
        s1 + 16.0 * s2 + 0.0625 * s3 + g[7],
    ]


def to_points(x):
    x0, x1, x2, x3, x4, x5, x6, x7 = x
    f3, f4 = 5.0 * x3, 5.0 * x4
    e1, o1 = (x6 + x2) - 4.25 * x4, (x5 + x1) - 4.25 * x3
    e2, o2 = (x2 - f4) + 4.0 * x6, (x1 - f3) + 4.0 * x5
    e3, o3 = (4.0 * x2 - f4) + x6, (4.0 * x1 - f3) + x5
    o2, o3 = o2 + o2, 0.5 * o3
    return [
        (x0 - x6) + 5.25 * (x4 - x2),
        e1 + o1,
        e1 - o1,
        e2 + o2,
        e2 - o2,
        e3 + o3,
        e3 - o3,
        (x7 - x1) + 5.25 * (x3 - x5),
    ]


def from_points(m):
    s1, d1 = m[1] + m[2], m[1] - m[2]
    s2, d2 = m[3] + m[4], m[3] - m[4]
    s3, d3 = m[5] + m[6], m[5] - m[6]
    return [
        (m[0] + s1) + (s2 + s3),
        (d1 + 2.0 * d2) + 0.5 * d3,
        (s1 + 4.0 * s2) + 0.25 * s3,
        ((d1 + 8.0 * d2) + 0.125 * d3) + m[7],
    ]


def outputs_to_points(y):
    y0, y1, y2, y3 = y
    a, b = y0 + y2, y1 + y3
    c, d = y0 + 4.0 * y2, 2.0 * y1 + 8.0 * y3
    e, f = y0 + 0.25 * y2, 0.5 * y1 + 0.125 * y3
    return [y0, a + b, a - b, c + d, c - d, e + f, e - f, y3]


def spread_taps(taps, wide_taps, flip):
    for j in range(5):
        column = [taps[5 * i + j : 5 * i + j + 1, :] for i in range(5)]
        if flip:
            column = column[::-1]
        place = 4 - j if flip else j
        for p, value in enumerate(point_taps(column)):
            wide_taps[5 * p + place] = jnp.broadcast_to(value, (8, 128))


def edge_columns(value):
    split = value.reshape(BLOCK, 2, 8, 128)
    block = lax.broadcasted_iota(jnp.int32, (2, 2, 8, 128), 2)
    left = jnp.where(block > 0, pltpu.roll(split[BLOCK - 2 :], 1, 2), 0.0)
    right = jnp.where(block < 7, pltpu.roll(split[:2], 7, 2), 0.0)
    return left.reshape(2, SUB, 128), right.reshape(2, SUB, 128)


def store_row(ref, r, value):
    left, right = edge_columns(value)
    ref[r, 0:2] = left
    ref[r, 2 : 2 + BLOCK] = value
    ref[r, 2 + BLOCK :] = right


def conv_rows(ref, q, h, wide_taps):
    points = to_points([ref[4 * q + n, :, 8 * h : 8 * h + 8, :] for n in range(8)])
    totals = []
    for p in range(8):
        total = points[p][0:BLOCK] * wide_taps[5 * p][None]
        for j in range(1, 5):
            total = total + points[p][j : j + BLOCK] * wide_taps[5 * p + j][None]
        totals.append(total)
    return from_points(totals)


def pad_mask():
    block = lax.broadcasted_iota(jnp.int32, (4, 8, 128), 1)
    return jnp.where(block < 7, 1.0, 0.0)


def gate_row(depth, dgated, gates, h, keep):
    gate = gates[h : h + 1, :][None]
    pull = gates[2 + h : 3 + h, :][None]
    sig = sigmoid(depth)
    act = depth * sig
    gated = act * gate
    ddepth = (dgated * gate + pull) * (sig + act - act * sig)
    ddepth = jnp.concatenate([ddepth[:9], ddepth[9:] * keep], axis=0)
    return gated, ddepth


def unpermute(value, out, r):
    for img in range(2):
        out[img, r] = dot_tn(value, one_hot(img, False)).astype(BF16)


def all_channels_out(rows_in, weights, base, shift, out):
    def chunk(q, carry):
        block = rows_in[pl.ds(pl.multiple_of(4 * PIX * q, 4 * PIX), 4 * PIX), :]
        product = dot_nn(block, weights[...]).reshape(4, PIX, C)
        for n in range(4):
            value = product[n] + base[4 * q + n + shift].astype(F32)
            unpermute(value.astype(BF16), out, 4 * q + n)
        return carry

    lax.fori_loop(0, 3, chunk, 0)


def all_channels_grad(rows_in, turned, grad):
    def lanes(q, carry):
        span = pl.ds(pl.multiple_of(384 * q, 128), 384)
        grad[:, span] = dot_nn(turned[...], rows_in[:, span])
        return carry

    lax.fori_loop(0, 3, lanes, 0)


def to_dp(src, dst, send, recv, by_sender=False):
    me_s, me_d = lax.axis_index("space"), lax.axis_index("dp")
    copies = []
    for k in range(1, ND):
        target = lax.rem(me_d + k, ND)
        copies.append(
            pltpu.make_async_remote_copy(
                src_ref=src.at[target],
                dst_ref=dst.at[me_d] if by_sender else dst.at[k],
                send_sem=send.at[k],
                recv_sem=recv.at[k],
                device_id=(me_s, target),
                device_id_type=MESH,
            )
        )
    return copies


def to_space(ref, send, recv):
    me_s, me_d = lax.axis_index("space"), lax.axis_index("dp")
    copies = []
    for k in range(1, NS):
        copies.append(
            pltpu.make_async_remote_copy(
                src_ref=ref.at[me_s],
                dst_ref=ref.at[me_s],
                send_sem=send.at[k],
                recv_sem=recv.at[k],
                device_id=(lax.rem(me_s + k, NS), me_d),
                device_id_type=MESH,
            )
        )
    return copies


def to_neighbours(down_src, down_dst, up_src, up_dst, send, recv):
    me_s, me_d = lax.axis_index("space"), lax.axis_index("dp")
    down = pltpu.make_async_remote_copy(
        src_ref=down_src,
        dst_ref=down_dst,
        send_sem=send[0],
        recv_sem=recv[0],
        device_id=(lax.rem(me_s + 1, NS), me_d),
        device_id_type=MESH,
    )
    up = pltpu.make_async_remote_copy(
        src_ref=up_src,
        dst_ref=up_dst,
        send_sem=send[1],
        recv_sem=recv[1],
        device_id=(lax.rem(me_s + NS - 1, NS), me_d),
        device_id_type=MESH,
    )
    return down, up


def dp_sum(copies, piece, got):
    total = piece[lax.axis_index("dp")].astype(F32)
    for k, copy in enumerate(copies):
        copy.wait()
        total = total + got[k + 1].astype(F32)
    return total


def space_sum(copies, ref):
    for copy in copies:
        copy.wait()
    total = ref[0].astype(F32)
    for s in range(1, NS):
        total = total + ref[s].astype(F32)
    return total


EARLY = C + 32


def block_kernel(
    wet, wpr, taps, wrt, wx_own, bex, bred, feats, cot,
    out, out_grad, early, late, mail_out,
    stage, pack, full, top, bottom, flatw, fp, cp, fpt, cpt, we, wp, misc,
    wide_taps, ex, dgs, saved, depth, sums, packed, landed, lanes, vecs, gates, msgs, mail,
    edge, above, below, gated, dpre, acc, held, flat, flat_taps,
    epiece, egot, espace, lpiece, lgot, lspace, tpiece, tgot, tspace,
    wsend, wrecv, hsend, hrecv, csend, crecv, ssend, srecv, msend, mrecv,
    dsend, drecv, esend, erecv, fsend, frecv, lsend, lrecv, gsend, grecv,
    tsend, trecv, usend, urecv,
):
    me_s, me_d = lax.axis_index("space"), lax.axis_index("dp")
    core = lax.rem(me_s, 2)
    barrier = pltpu.get_barrier_semaphore()
    for k in range(1, ND):
        pl.semaphore_signal(
            barrier, inc=1, device_id=(me_s, lax.rem(me_d + k, ND)), device_id_type=MESH
        )
    for k in range(1, NS):
        pl.semaphore_signal(
            barrier, inc=1, device_id=(lax.rem(me_s + k, NS), me_d), device_id_type=MESH
        )

    stage[...] = jnp.zeros_like(stage)
    stage[0, 0:PART, 0:C] = wet[...].astype(F32)
    stage[1, 0:PART, 0:C] = wpr[...].astype(F32)
    side = slice(C, C + PART)
    for i in range(5):
        stage[0, 5 * i : 5 * i + 5, side] = taps[i].astype(F32)
    stage[0, 32 : 32 + SE, side] = wrt[...].astype(F32)
    stage[1, 0:SE, side] = wx_own[...].astype(F32)
    stage[1, 48:49, side] = bex[...].astype(F32)
    pack[...] = stage[...].astype(BF16)
    pl.semaphore_wait(barrier, NS + ND - 2)
    copies = []
    for k in range(1, ND):
        copy = pltpu.make_async_remote_copy(
            src_ref=pack.at[core],
            dst_ref=full.at[core, me_d],
            send_sem=wsend.at[k],
            recv_sem=wrecv.at[k],
            device_id=(me_s, lax.rem(me_d + k, ND)),
            device_id_type=MESH,
        )
        copy.start()
        copies.append(copy)
    halo = to_neighbours(
        feats.at[:, pl.ds(ROWS - 2, 2)],
        top,
        feats.at[:, pl.ds(0, 2)],
        bottom,
        (hsend.at[0], hsend.at[1]),
        (hrecv.at[0], hrecv.at[1]),
    )
    for copy in halo:
        copy.start()
    full[core, me_d] = pack[core]
    spread = (one_hot(0, False), one_hot(1, False))
    gather_t = (one_hot(0, True), one_hot(1, True))

    def permute(r, carry):
        for src, dst, shift in ((feats, fp, 2), (cot, cp, 0)):
            a, b = src[0, r], src[1, r]
            dst[r + shift] = (dot_nt(spread[0], a) + dot_nt(spread[1], b)).astype(BF16)
        return carry

    lax.fori_loop(0, ROWS, permute, 0)
    for r in range(ROWS):
        for src, dst in ((feats, fpt), (cot, cpt)):
            value = dot_nn(src[0, r], gather_t[0]) + dot_nn(src[1, r], gather_t[1])
            dst[:, PIX * r : PIX * (r + 1)] = value.astype(BF16)
    for copy in copies:
        copy.wait()
    share = pltpu.make_async_remote_copy(
        src_ref=full.at[core],
        dst_ref=full.at[core],
        send_sem=csend,
        recv_sem=crecv,
        device_id=(me_s + 1 - 2 * core, me_d),
        device_id_type=MESH,
    )
    share.start()
    for copy in halo:
        copy.wait()
    has_top = jnp.where(me_s > 0, 1.0, 0.0)
    has_bottom = jnp.where(me_s < NS - 1, 1.0, 0.0)
    for r in range(2):
        value = dot_nt(spread[0], top[0, r]) + dot_nt(spread[1], top[1, r])
        fp[r] = (value * has_top).astype(BF16)
        value = dot_nt(spread[0], bottom[0, r]) + dot_nt(spread[1], bottom[1, r])
        fp[ROWS + 2 + r] = (value * has_bottom).astype(BF16)
    share.wait()
    for half, whole in ((0, we), (1, wp)):
        for d in range(ND):
            part = full[half, d].astype(F32)
            flatw[d * SLOT : (d + 1) * SLOT, :] = part[0:SLOT, 0:C]
            span = slice(d * SLOT, (d + 1) * SLOT)
            if half == 0:
                misc[0:80, span] = part[:, C : C + SLOT]
            else:
                misc[80:136, span] = part[0:56, C : C + SLOT]
        whole[...] = flatw[...].astype(BF16)

    keep = pad_mask()

    def lane_of(t):
        return pl.ds(pl.multiple_of(128 * t, 128), 128)

    def cot_matmul(t):
        def chunk(q, carry):
            rows = pl.ds(6 * q, 6)
            product = dot_nt(cp[rows].reshape(6 * PIX, C), wp[lane_of(t), :])
            dgs[rows] = product.reshape(6, BLOCK, SUB, 128)
            return carry

        lax.fori_loop(0, 2, chunk, 0)

    def first(t, carry):
        spread_taps(misc[0:32, lane_of(t)], wide_taps, False)

        def expand(q, carry):
            pre = dot_nt(fp[pl.ds(8 * q, 8)].reshape(8 * PIX, C), we[lane_of(t), :])
            value = swish(pre).astype(BF16).astype(F32).reshape(8, BLOCK, SUB, 128)
            for n in range(8):
                store_row(ex, 8 * q + n, value[n])
            return carry

        lax.fori_loop(0, 2, expand, 0)
        cot_matmul(t)

        def conv(q, carry):
            pools, grads = list(carry[:2]), list(carry[2:])
            for h in range(2):
                rows = slice(8 * h, 8 * h + 8)
                for n, total in enumerate(conv_rows(ex, q, h, wide_taps)):
                    depth[t, 4 * q + n, :, rows, :] = total
                    act = swish(total)
                    grads[h] = grads[h] + jnp.sum(act * dgs[4 * q + n, :, rows, :], axis=0)
                    pools[h] = pools[h] + jnp.sum(act[:9], axis=0)
                    pools[h] = pools[h] + jnp.sum(act[9:] * keep, axis=0)
            for n in range(4):
                saved[t, 4 * q + n] = ex[4 * q + n].astype(BF16)
            return (*pools, *grads)

        zero = jnp.zeros((8, 128), F32)
        parts = lax.fori_loop(0, ROWS // 4, conv, (zero,) * 4)
        for r in range(ROWS, HROWS):
            saved[t, r] = ex[r].astype(BF16)
        for k in range(4):
            sums[t, k : k + 1, :] = jnp.sum(parts[k], axis=0, keepdims=True)
        return carry

    lax.fori_loop(0, TILES, first, 0)

    packed[...] = jnp.zeros_like(packed)
    for t in range(TILES):
        packed[t // 2, 4 * (t % 2) : 4 * (t % 2) + 4, :] = sums[t, 0:4, :]
    landed[me_s] = packed[...]
    copies = to_space(landed, ssend, srecv)
    for copy in copies:
        copy.start()
    total = space_sum(copies, landed)
    for t in range(TILES):
        lanes[0:4, 128 * t : 128 * (t + 1)] = total[t // 2, 4 * (t % 2) : 4 * (t % 2) + 4]
    lanes[:, CP:] = jnp.zeros((8, 128), F32)
    wr = misc[32 : 32 + SE, :]
    wx = misc[80 : 80 + SE, :]
    pooled = lanes[0:2, 0:CP] / AREA
    dgate = lanes[2:4, 0:CP]
    squeeze_pre = dot_nt(pooled, wr, HIGH) + bred[...].astype(F32)
    squeeze = swish(squeeze_pre)
    gate = sigmoid(dot_nn(squeeze, wx, HIGH) + misc[128:129, :])
    dlogit = dgate * gate * (1.0 - gate)
    dsq = dot_nt(dlogit, wx, HIGH) * swish_grad(squeeze_pre)
    dpooled = dot_nn(dsq, wr, HIGH)
    gates[0:2, :] = gate
    gates[2:4, :] = dpooled / AREA
    gates[4:8, :] = jnp.zeros((4, CP), F32)
    lanes[0:2, 0:CP] = pooled
    lanes[2:4, 0:CP] = dlogit
    vecs[...] = jnp.zeros((8, 128), F32)
    vecs[4:6, 0:SE] = squeeze
    vecs[6:8, 0:SE] = dsq
    for d in range(ND):
        msgs[d, 0:4, :] = lanes[0:4, SLOT * d : SLOT * d + 128]
        msgs[d, 4:8, :] = vecs[4:8, :]
    mail[me_d] = msgs[me_d]
    small = to_dp(msgs, mail, msend, mrecv, True)
    for copy in small:
        copy.start()

    def edge_copies(t):
        return to_neighbours(
            edge.at[t, 1],
            above.at[t],
            edge.at[t, 0],
            below.at[t],
            (dsend.at[0, t], dsend.at[1, t]),
            (drecv.at[0, t], drecv.at[1, t]),
        )

    def second(t, carry):
        cot_matmul(t)

        def pointwise(r, carry):
            both = []
            for h in range(2):
                rows = slice(8 * h, 8 * h + 8)
                value, ddepth = gate_row(
                    depth[t, r, :, rows, :], dgs[r, :, rows, :], gates.at[:, lane_of(t)], h, keep
                )
                depth[t, r, :, rows, :] = ddepth.astype(BF16).astype(F32)
                both.append(value)
            gated[pl.ds(pl.multiple_of(r * PIX, PIX), PIX), lane_of(t)] = (
                jnp.concatenate(both, axis=1).reshape(PIX, 128).astype(BF16)
            )
            return carry

        lax.fori_loop(0, ROWS, pointwise, 0)
        for n in range(2):
            edge[t, 0, n] = depth[t, n].astype(BF16)
            edge[t, 1, n] = depth[t, ROWS - 2 + n].astype(BF16)
        for copy in edge_copies(t):
            copy.start()
        return carry

    lax.fori_loop(0, TILES, second, 0)

    def pieces_of(source, rows, piece):
        for d in range(ND):
            piece[d] = source[0:rows, SLOT * d : SLOT * d + 128].astype(BF16)

    flat[:, CP:] = jnp.zeros((C, 128), F32)
    flat_taps[...] = jnp.zeros_like(flat_taps)
    all_channels_grad(gated, cpt, flat)
    pieces_of(flat, C, epiece)
    for copy in to_dp(epiece, egot, esend, erecv):
        copy.start()

    def third(t, carry):
        spread_taps(misc[0:32, lane_of(t)], wide_taps, True)

        def middle(r, carry):
            store_row(ex, r + 2, depth[t, r])
            return carry

        lax.fori_loop(0, ROWS, middle, 0)

        def chunk(q, carry):
            pre = dot_nt(fp[pl.ds(6 * q + 2, 6)].reshape(6 * PIX, C), we[lane_of(t), :])
            dgs[pl.ds(6 * q, 6)] = swish_grad(pre).reshape(6, BLOCK, SUB, 128)
            return carry

        lax.fori_loop(0, 2, chunk, 0)
        for copy in edge_copies(t):
            copy.wait()
        for n in range(2):
            store_row(ex, n, above[t, n].astype(F32) * has_top)
            store_row(ex, ROWS + 2 + n, below[t, n].astype(F32) * has_bottom)

        def conv(q, carry):
            both = []
            for h in range(2):
                rows = slice(8 * h, 8 * h + 8)
                values = conv_rows(ex, q, h, wide_taps)
                both.append([value * dgs[4 * q + n, :, rows, :] for n, value in enumerate(values)])
            for n in range(4):
                value = jnp.concatenate([both[0][n], both[1][n]], axis=1)
                span = pl.ds(pl.multiple_of((4 * q + n) * PIX, PIX), PIX)
                dpre[span, lane_of(t)] = value.reshape(PIX, 128).astype(BF16)
            return carry

        lax.fori_loop(0, ROWS // 4, conv, 0)

        @pl.when(t == TILES // 2)
        def _():
            total = dp_sum(to_dp(epiece, egot, esend, erecv), epiece, egot)
            espace[me_s] = total.astype(BF16)
            for copy in to_space(espace, fsend, frecv):
                copy.start()

        return carry

    lax.fori_loop(0, TILES, third, 0)

    all_channels_grad(dpre, fpt, flat)
    pieces_of(flat, C, lpiece)
    for copy in to_dp(lpiece, lgot, lsend, lrecv):
        copy.start()

    def tap_grads(t, carry):
        acc[...] = jnp.zeros_like(acc)

        def window(q, carry):
            for h in range(2):
                rows = slice(8 * h, 8 * h + 8)
                for low, high in ((0, 9), (9, WIDE)):
                    points = to_points(
                        [saved[t, 4 * q + n].astype(F32)[low:high, rows, :] for n in range(8)]
                    )
                    for p in range(8):
                        held[p, low:high] = points[p]
                mine = outputs_to_points([depth[t, 4 * q + n, :, rows, :] for n in range(4)])
                for p in range(8):
                    source = held[p]
                    for j in range(5):
                        k = 5 * p + j
                        acc[k] = acc[k] + jnp.sum(mine[p] * source[j : j + BLOCK], axis=0)
            return carry

        lax.fori_loop(0, ROWS // 4, window, 0)
        for j in range(5):
            sums_at = [jnp.sum(acc[5 * p + j], axis=0, keepdims=True) for p in range(8)]
            for i, value in enumerate(taps_from_points(sums_at)):
                flat_taps[5 * i + j : 5 * i + j + 1, lane_of(t)] = value

        @pl.when(t == TILES // 2)
        def _():
            total = dp_sum(to_dp(lpiece, lgot, lsend, lrecv), lpiece, lgot)
            lspace[me_s] = total.astype(BF16)
            for copy in to_space(lspace, gsend, grecv):
                copy.start()

        return carry

    lax.fori_loop(0, TILES, tap_grads, 0)
    pieces_of(flat_taps, 32, tpiece)
    copies = to_dp(tpiece, tgot, tsend, trecv)
    for copy in copies:
        copy.start()

    all_channels_out(dpre, we, cp, 0, out_grad)
    tspace[me_s] = dp_sum(copies, tpiece, tgot).astype(BF16)
    copies = to_space(tspace, usend, urecv)
    for copy in copies:
        copy.start()
    all_channels_out(gated, wp, fp, 2, out)
    for copy in small:
        copy.wait()
    mail_out[...] = mail[...]
    early[0:C] = space_sum(to_space(espace, fsend, frecv), espace)
    late[...] = space_sum(to_space(lspace, gsend, grecv), lspace)
    early[C:] = space_sum(copies, tspace)


def block(*args):
    def bf16(*shape):
        return pltpu.VMEM(shape, BF16)

    def f32(*shape):
        return pltpu.VMEM(shape, F32)

    def sems(*shape):
        return pltpu.SemaphoreType.DMA(shape)

    one = pltpu.SemaphoreType.DMA
    return pl.pallas_call(
        block_kernel,
        out_shape=(
            jax.ShapeDtypeStruct((IMGS, ROWS, C, COLS), BF16),
            jax.ShapeDtypeStruct((IMGS, ROWS, C, COLS), BF16),
            jax.ShapeDtypeStruct((EARLY, 128), F32),
            jax.ShapeDtypeStruct((C, 128), F32),
            jax.ShapeDtypeStruct((ND, 8, 128), F32),
        ),
        in_specs=[VMEM] * 9,
        out_specs=(VMEM,) * 5,
        scratch_shapes=[
            f32(2, 80, 256),
            bf16(2, 80, 256),
            bf16(2, ND, 80, 256),
            bf16(IMGS, 2, C, COLS),
            bf16(IMGS, 2, C, COLS),
            f32(CP, C),
            bf16(HROWS, PIX, C),
            bf16(ROWS, PIX, C),
            bf16(C, ROWS * PIX),
            bf16(C, ROWS * PIX),
            bf16(CP, C),
            bf16(CP, C),
            f32(136, CP),
            f32(40, 8, 128),
            f32(HROWS, WIDE, SUB, 128),
            f32(ROWS, BLOCK, SUB, 128),
            bf16(TILES, HROWS, WIDE, SUB, 128),
            f32(TILES, ROWS, BLOCK, SUB, 128),
            f32(TILES, 8, 128),
            f32(5, 8, 128),
            f32(NS, 5, 8, 128),
            f32(8, CP + 128),
            f32(8, 128),
            f32(8, CP),
            f32(ND, 8, 128),
            f32(ND, 8, 128),
            bf16(TILES, 2, 2, BLOCK, SUB, 128),
            bf16(TILES, 2, BLOCK, SUB, 128),
            bf16(TILES, 2, BLOCK, SUB, 128),
            bf16(ROWS * PIX, CP),
            bf16(ROWS * PIX, CP),
            f32(40, 8, 128),
            f32(8, WIDE, 8, 128),
            f32(C, CP + 128),
            f32(32, CP + 128),
            bf16(ND, C, 128),
            bf16(ND, C, 128),
            bf16(NS, C, 128),
            bf16(ND, C, 128),
            bf16(ND, C, 128),
            bf16(NS, C, 128),
            bf16(ND, 32, 128),
            bf16(ND, 32, 128),
            bf16(NS, 32, 128),
            sems(ND),
            sems(ND),
            sems(2),
            sems(2),
            one,
            one,
            sems(NS),
            sems(NS),
            sems(ND),
            sems(ND),
            sems(2, TILES),
            sems(2, TILES),
            sems(ND),
            sems(ND),
            sems(NS),
            sems(NS),
            sems(ND),
            sems(ND),
            sems(NS),
            sems(NS),
            sems(ND),
            sems(ND),
            sems(NS),
            sems(NS),
        ],
        compiler_params=pltpu.CompilerParams(
            collective_id=0, has_side_effects=True, vmem_limit_bytes=63 * 2**20
        ),
        name="block",
    )(*args)


def finish_kernel(
    early, late, mail, raw, raw_grad,
    gexp, gdepth, greduce, gexcite, gbex, gproj, gbred, out, out_grad,
):
    out[...] = raw[...]
    out_grad[...] = raw_grad[...]

    @pl.when(pl.program_id(0) == 0)
    def _():
        gexp[...] = late[...].T[0:PART]
        gproj[...] = early[0:C].T[0:PART]
        for i in range(5):
            gdepth[i] = early[C + 5 * i : C + 5 * i + 5, 0:PART]
        rows = [mail[d] for d in range(ND)]
        pool_all = jnp.concatenate([row[0:2] for row in rows], axis=0)
        dlog_all = jnp.concatenate([row[2:4] for row in rows], axis=0)
        sq_all = jnp.concatenate([row[4:6] for row in rows], axis=0)
        dsq_all = jnp.concatenate([row[6:8] for row in rows], axis=0)
        greduce[...] = dot_tn(dsq_all, pool_all, HIGH)[0:SE, 0:PART]
        gexcite[...] = dot_tn(sq_all, dlog_all, HIGH)[0:SE, 0:PART]
        gbex[...] = jnp.sum(dlog_all, axis=0, keepdims=True)[:, 0:PART]
        gbred[...] = jnp.sum(dsq_all, axis=0, keepdims=True)[:, 0:SE]


def finish(early, late, mail, raw, raw_grad):
    def whole(*shape):
        zeros = (0,) * len(shape)
        return pl.BlockSpec(shape, lambda n: zeros)

    part = pl.BlockSpec((IMGS, 3, C, COLS), lambda n: (0, n, 0, 0))
    shapes = ((PART, C), (5, 5, PART), (SE, PART), (SE, PART), (1, PART), (PART, C), (1, SE))
    return pl.pallas_call(
        finish_kernel,
        grid=(ROWS // 3,),
        out_shape=tuple(jax.ShapeDtypeStruct(shape, F32) for shape in shapes)
        + (jax.ShapeDtypeStruct((IMGS, ROWS, C, COLS), BF16),) * 2,
        in_specs=[whole(EARLY, 128), whole(C, 128), whole(ND, 8, 128), part, part],
        out_specs=tuple(whole(*shape) for shape in shapes) + (part, part),
        name="finish",
    )(early, late, mail, raw, raw_grad)


def on_device(
    features, w_expand, w_depth, w_reduce, b_reduce, w_excite, b_excite, w_project, cotangent
):
    raw, raw_grad, early, late, mail = block(
        w_expand.T,
        w_project,
        w_depth,
        w_reduce.T,
        w_excite,
        b_excite[None, :],
        b_reduce[None, :],
        features.swapaxes(2, 3),
        cotangent.swapaxes(2, 3),
    )
    (
        s_expand, s_depth, s_reduce, s_excite, s_bexcite, s_project, s_breduce, output, grad,
    ) = finish(early, late, mail, raw, raw_grad)
    return (
        output.swapaxes(2, 3),
        grad.swapaxes(2, 3),
        s_expand.T,
        s_depth,
        s_reduce.T,
        s_excite,
        s_bexcite[0],
        s_project,
        s_breduce[0],
    )


def solution(mesh):
    return jax.shard_map(
        on_device,
        mesh=mesh,
        in_specs=(
            P("dp", "space", None, None),
            P(None, "dp"),
            P(None, None, "dp"),
            P("dp", None),
            P(),
            P(None, "dp"),
            P("dp"),
            P("dp", None),
            P("dp", "space", None, None),
        ),
        out_specs=(
            P("dp", "space", None, None),
            P("dp", "space", None, None),
            P(None, "dp"),
            P(None, None, "dp"),
            P("dp", None),
            P(None, "dp"),
            P("dp"),
            P("dp", None),
            P(),
        ),
        check_vma=False,
    )
```

```python
import functools

import jax
import jax.numpy as jnp
from jax import lax
from jax.experimental import pallas as pl
from jax.experimental.pallas import tpu as pltpu
from jax.sharding import PartitionSpec as P

F32 = jnp.float32
BF16 = jnp.bfloat16
MESH = pl.DeviceIdType.MESH
HIGH = lax.Precision.HIGHEST

IMGS, ROWS, COLS, C, SE = 2, 12, 100, 176, 44
BLOCK, SUB = 13, 16
PIX = BLOCK * SUB
WIDE = BLOCK + 4
HROWS = ROWS + 4
PART, SLOT = 66, 72
CP = 16 * SLOT
TILES = CP // 128
AREA = 9600.0
NS, ND = 8, 16

VMEM = pl.BlockSpec(memory_space=pltpu.VMEM)
ANY = pl.BlockSpec(memory_space=pl.ANY)


def sigmoid(value):
    return 0.5 * jnp.tanh(0.5 * value) + 0.5


def swish(value):
    half = 0.5 * value
    return half + half * jnp.tanh(half)


def swish_grad(value):
    sig = sigmoid(value)
    act = value * sig
    return sig + act - act * sig


def dot_nt(left, right, precision=None):
    return lax.dot_general(
        left, right, (((1,), (1,)), ((), ())), precision=precision, preferred_element_type=F32
    )


def dot_tn(left, right, precision=None):
    return lax.dot_general(
        left, right, (((0,), (0,)), ((), ())), precision=precision, preferred_element_type=F32
    )


def dot_nn(left, right, precision=None):
    return lax.dot_general(
        left, right, (((1,), (0,)), ((), ())), precision=precision, preferred_element_type=F32
    )


def one_hot(img, transposed):
    shape = (COLS, PIX) if transposed else (PIX, COLS)
    place = lax.broadcasted_iota(jnp.int32, shape, 1 if transposed else 0)
    col = lax.broadcasted_iota(jnp.int32, shape, 0 if transposed else 1)
    wanted = (col % BLOCK) * SUB + img * 8 + col // BLOCK
    return jnp.where(place == wanted, 1.0, 0.0).astype(BF16)


def point_taps(taps):
    w0, w1, w2, w3, w4 = taps
    even, odd = w0 + w2 + w4, w1 + w3
    even2, odd2 = w0 + 4.0 * w2 + 16.0 * w4, 2.0 * w1 + 8.0 * w3
    even3, odd3 = w0 + 0.25 * w2 + 0.0625 * w4, 0.5 * w1 + 0.125 * w3
    return [
        w0,
        (even + odd) * (-2.0 / 9.0),
        (even - odd) * (-2.0 / 9.0),
        (even2 + odd2) * (1.0 / 360.0),
        (even2 - odd2) * (1.0 / 360.0),
        (even3 + odd3) * (32.0 / 45.0),
        (even3 - odd3) * (32.0 / 45.0),
        w4,
    ]


def taps_from_points(g):
    s1, d1 = (g[1] + g[2]) * (-2.0 / 9.0), (g[1] - g[2]) * (-2.0 / 9.0)
    s2, d2 = (g[3] + g[4]) * (1.0 / 360.0), (g[3] - g[4]) * (1.0 / 360.0)
    s3, d3 = (g[5] + g[6]) * (32.0 / 45.0), (g[5] - g[6]) * (32.0 / 45.0)
    return [
        g[0] + s1 + s2 + s3,
        d1 + 2.0 * d2 + 0.5 * d3,
        s1 + 4.0 * s2 + 0.25 * s3,
        d1 + 8.0 * d2 + 0.125 * d3,
        s1 + 16.0 * s2 + 0.0625 * s3 + g[7],
    ]


def to_points(x):
    x0, x1, x2, x3, x4, x5, x6, x7 = x
    f3, f4 = 5.0 * x3, 5.0 * x4
    e1, o1 = (x6 + x2) - 4.25 * x4, (x5 + x1) - 4.25 * x3
    e2, o2 = (x2 - f4) + 4.0 * x6, (x1 - f3) + 4.0 * x5
    e3, o3 = (4.0 * x2 - f4) + x6, (4.0 * x1 - f3) + x5
    o2, o3 = o2 + o2, 0.5 * o3
    return [
        (x0 - x6) + 5.25 * (x4 - x2),
        e1 + o1,
        e1 - o1,
        e2 + o2,
        e2 - o2,
        e3 + o3,
        e3 - o3,
        (x7 - x1) + 5.25 * (x3 - x5),
    ]


def from_points(m):
    s1, d1 = m[1] + m[2], m[1] - m[2]
    s2, d2 = m[3] + m[4], m[3] - m[4]
    s3, d3 = m[5] + m[6], m[5] - m[6]
    return [
        (m[0] + s1) + (s2 + s3),
        (d1 + 2.0 * d2) + 0.5 * d3,
        (s1 + 4.0 * s2) + 0.25 * s3,
        ((d1 + 8.0 * d2) + 0.125 * d3) + m[7],
    ]


def outputs_to_points(y):
    y0, y1, y2, y3 = y
    a, b = y0 + y2, y1 + y3
    c, d = y0 + 4.0 * y2, 2.0 * y1 + 8.0 * y3
    e, f = y0 + 0.25 * y2, 0.5 * y1 + 0.125 * y3
    return [y0, a + b, a - b, c + d, c - d, e + f, e - f, y3]


def spread_taps(taps, wide_taps, flip):
    for j in range(5):
        column = [taps[5 * i + j : 5 * i + j + 1, :] for i in range(5)]
        if flip:
            column = column[::-1]
        place = 4 - j if flip else j
        for p, value in enumerate(point_taps(column)):
            wide_taps[5 * p + place] = jnp.broadcast_to(value, (8, 128))


def edge_columns(value):
    split = value.reshape(BLOCK, 2, 8, 128)
    block = lax.broadcasted_iota(jnp.int32, (2, 2, 8, 128), 2)
    left = jnp.where(block > 0, pltpu.roll(split[BLOCK - 2 :], 1, 2), 0.0)
    right = jnp.where(block < 7, pltpu.roll(split[:2], 7, 2), 0.0)
    return left.reshape(2, SUB, 128), right.reshape(2, SUB, 128)


def store_row(ref, r, value):
    left, right = edge_columns(value)
    ref[r, 0:2] = left
    ref[r, 2 : 2 + BLOCK] = value
    ref[r, 2 + BLOCK :] = right


def conv_rows(ref, q, h, wide_taps):
    points = to_points([ref[4 * q + n, :, 8 * h : 8 * h + 8, :] for n in range(8)])
    totals = []
    for p in range(8):
        total = points[p][0:BLOCK] * wide_taps[5 * p][None]
        for j in range(1, 5):
            total = total + points[p][j : j + BLOCK] * wide_taps[5 * p + j][None]
        totals.append(total)
    return from_points(totals)


def pad_mask():
    block = lax.broadcasted_iota(jnp.int32, (4, 8, 128), 1)
    return jnp.where(block < 7, 1.0, 0.0)


def gate_row(depth, dgated, gates, h, keep):
    gate = gates[h : h + 1, :][None]
    pull = gates[2 + h : 3 + h, :][None]
    sig = sigmoid(depth)
    act = depth * sig
    gated = act * gate
    ddepth = (dgated * gate + pull) * (sig + act - act * sig)
    ddepth = jnp.concatenate([ddepth[:9], ddepth[9:] * keep], axis=0)
    return gated, ddepth


def unpermute(value, out, r):
    for img in range(2):
        out[img, r] = dot_tn(value, one_hot(img, False)).astype(BF16)


def all_channels_out(rows_in, weights, base, shift, out):
    def chunk(q, carry):
        block = rows_in[pl.ds(pl.multiple_of(4 * PIX * q, 4 * PIX), 4 * PIX), :]
        product = dot_nn(block, weights[...]).reshape(4, PIX, C)
        for n in range(4):
            value = product[n] + base[4 * q + n + shift].astype(F32)
            unpermute(value.astype(BF16), out, 4 * q + n)
        return carry

    lax.fori_loop(0, 3, chunk, 0)


def all_channels_grad(rows_in, turned, grad):
    def lanes(q, carry):
        span = pl.ds(pl.multiple_of(384 * q, 128), 384)
        grad[:, span] = dot_nn(turned[...], rows_in[:, span])
        return carry

    lax.fori_loop(0, 3, lanes, 0)


def to_dp(src, dst, send, recv, by_sender=False):
    me_s, me_d = lax.axis_index("space"), lax.axis_index("dp")
    copies = []
    for k in range(1, ND):
        target = lax.rem(me_d + k, ND)
        copies.append(
            pltpu.make_async_remote_copy(
                src_ref=src.at[target],
                dst_ref=dst.at[me_d] if by_sender else dst.at[k],
                send_sem=send.at[k],
                recv_sem=recv.at[k],
                device_id=(me_s, target),
                device_id_type=MESH,
            )
        )
    return copies


def to_space(ref, send, recv):
    me_s, me_d = lax.axis_index("space"), lax.axis_index("dp")
    copies = []
    for k in range(1, NS):
        copies.append(
            pltpu.make_async_remote_copy(
                src_ref=ref.at[me_s],
                dst_ref=ref.at[me_s],
                send_sem=send.at[k],
                recv_sem=recv.at[k],
                device_id=(lax.rem(me_s + k, NS), me_d),
                device_id_type=MESH,
            )
        )
    return copies


def to_neighbours(down_src, down_dst, up_src, up_dst, send, recv):
    me_s, me_d = lax.axis_index("space"), lax.axis_index("dp")
    down = pltpu.make_async_remote_copy(
        src_ref=down_src,
        dst_ref=down_dst,
        send_sem=send[0],
        recv_sem=recv[0],
        device_id=(lax.rem(me_s + 1, NS), me_d),
        device_id_type=MESH,
    )
    up = pltpu.make_async_remote_copy(
        src_ref=up_src,
        dst_ref=up_dst,
        send_sem=send[1],
        recv_sem=recv[1],
        device_id=(lax.rem(me_s + NS - 1, NS), me_d),
        device_id_type=MESH,
    )
    return down, up


def dp_sum(copies, piece, got):
    total = piece[lax.axis_index("dp")].astype(F32)
    for k, copy in enumerate(copies):
        copy.wait()
        total = total + got[k + 1].astype(F32)
    return total


def space_sum(copies, ref):
    for copy in copies:
        copy.wait()
    total = ref[0].astype(F32)
    for s in range(1, NS):
        total = total + ref[s].astype(F32)
    return total


EARLY = C + 32


def block_kernel(
    wet, wpr, taps, wrt, wx_own, bex, bred, feats_in, cot_in,
    out, out_grad, early, late, mail_out,
    feats, cot, stage, pack, full, top, bottom, flatw, fp, cp, fpt, cpt, we, wp, misc,
    wide_taps, ex, dgs, coming_pre, coming_dg, saved, depth, sums, packed, landed, lanes, vecs, gates, msgs, mail,
    edge, above, below, gated, dpre, acc, held, flat, flat_taps,
    epiece, egot, espace, lpiece, lgot, lspace, tpiece, tgot, tspace,
    wsend, wrecv, hsend, hrecv, csend, crecv, ssend, srecv, msend, mrecv,
    dsend, drecv, esend, erecv, fsend, frecv, lsend, lrecv, gsend, grecv,
    tsend, trecv, usend, urecv, insem,
):
    me_s, me_d = lax.axis_index("space"), lax.axis_index("dp")
    core = lax.rem(me_s, 2)
    barrier = pltpu.get_barrier_semaphore()
    for k in range(1, ND):
        pl.semaphore_signal(
            barrier, inc=1, device_id=(me_s, lax.rem(me_d + k, ND)), device_id_type=MESH
        )
    for k in range(1, NS):
        pl.semaphore_signal(
            barrier, inc=1, device_id=(lax.rem(me_s + k, NS), me_d), device_id_type=MESH
        )

    arrive = [
        pltpu.make_async_copy(feats_in, feats, insem.at[0]),
        pltpu.make_async_copy(cot_in, cot, insem.at[1]),
    ]
    for copy in arrive:
        copy.start()

    stage[...] = jnp.zeros_like(stage)
    stage[0, 0:PART, 0:C] = wet[...].astype(F32)
    stage[1, 0:PART, 0:C] = wpr[...].astype(F32)
    side = slice(C, C + PART)
    for i in range(5):
        stage[0, 5 * i : 5 * i + 5, side] = taps[i].astype(F32)
    stage[0, 32 : 32 + SE, side] = wrt[...].astype(F32)
    stage[1, 0:SE, side] = wx_own[...].astype(F32)
    stage[1, 48:49, side] = bex[...].astype(F32)
    pack[...] = stage[...].astype(BF16)
    pl.semaphore_wait(barrier, NS + ND - 2)
    copies = []
    for k in range(1, ND):
        copy = pltpu.make_async_remote_copy(
            src_ref=pack.at[core],
            dst_ref=full.at[core, me_d],
            send_sem=wsend.at[k],
            recv_sem=wrecv.at[k],
            device_id=(me_s, lax.rem(me_d + k, ND)),
            device_id_type=MESH,
        )
        copy.start()
        copies.append(copy)
    for copy in arrive:
        copy.wait()
    halo = to_neighbours(
        feats.at[:, pl.ds(ROWS - 2, 2)],
        top,
        feats.at[:, pl.ds(0, 2)],
        bottom,
        (hsend.at[0], hsend.at[1]),
        (hrecv.at[0], hrecv.at[1]),
    )
    for copy in halo:
        copy.start()
    full[core, me_d] = pack[core]
    spread = (one_hot(0, False), one_hot(1, False))
    gather_t = (one_hot(0, True), one_hot(1, True))

    def permute(r, carry):
        for src, dst, shift in ((feats, fp, 2), (cot, cp, 0)):
            a, b = src[0, r], src[1, r]
            dst[r + shift] = (dot_nt(spread[0], a) + dot_nt(spread[1], b)).astype(BF16)
        return carry

    lax.fori_loop(0, ROWS, permute, 0)
    for r in range(ROWS):
        for src, dst in ((feats, fpt), (cot, cpt)):
            value = dot_nn(src[0, r], gather_t[0]) + dot_nn(src[1, r], gather_t[1])
            dst[:, PIX * r : PIX * (r + 1)] = value.astype(BF16)
    for copy in copies:
        copy.wait()
    share = pltpu.make_async_remote_copy(
        src_ref=full.at[core],
        dst_ref=full.at[core],
        send_sem=csend,
        recv_sem=crecv,
        device_id=(me_s + 1 - 2 * core, me_d),
        device_id_type=MESH,
    )
    share.start()
    for copy in halo:
        copy.wait()
    has_top = jnp.where(me_s > 0, 1.0, 0.0)
    has_bottom = jnp.where(me_s < NS - 1, 1.0, 0.0)
    for r in range(2):
        value = dot_nt(spread[0], top[0, r]) + dot_nt(spread[1], top[1, r])
        fp[r] = (value * has_top).astype(BF16)
        value = dot_nt(spread[0], bottom[0, r]) + dot_nt(spread[1], bottom[1, r])
        fp[ROWS + 2 + r] = (value * has_bottom).astype(BF16)
    share.wait()
    for half, whole in ((0, we), (1, wp)):
        for d in range(ND):
            part = full[half, d].astype(F32)
            flatw[d * SLOT : (d + 1) * SLOT, :] = part[0:SLOT, 0:C]
            span = slice(d * SLOT, (d + 1) * SLOT)
            if half == 0:
                misc[0:80, span] = part[:, C : C + SLOT]
            else:
                misc[80:136, span] = part[0:56, C : C + SLOT]
        whole[...] = flatw[...].astype(BF16)

    keep = pad_mask()

    def lane_of(t):
        return pl.ds(pl.multiple_of(128 * t, 128), 128)

    def pre_rows(t, start, count):
        product = dot_nt(fp[pl.ds(start, count)].reshape(count * PIX, C), we[lane_of(t), :])
        coming_pre[pl.ds(start, count)] = product.reshape(count, BLOCK, SUB, 128)

    def cot_rows(t, start, count):
        product = dot_nt(cp[pl.ds(start, count)].reshape(count * PIX, C), wp[lane_of(t), :])
        coming_dg[pl.ds(start, count)] = product.reshape(count, BLOCK, SUB, 128)

    def next_tile(t):
        return jnp.minimum(t + 1, TILES - 1)

    def take_dg():
        def row(r, carry):
            dgs[r] = coming_dg[r]
            return carry

        lax.fori_loop(0, ROWS, row, 0)

    def first(t, carry):
        spread_taps(misc[0:32, lane_of(t)], wide_taps, False)

        def expand(q, carry):
            for n in range(4):
                value = swish(coming_pre[4 * q + n]).astype(BF16).astype(F32)
                store_row(ex, 4 * q + n, value)
            return carry

        lax.fori_loop(0, HROWS // 4, expand, 0)
        take_dg()

        def conv(q, carry):
            pools, grads = list(carry[:2]), list(carry[2:])
            for h in range(2):
                rows = slice(8 * h, 8 * h + 8)
                for n, total in enumerate(conv_rows(ex, q, h, wide_taps)):
                    depth[t, 4 * q + n, :, rows, :] = total
                    act = swish(total)
                    grads[h] = grads[h] + jnp.sum(act * dgs[4 * q + n, :, rows, :], axis=0)
                    pools[h] = pools[h] + jnp.sum(act[:9], axis=0)
                    pools[h] = pools[h] + jnp.sum(act[9:] * keep, axis=0)
            for n in range(4):
                saved[t, 4 * q + n] = ex[4 * q + n].astype(BF16)
            pre_rows(next_tile(t), jnp.minimum(6 * q, HROWS - 6), 6)
            cot_rows(next_tile(t), 4 * q, 4)
            return (*pools, *grads)

        zero = jnp.zeros((8, 128), F32)
        parts = lax.fori_loop(0, ROWS // 4, conv, (zero,) * 4)
        for r in range(ROWS, HROWS):
            saved[t, r] = ex[r].astype(BF16)
        for k in range(4):
            sums[t, k : k + 1, :] = jnp.sum(parts[k], axis=0, keepdims=True)
        return carry

    def begin(q, carry):
        pre_rows(0, 8 * q, 8)
        cot_rows(0, 6 * q, 6)
        return carry

    lax.fori_loop(0, 2, begin, 0)
    lax.fori_loop(0, TILES, first, 0)

    packed[...] = jnp.zeros_like(packed)
    for t in range(TILES):
        packed[t // 2, 4 * (t % 2) : 4 * (t % 2) + 4, :] = sums[t, 0:4, :]
    landed[me_s] = packed[...]
    copies = to_space(landed, ssend, srecv)
    for copy in copies:
        copy.start()

    def begin_again(q, carry):
        cot_rows(0, 6 * q, 6)
        return carry

    lax.fori_loop(0, 2, begin_again, 0)
    total = space_sum(copies, landed)
    for t in range(TILES):
        lanes[0:4, 128 * t : 128 * (t + 1)] = total[t // 2, 4 * (t % 2) : 4 * (t % 2) + 4]
    lanes[:, CP:] = jnp.zeros((8, 128), F32)
    wr = misc[32 : 32 + SE, :]
    wx = misc[80 : 80 + SE, :]
    pooled = lanes[0:2, 0:CP] / AREA
    dgate = lanes[2:4, 0:CP]
    squeeze_pre = dot_nt(pooled, wr, HIGH) + bred[...].astype(F32)
    squeeze = swish(squeeze_pre)
    gate = sigmoid(dot_nn(squeeze, wx, HIGH) + misc[128:129, :])
    dlogit = dgate * gate * (1.0 - gate)
    dsq = dot_nt(dlogit, wx, HIGH) * swish_grad(squeeze_pre)
    dpooled = dot_nn(dsq, wr, HIGH)
    gates[0:2, :] = gate
    gates[2:4, :] = dpooled / AREA
    gates[4:8, :] = jnp.zeros((4, CP), F32)
    lanes[0:2, 0:CP] = pooled
    lanes[2:4, 0:CP] = dlogit
    vecs[...] = jnp.zeros((8, 128), F32)
    vecs[4:6, 0:SE] = squeeze
    vecs[6:8, 0:SE] = dsq
    for d in range(ND):
        msgs[d, 0:4, :] = lanes[0:4, SLOT * d : SLOT * d + 128]
        msgs[d, 4:8, :] = vecs[4:8, :]
    mail[me_d] = msgs[me_d]
    small = to_dp(msgs, mail, msend, mrecv, True)
    for copy in small:
        copy.start()

    def edge_copies(t):
        return to_neighbours(
            edge.at[t, 1],
            above.at[t],
            edge.at[t, 0],
            below.at[t],
            (dsend.at[0, t], dsend.at[1, t]),
            (drecv.at[0, t], drecv.at[1, t]),
        )

    def second(t, carry):
        take_dg()

        def pointwise(q, carry):
            for n in range(4):
                r = 4 * q + n
                both = []
                for h in range(2):
                    rows = slice(8 * h, 8 * h + 8)
                    value, ddepth = gate_row(
                        depth[t, r, :, rows, :],
                        dgs[r, :, rows, :],
                        gates.at[:, lane_of(t)],
                        h,
                        keep,
                    )
                    depth[t, r, :, rows, :] = ddepth.astype(BF16).astype(F32)
                    both.append(value)
                gated[pl.ds(pl.multiple_of(r * PIX, PIX), PIX), lane_of(t)] = (
                    jnp.concatenate(both, axis=1).reshape(PIX, 128).astype(BF16)
                )
            cot_rows(next_tile(t), 4 * q, 4)
            return carry

        lax.fori_loop(0, ROWS // 4, pointwise, 0)
        for n in range(2):
            edge[t, 0, n] = depth[t, n].astype(BF16)
            edge[t, 1, n] = depth[t, ROWS - 2 + n].astype(BF16)
        for copy in edge_copies(t):
            copy.start()
        return carry

    lax.fori_loop(0, TILES, second, 0)

    def pieces_of(source, rows, piece):
        for d in range(ND):
            piece[d] = source[0:rows, SLOT * d : SLOT * d + 128].astype(BF16)

    flat[:, CP:] = jnp.zeros((C, 128), F32)
    flat_taps[...] = jnp.zeros_like(flat_taps)
    all_channels_grad(gated, cpt, flat)
    pieces_of(flat, C, epiece)
    for copy in to_dp(epiece, egot, esend, erecv):
        copy.start()

    def third(t, carry):
        spread_taps(misc[0:32, lane_of(t)], wide_taps, True)

        def middle(r, carry):
            store_row(ex, r + 2, depth[t, r])
            return carry

        lax.fori_loop(0, ROWS, middle, 0)

        def slopes(q, carry):
            for n in range(4):
                dgs[4 * q + n] = swish_grad(coming_pre[4 * q + n + 2])
            return carry

        lax.fori_loop(0, ROWS // 4, slopes, 0)
        for copy in edge_copies(t):
            copy.wait()
        for n in range(2):
            store_row(ex, n, above[t, n].astype(F32) * has_top)
            store_row(ex, ROWS + 2 + n, below[t, n].astype(F32) * has_bottom)

        def conv(q, carry):
            both = []
            for h in range(2):
                rows = slice(8 * h, 8 * h + 8)
                values = conv_rows(ex, q, h, wide_taps)
                both.append([value * dgs[4 * q + n, :, rows, :] for n, value in enumerate(values)])
            for n in range(4):
                value = jnp.concatenate([both[0][n], both[1][n]], axis=1)
                span = pl.ds(pl.multiple_of((4 * q + n) * PIX, PIX), PIX)
                dpre[span, lane_of(t)] = value.reshape(PIX, 128).astype(BF16)
            pre_rows(next_tile(t), 4 * q + 2, 4)
            return carry

        lax.fori_loop(0, ROWS // 4, conv, 0)

        @pl.when(t == TILES // 2)
        def _():
            total = dp_sum(to_dp(epiece, egot, esend, erecv), epiece, egot)
            espace[me_s] = total.astype(BF16)
            for copy in to_space(espace, fsend, frecv):
                copy.start()

        return carry

    def begin_third(q, carry):
        pre_rows(0, 6 * q + 2, 6)
        return carry

    lax.fori_loop(0, 2, begin_third, 0)
    lax.fori_loop(0, TILES, third, 0)

    all_channels_grad(dpre, fpt, flat)
    pieces_of(flat, C, lpiece)
    for copy in to_dp(lpiece, lgot, lsend, lrecv):
        copy.start()

    def tap_grads(t, carry):
        acc[...] = jnp.zeros_like(acc)

        def window(q, carry):
            for h in range(2):
                rows = slice(8 * h, 8 * h + 8)
                for low, high in ((0, 9), (9, WIDE)):
                    points = to_points(
                        [saved[t, 4 * q + n].astype(F32)[low:high, rows, :] for n in range(8)]
                    )
                    for p in range(8):
                        held[p, low:high] = points[p]
                mine = outputs_to_points([depth[t, 4 * q + n, :, rows, :] for n in range(4)])
                for p in range(8):
                    source = held[p]
                    for j in range(5):
                        k = 5 * p + j
                        acc[k] = acc[k] + jnp.sum(mine[p] * source[j : j + BLOCK], axis=0)
            return carry

        lax.fori_loop(0, ROWS // 4, window, 0)
        for j in range(5):
            sums_at = [jnp.sum(acc[5 * p + j], axis=0, keepdims=True) for p in range(8)]
            for i, value in enumerate(taps_from_points(sums_at)):
                flat_taps[5 * i + j : 5 * i + j + 1, lane_of(t)] = value

        @pl.when(t == TILES // 2)
        def _():
            total = dp_sum(to_dp(lpiece, lgot, lsend, lrecv), lpiece, lgot)
            lspace[me_s] = total.astype(BF16)
            for copy in to_space(lspace, gsend, grecv):
                copy.start()

        return carry

    lax.fori_loop(0, TILES, tap_grads, 0)
    pieces_of(flat_taps, 32, tpiece)
    copies = to_dp(tpiece, tgot, tsend, trecv)
    for copy in copies:
        copy.start()

    all_channels_out(dpre, we, cp, 0, out_grad)
    tspace[me_s] = dp_sum(copies, tpiece, tgot).astype(BF16)
    copies = to_space(tspace, usend, urecv)
    for copy in copies:
        copy.start()
    all_channels_out(gated, wp, fp, 2, out)
    for copy in small:
        copy.wait()
    mail_out[...] = mail[...]
    early[0:C] = space_sum(to_space(espace, fsend, frecv), espace)
    late[...] = space_sum(to_space(lspace, gsend, grecv), lspace)
    early[C:] = space_sum(copies, tspace)


def block(*args):
    def bf16(*shape):
        return pltpu.VMEM(shape, BF16)

    def f32(*shape):
        return pltpu.VMEM(shape, F32)

    def sems(*shape):
        return pltpu.SemaphoreType.DMA(shape)

    one = pltpu.SemaphoreType.DMA
    return pl.pallas_call(
        block_kernel,
        out_shape=(
            jax.ShapeDtypeStruct((IMGS, ROWS, C, COLS), BF16),
            jax.ShapeDtypeStruct((IMGS, ROWS, C, COLS), BF16),
            jax.ShapeDtypeStruct((EARLY, 128), F32),
            jax.ShapeDtypeStruct((C, 128), F32),
            jax.ShapeDtypeStruct((ND, 8, 128), F32),
        ),
        in_specs=[VMEM] * 7 + [ANY] * 2,
        out_specs=(VMEM,) * 5,
        scratch_shapes=[
            bf16(IMGS, ROWS, C, COLS),
            bf16(IMGS, ROWS, C, COLS),
            f32(2, 80, 256),
            bf16(2, 80, 256),
            bf16(2, ND, 80, 256),
            bf16(IMGS, 2, C, COLS),
            bf16(IMGS, 2, C, COLS),
            f32(CP, C),
            bf16(HROWS, PIX, C),
            bf16(ROWS, PIX, C),
            bf16(C, ROWS * PIX),
            bf16(C, ROWS * PIX),
            bf16(CP, C),
            bf16(CP, C),
            f32(136, CP),
            f32(40, 8, 128),
            f32(HROWS, WIDE, SUB, 128),
            f32(ROWS, BLOCK, SUB, 128),
            f32(HROWS, BLOCK, SUB, 128),
            f32(ROWS, BLOCK, SUB, 128),
            bf16(TILES, HROWS, WIDE, SUB, 128),
            f32(TILES, ROWS, BLOCK, SUB, 128),
            f32(TILES, 8, 128),
            f32(5, 8, 128),
            f32(NS, 5, 8, 128),
            f32(8, CP + 128),
            f32(8, 128),
            f32(8, CP),
            f32(ND, 8, 128),
            f32(ND, 8, 128),
            bf16(TILES, 2, 2, BLOCK, SUB, 128),
            bf16(TILES, 2, BLOCK, SUB, 128),
            bf16(TILES, 2, BLOCK, SUB, 128),
            bf16(ROWS * PIX, CP),
            bf16(ROWS * PIX, CP),
            f32(40, 8, 128),
            f32(8, WIDE, 8, 128),
            f32(C, CP + 128),
            f32(32, CP + 128),
            bf16(ND, C, 128),
            bf16(ND, C, 128),
            bf16(NS, C, 128),
            bf16(ND, C, 128),
            bf16(ND, C, 128),
            bf16(NS, C, 128),
            bf16(ND, 32, 128),
            bf16(ND, 32, 128),
            bf16(NS, 32, 128),
            sems(ND),
            sems(ND),
            sems(2),
            sems(2),
            one,
            one,
            sems(NS),
            sems(NS),
            sems(ND),
            sems(ND),
            sems(2, TILES),
            sems(2, TILES),
            sems(ND),
            sems(ND),
            sems(NS),
            sems(NS),
            sems(ND),
            sems(ND),
            sems(NS),
            sems(NS),
            sems(ND),
            sems(ND),
            sems(NS),
            sems(NS),
            sems(2),
        ],
        compiler_params=pltpu.CompilerParams(
            collective_id=0, has_side_effects=True, vmem_limit_bytes=63 * 2**20
        ),
        name="block",
    )(*args)


def finish_kernel(
    early, late, mail, raw, raw_grad,
    gexp, gdepth, greduce, gexcite, gbex, gproj, gbred, out, out_grad,
):
    out[...] = raw[...]
    out_grad[...] = raw_grad[...]

    @pl.when(pl.program_id(0) == 0)
    def _():
        gexp[...] = late[...].T[0:PART]
        gproj[...] = early[0:C].T[0:PART]
        for i in range(5):
            gdepth[i] = early[C + 5 * i : C + 5 * i + 5, 0:PART]
        rows = [mail[d] for d in range(ND)]
        pool_all = jnp.concatenate([row[0:2] for row in rows], axis=0)
        dlog_all = jnp.concatenate([row[2:4] for row in rows], axis=0)
        sq_all = jnp.concatenate([row[4:6] for row in rows], axis=0)
        dsq_all = jnp.concatenate([row[6:8] for row in rows], axis=0)
        greduce[...] = dot_tn(dsq_all, pool_all, HIGH)[0:SE, 0:PART]
        gexcite[...] = dot_tn(sq_all, dlog_all, HIGH)[0:SE, 0:PART]
        gbex[...] = jnp.sum(dlog_all, axis=0, keepdims=True)[:, 0:PART]
        gbred[...] = jnp.sum(dsq_all, axis=0, keepdims=True)[:, 0:SE]


def finish(early, late, mail, raw, raw_grad):
    def whole(*shape):
        zeros = (0,) * len(shape)
        return pl.BlockSpec(shape, lambda n: zeros)

    part = pl.BlockSpec((IMGS, 6, C, COLS), lambda n: (0, n, 0, 0))
    shapes = ((PART, C), (5, 5, PART), (SE, PART), (SE, PART), (1, PART), (PART, C), (1, SE))
    return pl.pallas_call(
        finish_kernel,
        grid=(ROWS // 6,),
        out_shape=tuple(jax.ShapeDtypeStruct(shape, F32) for shape in shapes)
        + (jax.ShapeDtypeStruct((IMGS, ROWS, C, COLS), BF16),) * 2,
        in_specs=[whole(EARLY, 128), whole(C, 128), whole(ND, 8, 128), part, part],
        out_specs=tuple(whole(*shape) for shape in shapes) + (part, part),
        name="finish",
    )(early, late, mail, raw, raw_grad)


def on_device(
    features, w_expand, w_depth, w_reduce, b_reduce, w_excite, b_excite, w_project, cotangent
):
    raw, raw_grad, early, late, mail = block(
        w_expand.T,
        w_project,
        w_depth,
        w_reduce.T,
        w_excite,
        b_excite[None, :],
        b_reduce[None, :],
        features.swapaxes(2, 3),
        cotangent.swapaxes(2, 3),
    )
    (
        s_expand, s_depth, s_reduce, s_excite, s_bexcite, s_project, s_breduce, output, grad,
    ) = finish(early, late, mail, raw, raw_grad)
    return (
        output.swapaxes(2, 3),
        grad.swapaxes(2, 3),
        s_expand.T,
        s_depth,
        s_reduce.T,
        s_excite,
        s_bexcite[0],
        s_project,
        s_breduce[0],
    )


def solution(mesh):
    return jax.shard_map(
        on_device,
        mesh=mesh,
        in_specs=(
            P("dp", "space", None, None),
            P(None, "dp"),
            P(None, None, "dp"),
            P("dp", None),
            P(),
            P(None, "dp"),
            P("dp"),
            P("dp", None),
            P("dp", "space", None, None),
        ),
        out_specs=(
            P("dp", "space", None, None),
            P("dp", "space", None, None),
            P(None, "dp"),
            P(None, None, "dp"),
            P("dp", None),
            P(None, "dp"),
            P("dp"),
            P("dp", None),
            P(),
        ),
        check_vma=False,
    )
```

```python
import functools

import jax
import jax.numpy as jnp
from jax import lax
from jax.experimental import pallas as pl
from jax.experimental.pallas import tpu as pltpu
from jax.sharding import PartitionSpec as P

F32 = jnp.float32
BF16 = jnp.bfloat16
MESH = pl.DeviceIdType.MESH
HIGH = lax.Precision.HIGHEST

IMGS, ROWS, COLS, C, SE = 2, 12, 100, 176, 44
BLOCK, SUB = 13, 16
PIX = BLOCK * SUB
WIDE = BLOCK + 4
HROWS = ROWS + 4
PART, SLOT = 66, 72
CP = 16 * SLOT
TILES = CP // 128
AREA = 9600.0
NS, ND = 8, 16

VMEM = pl.BlockSpec(memory_space=pltpu.VMEM)
ANY = pl.BlockSpec(memory_space=pl.ANY)


def sigmoid(value):
    return 0.5 * jnp.tanh(0.5 * value) + 0.5


def swish(value):
    half = 0.5 * value
    return half + half * jnp.tanh(half)


def swish_grad(value):
    sig = sigmoid(value)
    act = value * sig
    return sig + act - act * sig


def dot_nt(left, right, precision=None):
    return lax.dot_general(
        left, right, (((1,), (1,)), ((), ())), precision=precision, preferred_element_type=F32
    )


def dot_tn(left, right, precision=None):
    return lax.dot_general(
        left, right, (((0,), (0,)), ((), ())), precision=precision, preferred_element_type=F32
    )


def dot_nn(left, right, precision=None):
    return lax.dot_general(
        left, right, (((1,), (0,)), ((), ())), precision=precision, preferred_element_type=F32
    )


def one_hot(img, transposed):
    shape = (COLS, PIX) if transposed else (PIX, COLS)
    place = lax.broadcasted_iota(jnp.int32, shape, 1 if transposed else 0)
    col = lax.broadcasted_iota(jnp.int32, shape, 0 if transposed else 1)
    wanted = (col % BLOCK) * SUB + img * 8 + col // BLOCK
    return jnp.where(place == wanted, 1.0, 0.0).astype(BF16)


def point_taps(taps):
    w0, w1, w2, w3, w4 = taps
    even, odd = w0 + w2 + w4, w1 + w3
    even2, odd2 = w0 + 4.0 * w2 + 16.0 * w4, 2.0 * w1 + 8.0 * w3
    even3, odd3 = w0 + 0.25 * w2 + 0.0625 * w4, 0.5 * w1 + 0.125 * w3
    return [
        w0,
        (even + odd) * (-2.0 / 9.0),
        (even - odd) * (-2.0 / 9.0),
        (even2 + odd2) * (1.0 / 360.0),
        (even2 - odd2) * (1.0 / 360.0),
        (even3 + odd3) * (32.0 / 45.0),
        (even3 - odd3) * (32.0 / 45.0),
        w4,
    ]


def taps_from_points(g):
    s1, d1 = (g[1] + g[2]) * (-2.0 / 9.0), (g[1] - g[2]) * (-2.0 / 9.0)
    s2, d2 = (g[3] + g[4]) * (1.0 / 360.0), (g[3] - g[4]) * (1.0 / 360.0)
    s3, d3 = (g[5] + g[6]) * (32.0 / 45.0), (g[5] - g[6]) * (32.0 / 45.0)
    return [
        g[0] + s1 + s2 + s3,
        d1 + 2.0 * d2 + 0.5 * d3,
        s1 + 4.0 * s2 + 0.25 * s3,
        d1 + 8.0 * d2 + 0.125 * d3,
        s1 + 16.0 * s2 + 0.0625 * s3 + g[7],
    ]


def to_points(x):
    x0, x1, x2, x3, x4, x5, x6, x7 = x
    f3, f4 = 5.0 * x3, 5.0 * x4
    e1, o1 = (x6 + x2) - 4.25 * x4, (x5 + x1) - 4.25 * x3
    e2, o2 = (x2 - f4) + 4.0 * x6, (x1 - f3) + 4.0 * x5
    e3, o3 = (4.0 * x2 - f4) + x6, (4.0 * x1 - f3) + x5
    o2, o3 = o2 + o2, 0.5 * o3
    return [
        (x0 - x6) + 5.25 * (x4 - x2),
        e1 + o1,
        e1 - o1,
        e2 + o2,
        e2 - o2,
        e3 + o3,
        e3 - o3,
        (x7 - x1) + 5.25 * (x3 - x5),
    ]


def from_points(m):
    s1, d1 = m[1] + m[2], m[1] - m[2]
    s2, d2 = m[3] + m[4], m[3] - m[4]
    s3, d3 = m[5] + m[6], m[5] - m[6]
    return [
        (m[0] + s1) + (s2 + s3),
        (d1 + 2.0 * d2) + 0.5 * d3,
        (s1 + 4.0 * s2) + 0.25 * s3,
        ((d1 + 8.0 * d2) + 0.125 * d3) + m[7],
    ]


def outputs_to_points(y):
    y0, y1, y2, y3 = y
    a, b = y0 + y2, y1 + y3
    c, d = y0 + 4.0 * y2, 2.0 * y1 + 8.0 * y3
    e, f = y0 + 0.25 * y2, 0.5 * y1 + 0.125 * y3
    return [y0, a + b, a - b, c + d, c - d, e + f, e - f, y3]


def dot_split(left, right, dims):
    high = left.astype(BF16)
    rest = left - high.astype(F32)
    middle = rest.astype(BF16)
    low = (rest - middle.astype(F32)).astype(BF16)
    parts = jnp.concatenate([high.astype(F32), middle.astype(F32), low.astype(F32)], axis=0)
    product = lax.dot_general(
        parts.astype(BF16), right.astype(BF16), (dims, ((), ())), preferred_element_type=F32
    )
    count = left.shape[0]
    return (product[2 * count :] + product[count : 2 * count]) + product[:count]


def spread_taps(taps, wide_taps, flip):
    for j in range(5):
        column = [taps[5 * i + j : 5 * i + j + 1, :] for i in range(5)]
        if flip:
            column = column[::-1]
        place = 4 - j if flip else j
        for p, value in enumerate(point_taps(column)):
            wide_taps[5 * p + place] = jnp.broadcast_to(value, (8, 128))


def with_edges(value):
    block = lax.broadcasted_iota(jnp.int32, (2, 8, 128), 1)
    left = jnp.where(block > 0, pltpu.roll(value[BLOCK - 2 :], 1, 1), 0.0)
    right = jnp.where(block < 7, pltpu.roll(value[:2], 7, 1), 0.0)
    return jnp.concatenate([left, value, right], axis=0)


def conv_rows(ref, q, h, wide_taps):
    points = to_points([ref[4 * q + n, :, 8 * h : 8 * h + 8, :] for n in range(8)])
    totals = []
    for p in range(8):
        source = with_edges(points[p])
        total = source[0:BLOCK] * wide_taps[5 * p][None]
        for j in range(1, 5):
            total = total + source[j : j + BLOCK] * wide_taps[5 * p + j][None]
        totals.append(total)
    return from_points(totals)


def pad_mask():
    block = lax.broadcasted_iota(jnp.int32, (4, 8, 128), 1)
    return jnp.where(block < 7, 1.0, 0.0)


def gate_row(depth, dgated, gates, h, keep):
    gate = gates[h : h + 1, :][None]
    pull = gates[2 + h : 3 + h, :][None]
    sig = sigmoid(depth)
    act = depth * sig
    gated = act * gate
    ddepth = (dgated * gate + pull) * (sig + act - act * sig)
    ddepth = jnp.concatenate([ddepth[:9], ddepth[9:] * keep], axis=0)
    return gated, ddepth


def unpermute(value, out, r):
    for img in range(2):
        out[img, r] = dot_tn(value, one_hot(img, False)).astype(BF16)


def all_channels_out(rows_in, weights, base, shift, out):
    def chunk(q, carry):
        block = rows_in[pl.ds(pl.multiple_of(4 * PIX * q, 4 * PIX), 4 * PIX), :]
        product = dot_nn(block, weights[...]).reshape(4, PIX, C)
        for n in range(4):
            value = product[n] + base[4 * q + n + shift].astype(F32)
            unpermute(value.astype(BF16), out, 4 * q + n)
        return carry

    lax.fori_loop(0, 3, chunk, 0)


def all_channels_grad(rows_in, turned, grad):
    def lanes(q, carry):
        span = pl.ds(pl.multiple_of(384 * q, 128), 384)
        grad[:, span] = dot_nn(turned[...], rows_in[:, span])
        return carry

    lax.fori_loop(0, 3, lanes, 0)


def to_dp(src, dst, send, recv, by_sender=False):
    me_s, me_d = lax.axis_index("space"), lax.axis_index("dp")
    copies = []
    for k in range(1, ND):
        target = lax.rem(me_d + k, ND)
        copies.append(
            pltpu.make_async_remote_copy(
                src_ref=src.at[target],
                dst_ref=dst.at[me_d] if by_sender else dst.at[k],
                send_sem=send.at[k],
                recv_sem=recv.at[k],
                device_id=(me_s, target),
                device_id_type=MESH,
            )
        )
    return copies


def to_space(ref, send, recv):
    me_s, me_d = lax.axis_index("space"), lax.axis_index("dp")
    copies = []
    for k in range(1, NS):
        copies.append(
            pltpu.make_async_remote_copy(
                src_ref=ref.at[me_s],
                dst_ref=ref.at[me_s],
                send_sem=send.at[k],
                recv_sem=recv.at[k],
                device_id=(lax.rem(me_s + k, NS), me_d),
                device_id_type=MESH,
            )
        )
    return copies


def to_neighbours(down_src, down_dst, up_src, up_dst, send, recv):
    me_s, me_d = lax.axis_index("space"), lax.axis_index("dp")
    down = pltpu.make_async_remote_copy(
        src_ref=down_src,
        dst_ref=down_dst,
        send_sem=send[0],
        recv_sem=recv[0],
        device_id=(lax.rem(me_s + 1, NS), me_d),
        device_id_type=MESH,
    )
    up = pltpu.make_async_remote_copy(
        src_ref=up_src,
        dst_ref=up_dst,
        send_sem=send[1],
        recv_sem=recv[1],
        device_id=(lax.rem(me_s + NS - 1, NS), me_d),
        device_id_type=MESH,
    )
    return down, up


def dp_sum(copies, piece, got):
    total = piece[lax.axis_index("dp")].astype(F32)
    for k, copy in enumerate(copies):
        copy.wait()
        total = total + got[k + 1].astype(F32)
    return total


def space_sum(copies, ref):
    for copy in copies:
        copy.wait()
    total = ref[0].astype(F32)
    for s in range(1, NS):
        total = total + ref[s].astype(F32)
    return total


EARLY = C + 32


def block_kernel(
    wet, wpr, taps, wrt, wx_own, bex, bred, feats_in, cot_in,
    out, out_grad_to, early, late, mail_out,
    out_grad, feats, cot, stage, pack, full, top, bottom, flatw, fp, cp, fpt, cpt, we, wp, misc,
    wide_taps, ex, dgs, coming_pre, coming_dg, saved, depth, sums, packed, landed, lanes, vecs, gates, msgs, mail,
    edge, above, below, gated, dpre, acc, held, flat, flat_taps,
    epiece, egot, espace, lpiece, lgot, lspace, tpiece, tgot, tspace,
    wsend, wrecv, hsend, hrecv, csend, crecv, ssend, srecv, msend, mrecv,
    dsend, drecv, esend, erecv, fsend, frecv, lsend, lrecv, gsend, grecv,
    tsend, trecv, usend, urecv, insem,
):
    me_s, me_d = lax.axis_index("space"), lax.axis_index("dp")
    core = lax.rem(me_s, 2)
    barrier = pltpu.get_barrier_semaphore()
    for k in range(1, ND):
        pl.semaphore_signal(
            barrier, inc=1, device_id=(me_s, lax.rem(me_d + k, ND)), device_id_type=MESH
        )
    for k in range(1, NS):
        pl.semaphore_signal(
            barrier, inc=1, device_id=(lax.rem(me_s + k, NS), me_d), device_id_type=MESH
        )

    arrive = [
        pltpu.make_async_copy(feats_in, feats, insem.at[0]),
        pltpu.make_async_copy(cot_in, cot, insem.at[1]),
    ]
    for copy in arrive:
        copy.start()

    stage[...] = jnp.zeros_like(stage)
    stage[0, 0:PART, 0:C] = wet[...].astype(F32)
    stage[1, 0:PART, 0:C] = wpr[...].astype(F32)
    side = slice(C, C + PART)
    for i in range(5):
        stage[0, 5 * i : 5 * i + 5, side] = taps[i].astype(F32)
    stage[0, 32 : 32 + SE, side] = wrt[...].astype(F32)
    stage[1, 0:SE, side] = wx_own[...].astype(F32)
    stage[1, 48:49, side] = bex[...].astype(F32)
    pack[...] = stage[...].astype(BF16)
    pl.semaphore_wait(barrier, NS + ND - 2)
    copies = []
    for k in range(1, ND):
        copy = pltpu.make_async_remote_copy(
            src_ref=pack.at[core],
            dst_ref=full.at[core, me_d],
            send_sem=wsend.at[k],
            recv_sem=wrecv.at[k],
            device_id=(me_s, lax.rem(me_d + k, ND)),
            device_id_type=MESH,
        )
        copy.start()
        copies.append(copy)
    for copy in arrive:
        copy.wait()
    halo = to_neighbours(
        feats.at[:, pl.ds(ROWS - 2, 2)],
        top,
        feats.at[:, pl.ds(0, 2)],
        bottom,
        (hsend.at[0], hsend.at[1]),
        (hrecv.at[0], hrecv.at[1]),
    )
    for copy in halo:
        copy.start()
    full[core, me_d] = pack[core]
    spread = (one_hot(0, False), one_hot(1, False))
    gather_t = (one_hot(0, True), one_hot(1, True))

    def permute(r, carry):
        for src, dst, shift in ((feats, fp, 2), (cot, cp, 0)):
            a, b = src[0, r], src[1, r]
            dst[r + shift] = (dot_nt(spread[0], a) + dot_nt(spread[1], b)).astype(BF16)
        return carry

    lax.fori_loop(0, ROWS, permute, 0)
    for r in range(ROWS):
        for src, dst in ((feats, fpt), (cot, cpt)):
            value = dot_nn(src[0, r], gather_t[0]) + dot_nn(src[1, r], gather_t[1])
            dst[:, PIX * r : PIX * (r + 1)] = value.astype(BF16)
    for copy in copies:
        copy.wait()
    share = pltpu.make_async_remote_copy(
        src_ref=full.at[core],
        dst_ref=full.at[core],
        send_sem=csend,
        recv_sem=crecv,
        device_id=(me_s + 1 - 2 * core, me_d),
        device_id_type=MESH,
    )
    share.start()
    for copy in halo:
        copy.wait()
    has_top = jnp.where(me_s > 0, 1.0, 0.0)
    has_bottom = jnp.where(me_s < NS - 1, 1.0, 0.0)
    for r in range(2):
        value = dot_nt(spread[0], top[0, r]) + dot_nt(spread[1], top[1, r])
        fp[r] = (value * has_top).astype(BF16)
        value = dot_nt(spread[0], bottom[0, r]) + dot_nt(spread[1], bottom[1, r])
        fp[ROWS + 2 + r] = (value * has_bottom).astype(BF16)
    share.wait()
    for half, whole in ((0, we), (1, wp)):
        for d in range(ND):
            part = full[half, d].astype(F32)
            flatw[d * SLOT : (d + 1) * SLOT, :] = part[0:SLOT, 0:C]
            span = slice(d * SLOT, (d + 1) * SLOT)
            if half == 0:
                misc[0:80, span] = part[:, C : C + SLOT]
            else:
                misc[80:136, span] = part[0:56, C : C + SLOT]
        whole[...] = flatw[...].astype(BF16)

    keep = pad_mask()

    def lane_of(t):
        return pl.ds(pl.multiple_of(128 * t, 128), 128)

    def pre_rows(t, start, count):
        product = dot_nt(fp[pl.ds(start, count)].reshape(count * PIX, C), we[lane_of(t), :])
        coming_pre[pl.ds(start, count)] = product.reshape(count, BLOCK, SUB, 128)

    def cot_rows(t, start, count):
        product = dot_nt(cp[pl.ds(start, count)].reshape(count * PIX, C), wp[lane_of(t), :])
        coming_dg[pl.ds(start, count)] = product.reshape(count, BLOCK, SUB, 128)

    def next_tile(t):
        return jnp.minimum(t + 1, TILES - 1)

    def take_dg():
        def row(r, carry):
            dgs[r] = coming_dg[r]
            return carry

        lax.fori_loop(0, ROWS, row, 0)

    def first(t, carry):
        spread_taps(misc[0:32, lane_of(t)], wide_taps, False)

        def expand(q, carry):
            for n in range(4):
                value = swish(coming_pre[4 * q + n]).astype(BF16).astype(F32)
                ex[4 * q + n] = value
            return carry

        lax.fori_loop(0, HROWS // 4, expand, 0)
        take_dg()

        def conv(q, carry):
            pools, grads = list(carry[:2]), list(carry[2:])
            for h in range(2):
                rows = slice(8 * h, 8 * h + 8)
                for n, total in enumerate(conv_rows(ex, q, h, wide_taps)):
                    depth[t, 4 * q + n, :, rows, :] = total
                    act = swish(total)
                    grads[h] = grads[h] + jnp.sum(act * dgs[4 * q + n, :, rows, :], axis=0)
                    pools[h] = pools[h] + jnp.sum(act[:9], axis=0)
                    pools[h] = pools[h] + jnp.sum(act[9:] * keep, axis=0)
            for n in range(4):
                saved[t, 4 * q + n] = ex[4 * q + n].astype(BF16)
            pre_rows(next_tile(t), jnp.minimum(6 * q, HROWS - 6), 6)
            cot_rows(next_tile(t), 4 * q, 4)
            return (*pools, *grads)

        zero = jnp.zeros((8, 128), F32)
        parts = lax.fori_loop(0, ROWS // 4, conv, (zero,) * 4)
        for r in range(ROWS, HROWS):
            saved[t, r] = ex[r].astype(BF16)
        for k in range(4):
            sums[t, k : k + 1, :] = jnp.sum(parts[k], axis=0, keepdims=True)
        return carry

    def begin(q, carry):
        pre_rows(0, 8 * q, 8)
        cot_rows(0, 6 * q, 6)
        return carry

    lax.fori_loop(0, 2, begin, 0)
    lax.fori_loop(0, TILES, first, 0)

    packed[...] = jnp.zeros_like(packed)
    for t in range(TILES):
        packed[t // 2, 4 * (t % 2) : 4 * (t % 2) + 4, :] = sums[t, 0:4, :]
    landed[me_s] = packed[...]
    copies = to_space(landed, ssend, srecv)
    for copy in copies:
        copy.start()

    def begin_again(q, carry):
        cot_rows(0, 6 * q, 6)
        return carry

    lax.fori_loop(0, 2, begin_again, 0)
    total = space_sum(copies, landed)
    for t in range(TILES):
        lanes[0:4, 128 * t : 128 * (t + 1)] = total[t // 2, 4 * (t % 2) : 4 * (t % 2) + 4]
    lanes[:, CP:] = jnp.zeros((8, 128), F32)
    wr = misc[32 : 32 + SE, :]
    wx = misc[80 : 80 + SE, :]
    pooled = lanes[0:2, 0:CP] / AREA
    dgate = lanes[2:4, 0:CP]
    squeeze_pre = dot_split(pooled, wr, ((1,), (1,))) + bred[...].astype(F32)
    squeeze = swish(squeeze_pre)
    gate = sigmoid(dot_split(squeeze, wx, ((1,), (0,))) + misc[128:129, :])
    dlogit = dgate * gate * (1.0 - gate)
    dsq = dot_split(dlogit, wx, ((1,), (1,))) * swish_grad(squeeze_pre)
    dpooled = dot_split(dsq, wr, ((1,), (0,)))
    gates[0:2, :] = gate
    gates[2:4, :] = dpooled / AREA
    gates[4:8, :] = jnp.zeros((4, CP), F32)
    lanes[0:2, 0:CP] = pooled
    lanes[2:4, 0:CP] = dlogit
    vecs[...] = jnp.zeros((8, 128), F32)
    vecs[4:6, 0:SE] = squeeze
    vecs[6:8, 0:SE] = dsq
    for d in range(ND):
        msgs[d, 0:4, :] = lanes[0:4, SLOT * d : SLOT * d + 128]
        msgs[d, 4:8, :] = vecs[4:8, :]
    mail[me_d] = msgs[me_d]
    small = to_dp(msgs, mail, msend, mrecv, True)
    for copy in small:
        copy.start()

    def edge_copies(t):
        return to_neighbours(
            edge.at[t, 1],
            above.at[t],
            edge.at[t, 0],
            below.at[t],
            (dsend.at[0, t], dsend.at[1, t]),
            (drecv.at[0, t], drecv.at[1, t]),
        )

    def second(t, carry):
        take_dg()

        def pointwise(q, carry):
            for n in range(4):
                r = 4 * q + n
                both = []
                for h in range(2):
                    rows = slice(8 * h, 8 * h + 8)
                    value, ddepth = gate_row(
                        depth[t, r, :, rows, :],
                        dgs[r, :, rows, :],
                        gates.at[:, lane_of(t)],
                        h,
                        keep,
                    )
                    depth[t, r, :, rows, :] = ddepth.astype(BF16).astype(F32)
                    both.append(value)
                gated[pl.ds(pl.multiple_of(r * PIX, PIX), PIX), lane_of(t)] = (
                    jnp.concatenate(both, axis=1).reshape(PIX, 128).astype(BF16)
                )
            cot_rows(next_tile(t), 4 * q, 4)
            return carry

        lax.fori_loop(0, ROWS // 4, pointwise, 0)
        for n in range(2):
            edge[t, 0, n] = depth[t, n].astype(BF16)
            edge[t, 1, n] = depth[t, ROWS - 2 + n].astype(BF16)
        for copy in edge_copies(t):
            copy.start()
        return carry

    lax.fori_loop(0, TILES, second, 0)

    def pieces_of(source, rows, piece):
        for d in range(ND):
            piece[d] = source[0:rows, SLOT * d : SLOT * d + 128].astype(BF16)

    flat[:, CP:] = jnp.zeros((C, 128), F32)
    flat_taps[...] = jnp.zeros_like(flat_taps)
    all_channels_grad(gated, cpt, flat)
    pieces_of(flat, C, epiece)
    for copy in to_dp(epiece, egot, esend, erecv):
        copy.start()

    def third(t, carry):
        spread_taps(misc[0:32, lane_of(t)], wide_taps, True)

        def middle(r, carry):
            ex[r + 2] = depth[t, r]
            return carry

        lax.fori_loop(0, ROWS, middle, 0)

        def slopes(q, carry):
            for n in range(4):
                dgs[4 * q + n] = swish_grad(coming_pre[4 * q + n + 2])
            return carry

        lax.fori_loop(0, ROWS // 4, slopes, 0)
        for copy in edge_copies(t):
            copy.wait()
        for n in range(2):
            ex[n] = above[t, n].astype(F32) * has_top
            ex[ROWS + 2 + n] = below[t, n].astype(F32) * has_bottom

        def conv(q, carry):
            both = []
            for h in range(2):
                rows = slice(8 * h, 8 * h + 8)
                values = conv_rows(ex, q, h, wide_taps)
                both.append([value * dgs[4 * q + n, :, rows, :] for n, value in enumerate(values)])
            for n in range(4):
                value = jnp.concatenate([both[0][n], both[1][n]], axis=1)
                span = pl.ds(pl.multiple_of((4 * q + n) * PIX, PIX), PIX)
                dpre[span, lane_of(t)] = value.reshape(PIX, 128).astype(BF16)
            pre_rows(next_tile(t), 4 * q + 2, 4)
            return carry

        lax.fori_loop(0, ROWS // 4, conv, 0)

        @pl.when(t == TILES // 2)
        def _():
            total = dp_sum(to_dp(epiece, egot, esend, erecv), epiece, egot)
            espace[me_s] = total.astype(BF16)
            for copy in to_space(espace, fsend, frecv):
                copy.start()

        return carry

    def begin_third(q, carry):
        pre_rows(0, 6 * q + 2, 6)
        return carry

    lax.fori_loop(0, 2, begin_third, 0)
    lax.fori_loop(0, TILES, third, 0)

    all_channels_grad(dpre, fpt, flat)
    pieces_of(flat, C, lpiece)
    for copy in to_dp(lpiece, lgot, lsend, lrecv):
        copy.start()

    def tap_grads(t, carry):
        acc[...] = jnp.zeros_like(acc)

        def window(q, carry):
            for h in range(2):
                rows = slice(8 * h, 8 * h + 8)
                points = to_points([saved[t, 4 * q + n].astype(F32)[:, rows, :] for n in range(8)])
                for p in range(8):
                    held[p] = with_edges(points[p])
                mine = outputs_to_points([depth[t, 4 * q + n, :, rows, :] for n in range(4)])
                for p in range(8):
                    source = held[p]
                    for j in range(5):
                        k = 5 * p + j
                        acc[k] = acc[k] + jnp.sum(mine[p] * source[j : j + BLOCK], axis=0)
            return carry

        lax.fori_loop(0, ROWS // 4, window, 0)
        for j in range(5):
            sums_at = [jnp.sum(acc[5 * p + j], axis=0, keepdims=True) for p in range(8)]
            for i, value in enumerate(taps_from_points(sums_at)):
                flat_taps[5 * i + j : 5 * i + j + 1, lane_of(t)] = value

        @pl.when(t == TILES // 2)
        def _():
            total = dp_sum(to_dp(lpiece, lgot, lsend, lrecv), lpiece, lgot)
            lspace[me_s] = total.astype(BF16)
            for copy in to_space(lspace, gsend, grecv):
                copy.start()

        return carry

    lax.fori_loop(0, TILES, tap_grads, 0)
    pieces_of(flat_taps, 32, tpiece)
    copies = to_dp(tpiece, tgot, tsend, trecv)
    for copy in copies:
        copy.start()

    all_channels_out(dpre, we, cp, 0, out_grad)
    leave = pltpu.make_async_copy(out_grad, out_grad_to, insem.at[0])
    leave.start()
    tspace[me_s] = dp_sum(copies, tpiece, tgot).astype(BF16)
    copies = to_space(tspace, usend, urecv)
    for copy in copies:
        copy.start()
    all_channels_out(gated, wp, fp, 2, out)
    for copy in small:
        copy.wait()
    mail_out[...] = mail[...]
    early[0:C] = space_sum(to_space(espace, fsend, frecv), espace)
    late[...] = space_sum(to_space(lspace, gsend, grecv), lspace)
    early[C:] = space_sum(copies, tspace)
    leave.wait()


def block(*args):
    def bf16(*shape):
        return pltpu.VMEM(shape, BF16)

    def f32(*shape):
        return pltpu.VMEM(shape, F32)

    def sems(*shape):
        return pltpu.SemaphoreType.DMA(shape)

    one = pltpu.SemaphoreType.DMA
    return pl.pallas_call(
        block_kernel,
        out_shape=(
            jax.ShapeDtypeStruct((IMGS, ROWS, C, COLS), BF16),
            jax.ShapeDtypeStruct((IMGS, ROWS, C, COLS), BF16),
            jax.ShapeDtypeStruct((EARLY, 128), F32),
            jax.ShapeDtypeStruct((C, 128), F32),
            jax.ShapeDtypeStruct((ND, 8, 128), F32),
        ),
        in_specs=[VMEM] * 7 + [ANY] * 2,
        out_specs=(VMEM, ANY, VMEM, VMEM, VMEM),
        scratch_shapes=[
            bf16(IMGS, ROWS, C, COLS),
            bf16(IMGS, ROWS, C, COLS),
            bf16(IMGS, ROWS, C, COLS),
            f32(2, 80, 256),
            bf16(2, 80, 256),
            bf16(2, ND, 80, 256),
            bf16(IMGS, 2, C, COLS),
            bf16(IMGS, 2, C, COLS),
            f32(CP, C),
            bf16(HROWS, PIX, C),
            bf16(ROWS, PIX, C),
            bf16(C, ROWS * PIX),
            bf16(C, ROWS * PIX),
            bf16(CP, C),
            bf16(CP, C),
            f32(136, CP),
            f32(40, 8, 128),
            f32(HROWS, BLOCK, SUB, 128),
            f32(ROWS, BLOCK, SUB, 128),
            f32(HROWS, BLOCK, SUB, 128),
            f32(ROWS, BLOCK, SUB, 128),
            bf16(TILES, HROWS, BLOCK, SUB, 128),
            f32(TILES, ROWS, BLOCK, SUB, 128),
            f32(TILES, 8, 128),
            f32(5, 8, 128),
            f32(NS, 5, 8, 128),
            f32(8, CP + 128),
            f32(8, 128),
            f32(8, CP),
            f32(ND, 8, 128),
            f32(ND, 8, 128),
            bf16(TILES, 2, 2, BLOCK, SUB, 128),
            bf16(TILES, 2, BLOCK, SUB, 128),
            bf16(TILES, 2, BLOCK, SUB, 128),
            bf16(ROWS * PIX, CP),
            bf16(ROWS * PIX, CP),
            f32(40, 8, 128),
            f32(8, WIDE, 8, 128),
            f32(C, CP + 128),
            f32(32, CP + 128),
            bf16(ND, C, 128),
            bf16(ND, C, 128),
            bf16(NS, C, 128),
            bf16(ND, C, 128),
            bf16(ND, C, 128),
            bf16(NS, C, 128),
            bf16(ND, 32, 128),
            bf16(ND, 32, 128),
            bf16(NS, 32, 128),
            sems(ND),
            sems(ND),
            sems(2),
            sems(2),
            one,
            one,
            sems(NS),
            sems(NS),
            sems(ND),
            sems(ND),
            sems(2, TILES),
            sems(2, TILES),
            sems(ND),
            sems(ND),
            sems(NS),
            sems(NS),
            sems(ND),
            sems(ND),
            sems(NS),
            sems(NS),
            sems(ND),
            sems(ND),
            sems(NS),
            sems(NS),
            sems(2),
        ],
        compiler_params=pltpu.CompilerParams(
            collective_id=0, has_side_effects=True, vmem_limit_bytes=63 * 2**20
        ),
        name="block",
    )(*args)


def finish_kernel(
    early, late, mail, raw, raw_grad,
    gexp, gdepth, greduce, gexcite, gbex, gproj, gbred, out, out_grad,
):
    out[...] = raw[...]
    out_grad[...] = raw_grad[...]

    @pl.when(pl.program_id(0) == 0)
    def _():
        gexp[...] = late[...].T[0:PART]
        gproj[...] = early[0:C].T[0:PART]
        for i in range(5):
            gdepth[i] = early[C + 5 * i : C + 5 * i + 5, 0:PART]
        rows = [mail[d] for d in range(ND)]
        pool_all = jnp.concatenate([row[0:2] for row in rows], axis=0)
        dlog_all = jnp.concatenate([row[2:4] for row in rows], axis=0)
        sq_all = jnp.concatenate([row[4:6] for row in rows], axis=0)
        dsq_all = jnp.concatenate([row[6:8] for row in rows], axis=0)
        greduce[...] = dot_tn(dsq_all, pool_all, HIGH)[0:SE, 0:PART]
        gexcite[...] = dot_tn(sq_all, dlog_all, HIGH)[0:SE, 0:PART]
        gbex[...] = jnp.sum(dlog_all, axis=0, keepdims=True)[:, 0:PART]
        gbred[...] = jnp.sum(dsq_all, axis=0, keepdims=True)[:, 0:SE]


def finish(early, late, mail, raw, raw_grad):
    def whole(*shape):
        zeros = (0,) * len(shape)
        return pl.BlockSpec(shape, lambda n: zeros)

    part = pl.BlockSpec((IMGS, 6, C, COLS), lambda n: (0, n, 0, 0))
    shapes = ((PART, C), (5, 5, PART), (SE, PART), (SE, PART), (1, PART), (PART, C), (1, SE))
    return pl.pallas_call(
        finish_kernel,
        grid=(ROWS // 6,),
        out_shape=tuple(jax.ShapeDtypeStruct(shape, F32) for shape in shapes)
        + (jax.ShapeDtypeStruct((IMGS, ROWS, C, COLS), BF16),) * 2,
        in_specs=[whole(EARLY, 128), whole(C, 128), whole(ND, 8, 128), part, part],
        out_specs=tuple(whole(*shape) for shape in shapes) + (part, part),
        name="finish",
    )(early, late, mail, raw, raw_grad)


def on_device(
    features, w_expand, w_depth, w_reduce, b_reduce, w_excite, b_excite, w_project, cotangent
):
    raw, raw_grad, early, late, mail = block(
        w_expand.T,
        w_project,
        w_depth,
        w_reduce.T,
        w_excite,
        b_excite[None, :],
        b_reduce[None, :],
        features.swapaxes(2, 3),
        cotangent.swapaxes(2, 3),
    )
    (
        s_expand, s_depth, s_reduce, s_excite, s_bexcite, s_project, s_breduce, output, grad,
    ) = finish(early, late, mail, raw, raw_grad)
    return (
        output.swapaxes(2, 3),
        grad.swapaxes(2, 3),
        s_expand.T,
        s_depth,
        s_reduce.T,
        s_excite,
        s_bexcite[0],
        s_project,
        s_breduce[0],
    )


def solution(mesh):
    return jax.shard_map(
        on_device,
        mesh=mesh,
        in_specs=(
            P("dp", "space", None, None),
            P(None, "dp"),
            P(None, None, "dp"),
            P("dp", None),
            P(),
            P(None, "dp"),
            P("dp"),
            P("dp", None),
            P("dp", "space", None, None),
        ),
        out_specs=(
            P("dp", "space", None, None),
            P("dp", "space", None, None),
            P(None, "dp"),
            P(None, None, "dp"),
            P("dp", None),
            P(None, "dp"),
            P("dp"),
            P("dp", None),
            P(),
        ),
        check_vma=False,
    )
```

```python
import functools

import jax
import jax.numpy as jnp
from jax import lax
from jax.experimental import pallas as pl
from jax.experimental.pallas import tpu as pltpu
from jax.sharding import PartitionSpec as P

F32 = jnp.float32
BF16 = jnp.bfloat16
MESH = pl.DeviceIdType.MESH
HIGH = lax.Precision.HIGHEST

IMGS, ROWS, COLS, C, SE = 2, 12, 100, 176, 44
BLOCK, SUB = 13, 16
PIX = BLOCK * SUB
WIDE = BLOCK + 4
HROWS = ROWS + 4
PART, SLOT = 66, 72
CP = 16 * SLOT
TILES = CP // 128
AREA = 9600.0
NS, ND = 8, 16

VMEM = pl.BlockSpec(memory_space=pltpu.VMEM)
ANY = pl.BlockSpec(memory_space=pl.ANY)


def sigmoid(value):
    return 0.5 * jnp.tanh(0.5 * value) + 0.5


def swish(value):
    half = 0.5 * value
    return half + half * jnp.tanh(half)


def swish_grad(value):
    sig = sigmoid(value)
    act = value * sig
    return sig + act - act * sig


def twice_swish_grad(value):
    half = 0.5 * value
    twice = 1.0 + jnp.tanh(half)
    return twice * ((value - half * twice) + 1.0)


def dot_nt(left, right, precision=None):
    return lax.dot_general(
        left, right, (((1,), (1,)), ((), ())), precision=precision, preferred_element_type=F32
    )


def dot_tn(left, right, precision=None):
    return lax.dot_general(
        left, right, (((0,), (0,)), ((), ())), precision=precision, preferred_element_type=F32
    )


def dot_nn(left, right, precision=None):
    return lax.dot_general(
        left, right, (((1,), (0,)), ((), ())), precision=precision, preferred_element_type=F32
    )


def one_hot(img, transposed):
    shape = (COLS, PIX) if transposed else (PIX, COLS)
    place = lax.broadcasted_iota(jnp.int32, shape, 1 if transposed else 0)
    col = lax.broadcasted_iota(jnp.int32, shape, 0 if transposed else 1)
    wanted = (col % BLOCK) * SUB + img * 8 + col // BLOCK
    return jnp.where(place == wanted, 1.0, 0.0).astype(BF16)


def point_taps(taps):
    w0, w1, w2, w3, w4 = taps
    even, odd = w0 + w2 + w4, w1 + w3
    even2, odd2 = w0 + 4.0 * w2 + 16.0 * w4, 2.0 * w1 + 8.0 * w3
    even3, odd3 = w0 + 0.25 * w2 + 0.0625 * w4, 0.5 * w1 + 0.125 * w3
    return [
        w0,
        (even + odd) * (-2.0 / 9.0),
        (even - odd) * (-2.0 / 9.0),
        (even2 + odd2) * (1.0 / 360.0),
        (even2 - odd2) * (1.0 / 360.0),
        (even3 + odd3) * (32.0 / 45.0),
        (even3 - odd3) * (32.0 / 45.0),
        w4,
    ]


def taps_from_points(g):
    s1, d1 = (g[1] + g[2]) * (-2.0 / 9.0), (g[1] - g[2]) * (-2.0 / 9.0)
    s2, d2 = (g[3] + g[4]) * (1.0 / 360.0), (g[3] - g[4]) * (1.0 / 360.0)
    s3, d3 = (g[5] + g[6]) * (32.0 / 45.0), (g[5] - g[6]) * (32.0 / 45.0)
    return [
        g[0] + s1 + s2 + s3,
        d1 + 2.0 * d2 + 0.5 * d3,
        s1 + 4.0 * s2 + 0.25 * s3,
        d1 + 8.0 * d2 + 0.125 * d3,
        s1 + 16.0 * s2 + 0.0625 * s3 + g[7],
    ]


def to_points(x):
    x0, x1, x2, x3, x4, x5, x6, x7 = x
    f3, f4 = 5.0 * x3, 5.0 * x4
    e1, o1 = (x6 + x2) - 4.25 * x4, (x5 + x1) - 4.25 * x3
    e2, o2 = (x2 - f4) + 4.0 * x6, (x1 - f3) + 4.0 * x5
    e3, o3 = (4.0 * x2 - f4) + x6, (4.0 * x1 - f3) + x5
    o2, o3 = o2 + o2, 0.5 * o3
    return [
        (x0 - x6) + 5.25 * (x4 - x2),
        e1 + o1,
        e1 - o1,
        e2 + o2,
        e2 - o2,
        e3 + o3,
        e3 - o3,
        (x7 - x1) + 5.25 * (x3 - x5),
    ]


def from_points(m):
    s1, d1 = m[1] + m[2], m[1] - m[2]
    s2, d2 = m[3] + m[4], m[3] - m[4]
    s3, d3 = m[5] + m[6], m[5] - m[6]
    return [
        (m[0] + s1) + (s2 + s3),
        (d1 + 2.0 * d2) + 0.5 * d3,
        (s1 + 4.0 * s2) + 0.25 * s3,
        ((d1 + 8.0 * d2) + 0.125 * d3) + m[7],
    ]


def outputs_to_points(y):
    y0, y1, y2, y3 = y
    a, b = y0 + y2, y1 + y3
    c, d = y0 + 4.0 * y2, 2.0 * y1 + 8.0 * y3
    e, f = y0 + 0.25 * y2, 0.5 * y1 + 0.125 * y3
    return [y0, a + b, a - b, c + d, c - d, e + f, e - f, y3]


def dot_split(left, right, dims):
    high = left.astype(BF16)
    rest = left - high.astype(F32)
    middle = rest.astype(BF16)
    low = (rest - middle.astype(F32)).astype(BF16)
    parts = jnp.concatenate([high.astype(F32), middle.astype(F32), low.astype(F32)], axis=0)
    product = lax.dot_general(
        parts.astype(BF16), right.astype(BF16), (dims, ((), ())), preferred_element_type=F32
    )
    count = left.shape[0]
    return (product[2 * count :] + product[count : 2 * count]) + product[:count]


def spread_taps(taps, wide_taps, flip):
    for j in range(5):
        column = [taps[5 * i + j : 5 * i + j + 1, :] for i in range(5)]
        if flip:
            column = [0.5 * value for value in column[::-1]]
        place = 4 - j if flip else j
        for p, value in enumerate(point_taps(column)):
            wide_taps[5 * p + place] = jnp.broadcast_to(value, (8, 128))


def with_edges(value):
    block = lax.broadcasted_iota(jnp.int32, (2, 8, 128), 1)
    left = jnp.where(block > 0, pltpu.roll(value[BLOCK - 2 :], 1, 1), 0.0)
    right = jnp.where(block < 7, pltpu.roll(value[:2], 7, 1), 0.0)
    return jnp.concatenate([left, value, right], axis=0)


def conv_rows(ref, q, h, wide_taps):
    points = to_points([ref[4 * q + n, :, 8 * h : 8 * h + 8, :] for n in range(8)])
    totals = []
    for p in range(8):
        source = with_edges(points[p])
        total = source[0:BLOCK] * wide_taps[5 * p][None]
        for j in range(1, 5):
            total = total + source[j : j + BLOCK] * wide_taps[5 * p + j][None]
        totals.append(total)
    return from_points(totals)


def pad_mask():
    block = lax.broadcasted_iota(jnp.int32, (4, 8, 128), 1)
    return jnp.where(block < 7, 1.0, 0.0)


def gate_row(depth, dgated, gates, h, keep):
    gate = gates[h : h + 1, :][None]
    half_gate = gates[2 + h : 3 + h, :][None]
    half_pull = gates[4 + h : 5 + h, :][None]
    half = 0.5 * depth
    twice = 1.0 + jnp.tanh(half)
    act = half * twice
    gated = act * gate
    ddepth = (dgated * half_gate + half_pull) * (twice * ((depth - act) + 1.0))
    ddepth = jnp.concatenate([ddepth[:9], ddepth[9:] * keep], axis=0)
    return gated, ddepth


def unpermute(value, out, r):
    for img in range(2):
        out[img, r] = dot_tn(value, one_hot(img, False)).astype(BF16)


def all_channels_out(rows_in, weights, base, shift, out):
    def chunk(q, carry):
        block = rows_in[pl.ds(pl.multiple_of(4 * PIX * q, 4 * PIX), 4 * PIX), :]
        product = dot_nn(block, weights[...]).reshape(4, PIX, C)
        for n in range(4):
            value = product[n] + base[4 * q + n + shift].astype(F32)
            unpermute(value.astype(BF16), out, 4 * q + n)
        return carry

    lax.fori_loop(0, 3, chunk, 0)


def all_channels_grad(rows_in, turned, grad):
    def lanes(q, carry):
        span = pl.ds(pl.multiple_of(384 * q, 128), 384)
        grad[:, span] = dot_nn(turned[...], rows_in[:, span])
        return carry

    lax.fori_loop(0, 3, lanes, 0)


def to_dp(src, dst, send, recv, by_sender=False):
    me_s, me_d = lax.axis_index("space"), lax.axis_index("dp")
    copies = []
    for k in range(1, ND):
        target = lax.rem(me_d + k, ND)
        copies.append(
            pltpu.make_async_remote_copy(
                src_ref=src.at[target],
                dst_ref=dst.at[me_d] if by_sender else dst.at[k],
                send_sem=send.at[k],
                recv_sem=recv.at[k],
                device_id=(me_s, target),
                device_id_type=MESH,
            )
        )
    return copies


def to_space(ref, send, recv):
    me_s, me_d = lax.axis_index("space"), lax.axis_index("dp")
    copies = []
    for k in range(1, NS):
        copies.append(
            pltpu.make_async_remote_copy(
                src_ref=ref.at[me_s],
                dst_ref=ref.at[me_s],
                send_sem=send.at[k],
                recv_sem=recv.at[k],
                device_id=(lax.rem(me_s + k, NS), me_d),
                device_id_type=MESH,
            )
        )
    return copies


def to_neighbours(down_src, down_dst, up_src, up_dst, send, recv):
    me_s, me_d = lax.axis_index("space"), lax.axis_index("dp")
    down = pltpu.make_async_remote_copy(
        src_ref=down_src,
        dst_ref=down_dst,
        send_sem=send[0],
        recv_sem=recv[0],
        device_id=(lax.rem(me_s + 1, NS), me_d),
        device_id_type=MESH,
    )
    up = pltpu.make_async_remote_copy(
        src_ref=up_src,
        dst_ref=up_dst,
        send_sem=send[1],
        recv_sem=recv[1],
        device_id=(lax.rem(me_s + NS - 1, NS), me_d),
        device_id_type=MESH,
    )
    return down, up


def dp_sum(copies, piece, got):
    total = piece[lax.axis_index("dp")].astype(F32)
    for k, copy in enumerate(copies):
        copy.wait()
        total = total + got[k + 1].astype(F32)
    return total


def space_sum(copies, ref):
    for copy in copies:
        copy.wait()
    total = ref[0].astype(F32)
    for s in range(1, NS):
        total = total + ref[s].astype(F32)
    return total


EARLY = C + 32


def block_kernel(
    wet, wpr, taps, wrt, wx_own, bex, bred, feats_in, cot_in,
    out_to, out_grad_to, early, late, mail_out,
    out, out_grad, feats, cot, stage, pack, full, top, bottom, flatw, fp, cp, fpt, cpt, we, wp, misc,
    wide_taps, ex, dgs, coming_pre, coming_dg, saved, depth, sums, packed, landed, lanes, vecs, gates, msgs, mail,
    edge, above, below, gated, dpre, acc, held, flat, flat_taps,
    epiece, egot, espace, lpiece, lgot, lspace, tpiece, tgot, tspace,
    wsend, wrecv, hsend, hrecv, csend, crecv, ssend, srecv, msend, mrecv,
    dsend, drecv, esend, erecv, fsend, frecv, lsend, lrecv, gsend, grecv,
    tsend, trecv, usend, urecv, insem,
):
    me_s, me_d = lax.axis_index("space"), lax.axis_index("dp")
    core = lax.rem(me_s, 2)
    barrier = pltpu.get_barrier_semaphore()
    for k in range(1, ND):
        pl.semaphore_signal(
            barrier, inc=1, device_id=(me_s, lax.rem(me_d + k, ND)), device_id_type=MESH
        )
    for k in range(1, NS):
        pl.semaphore_signal(
            barrier, inc=1, device_id=(lax.rem(me_s + k, NS), me_d), device_id_type=MESH
        )

    arrive = [
        pltpu.make_async_copy(feats_in, feats, insem.at[0]),
        pltpu.make_async_copy(cot_in, cot, insem.at[1]),
    ]
    for copy in arrive:
        copy.start()

    stage[...] = jnp.zeros_like(stage)
    stage[0, 0:PART, 0:C] = wet[...].astype(F32)
    stage[1, 0:PART, 0:C] = wpr[...].astype(F32)
    side = slice(C, C + PART)
    for i in range(5):
        stage[0, 5 * i : 5 * i + 5, side] = taps[i].astype(F32)
    stage[0, 32 : 32 + SE, side] = wrt[...].astype(F32)
    stage[1, 0:SE, side] = wx_own[...].astype(F32)
    stage[1, 48:49, side] = bex[...].astype(F32)
    pack[...] = stage[...].astype(BF16)
    pl.semaphore_wait(barrier, NS + ND - 2)
    copies = []
    for k in range(1, ND):
        copy = pltpu.make_async_remote_copy(
            src_ref=pack.at[core],
            dst_ref=full.at[core, me_d],
            send_sem=wsend.at[k],
            recv_sem=wrecv.at[k],
            device_id=(me_s, lax.rem(me_d + k, ND)),
            device_id_type=MESH,
        )
        copy.start()
        copies.append(copy)
    for copy in arrive:
        copy.wait()
    halo = to_neighbours(
        feats.at[:, pl.ds(ROWS - 2, 2)],
        top,
        feats.at[:, pl.ds(0, 2)],
        bottom,
        (hsend.at[0], hsend.at[1]),
        (hrecv.at[0], hrecv.at[1]),
    )
    for copy in halo:
        copy.start()
    full[0, me_d] = pack[0]
    full[1, me_d] = pack[1]
    spread = (one_hot(0, False), one_hot(1, False))
    gather_t = (one_hot(0, True), one_hot(1, True))

    def permute(r, carry):
        for src, dst, shift in ((feats, fp, 2), (cot, cp, 0)):
            a, b = src[0, r], src[1, r]
            dst[r + shift] = (dot_nt(spread[0], a) + dot_nt(spread[1], b)).astype(BF16)
        return carry

    lax.fori_loop(0, ROWS, permute, 0)
    for r in range(ROWS):
        for src, dst in ((feats, fpt), (cot, cpt)):
            value = dot_nn(src[0, r], gather_t[0]) + dot_nn(src[1, r], gather_t[1])
            dst[:, PIX * r : PIX * (r + 1)] = value.astype(BF16)
    shares = []
    for k, copy in enumerate(copies, 1):
        copy.wait_recv()
        sender = lax.rem(me_d + ND - k, ND)
        share = pltpu.make_async_remote_copy(
            src_ref=full.at[core, sender],
            dst_ref=full.at[core, sender],
            send_sem=csend.at[k],
            recv_sem=crecv.at[k],
            device_id=(me_s + 1 - 2 * core, me_d),
            device_id_type=MESH,
        )
        share.start()
        shares.append(share)
    for copy in halo:
        copy.wait()
    has_top = jnp.where(me_s > 0, 1.0, 0.0)
    has_bottom = jnp.where(me_s < NS - 1, 1.0, 0.0)
    for r in range(2):
        value = dot_nt(spread[0], top[0, r]) + dot_nt(spread[1], top[1, r])
        fp[r] = (value * has_top).astype(BF16)
        value = dot_nt(spread[0], bottom[0, r]) + dot_nt(spread[1], bottom[1, r])
        fp[ROWS + 2 + r] = (value * has_bottom).astype(BF16)
    for copy in copies:
        copy.wait_send()
    for share in shares:
        share.wait()
    for half, whole in ((0, we), (1, wp)):
        for d in range(ND):
            part = full[half, d].astype(F32)
            flatw[d * SLOT : (d + 1) * SLOT, :] = part[0:SLOT, 0:C]
            span = slice(d * SLOT, (d + 1) * SLOT)
            if half == 0:
                misc[0:80, span] = part[:, C : C + SLOT]
            else:
                misc[80:136, span] = part[0:56, C : C + SLOT]
        whole[...] = flatw[...].astype(BF16)

    keep = pad_mask()

    def lane_of(t):
        return pl.ds(pl.multiple_of(128 * t, 128), 128)

    def pre_rows(t, start, count):
        product = dot_nt(fp[pl.ds(start, count)].reshape(count * PIX, C), we[lane_of(t), :])
        coming_pre[pl.ds(start, count)] = product.reshape(count, BLOCK, SUB, 128)

    def cot_rows(t, start, count):
        product = dot_nt(cp[pl.ds(start, count)].reshape(count * PIX, C), wp[lane_of(t), :])
        coming_dg[pl.ds(start, count)] = product.reshape(count, BLOCK, SUB, 128)

    def next_tile(t):
        return jnp.minimum(t + 1, TILES - 1)

    def take_dg():
        def row(r, carry):
            dgs[r] = coming_dg[r]
            return carry

        lax.fori_loop(0, ROWS, row, 0)

    def first(t, carry):
        spread_taps(misc[0:32, lane_of(t)], wide_taps, False)

        def expand(q, carry):
            for n in range(4):
                ex[4 * q + n] = swish(coming_pre[4 * q + n])
            return carry

        lax.fori_loop(0, HROWS // 4, expand, 0)
        take_dg()

        def conv(q, carry):
            pools, grads = list(carry[:2]), list(carry[2:])
            for h in range(2):
                rows = slice(8 * h, 8 * h + 8)
                for n, total in enumerate(conv_rows(ex, q, h, wide_taps)):
                    depth[t, 4 * q + n, :, rows, :] = total
                    act = swish(total)
                    grads[h] = grads[h] + jnp.sum(act * dgs[4 * q + n, :, rows, :], axis=0)
                    pools[h] = pools[h] + jnp.sum(act[:9], axis=0)
                    pools[h] = pools[h] + jnp.sum(act[9:] * keep, axis=0)
            for n in range(4):
                saved[t, 4 * q + n] = ex[4 * q + n].astype(BF16)
            pre_rows(next_tile(t), jnp.minimum(6 * q, HROWS - 6), 6)
            cot_rows(next_tile(t), 4 * q, 4)
            return (*pools, *grads)

        zero = jnp.zeros((8, 128), F32)
        parts = lax.fori_loop(0, ROWS // 4, conv, (zero,) * 4)
        for r in range(ROWS, HROWS):
            saved[t, r] = ex[r].astype(BF16)
        for k in range(4):
            sums[t, k : k + 1, :] = jnp.sum(parts[k], axis=0, keepdims=True)
        return carry

    def begin(q, carry):
        pre_rows(0, 8 * q, 8)
        cot_rows(0, 6 * q, 6)
        return carry

    lax.fori_loop(0, 2, begin, 0)
    lax.fori_loop(0, TILES, first, 0)

    packed[...] = jnp.zeros_like(packed)
    for t in range(TILES):
        packed[t // 2, 4 * (t % 2) : 4 * (t % 2) + 4, :] = sums[t, 0:4, :]
    landed[me_s] = packed[...]
    copies = to_space(landed, ssend, srecv)
    for copy in copies:
        copy.start()

    def begin_again(q, carry):
        cot_rows(0, 6 * q, 6)
        return carry

    lax.fori_loop(0, 2, begin_again, 0)
    total = space_sum(copies, landed)
    for t in range(TILES):
        lanes[0:4, 128 * t : 128 * (t + 1)] = total[t // 2, 4 * (t % 2) : 4 * (t % 2) + 4]
    lanes[:, CP:] = jnp.zeros((8, 128), F32)
    wr = misc[32 : 32 + SE, :]
    wx = misc[80 : 80 + SE, :]
    pooled = lanes[0:2, 0:CP] / AREA
    dgate = lanes[2:4, 0:CP]
    squeeze_pre = dot_split(pooled, wr, ((1,), (1,))) + bred[...].astype(F32)
    squeeze = swish(squeeze_pre)
    gate = sigmoid(dot_split(squeeze, wx, ((1,), (0,))) + misc[128:129, :])
    dlogit = dgate * gate * (1.0 - gate)
    dsq = dot_split(dlogit, wx, ((1,), (1,))) * swish_grad(squeeze_pre)
    dpooled = dot_split(dsq, wr, ((1,), (0,)))
    gates[0:2, :] = gate
    gates[2:4, :] = 0.5 * gate
    gates[4:6, :] = dpooled * (0.5 / AREA)
    gates[6:8, :] = jnp.zeros((2, CP), F32)
    lanes[0:2, 0:CP] = pooled
    lanes[2:4, 0:CP] = dlogit
    vecs[...] = jnp.zeros((8, 128), F32)
    vecs[4:6, 0:SE] = squeeze
    vecs[6:8, 0:SE] = dsq
    for d in range(ND):
        msgs[d, 0:4, :] = lanes[0:4, SLOT * d : SLOT * d + 128]
        msgs[d, 4:8, :] = vecs[4:8, :]
    mail[me_d] = msgs[me_d]
    small = to_dp(msgs, mail, msend, mrecv, True)
    for copy in small:
        copy.start()

    def edge_copies(t):
        return to_neighbours(
            edge.at[t, 1],
            above.at[t],
            edge.at[t, 0],
            below.at[t],
            (dsend.at[0, t], dsend.at[1, t]),
            (drecv.at[0, t], drecv.at[1, t]),
        )

    def second(t, carry):
        take_dg()

        def pointwise(q, carry):
            for n in range(4):
                r = 4 * q + n
                both = []
                for h in range(2):
                    rows = slice(8 * h, 8 * h + 8)
                    value, ddepth = gate_row(
                        depth[t, r, :, rows, :],
                        dgs[r, :, rows, :],
                        gates.at[:, lane_of(t)],
                        h,
                        keep,
                    )
                    depth[t, r, :, rows, :] = ddepth
                    both.append(value)
                gated[pl.ds(pl.multiple_of(r * PIX, PIX), PIX), lane_of(t)] = (
                    jnp.concatenate(both, axis=1).reshape(PIX, 128).astype(BF16)
                )
            cot_rows(next_tile(t), 4 * q, 4)
            return carry

        lax.fori_loop(0, ROWS // 4, pointwise, 0)
        for n in range(2):
            edge[t, 0, n] = depth[t, n].astype(BF16)
            edge[t, 1, n] = depth[t, ROWS - 2 + n].astype(BF16)
        for copy in edge_copies(t):
            copy.start()
        return carry

    lax.fori_loop(0, TILES, second, 0)

    def pieces_of(source, rows, piece):
        for d in range(ND):
            piece[d] = source[0:rows, SLOT * d : SLOT * d + 128].astype(BF16)

    flat[:, CP:] = jnp.zeros((C, 128), F32)
    flat_taps[...] = jnp.zeros_like(flat_taps)
    all_channels_grad(gated, cpt, flat)
    pieces_of(flat, C, epiece)
    for copy in to_dp(epiece, egot, esend, erecv):
        copy.start()

    def third(t, carry):
        spread_taps(misc[0:32, lane_of(t)], wide_taps, True)

        def middle(r, carry):
            ex[r + 2] = depth[t, r]
            return carry

        lax.fori_loop(0, ROWS, middle, 0)

        def slopes(q, carry):
            for n in range(4):
                dgs[4 * q + n] = twice_swish_grad(coming_pre[4 * q + n + 2])
            return carry

        lax.fori_loop(0, ROWS // 4, slopes, 0)
        for copy in edge_copies(t):
            copy.wait()
        for n in range(2):
            ex[n] = above[t, n].astype(F32) * has_top
            ex[ROWS + 2 + n] = below[t, n].astype(F32) * has_bottom

        def conv(q, carry):
            both = []
            for h in range(2):
                rows = slice(8 * h, 8 * h + 8)
                values = conv_rows(ex, q, h, wide_taps)
                both.append([value * dgs[4 * q + n, :, rows, :] for n, value in enumerate(values)])
            for n in range(4):
                value = jnp.concatenate([both[0][n], both[1][n]], axis=1)
                span = pl.ds(pl.multiple_of((4 * q + n) * PIX, PIX), PIX)
                dpre[span, lane_of(t)] = value.reshape(PIX, 128).astype(BF16)
            pre_rows(next_tile(t), 4 * q + 2, 4)
            return carry

        lax.fori_loop(0, ROWS // 4, conv, 0)

        @pl.when(t == TILES // 2)
        def _():
            total = dp_sum(to_dp(epiece, egot, esend, erecv), epiece, egot)
            espace[me_s] = total.astype(BF16)
            for copy in to_space(espace, fsend, frecv):
                copy.start()

        return carry

    def begin_third(q, carry):
        pre_rows(0, 6 * q + 2, 6)
        return carry

    lax.fori_loop(0, 2, begin_third, 0)
    lax.fori_loop(0, TILES, third, 0)

    all_channels_grad(dpre, fpt, flat)
    pieces_of(flat, C, lpiece)
    for copy in to_dp(lpiece, lgot, lsend, lrecv):
        copy.start()

    def tap_grads(t, carry):
        acc[...] = jnp.zeros_like(acc)

        def window(q, carry):
            for h in range(2):
                rows = slice(8 * h, 8 * h + 8)
                points = to_points([saved[t, 4 * q + n].astype(F32)[:, rows, :] for n in range(8)])
                for p in range(8):
                    held[p] = with_edges(points[p])
                mine = outputs_to_points([depth[t, 4 * q + n, :, rows, :] for n in range(4)])
                for p in range(8):
                    source = held[p]
                    for j in range(5):
                        k = 5 * p + j
                        acc[k] = acc[k] + jnp.sum(mine[p] * source[j : j + BLOCK], axis=0)
            return carry

        lax.fori_loop(0, ROWS // 4, window, 0)
        for j in range(5):
            sums_at = [jnp.sum(acc[5 * p + j], axis=0, keepdims=True) for p in range(8)]
            for i, value in enumerate(taps_from_points(sums_at)):
                flat_taps[5 * i + j : 5 * i + j + 1, lane_of(t)] = value

        @pl.when(t == TILES // 2)
        def _():
            total = dp_sum(to_dp(lpiece, lgot, lsend, lrecv), lpiece, lgot)
            lspace[me_s] = total.astype(BF16)
            for copy in to_space(lspace, gsend, grecv):
                copy.start()

        return carry

    lax.fori_loop(0, TILES, tap_grads, 0)
    pieces_of(flat_taps, 32, tpiece)
    copies = to_dp(tpiece, tgot, tsend, trecv)
    for copy in copies:
        copy.start()

    all_channels_out(dpre, we, cp, 0, out_grad)
    leave = pltpu.make_async_copy(out_grad, out_grad_to, insem.at[0])
    leave.start()
    tspace[me_s] = dp_sum(copies, tpiece, tgot).astype(BF16)
    copies = to_space(tspace, usend, urecv)
    for copy in copies:
        copy.start()
    all_channels_out(gated, wp, fp, 2, out)
    leave_too = pltpu.make_async_copy(out, out_to, insem.at[1])
    leave_too.start()
    for copy in small:
        copy.wait()
    mail_out[...] = mail[...]
    early[0:C] = space_sum(to_space(espace, fsend, frecv), espace)
    late[...] = space_sum(to_space(lspace, gsend, grecv), lspace)
    early[C:] = space_sum(copies, tspace)
    leave.wait()
    leave_too.wait()


def block(*args):
    def bf16(*shape):
        return pltpu.VMEM(shape, BF16)

    def f32(*shape):
        return pltpu.VMEM(shape, F32)

    def sems(*shape):
        return pltpu.SemaphoreType.DMA(shape)

    return pl.pallas_call(
        block_kernel,
        out_shape=(
            jax.ShapeDtypeStruct((IMGS, ROWS, C, COLS), BF16),
            jax.ShapeDtypeStruct((IMGS, ROWS, C, COLS), BF16),
            jax.ShapeDtypeStruct((EARLY, 128), F32),
            jax.ShapeDtypeStruct((C, 128), F32),
            jax.ShapeDtypeStruct((ND, 8, 128), F32),
        ),
        in_specs=[VMEM] * 7 + [ANY] * 2,
        out_specs=(ANY, ANY, VMEM, VMEM, VMEM),
        scratch_shapes=[
            bf16(IMGS, ROWS, C, COLS),
            bf16(IMGS, ROWS, C, COLS),
            bf16(IMGS, ROWS, C, COLS),
            bf16(IMGS, ROWS, C, COLS),
            f32(2, 80, 256),
            bf16(2, 80, 256),
            bf16(2, ND, 80, 256),
            bf16(IMGS, 2, C, COLS),
            bf16(IMGS, 2, C, COLS),
            f32(CP, C),
            bf16(HROWS, PIX, C),
            bf16(ROWS, PIX, C),
            bf16(C, ROWS * PIX),
            bf16(C, ROWS * PIX),
            bf16(CP, C),
            bf16(CP, C),
            f32(136, CP),
            f32(40, 8, 128),
            f32(HROWS, BLOCK, SUB, 128),
            f32(ROWS, BLOCK, SUB, 128),
            f32(HROWS, BLOCK, SUB, 128),
            f32(ROWS, BLOCK, SUB, 128),
            bf16(TILES, HROWS, BLOCK, SUB, 128),
            f32(TILES, ROWS, BLOCK, SUB, 128),
            f32(TILES, 8, 128),
            f32(5, 8, 128),
            f32(NS, 5, 8, 128),
            f32(8, CP + 128),
            f32(8, 128),
            f32(8, CP),
            f32(ND, 8, 128),
            f32(ND, 8, 128),
            bf16(TILES, 2, 2, BLOCK, SUB, 128),
            bf16(TILES, 2, BLOCK, SUB, 128),
            bf16(TILES, 2, BLOCK, SUB, 128),
            bf16(ROWS * PIX, CP),
            bf16(ROWS * PIX, CP),
            f32(40, 8, 128),
            f32(8, WIDE, 8, 128),
            f32(C, CP + 128),
            f32(32, CP + 128),
            bf16(ND, C, 128),
            bf16(ND, C, 128),
            bf16(NS, C, 128),
            bf16(ND, C, 128),
            bf16(ND, C, 128),
            bf16(NS, C, 128),
            bf16(ND, 32, 128),
            bf16(ND, 32, 128),
            bf16(NS, 32, 128),
            sems(ND),
            sems(ND),
            sems(2),
            sems(2),
            sems(ND),
            sems(ND),
            sems(NS),
            sems(NS),
            sems(ND),
            sems(ND),
            sems(2, TILES),
            sems(2, TILES),
            sems(ND),
            sems(ND),
            sems(NS),
            sems(NS),
            sems(ND),
            sems(ND),
            sems(NS),
            sems(NS),
            sems(ND),
            sems(ND),
            sems(NS),
            sems(NS),
            sems(2),
        ],
        compiler_params=pltpu.CompilerParams(
            collective_id=0, has_side_effects=True, vmem_limit_bytes=63 * 2**20
        ),
        name="block",
    )(*args)


def finish_kernel(
    early, late, mail, raw, raw_grad,
    gexp, gdepth, greduce, gexcite, gbex, gproj, gbred, out, out_grad,
):
    out[...] = raw[...]
    out_grad[...] = raw_grad[...]

    @pl.when(pl.program_id(0) == 0)
    def _():
        gexp[...] = late[...].T[0:PART]
        gproj[...] = early[0:C].T[0:PART]
        for i in range(5):
            gdepth[i] = early[C + 5 * i : C + 5 * i + 5, 0:PART]
        rows = [mail[d] for d in range(ND)]
        pool_all = jnp.concatenate([row[0:2] for row in rows], axis=0)
        dlog_all = jnp.concatenate([row[2:4] for row in rows], axis=0)
        sq_all = jnp.concatenate([row[4:6] for row in rows], axis=0)
        dsq_all = jnp.concatenate([row[6:8] for row in rows], axis=0)
        greduce[...] = dot_tn(dsq_all, pool_all, HIGH)[0:SE, 0:PART]
        gexcite[...] = dot_tn(sq_all, dlog_all, HIGH)[0:SE, 0:PART]
        gbex[...] = jnp.sum(dlog_all, axis=0, keepdims=True)[:, 0:PART]
        gbred[...] = jnp.sum(dsq_all, axis=0, keepdims=True)[:, 0:SE]


def finish(early, late, mail, raw, raw_grad):
    def whole(*shape):
        zeros = (0,) * len(shape)
        return pl.BlockSpec(shape, lambda n: zeros)

    part = pl.BlockSpec((IMGS, 6, C, COLS), lambda n: (0, n, 0, 0))
    shapes = ((PART, C), (5, 5, PART), (SE, PART), (SE, PART), (1, PART), (PART, C), (1, SE))
    return pl.pallas_call(
        finish_kernel,
        grid=(ROWS // 6,),
        out_shape=tuple(jax.ShapeDtypeStruct(shape, F32) for shape in shapes)
        + (jax.ShapeDtypeStruct((IMGS, ROWS, C, COLS), BF16),) * 2,
        in_specs=[whole(EARLY, 128), whole(C, 128), whole(ND, 8, 128), part, part],
        out_specs=tuple(whole(*shape) for shape in shapes) + (part, part),
        name="finish",
    )(early, late, mail, raw, raw_grad)


def on_device(
    features, w_expand, w_depth, w_reduce, b_reduce, w_excite, b_excite, w_project, cotangent
):
    raw, raw_grad, early, late, mail = block(
        w_expand.T,
        w_project,
        w_depth,
        w_reduce.T,
        w_excite,
        b_excite[None, :],
        b_reduce[None, :],
        features.swapaxes(2, 3),
        cotangent.swapaxes(2, 3),
    )
    (
        s_expand, s_depth, s_reduce, s_excite, s_bexcite, s_project, s_breduce, output, grad,
    ) = finish(early, late, mail, raw, raw_grad)
    return (
        output.swapaxes(2, 3),
        grad.swapaxes(2, 3),
        s_expand.T,
        s_depth,
        s_reduce.T,
        s_excite,
        s_bexcite[0],
        s_project,
        s_breduce[0],
    )


def solution(mesh):
    return jax.shard_map(
        on_device,
        mesh=mesh,
        in_specs=(
            P("dp", "space", None, None),
            P(None, "dp"),
            P(None, None, "dp"),
            P("dp", None),
            P(),
            P(None, "dp"),
            P("dp"),
            P("dp", None),
            P("dp", "space", None, None),
        ),
        out_specs=(
            P("dp", "space", None, None),
            P("dp", "space", None, None),
            P(None, "dp"),
            P(None, None, "dp"),
            P("dp", None),
            P(None, "dp"),
            P("dp"),
            P("dp", None),
            P(),
        ),
        check_vma=False,
    )
```

```python
import functools

import jax
import jax.numpy as jnp
from jax import lax
from jax.experimental import pallas as pl
from jax.experimental.pallas import tpu as pltpu
from jax.sharding import PartitionSpec as P

F32 = jnp.float32
BF16 = jnp.bfloat16
MESH = pl.DeviceIdType.MESH
HIGH = lax.Precision.HIGHEST

IMGS, ROWS, COLS, C, SE = 2, 12, 100, 176, 44
BLOCK, SUB = 13, 16
PIX = BLOCK * SUB
WIDE = BLOCK + 4
HROWS = ROWS + 4
PART, SLOT = 66, 72
CP = 16 * SLOT
TILES = CP // 128
AREA = 9600.0
NS, ND = 8, 16

VMEM = pl.BlockSpec(memory_space=pltpu.VMEM)
ANY = pl.BlockSpec(memory_space=pl.ANY)


def sigmoid(value):
    return 0.5 * jnp.tanh(0.5 * value) + 0.5


def swish(value):
    half = 0.5 * value
    return half + half * jnp.tanh(half)


def swish_grad(value):
    sig = sigmoid(value)
    act = value * sig
    return sig + act - act * sig


def twice_swish_grad(value):
    half = 0.5 * value
    twice = 1.0 + jnp.tanh(half)
    return twice * ((value - half * twice) + 1.0)


def dot_nt(left, right, precision=None):
    return lax.dot_general(
        left, right, (((1,), (1,)), ((), ())), precision=precision, preferred_element_type=F32
    )


def dot_tn(left, right, precision=None):
    return lax.dot_general(
        left, right, (((0,), (0,)), ((), ())), precision=precision, preferred_element_type=F32
    )


def dot_nn(left, right, precision=None):
    return lax.dot_general(
        left, right, (((1,), (0,)), ((), ())), precision=precision, preferred_element_type=F32
    )


def one_hot(img, transposed):
    shape = (COLS, PIX) if transposed else (PIX, COLS)
    place = lax.broadcasted_iota(jnp.int32, shape, 1 if transposed else 0)
    col = lax.broadcasted_iota(jnp.int32, shape, 0 if transposed else 1)
    wanted = (col % BLOCK) * SUB + img * 8 + col // BLOCK
    return jnp.where(place == wanted, 1.0, 0.0).astype(BF16)


def point_taps(taps):
    w0, w1, w2, w3, w4 = taps
    even, odd = w0 + w2 + w4, w1 + w3
    even2, odd2 = w0 + 4.0 * w2 + 16.0 * w4, 2.0 * w1 + 8.0 * w3
    even3, odd3 = w0 + 0.25 * w2 + 0.0625 * w4, 0.5 * w1 + 0.125 * w3
    return [
        w0,
        (even + odd) * (-2.0 / 9.0),
        (even - odd) * (-2.0 / 9.0),
        (even2 + odd2) * (1.0 / 360.0),
        (even2 - odd2) * (1.0 / 360.0),
        (even3 + odd3) * (32.0 / 45.0),
        (even3 - odd3) * (32.0 / 45.0),
        w4,
    ]


def taps_from_points(g):
    s1, d1 = (g[1] + g[2]) * (-2.0 / 9.0), (g[1] - g[2]) * (-2.0 / 9.0)
    s2, d2 = (g[3] + g[4]) * (1.0 / 360.0), (g[3] - g[4]) * (1.0 / 360.0)
    s3, d3 = (g[5] + g[6]) * (32.0 / 45.0), (g[5] - g[6]) * (32.0 / 45.0)
    return [
        g[0] + s1 + s2 + s3,
        d1 + 2.0 * d2 + 0.5 * d3,
        s1 + 4.0 * s2 + 0.25 * s3,
        d1 + 8.0 * d2 + 0.125 * d3,
        s1 + 16.0 * s2 + 0.0625 * s3 + g[7],
    ]


def to_points(x):
    x0, x1, x2, x3, x4, x5, x6, x7 = x
    f3, f4 = 5.0 * x3, 5.0 * x4
    e1, o1 = (x6 + x2) - 4.25 * x4, (x5 + x1) - 4.25 * x3
    e2, o2 = (x2 - f4) + 4.0 * x6, (x1 - f3) + 4.0 * x5
    e3, o3 = (4.0 * x2 - f4) + x6, (4.0 * x1 - f3) + x5
    o2, o3 = o2 + o2, 0.5 * o3
    return [
        (x0 - x6) + 5.25 * (x4 - x2),
        e1 + o1,
        e1 - o1,
        e2 + o2,
        e2 - o2,
        e3 + o3,
        e3 - o3,
        (x7 - x1) + 5.25 * (x3 - x5),
    ]


def from_points(m):
    s1, d1 = m[1] + m[2], m[1] - m[2]
    s2, d2 = m[3] + m[4], m[3] - m[4]
    s3, d3 = m[5] + m[6], m[5] - m[6]
    return [
        (m[0] + s1) + (s2 + s3),
        (d1 + 2.0 * d2) + 0.5 * d3,
        (s1 + 4.0 * s2) + 0.25 * s3,
        ((d1 + 8.0 * d2) + 0.125 * d3) + m[7],
    ]


def outputs_to_points(y):
    y0, y1, y2, y3 = y
    a, b = y0 + y2, y1 + y3
    c, d = y0 + 4.0 * y2, 2.0 * y1 + 8.0 * y3
    e, f = y0 + 0.25 * y2, 0.5 * y1 + 0.125 * y3
    return [y0, a + b, a - b, c + d, c - d, e + f, e - f, y3]


def dot_split(left, right, dims):
    high = left.astype(BF16)
    rest = left - high.astype(F32)
    middle = rest.astype(BF16)
    low = (rest - middle.astype(F32)).astype(BF16)
    parts = jnp.concatenate([high.astype(F32), middle.astype(F32), low.astype(F32)], axis=0)
    product = lax.dot_general(
        parts.astype(BF16), right.astype(BF16), (dims, ((), ())), preferred_element_type=F32
    )
    count = left.shape[0]
    return (product[2 * count :] + product[count : 2 * count]) + product[:count]


def spread_taps(taps, wide_taps, flip):
    for j in range(5):
        column = [taps[5 * i + j : 5 * i + j + 1, :] for i in range(5)]
        if flip:
            column = [0.5 * value for value in column[::-1]]
        place = 4 - j if flip else j
        for p, value in enumerate(point_taps(column)):
            wide_taps[5 * p + place] = jnp.broadcast_to(value, (8, 128))


def with_edges(value):
    block = lax.broadcasted_iota(jnp.int32, (2, 8, 128), 1)
    left = jnp.where(block > 0, pltpu.roll(value[BLOCK - 2 :], 1, 1), 0.0)
    right = jnp.where(block < 7, pltpu.roll(value[:2], 7, 1), 0.0)
    return jnp.concatenate([left, value, right], axis=0)


def conv_rows(ref, q, h, wide_taps):
    points = to_points([ref[4 * q + n, :, 8 * h : 8 * h + 8, :] for n in range(8)])
    totals = []
    for p in range(8):
        source = with_edges(points[p])
        total = source[0:BLOCK] * wide_taps[5 * p][None]
        for j in range(1, 5):
            total = total + source[j : j + BLOCK] * wide_taps[5 * p + j][None]
        totals.append(total)
    return from_points(totals)


def pad_mask():
    block = lax.broadcasted_iota(jnp.int32, (4, 8, 128), 1)
    return jnp.where(block < 7, 1.0, 0.0)


def gate_row(depth, dgated, gates, h, keep):
    gate = gates[h : h + 1, :][None]
    half_gate = gates[2 + h : 3 + h, :][None]
    half_pull = gates[4 + h : 5 + h, :][None]
    half = 0.5 * depth
    twice = 1.0 + jnp.tanh(half)
    act = half * twice
    gated = act * gate
    ddepth = (dgated * half_gate + half_pull) * (twice * ((depth - act) + 1.0))
    ddepth = jnp.concatenate([ddepth[:9], ddepth[9:] * keep], axis=0)
    return gated, ddepth


def unpermute(value, out, r):
    for img in range(2):
        out[img, r] = dot_tn(value, one_hot(img, False)).astype(BF16)


def all_channels_out(rows_in, weights, base, shift, out):
    def chunk(q, carry):
        block = rows_in[pl.ds(pl.multiple_of(4 * PIX * q, 4 * PIX), 4 * PIX), :]
        product = dot_nn(block, weights[...]).reshape(4, PIX, C)
        for n in range(4):
            value = product[n] + base[4 * q + n + shift].astype(F32)
            unpermute(value.astype(BF16), out, 4 * q + n)
        return carry

    lax.fori_loop(0, 3, chunk, 0)


def all_channels_grad(rows_in, turned, grad):
    def lanes(q, carry):
        span = pl.ds(pl.multiple_of(384 * q, 128), 384)
        grad[:, span] = dot_nn(turned[...], rows_in[:, span])
        return carry

    lax.fori_loop(0, 3, lanes, 0)


OFFSETS = sorted(
    ((x, y) for x in range(4) for y in range(4) if x or y),
    key=lambda at: -(min(at[0], 4 - at[0]) + min(at[1], 4 - at[1])),
)


def dp_peer(k, sign):
    me_d = lax.axis_index("dp")
    x, y = OFFSETS[k - 1]
    column = lax.rem(lax.div(me_d, 4) + (x if sign > 0 else 4 - x), 4)
    return 4 * column + lax.rem(lax.rem(me_d, 4) + (y if sign > 0 else 4 - y), 4)


def to_dp(src, dst, send, recv, by_sender=False):
    me_s, me_d = lax.axis_index("space"), lax.axis_index("dp")
    copies = []
    for k in range(1, ND):
        target = dp_peer(k, 1)
        copies.append(
            pltpu.make_async_remote_copy(
                src_ref=src.at[target],
                dst_ref=dst.at[me_d] if by_sender else dst.at[k],
                send_sem=send.at[k],
                recv_sem=recv.at[k],
                device_id=(me_s, target),
                device_id_type=MESH,
            )
        )
    return copies


def to_space(ref, send, recv):
    me_s, me_d = lax.axis_index("space"), lax.axis_index("dp")
    copies = []
    for k in range(1, NS):
        copies.append(
            pltpu.make_async_remote_copy(
                src_ref=ref.at[me_s],
                dst_ref=ref.at[me_s],
                send_sem=send.at[k],
                recv_sem=recv.at[k],
                device_id=(lax.rem(me_s + k, NS), me_d),
                device_id_type=MESH,
            )
        )
    return copies


def to_neighbours(down_src, down_dst, up_src, up_dst, send, recv):
    me_s, me_d = lax.axis_index("space"), lax.axis_index("dp")
    down = pltpu.make_async_remote_copy(
        src_ref=down_src,
        dst_ref=down_dst,
        send_sem=send[0],
        recv_sem=recv[0],
        device_id=(lax.rem(me_s + 1, NS), me_d),
        device_id_type=MESH,
    )
    up = pltpu.make_async_remote_copy(
        src_ref=up_src,
        dst_ref=up_dst,
        send_sem=send[1],
        recv_sem=recv[1],
        device_id=(lax.rem(me_s + NS - 1, NS), me_d),
        device_id_type=MESH,
    )
    return down, up


def dp_sum(copies, piece, got):
    total = piece[lax.axis_index("dp")].astype(F32)
    for k, copy in enumerate(copies):
        copy.wait()
        total = total + got[k + 1].astype(F32)
    return total


def space_sum(copies, ref):
    for copy in copies:
        copy.wait()
    total = ref[0].astype(F32)
    for s in range(1, NS):
        total = total + ref[s].astype(F32)
    return total


EARLY = C + 32


def block_kernel(
    wet, wpr, taps, wrt, wx_own, bex, bred, feats_in, cot_in,
    out_to, out_grad_to, early, late, mail_out,
    out, out_grad, feats, cot, stage, pack, full, top, bottom, flatw, fp, cp, fpt, cpt, we, wp, misc,
    wide_taps, ex, dgs, coming_pre, coming_dg, saved, depth, sums, packed, landed, lanes, vecs, gates, msgs, mail,
    edge, above, below, gated, dpre, acc, held, flat, flat_taps,
    epiece, egot, espace, lpiece, lgot, lspace, tpiece, tgot, tspace,
    wsend, wrecv, hsend, hrecv, csend, crecv, ssend, srecv, msend, mrecv,
    dsend, drecv, esend, erecv, fsend, frecv, lsend, lrecv, gsend, grecv,
    tsend, trecv, usend, urecv, insem,
):
    me_s, me_d = lax.axis_index("space"), lax.axis_index("dp")
    core = lax.rem(me_s, 2)
    barrier = pltpu.get_barrier_semaphore()
    for k in range(1, ND):
        pl.semaphore_signal(
            barrier, inc=1, device_id=(me_s, dp_peer(k, 1)), device_id_type=MESH
        )
    for k in range(1, NS):
        pl.semaphore_signal(
            barrier, inc=1, device_id=(lax.rem(me_s + k, NS), me_d), device_id_type=MESH
        )

    arrive = [
        pltpu.make_async_copy(feats_in, feats, insem.at[0]),
        pltpu.make_async_copy(cot_in, cot, insem.at[1]),
    ]
    for copy in arrive:
        copy.start()

    stage[...] = jnp.zeros_like(stage)
    stage[0, 0:PART, 0:C] = wet[...].astype(F32)
    stage[1, 0:PART, 0:C] = wpr[...].astype(F32)
    side = slice(C, C + PART)
    for i in range(5):
        stage[0, 5 * i : 5 * i + 5, side] = taps[i].astype(F32)
    stage[0, 32 : 32 + SE, side] = wrt[...].astype(F32)
    stage[1, 0:SE, side] = wx_own[...].astype(F32)
    stage[1, 48:49, side] = bex[...].astype(F32)
    pack[...] = stage[...].astype(BF16)
    pl.semaphore_wait(barrier, NS + ND - 2)
    copies = []
    for k in range(1, ND):
        copy = pltpu.make_async_remote_copy(
            src_ref=pack.at[core],
            dst_ref=full.at[core, me_d],
            send_sem=wsend.at[k],
            recv_sem=wrecv.at[k],
            device_id=(me_s, dp_peer(k, 1)),
            device_id_type=MESH,
        )
        copy.start()
        copies.append(copy)
    for copy in arrive:
        copy.wait()
    halo = to_neighbours(
        feats.at[:, pl.ds(ROWS - 2, 2)],
        top,
        feats.at[:, pl.ds(0, 2)],
        bottom,
        (hsend.at[0], hsend.at[1]),
        (hrecv.at[0], hrecv.at[1]),
    )
    for copy in halo:
        copy.start()
    full[0, me_d] = pack[0]
    full[1, me_d] = pack[1]
    spread = (one_hot(0, False), one_hot(1, False))
    gather_t = (one_hot(0, True), one_hot(1, True))

    def permute(r, carry):
        for src, dst, shift in ((feats, fp, 2), (cot, cp, 0)):
            a, b = src[0, r], src[1, r]
            dst[r + shift] = (dot_nt(spread[0], a) + dot_nt(spread[1], b)).astype(BF16)
        return carry

    lax.fori_loop(0, ROWS, permute, 0)
    for r in range(ROWS):
        for src, dst in ((feats, fpt), (cot, cpt)):
            value = dot_nn(src[0, r], gather_t[0]) + dot_nn(src[1, r], gather_t[1])
            dst[:, PIX * r : PIX * (r + 1)] = value.astype(BF16)
    shares = []
    for k, copy in enumerate(copies, 1):
        copy.wait_recv()
        sender = dp_peer(k, -1)
        share = pltpu.make_async_remote_copy(
            src_ref=full.at[core, sender],
            dst_ref=full.at[core, sender],
            send_sem=csend.at[k],
            recv_sem=crecv.at[k],
            device_id=(me_s + 1 - 2 * core, me_d),
            device_id_type=MESH,
        )
        share.start()
        shares.append(share)
    for copy in halo:
        copy.wait()
    has_top = jnp.where(me_s > 0, 1.0, 0.0)
    has_bottom = jnp.where(me_s < NS - 1, 1.0, 0.0)
    for r in range(2):
        value = dot_nt(spread[0], top[0, r]) + dot_nt(spread[1], top[1, r])
        fp[r] = (value * has_top).astype(BF16)
        value = dot_nt(spread[0], bottom[0, r]) + dot_nt(spread[1], bottom[1, r])
        fp[ROWS + 2 + r] = (value * has_bottom).astype(BF16)
    for copy in copies:
        copy.wait_send()
    for share in shares:
        share.wait()
    for half, whole in ((0, we), (1, wp)):
        for d in range(ND):
            part = full[half, d].astype(F32)
            flatw[d * SLOT : (d + 1) * SLOT, :] = part[0:SLOT, 0:C]
            span = slice(d * SLOT, (d + 1) * SLOT)
            if half == 0:
                misc[0:80, span] = part[:, C : C + SLOT]
            else:
                misc[80:136, span] = part[0:56, C : C + SLOT]
        whole[...] = flatw[...].astype(BF16)

    keep = pad_mask()

    def lane_of(t):
        return pl.ds(pl.multiple_of(128 * t, 128), 128)

    def pre_rows(t, start, count):
        product = dot_nt(fp[pl.ds(start, count)].reshape(count * PIX, C), we[lane_of(t), :])
        coming_pre[pl.ds(start, count)] = product.reshape(count, BLOCK, SUB, 128)

    def cot_rows(t, start, count):
        product = dot_nt(cp[pl.ds(start, count)].reshape(count * PIX, C), wp[lane_of(t), :])
        coming_dg[pl.ds(start, count)] = product.reshape(count, BLOCK, SUB, 128)

    def next_tile(t):
        return jnp.minimum(t + 1, TILES - 1)

    def take_dg():
        def row(r, carry):
            dgs[r] = coming_dg[r]
            return carry

        lax.fori_loop(0, ROWS, row, 0)

    def first(t, carry):
        spread_taps(misc[0:32, lane_of(t)], wide_taps, False)

        def expand(q, carry):
            for n in range(4):
                ex[4 * q + n] = swish(coming_pre[4 * q + n])
            return carry

        lax.fori_loop(0, HROWS // 4, expand, 0)
        take_dg()

        def conv(q, carry):
            pools, grads = list(carry[:2]), list(carry[2:])
            for h in range(2):
                rows = slice(8 * h, 8 * h + 8)
                for n, total in enumerate(conv_rows(ex, q, h, wide_taps)):
                    depth[t, 4 * q + n, :, rows, :] = total
                    act = swish(total)
                    grads[h] = grads[h] + jnp.sum(act * dgs[4 * q + n, :, rows, :], axis=0)
                    pools[h] = pools[h] + jnp.sum(act[:9], axis=0)
                    pools[h] = pools[h] + jnp.sum(act[9:] * keep, axis=0)
            for n in range(4):
                saved[t, 4 * q + n] = ex[4 * q + n].astype(BF16)
            pre_rows(next_tile(t), jnp.minimum(6 * q, HROWS - 6), 6)
            cot_rows(next_tile(t), 4 * q, 4)
            return (*pools, *grads)

        zero = jnp.zeros((8, 128), F32)
        parts = lax.fori_loop(0, ROWS // 4, conv, (zero,) * 4)
        for r in range(ROWS, HROWS):
            saved[t, r] = ex[r].astype(BF16)
        for k in range(4):
            sums[t, k : k + 1, :] = jnp.sum(parts[k], axis=0, keepdims=True)
        return carry

    def begin(q, carry):
        pre_rows(0, 8 * q, 8)
        cot_rows(0, 6 * q, 6)
        return carry

    lax.fori_loop(0, 2, begin, 0)
    lax.fori_loop(0, TILES, first, 0)

    packed[...] = jnp.zeros_like(packed)
    for t in range(TILES):
        packed[t // 2, 4 * (t % 2) : 4 * (t % 2) + 4, :] = sums[t, 0:4, :]
    landed[me_s] = packed[...]
    copies = to_space(landed, ssend, srecv)
    for copy in copies:
        copy.start()

    def begin_again(q, carry):
        cot_rows(0, 6 * q, 6)
        return carry

    lax.fori_loop(0, 2, begin_again, 0)
    total = space_sum(copies, landed)
    for t in range(TILES):
        lanes[0:4, 128 * t : 128 * (t + 1)] = total[t // 2, 4 * (t % 2) : 4 * (t % 2) + 4]
    lanes[:, CP:] = jnp.zeros((8, 128), F32)
    wr = misc[32 : 32 + SE, :]
    wx = misc[80 : 80 + SE, :]
    pooled = lanes[0:2, 0:CP] / AREA
    dgate = lanes[2:4, 0:CP]
    squeeze_pre = dot_split(pooled, wr, ((1,), (1,))) + bred[...].astype(F32)
    squeeze = swish(squeeze_pre)
    gate = sigmoid(dot_split(squeeze, wx, ((1,), (0,))) + misc[128:129, :])
    dlogit = dgate * gate * (1.0 - gate)
    dsq = dot_split(dlogit, wx, ((1,), (1,))) * swish_grad(squeeze_pre)
    dpooled = dot_split(dsq, wr, ((1,), (0,)))
    gates[0:2, :] = gate
    gates[2:4, :] = 0.5 * gate
    gates[4:6, :] = dpooled * (0.5 / AREA)
    gates[6:8, :] = jnp.zeros((2, CP), F32)
    lanes[0:2, 0:CP] = pooled
    lanes[2:4, 0:CP] = dlogit
    vecs[...] = jnp.zeros((8, 128), F32)
    vecs[4:6, 0:SE] = squeeze
    vecs[6:8, 0:SE] = dsq
    for d in range(ND):
        msgs[d, 0:4, :] = lanes[0:4, SLOT * d : SLOT * d + 128]
        msgs[d, 4:8, :] = vecs[4:8, :]
    mail[me_d] = msgs[me_d]
    small = to_dp(msgs, mail, msend, mrecv, True)
    for copy in small:
        copy.start()

    def edge_copies(t):
        return to_neighbours(
            edge.at[t, 1],
            above.at[t],
            edge.at[t, 0],
            below.at[t],
            (dsend.at[0, t], dsend.at[1, t]),
            (drecv.at[0, t], drecv.at[1, t]),
        )

    def second(t, carry):
        take_dg()

        def pointwise(q, carry):
            for n in range(4):
                r = 4 * q + n
                both = []
                for h in range(2):
                    rows = slice(8 * h, 8 * h + 8)
                    value, ddepth = gate_row(
                        depth[t, r, :, rows, :],
                        dgs[r, :, rows, :],
                        gates.at[:, lane_of(t)],
                        h,
                        keep,
                    )
                    depth[t, r, :, rows, :] = ddepth.astype(BF16).astype(F32)
                    both.append(value)
                gated[pl.ds(pl.multiple_of(r * PIX, PIX), PIX), lane_of(t)] = (
                    jnp.concatenate(both, axis=1).reshape(PIX, 128).astype(BF16)
                )
            cot_rows(next_tile(t), 4 * q, 4)
            return carry

        lax.fori_loop(0, ROWS // 4, pointwise, 0)
        for n in range(2):
            edge[t, 0, n] = depth[t, n].astype(BF16)
            edge[t, 1, n] = depth[t, ROWS - 2 + n].astype(BF16)
        for copy in edge_copies(t):
            copy.start()
        return carry

    lax.fori_loop(0, TILES, second, 0)

    def pieces_of(source, rows, piece):
        for d in range(ND):
            piece[d] = source[0:rows, SLOT * d : SLOT * d + 128].astype(BF16)

    flat[:, CP:] = jnp.zeros((C, 128), F32)
    flat_taps[...] = jnp.zeros_like(flat_taps)
    all_channels_grad(gated, cpt, flat)
    pieces_of(flat, C, epiece)
    for copy in to_dp(epiece, egot, esend, erecv):
        copy.start()

    def third(t, carry):
        spread_taps(misc[0:32, lane_of(t)], wide_taps, True)

        def middle(r, carry):
            ex[r + 2] = depth[t, r]
            return carry

        lax.fori_loop(0, ROWS, middle, 0)

        def slopes(q, carry):
            for n in range(4):
                dgs[4 * q + n] = twice_swish_grad(coming_pre[4 * q + n + 2])
            return carry

        lax.fori_loop(0, ROWS // 4, slopes, 0)
        for copy in edge_copies(t):
            copy.wait()
        for n in range(2):
            ex[n] = above[t, n].astype(F32) * has_top
            ex[ROWS + 2 + n] = below[t, n].astype(F32) * has_bottom

        def conv(q, carry):
            both = []
            for h in range(2):
                rows = slice(8 * h, 8 * h + 8)
                values = conv_rows(ex, q, h, wide_taps)
                both.append([value * dgs[4 * q + n, :, rows, :] for n, value in enumerate(values)])
            for n in range(4):
                value = jnp.concatenate([both[0][n], both[1][n]], axis=1)
                span = pl.ds(pl.multiple_of((4 * q + n) * PIX, PIX), PIX)
                dpre[span, lane_of(t)] = value.reshape(PIX, 128).astype(BF16)
            pre_rows(next_tile(t), 4 * q + 2, 4)
            return carry

        lax.fori_loop(0, ROWS // 4, conv, 0)

        @pl.when(t == TILES // 2)
        def _():
            total = dp_sum(to_dp(epiece, egot, esend, erecv), epiece, egot)
            espace[me_s] = total.astype(BF16)
            for copy in to_space(espace, fsend, frecv):
                copy.start()

        return carry

    def begin_third(q, carry):
        pre_rows(0, 6 * q + 2, 6)
        return carry

    lax.fori_loop(0, 2, begin_third, 0)
    lax.fori_loop(0, TILES, third, 0)

    all_channels_grad(dpre, fpt, flat)
    pieces_of(flat, C, lpiece)
    for copy in to_dp(lpiece, lgot, lsend, lrecv):
        copy.start()

    def tap_grads(t, carry):
        acc[...] = jnp.zeros_like(acc)

        def window(q, carry):
            for h in range(2):
                rows = slice(8 * h, 8 * h + 8)
                points = to_points([saved[t, 4 * q + n].astype(F32)[:, rows, :] for n in range(8)])
                for p in range(8):
                    held[p] = with_edges(points[p])
                mine = outputs_to_points([depth[t, 4 * q + n, :, rows, :] for n in range(4)])
                for p in range(8):
                    source = held[p]
                    for j in range(5):
                        k = 5 * p + j
                        acc[k] = acc[k] + jnp.sum(mine[p] * source[j : j + BLOCK], axis=0)
            return carry

        lax.fori_loop(0, ROWS // 4, window, 0)
        for j in range(5):
            sums_at = [jnp.sum(acc[5 * p + j], axis=0, keepdims=True) for p in range(8)]
            for i, value in enumerate(taps_from_points(sums_at)):
                flat_taps[5 * i + j : 5 * i + j + 1, lane_of(t)] = value

        @pl.when(t == TILES // 2)
        def _():
            total = dp_sum(to_dp(lpiece, lgot, lsend, lrecv), lpiece, lgot)
            lspace[me_s] = total.astype(BF16)
            for copy in to_space(lspace, gsend, grecv):
                copy.start()

        return carry

    lax.fori_loop(0, TILES, tap_grads, 0)
    pieces_of(flat_taps, 32, tpiece)
    copies = to_dp(tpiece, tgot, tsend, trecv)
    for copy in copies:
        copy.start()

    all_channels_out(dpre, we, cp, 0, out_grad)
    leave = pltpu.make_async_copy(out_grad, out_grad_to, insem.at[0])
    leave.start()
    tspace[me_s] = dp_sum(copies, tpiece, tgot).astype(BF16)
    copies = to_space(tspace, usend, urecv)
    for copy in copies:
        copy.start()
    all_channels_out(gated, wp, fp, 2, out)
    leave_too = pltpu.make_async_copy(out, out_to, insem.at[1])
    leave_too.start()
    for copy in small:
        copy.wait()
    mail_out[...] = mail[...]
    early[0:C] = space_sum(to_space(espace, fsend, frecv), espace)
    late[...] = space_sum(to_space(lspace, gsend, grecv), lspace)
    early[C:] = space_sum(copies, tspace)
    leave.wait()
    leave_too.wait()


def block(*args):
    def bf16(*shape):
        return pltpu.VMEM(shape, BF16)

    def f32(*shape):
        return pltpu.VMEM(shape, F32)

    def sems(*shape):
        return pltpu.SemaphoreType.DMA(shape)

    return pl.pallas_call(
        block_kernel,
        out_shape=(
            jax.ShapeDtypeStruct((IMGS, ROWS, C, COLS), BF16),
            jax.ShapeDtypeStruct((IMGS, ROWS, C, COLS), BF16),
            jax.ShapeDtypeStruct((EARLY, 128), F32),
            jax.ShapeDtypeStruct((C, 128), F32),
            jax.ShapeDtypeStruct((ND, 8, 128), F32),
        ),
        in_specs=[VMEM] * 7 + [ANY] * 2,
        out_specs=(ANY, ANY, VMEM, VMEM, VMEM),
        scratch_shapes=[
            bf16(IMGS, ROWS, C, COLS),
            bf16(IMGS, ROWS, C, COLS),
            bf16(IMGS, ROWS, C, COLS),
            bf16(IMGS, ROWS, C, COLS),
            f32(2, 80, 256),
            bf16(2, 80, 256),
            bf16(2, ND, 80, 256),
            bf16(IMGS, 2, C, COLS),
            bf16(IMGS, 2, C, COLS),
            f32(CP, C),
            bf16(HROWS, PIX, C),
            bf16(ROWS, PIX, C),
            bf16(C, ROWS * PIX),
            bf16(C, ROWS * PIX),
            bf16(CP, C),
            bf16(CP, C),
            f32(136, CP),
            f32(40, 8, 128),
            f32(HROWS, BLOCK, SUB, 128),
            f32(ROWS, BLOCK, SUB, 128),
            f32(HROWS, BLOCK, SUB, 128),
            f32(ROWS, BLOCK, SUB, 128),
            bf16(TILES, HROWS, BLOCK, SUB, 128),
            f32(TILES, ROWS, BLOCK, SUB, 128),
            f32(TILES, 8, 128),
            f32(5, 8, 128),
            f32(NS, 5, 8, 128),
            f32(8, CP + 128),
            f32(8, 128),
            f32(8, CP),
            f32(ND, 8, 128),
            f32(ND, 8, 128),
            bf16(TILES, 2, 2, BLOCK, SUB, 128),
            bf16(TILES, 2, BLOCK, SUB, 128),
            bf16(TILES, 2, BLOCK, SUB, 128),
            bf16(ROWS * PIX, CP),
            bf16(ROWS * PIX, CP),
            f32(40, 8, 128),
            f32(8, WIDE, 8, 128),
            f32(C, CP + 128),
            f32(32, CP + 128),
            bf16(ND, C, 128),
            bf16(ND, C, 128),
            bf16(NS, C, 128),
            bf16(ND, C, 128),
            bf16(ND, C, 128),
            bf16(NS, C, 128),
            bf16(ND, 32, 128),
            bf16(ND, 32, 128),
            bf16(NS, 32, 128),
            sems(ND),
            sems(ND),
            sems(2),
            sems(2),
            sems(ND),
            sems(ND),
            sems(NS),
            sems(NS),
            sems(ND),
            sems(ND),
            sems(2, TILES),
            sems(2, TILES),
            sems(ND),
            sems(ND),
            sems(NS),
            sems(NS),
            sems(ND),
            sems(ND),
            sems(NS),
            sems(NS),
            sems(ND),
            sems(ND),
            sems(NS),
            sems(NS),
            sems(2),
        ],
        compiler_params=pltpu.CompilerParams(
            collective_id=0, has_side_effects=True, vmem_limit_bytes=63 * 2**20
        ),
        name="block",
    )(*args)


def finish_kernel(
    early, late, mail, raw, raw_grad,
    gexp, gdepth, greduce, gexcite, gbex, gproj, gbred, out, out_grad,
):
    out[...] = raw[...]
    out_grad[...] = raw_grad[...]

    @pl.when(pl.program_id(0) == 0)
    def _():
        gexp[...] = late[...].T[0:PART]
        gproj[...] = early[0:C].T[0:PART]
        for i in range(5):
            gdepth[i] = early[C + 5 * i : C + 5 * i + 5, 0:PART]
        rows = [mail[d] for d in range(ND)]
        pool_all = jnp.concatenate([row[0:2] for row in rows], axis=0)
        dlog_all = jnp.concatenate([row[2:4] for row in rows], axis=0)
        sq_all = jnp.concatenate([row[4:6] for row in rows], axis=0)
        dsq_all = jnp.concatenate([row[6:8] for row in rows], axis=0)
        greduce[...] = dot_tn(dsq_all, pool_all, HIGH)[0:SE, 0:PART]
        gexcite[...] = dot_tn(sq_all, dlog_all, HIGH)[0:SE, 0:PART]
        gbex[...] = jnp.sum(dlog_all, axis=0, keepdims=True)[:, 0:PART]
        gbred[...] = jnp.sum(dsq_all, axis=0, keepdims=True)[:, 0:SE]


def finish(early, late, mail, raw, raw_grad):
    def whole(*shape):
        zeros = (0,) * len(shape)
        return pl.BlockSpec(shape, lambda n: zeros)

    part = pl.BlockSpec((IMGS, 6, C, COLS), lambda n: (0, n, 0, 0))
    shapes = ((PART, C), (5, 5, PART), (SE, PART), (SE, PART), (1, PART), (PART, C), (1, SE))
    return pl.pallas_call(
        finish_kernel,
        grid=(ROWS // 6,),
        out_shape=tuple(jax.ShapeDtypeStruct(shape, F32) for shape in shapes)
        + (jax.ShapeDtypeStruct((IMGS, ROWS, C, COLS), BF16),) * 2,
        in_specs=[whole(EARLY, 128), whole(C, 128), whole(ND, 8, 128), part, part],
        out_specs=tuple(whole(*shape) for shape in shapes) + (part, part),
        name="finish",
    )(early, late, mail, raw, raw_grad)


def on_device(
    features, w_expand, w_depth, w_reduce, b_reduce, w_excite, b_excite, w_project, cotangent
):
    raw, raw_grad, early, late, mail = block(
        w_expand.T,
        w_project,
        w_depth,
        w_reduce.T,
        w_excite,
        b_excite[None, :],
        b_reduce[None, :],
        features.swapaxes(2, 3),
        cotangent.swapaxes(2, 3),
    )
    (
        s_expand, s_depth, s_reduce, s_excite, s_bexcite, s_project, s_breduce, output, grad,
    ) = finish(early, late, mail, raw, raw_grad)
    return (
        output.swapaxes(2, 3),
        grad.swapaxes(2, 3),
        s_expand.T,
        s_depth,
        s_reduce.T,
        s_excite,
        s_bexcite[0],
        s_project,
        s_breduce[0],
    )


def solution(mesh):
    return jax.shard_map(
        on_device,
        mesh=mesh,
        in_specs=(
            P("dp", "space", None, None),
            P(None, "dp"),
            P(None, None, "dp"),
            P("dp", None),
            P(),
            P(None, "dp"),
            P("dp"),
            P("dp", None),
            P("dp", "space", None, None),
        ),
        out_specs=(
            P("dp", "space", None, None),
            P("dp", "space", None, None),
            P(None, "dp"),
            P(None, None, "dp"),
            P("dp", None),
            P(None, "dp"),
            P("dp"),
            P("dp", None),
            P(),
        ),
        check_vma=False,
    )
```

```python
import functools

import jax
import jax.numpy as jnp
from jax import lax
from jax.experimental import pallas as pl
from jax.experimental.pallas import tpu as pltpu
from jax.sharding import PartitionSpec as P

F32 = jnp.float32
BF16 = jnp.bfloat16
MESH = pl.DeviceIdType.MESH
HIGH = lax.Precision.HIGHEST

IMGS, ROWS, COLS, C, SE = 2, 12, 100, 176, 44
BLOCK, SUB = 13, 16
PIX = BLOCK * SUB
WIDE = BLOCK + 4
HROWS = ROWS + 4
PART, SLOT = 66, 72
CP = 16 * SLOT
TILES = CP // 128
AREA = 9600.0
NS, ND = 8, 16

VMEM = pl.BlockSpec(memory_space=pltpu.VMEM)
ANY = pl.BlockSpec(memory_space=pl.ANY)


def sigmoid(value):
    return 0.5 * jnp.tanh(0.5 * value) + 0.5


def swish(value):
    half = 0.5 * value
    return half + half * jnp.tanh(half)


def swish_grad(value):
    sig = sigmoid(value)
    act = value * sig
    return sig + act - act * sig


def twice_swish_grad(value):
    half = 0.5 * value
    twice = 1.0 + jnp.tanh(half)
    return twice * ((value - half * twice) + 1.0)


def dot_nt(left, right, precision=None):
    return lax.dot_general(
        left, right, (((1,), (1,)), ((), ())), precision=precision, preferred_element_type=F32
    )


def dot_tn(left, right, precision=None):
    return lax.dot_general(
        left, right, (((0,), (0,)), ((), ())), precision=precision, preferred_element_type=F32
    )


def dot_nn(left, right, precision=None):
    return lax.dot_general(
        left, right, (((1,), (0,)), ((), ())), precision=precision, preferred_element_type=F32
    )


def one_hot(img, transposed):
    shape = (COLS, PIX) if transposed else (PIX, COLS)
    place = lax.broadcasted_iota(jnp.int32, shape, 1 if transposed else 0)
    col = lax.broadcasted_iota(jnp.int32, shape, 0 if transposed else 1)
    wanted = (col % BLOCK) * SUB + img * 8 + col // BLOCK
    return jnp.where(place == wanted, 1.0, 0.0).astype(BF16)


def point_taps(taps):
    w0, w1, w2, w3, w4 = taps
    even, odd = w0 + w2 + w4, w1 + w3
    even2, odd2 = w0 + 4.0 * w2 + 16.0 * w4, 2.0 * w1 + 8.0 * w3
    even3, odd3 = w0 + 0.25 * w2 + 0.0625 * w4, 0.5 * w1 + 0.125 * w3
    return [
        w0,
        (even + odd) * (-2.0 / 9.0),
        (even - odd) * (-2.0 / 9.0),
        (even2 + odd2) * (1.0 / 360.0),
        (even2 - odd2) * (1.0 / 360.0),
        (even3 + odd3) * (32.0 / 45.0),
        (even3 - odd3) * (32.0 / 45.0),
        w4,
    ]


def taps_from_points(g):
    s1, d1 = (g[1] + g[2]) * (-2.0 / 9.0), (g[1] - g[2]) * (-2.0 / 9.0)
    s2, d2 = (g[3] + g[4]) * (1.0 / 360.0), (g[3] - g[4]) * (1.0 / 360.0)
    s3, d3 = (g[5] + g[6]) * (32.0 / 45.0), (g[5] - g[6]) * (32.0 / 45.0)
    return [
        g[0] + s1 + s2 + s3,
        d1 + 2.0 * d2 + 0.5 * d3,
        s1 + 4.0 * s2 + 0.25 * s3,
        d1 + 8.0 * d2 + 0.125 * d3,
        s1 + 16.0 * s2 + 0.0625 * s3 + g[7],
    ]


def to_points(x):
    x0, x1, x2, x3, x4, x5, x6, x7 = x
    f3, f4 = 5.0 * x3, 5.0 * x4
    e1, o1 = (x6 + x2) - 4.25 * x4, (x5 + x1) - 4.25 * x3
    e2, o2 = (x2 - f4) + 4.0 * x6, (x1 - f3) + 4.0 * x5
    e3, o3 = (4.0 * x2 - f4) + x6, (4.0 * x1 - f3) + x5
    o2, o3 = o2 + o2, 0.5 * o3
    return [
        (x0 - x6) + 5.25 * (x4 - x2),
        e1 + o1,
        e1 - o1,
        e2 + o2,
        e2 - o2,
        e3 + o3,
        e3 - o3,
        (x7 - x1) + 5.25 * (x3 - x5),
    ]


def from_points(m):
    s1, d1 = m[1] + m[2], m[1] - m[2]
    s2, d2 = m[3] + m[4], m[3] - m[4]
    s3, d3 = m[5] + m[6], m[5] - m[6]
    return [
        (m[0] + s1) + (s2 + s3),
        (d1 + 2.0 * d2) + 0.5 * d3,
        (s1 + 4.0 * s2) + 0.25 * s3,
        ((d1 + 8.0 * d2) + 0.125 * d3) + m[7],
    ]


def outputs_to_points(y):
    y0, y1, y2, y3 = y
    a, b = y0 + y2, y1 + y3
    c, d = y0 + 4.0 * y2, 2.0 * y1 + 8.0 * y3
    e, f = y0 + 0.25 * y2, 0.5 * y1 + 0.125 * y3
    return [y0, a + b, a - b, c + d, c - d, e + f, e - f, y3]


def dot_split(left, right, dims):
    high = left.astype(BF16)
    rest = left - high.astype(F32)
    middle = rest.astype(BF16)
    low = (rest - middle.astype(F32)).astype(BF16)
    parts = jnp.concatenate([high.astype(F32), middle.astype(F32), low.astype(F32)], axis=0)
    product = lax.dot_general(
        parts.astype(BF16), right.astype(BF16), (dims, ((), ())), preferred_element_type=F32
    )
    count = left.shape[0]
    return (product[2 * count :] + product[count : 2 * count]) + product[:count]


def spread_taps(taps, wide_taps, flip):
    for j in range(5):
        column = [taps[5 * i + j : 5 * i + j + 1, :] for i in range(5)]
        if flip:
            column = [0.5 * value for value in column[::-1]]
        place = 4 - j if flip else j
        for p, value in enumerate(point_taps(column)):
            wide_taps[5 * p + place] = jnp.broadcast_to(value, (8, 128))


def with_edges(value):
    block = lax.broadcasted_iota(jnp.int32, (2, 8, 128), 1)
    left = jnp.where(block > 0, pltpu.roll(value[BLOCK - 2 :], 1, 1), 0.0)
    right = jnp.where(block < 7, pltpu.roll(value[:2], 7, 1), 0.0)
    return jnp.concatenate([left, value, right], axis=0)


def conv_rows(ref, q, h, wide_taps):
    points = to_points([ref[4 * q + n, :, 8 * h : 8 * h + 8, :] for n in range(8)])
    totals = []
    for p in range(8):
        source = with_edges(points[p])
        total = source[0:BLOCK] * wide_taps[5 * p][None]
        for j in range(1, 5):
            total = total + source[j : j + BLOCK] * wide_taps[5 * p + j][None]
        totals.append(total)
    return from_points(totals)


def pad_mask():
    block = lax.broadcasted_iota(jnp.int32, (4, 8, 128), 1)
    return jnp.where(block < 7, 1.0, 0.0)


def gate_row(depth, dgated, gates, h, keep):
    gate = gates[h : h + 1, :][None]
    half_gate = gates[2 + h : 3 + h, :][None]
    half_pull = gates[4 + h : 5 + h, :][None]
    half = 0.5 * depth
    twice = 1.0 + jnp.tanh(half)
    act = half * twice
    gated = act * gate
    ddepth = (dgated * half_gate + half_pull) * (twice * ((depth - act) + 1.0))
    ddepth = jnp.concatenate([ddepth[:9], ddepth[9:] * keep], axis=0)
    return gated, ddepth


def unpermute(value, out, r):
    for img in range(2):
        out[img, r] = dot_tn(value, one_hot(img, False)).astype(BF16)


def all_channels_out(rows_in, weights, base, shift, out):
    def chunk(q, carry):
        block = rows_in[pl.ds(pl.multiple_of(4 * PIX * q, 4 * PIX), 4 * PIX), :]
        product = dot_nn(block, weights[...]).reshape(4, PIX, C)
        for n in range(4):
            value = product[n] + base[4 * q + n + shift].astype(F32)
            unpermute(value.astype(BF16), out, 4 * q + n)
        return carry

    lax.fori_loop(0, 3, chunk, 0)


def all_channels_grad(rows_in, turned, grad):
    def lanes(q, carry):
        span = pl.ds(pl.multiple_of(384 * q, 128), 384)
        grad[:, span] = dot_nn(turned[...], rows_in[:, span])
        return carry

    lax.fori_loop(0, 3, lanes, 0)


OFFSETS = sorted(
    ((x, y) for x in range(4) for y in range(4) if x or y),
    key=lambda at: -(min(at[0], 4 - at[0]) + min(at[1], 4 - at[1])),
)


def dp_peer(k, sign):
    me_d = lax.axis_index("dp")
    x, y = OFFSETS[k - 1]
    column = lax.rem(lax.div(me_d, 4) + (x if sign > 0 else 4 - x), 4)
    return 4 * column + lax.rem(lax.rem(me_d, 4) + (y if sign > 0 else 4 - y), 4)


def to_dp(src, dst, send, recv, by_sender=False):
    me_s, me_d = lax.axis_index("space"), lax.axis_index("dp")
    copies = []
    for k in range(1, ND):
        target = dp_peer(k, 1)
        copies.append(
            pltpu.make_async_remote_copy(
                src_ref=src.at[target],
                dst_ref=dst.at[me_d] if by_sender else dst.at[k],
                send_sem=send.at[k],
                recv_sem=recv.at[k],
                device_id=(me_s, target),
                device_id_type=MESH,
            )
        )
    return copies


def to_space(ref, send, recv):
    me_s, me_d = lax.axis_index("space"), lax.axis_index("dp")
    copies = []
    for k in (4, 5, 3, 6, 2, 7, 1):
        copies.append(
            pltpu.make_async_remote_copy(
                src_ref=ref.at[me_s],
                dst_ref=ref.at[me_s],
                send_sem=send.at[k],
                recv_sem=recv.at[k],
                device_id=(lax.rem(me_s + k, NS), me_d),
                device_id_type=MESH,
            )
        )
    return copies


def to_neighbours(down_src, down_dst, up_src, up_dst, send, recv):
    me_s, me_d = lax.axis_index("space"), lax.axis_index("dp")
    down = pltpu.make_async_remote_copy(
        src_ref=down_src,
        dst_ref=down_dst,
        send_sem=send[0],
        recv_sem=recv[0],
        device_id=(lax.rem(me_s + 1, NS), me_d),
        device_id_type=MESH,
    )
    up = pltpu.make_async_remote_copy(
        src_ref=up_src,
        dst_ref=up_dst,
        send_sem=send[1],
        recv_sem=recv[1],
        device_id=(lax.rem(me_s + NS - 1, NS), me_d),
        device_id_type=MESH,
    )
    return down, up


def dp_sum(copies, piece, got):
    total = piece[lax.axis_index("dp")].astype(F32)
    for k, copy in enumerate(copies):
        copy.wait()
        total = total + got[k + 1].astype(F32)
    return total


def space_sum(copies, ref):
    for copy in copies:
        copy.wait()
    total = ref[0].astype(F32)
    for s in range(1, NS):
        total = total + ref[s].astype(F32)
    return total


EARLY = C + 32


def block_kernel(
    wet, wpr, taps, wrt, wx_own, bex, bred, feats_in, cot_in,
    out_to, out_grad_to, early, late, mail_out,
    out, out_grad, feats, cot, stage, pack, full, top, bottom, flatw, fp, cp, fpt, cpt, we, wp, misc,
    wide_taps, ex, dgs, coming_pre, coming_dg, saved, depth, sums, packed, landed, lanes, vecs, gates, msgs, mail,
    edge, above, below, gated, dpre, acc, held, flat, flat_taps,
    epiece, egot, espace, lpiece, lgot, lspace, tpiece, tgot, tspace,
    wsend, wrecv, hsend, hrecv, csend, crecv, ssend, srecv, msend, mrecv,
    dsend, drecv, esend, erecv, fsend, frecv, lsend, lrecv, gsend, grecv,
    tsend, trecv, usend, urecv, insem,
):
    me_s, me_d = lax.axis_index("space"), lax.axis_index("dp")
    core = lax.rem(me_s, 2)
    barrier = pltpu.get_barrier_semaphore()
    for k in range(1, ND):
        pl.semaphore_signal(
            barrier, inc=1, device_id=(me_s, dp_peer(k, 1)), device_id_type=MESH
        )
    for k in range(1, NS):
        pl.semaphore_signal(
            barrier, inc=1, device_id=(lax.rem(me_s + k, NS), me_d), device_id_type=MESH
        )

    arrive = [
        pltpu.make_async_copy(feats_in, feats, insem.at[0]),
        pltpu.make_async_copy(cot_in, cot, insem.at[1]),
    ]
    for copy in arrive:
        copy.start()

    stage[...] = jnp.zeros_like(stage)
    stage[0, 0:PART, 0:C] = wet[...].astype(F32)
    stage[1, 0:PART, 0:C] = wpr[...].astype(F32)
    side = slice(C, C + PART)
    for i in range(5):
        stage[0, 5 * i : 5 * i + 5, side] = taps[i].astype(F32)
    stage[0, 32 : 32 + SE, side] = wrt[...].astype(F32)
    stage[1, 0:SE, side] = wx_own[...].astype(F32)
    stage[1, 48:49, side] = bex[...].astype(F32)
    pack[...] = stage[...].astype(BF16)
    pl.semaphore_wait(barrier, NS + ND - 2)
    copies = []
    for k in range(1, ND):
        copy = pltpu.make_async_remote_copy(
            src_ref=pack.at[core],
            dst_ref=full.at[core, me_d],
            send_sem=wsend.at[k],
            recv_sem=wrecv.at[k],
            device_id=(me_s, dp_peer(k, 1)),
            device_id_type=MESH,
        )
        copy.start()
        copies.append(copy)
    for copy in arrive:
        copy.wait()
    halo = to_neighbours(
        feats.at[:, pl.ds(ROWS - 2, 2)],
        top,
        feats.at[:, pl.ds(0, 2)],
        bottom,
        (hsend.at[0], hsend.at[1]),
        (hrecv.at[0], hrecv.at[1]),
    )
    for copy in halo:
        copy.start()
    full[0, me_d] = pack[0]
    full[1, me_d] = pack[1]
    spread = (one_hot(0, False), one_hot(1, False))
    gather_t = (one_hot(0, True), one_hot(1, True))

    def permute(r, carry):
        for src, dst, shift in ((feats, fp, 2), (cot, cp, 0)):
            a, b = src[0, r], src[1, r]
            dst[r + shift] = (dot_nt(spread[0], a) + dot_nt(spread[1], b)).astype(BF16)
        return carry

    lax.fori_loop(0, ROWS, permute, 0)
    for r in range(ROWS):
        for src, dst in ((feats, fpt), (cot, cpt)):
            value = dot_nn(src[0, r], gather_t[0]) + dot_nn(src[1, r], gather_t[1])
            dst[:, PIX * r : PIX * (r + 1)] = value.astype(BF16)
    shares = []
    for k, copy in enumerate(copies, 1):
        copy.wait_recv()
        sender = dp_peer(k, -1)
        share = pltpu.make_async_remote_copy(
            src_ref=full.at[core, sender],
            dst_ref=full.at[core, sender],
            send_sem=csend.at[k],
            recv_sem=crecv.at[k],
            device_id=(me_s + 1 - 2 * core, me_d),
            device_id_type=MESH,
        )
        share.start()
        shares.append(share)
    for copy in halo:
        copy.wait()
    has_top = jnp.where(me_s > 0, 1.0, 0.0)
    has_bottom = jnp.where(me_s < NS - 1, 1.0, 0.0)
    for r in range(2):
        value = dot_nt(spread[0], top[0, r]) + dot_nt(spread[1], top[1, r])
        fp[r] = (value * has_top).astype(BF16)
        value = dot_nt(spread[0], bottom[0, r]) + dot_nt(spread[1], bottom[1, r])
        fp[ROWS + 2 + r] = (value * has_bottom).astype(BF16)
    for copy in copies:
        copy.wait_send()
    for share in shares:
        share.wait()
    for half, whole in ((0, we), (1, wp)):
        for d in range(ND):
            part = full[half, d].astype(F32)
            flatw[d * SLOT : (d + 1) * SLOT, :] = part[0:SLOT, 0:C]
            span = slice(d * SLOT, (d + 1) * SLOT)
            if half == 0:
                misc[0:80, span] = part[:, C : C + SLOT]
            else:
                misc[80:136, span] = part[0:56, C : C + SLOT]
        whole[...] = flatw[...].astype(BF16)

    keep = pad_mask()

    def lane_of(t):
        return pl.ds(pl.multiple_of(128 * t, 128), 128)

    def pre_rows(t, start, count):
        product = dot_nt(fp[pl.ds(start, count)].reshape(count * PIX, C), we[lane_of(t), :])
        coming_pre[pl.ds(start, count)] = product.reshape(count, BLOCK, SUB, 128)

    def cot_rows(t, start, count):
        product = dot_nt(cp[pl.ds(start, count)].reshape(count * PIX, C), wp[lane_of(t), :])
        coming_dg[pl.ds(start, count)] = product.reshape(count, BLOCK, SUB, 128)

    def next_tile(t):
        return jnp.minimum(t + 1, TILES - 1)

    def take_dg():
        def row(r, carry):
            dgs[r] = coming_dg[r]
            return carry

        lax.fori_loop(0, ROWS, row, 0)

    def first(t, carry):
        spread_taps(misc[0:32, lane_of(t)], wide_taps, False)

        def expand(q, carry):
            for n in range(4):
                ex[4 * q + n] = swish(coming_pre[4 * q + n])
            return carry

        lax.fori_loop(0, HROWS // 4, expand, 0)
        take_dg()

        def conv(q, carry):
            pools, grads = list(carry[:2]), list(carry[2:])
            for h in range(2):
                rows = slice(8 * h, 8 * h + 8)
                for n, total in enumerate(conv_rows(ex, q, h, wide_taps)):
                    depth[t, 4 * q + n, :, rows, :] = total
                    act = swish(total)
                    grads[h] = grads[h] + jnp.sum(act * dgs[4 * q + n, :, rows, :], axis=0)
                    pools[h] = pools[h] + jnp.sum(act[:9], axis=0)
                    pools[h] = pools[h] + jnp.sum(act[9:] * keep, axis=0)
            for n in range(4):
                saved[t, 4 * q + n] = ex[4 * q + n].astype(BF16)
            pre_rows(next_tile(t), jnp.minimum(6 * q, HROWS - 6), 6)
            cot_rows(next_tile(t), 4 * q, 4)
            return (*pools, *grads)

        zero = jnp.zeros((8, 128), F32)
        parts = lax.fori_loop(0, ROWS // 4, conv, (zero,) * 4)
        for r in range(ROWS, HROWS):
            saved[t, r] = ex[r].astype(BF16)
        for k in range(4):
            sums[t, k : k + 1, :] = jnp.sum(parts[k], axis=0, keepdims=True)
        return carry

    def begin(q, carry):
        pre_rows(0, 8 * q, 8)
        cot_rows(0, 6 * q, 6)
        return carry

    lax.fori_loop(0, 2, begin, 0)
    lax.fori_loop(0, TILES, first, 0)

    packed[...] = jnp.zeros_like(packed)
    for t in range(TILES):
        packed[t // 2, 4 * (t % 2) : 4 * (t % 2) + 4, :] = sums[t, 0:4, :]
    landed[me_s] = packed[...]
    copies = to_space(landed, ssend, srecv)
    for copy in copies:
        copy.start()

    def begin_again(q, carry):
        cot_rows(0, 6 * q, 6)
        return carry

    lax.fori_loop(0, 2, begin_again, 0)
    total = space_sum(copies, landed)
    for t in range(TILES):
        lanes[0:4, 128 * t : 128 * (t + 1)] = total[t // 2, 4 * (t % 2) : 4 * (t % 2) + 4]
    lanes[:, CP:] = jnp.zeros((8, 128), F32)
    wr = misc[32 : 32 + SE, :]
    wx = misc[80 : 80 + SE, :]
    pooled = lanes[0:2, 0:CP] / AREA
    dgate = lanes[2:4, 0:CP]
    squeeze_pre = dot_split(pooled, wr, ((1,), (1,))) + bred[...].astype(F32)
    squeeze = swish(squeeze_pre)
    gate = sigmoid(dot_split(squeeze, wx, ((1,), (0,))) + misc[128:129, :])
    dlogit = dgate * gate * (1.0 - gate)
    dsq = dot_split(dlogit, wx, ((1,), (1,))) * swish_grad(squeeze_pre)
    dpooled = dot_split(dsq, wr, ((1,), (0,)))
    gates[0:2, :] = gate
    gates[2:4, :] = 0.5 * gate
    gates[4:6, :] = dpooled * (0.5 / AREA)
    gates[6:8, :] = jnp.zeros((2, CP), F32)
    lanes[0:2, 0:CP] = pooled
    lanes[2:4, 0:CP] = dlogit
    vecs[...] = jnp.zeros((8, 128), F32)
    vecs[4:6, 0:SE] = squeeze
    vecs[6:8, 0:SE] = dsq

    def edge_copies(t):
        return to_neighbours(
            edge.at[t, 1],
            above.at[t],
            edge.at[t, 0],
            below.at[t],
            (dsend.at[0, t], dsend.at[1, t]),
            (drecv.at[0, t], drecv.at[1, t]),
        )

    def second(t, carry):
        take_dg()

        def pointwise(q, carry):
            for n in range(4):
                r = 4 * q + n
                both = []
                for h in range(2):
                    rows = slice(8 * h, 8 * h + 8)
                    value, ddepth = gate_row(
                        depth[t, r, :, rows, :],
                        dgs[r, :, rows, :],
                        gates.at[:, lane_of(t)],
                        h,
                        keep,
                    )
                    depth[t, r, :, rows, :] = ddepth.astype(BF16).astype(F32)
                    both.append(value)
                gated[pl.ds(pl.multiple_of(r * PIX, PIX), PIX), lane_of(t)] = (
                    jnp.concatenate(both, axis=1).reshape(PIX, 128).astype(BF16)
                )
            cot_rows(next_tile(t), 4 * q, 4)
            return carry

        lax.fori_loop(0, ROWS // 4, pointwise, 0)
        for n in range(2):
            edge[t, 0, n] = depth[t, n].astype(BF16)
            edge[t, 1, n] = depth[t, ROWS - 2 + n].astype(BF16)
        for copy in edge_copies(t):
            copy.start()
        return carry

    lax.fori_loop(0, TILES, second, 0)

    def pieces_of(source, rows, piece):
        for d in range(ND):
            piece[d] = source[0:rows, SLOT * d : SLOT * d + 128].astype(BF16)

    flat[:, CP:] = jnp.zeros((C, 128), F32)
    flat_taps[...] = jnp.zeros_like(flat_taps)
    all_channels_grad(gated, cpt, flat)
    pieces_of(flat, C, epiece)
    for copy in to_dp(epiece, egot, esend, erecv):
        copy.start()

    def third(t, carry):
        spread_taps(misc[0:32, lane_of(t)], wide_taps, True)

        def middle(r, carry):
            ex[r + 2] = depth[t, r]
            return carry

        lax.fori_loop(0, ROWS, middle, 0)

        def slopes(q, carry):
            for n in range(4):
                dgs[4 * q + n] = twice_swish_grad(coming_pre[4 * q + n + 2])
            return carry

        lax.fori_loop(0, ROWS // 4, slopes, 0)
        for copy in edge_copies(t):
            copy.wait()
        for n in range(2):
            ex[n] = above[t, n].astype(F32) * has_top
            ex[ROWS + 2 + n] = below[t, n].astype(F32) * has_bottom

        def conv(q, carry):
            both = []
            for h in range(2):
                rows = slice(8 * h, 8 * h + 8)
                values = conv_rows(ex, q, h, wide_taps)
                both.append([value * dgs[4 * q + n, :, rows, :] for n, value in enumerate(values)])
            for n in range(4):
                value = jnp.concatenate([both[0][n], both[1][n]], axis=1)
                span = pl.ds(pl.multiple_of((4 * q + n) * PIX, PIX), PIX)
                dpre[span, lane_of(t)] = value.reshape(PIX, 128).astype(BF16)
            pre_rows(next_tile(t), 4 * q + 2, 4)
            return carry

        lax.fori_loop(0, ROWS // 4, conv, 0)

        @pl.when(t == TILES // 2)
        def _():
            total = dp_sum(to_dp(epiece, egot, esend, erecv), epiece, egot)
            espace[me_s] = total.astype(BF16)
            for copy in to_space(espace, fsend, frecv):
                copy.start()

        return carry

    def begin_third(q, carry):
        pre_rows(0, 6 * q + 2, 6)
        return carry

    lax.fori_loop(0, 2, begin_third, 0)
    lax.fori_loop(0, TILES, third, 0)

    all_channels_grad(dpre, fpt, flat)
    pieces_of(flat, C, lpiece)
    for copy in to_dp(lpiece, lgot, lsend, lrecv):
        copy.start()

    def tap_grads(t, carry):
        acc[...] = jnp.zeros_like(acc)

        def window(q, carry):
            for h in range(2):
                rows = slice(8 * h, 8 * h + 8)
                points = to_points([saved[t, 4 * q + n].astype(F32)[:, rows, :] for n in range(8)])
                for p in range(8):
                    held[p] = with_edges(points[p])
                mine = outputs_to_points([depth[t, 4 * q + n, :, rows, :] for n in range(4)])
                for p in range(8):
                    source = held[p]
                    for j in range(5):
                        k = 5 * p + j
                        acc[k] = acc[k] + jnp.sum(mine[p] * source[j : j + BLOCK], axis=0)
            return carry

        lax.fori_loop(0, ROWS // 4, window, 0)
        for j in range(5):
            sums_at = [jnp.sum(acc[5 * p + j], axis=0, keepdims=True) for p in range(8)]
            for i, value in enumerate(taps_from_points(sums_at)):
                flat_taps[5 * i + j : 5 * i + j + 1, lane_of(t)] = value

        @pl.when(t == TILES // 2)
        def _():
            total = dp_sum(to_dp(lpiece, lgot, lsend, lrecv), lpiece, lgot)
            lspace[me_s] = total.astype(BF16)
            for copy in to_space(lspace, gsend, grecv):
                copy.start()

        return carry

    lax.fori_loop(0, TILES, tap_grads, 0)
    pieces_of(flat_taps, 32, tpiece)
    copies = to_dp(tpiece, tgot, tsend, trecv)
    for copy in copies:
        copy.start()
    for d in range(ND):
        msgs[d, 0:4, :] = lanes[0:4, SLOT * d : SLOT * d + 128]
        msgs[d, 4:8, :] = vecs[4:8, :]
    mail[me_d] = msgs[me_d]
    small = to_dp(msgs, mail, msend, mrecv, True)
    for copy in small:
        copy.start()

    all_channels_out(dpre, we, cp, 0, out_grad)
    leave = pltpu.make_async_copy(out_grad, out_grad_to, insem.at[0])
    leave.start()
    tspace[me_s] = dp_sum(copies, tpiece, tgot).astype(BF16)
    copies = to_space(tspace, usend, urecv)
    for copy in copies:
        copy.start()
    all_channels_out(gated, wp, fp, 2, out)
    leave_too = pltpu.make_async_copy(out, out_to, insem.at[1])
    leave_too.start()
    for copy in small:
        copy.wait()
    mail_out[...] = mail[...]
    early[0:C] = space_sum(to_space(espace, fsend, frecv), espace)
    late[...] = space_sum(to_space(lspace, gsend, grecv), lspace)
    early[C:] = space_sum(copies, tspace)
    leave.wait()
    leave_too.wait()


def block(*args):
    def bf16(*shape):
        return pltpu.VMEM(shape, BF16)

    def f32(*shape):
        return pltpu.VMEM(shape, F32)

    def sems(*shape):
        return pltpu.SemaphoreType.DMA(shape)

    return pl.pallas_call(
        block_kernel,
        out_shape=(
            jax.ShapeDtypeStruct((IMGS, ROWS, C, COLS), BF16),
            jax.ShapeDtypeStruct((IMGS, ROWS, C, COLS), BF16),
            jax.ShapeDtypeStruct((EARLY, 128), F32),
            jax.ShapeDtypeStruct((C, 128), F32),
            jax.ShapeDtypeStruct((ND, 8, 128), F32),
        ),
        in_specs=[VMEM] * 7 + [ANY] * 2,
        out_specs=(ANY, ANY, VMEM, VMEM, VMEM),
        scratch_shapes=[
            bf16(IMGS, ROWS, C, COLS),
            bf16(IMGS, ROWS, C, COLS),
            bf16(IMGS, ROWS, C, COLS),
            bf16(IMGS, ROWS, C, COLS),
            f32(2, 80, 256),
            bf16(2, 80, 256),
            bf16(2, ND, 80, 256),
            bf16(IMGS, 2, C, COLS),
            bf16(IMGS, 2, C, COLS),
            f32(CP, C),
            bf16(HROWS, PIX, C),
            bf16(ROWS, PIX, C),
            bf16(C, ROWS * PIX),
            bf16(C, ROWS * PIX),
            bf16(CP, C),
            bf16(CP, C),
            f32(136, CP),
            f32(40, 8, 128),
            f32(HROWS, BLOCK, SUB, 128),
            f32(ROWS, BLOCK, SUB, 128),
            f32(HROWS, BLOCK, SUB, 128),
            f32(ROWS, BLOCK, SUB, 128),
            bf16(TILES, HROWS, BLOCK, SUB, 128),
            f32(TILES, ROWS, BLOCK, SUB, 128),
            f32(TILES, 8, 128),
            f32(5, 8, 128),
            f32(NS, 5, 8, 128),
            f32(8, CP + 128),
            f32(8, 128),
            f32(8, CP),
            f32(ND, 8, 128),
            f32(ND, 8, 128),
            bf16(TILES, 2, 2, BLOCK, SUB, 128),
            bf16(TILES, 2, BLOCK, SUB, 128),
            bf16(TILES, 2, BLOCK, SUB, 128),
            bf16(ROWS * PIX, CP),
            bf16(ROWS * PIX, CP),
            f32(40, 8, 128),
            f32(8, WIDE, 8, 128),
            f32(C, CP + 128),
            f32(32, CP + 128),
            bf16(ND, C, 128),
            bf16(ND, C, 128),
            bf16(NS, C, 128),
            bf16(ND, C, 128),
            bf16(ND, C, 128),
            bf16(NS, C, 128),
            bf16(ND, 32, 128),
            bf16(ND, 32, 128),
            bf16(NS, 32, 128),
            sems(ND),
            sems(ND),
            sems(2),
            sems(2),
            sems(ND),
            sems(ND),
            sems(NS),
            sems(NS),
            sems(ND),
            sems(ND),
            sems(2, TILES),
            sems(2, TILES),
            sems(ND),
            sems(ND),
            sems(NS),
            sems(NS),
            sems(ND),
            sems(ND),
            sems(NS),
            sems(NS),
            sems(ND),
            sems(ND),
            sems(NS),
            sems(NS),
            sems(2),
        ],
        compiler_params=pltpu.CompilerParams(
            collective_id=0, has_side_effects=True, vmem_limit_bytes=63 * 2**20
        ),
        name="block",
    )(*args)


def finish_kernel(
    early, late, mail, raw, raw_grad,
    gexp, gdepth, greduce, gexcite, gbex, gproj, gbred, out, out_grad,
):
    out[...] = raw[...]
    out_grad[...] = raw_grad[...]

    @pl.when(pl.program_id(0) == 0)
    def _():
        gexp[...] = late[...].T[0:PART]
        gproj[...] = early[0:C].T[0:PART]
        for i in range(5):
            gdepth[i] = early[C + 5 * i : C + 5 * i + 5, 0:PART]
        rows = [mail[d] for d in range(ND)]
        pool_all = jnp.concatenate([row[0:2] for row in rows], axis=0)
        dlog_all = jnp.concatenate([row[2:4] for row in rows], axis=0)
        sq_all = jnp.concatenate([row[4:6] for row in rows], axis=0)
        dsq_all = jnp.concatenate([row[6:8] for row in rows], axis=0)
        greduce[...] = dot_tn(dsq_all, pool_all, HIGH)[0:SE, 0:PART]
        gexcite[...] = dot_tn(sq_all, dlog_all, HIGH)[0:SE, 0:PART]
        gbex[...] = jnp.sum(dlog_all, axis=0, keepdims=True)[:, 0:PART]
        gbred[...] = jnp.sum(dsq_all, axis=0, keepdims=True)[:, 0:SE]


def finish(early, late, mail, raw, raw_grad):
    def whole(*shape):
        zeros = (0,) * len(shape)
        return pl.BlockSpec(shape, lambda n: zeros)

    part = pl.BlockSpec((IMGS, 6, C, COLS), lambda n: (0, n, 0, 0))
    shapes = ((PART, C), (5, 5, PART), (SE, PART), (SE, PART), (1, PART), (PART, C), (1, SE))
    return pl.pallas_call(
        finish_kernel,
        grid=(ROWS // 6,),
        out_shape=tuple(jax.ShapeDtypeStruct(shape, F32) for shape in shapes)
        + (jax.ShapeDtypeStruct((IMGS, ROWS, C, COLS), BF16),) * 2,
        in_specs=[whole(EARLY, 128), whole(C, 128), whole(ND, 8, 128), part, part],
        out_specs=tuple(whole(*shape) for shape in shapes) + (part, part),
        name="finish",
    )(early, late, mail, raw, raw_grad)


def on_device(
    features, w_expand, w_depth, w_reduce, b_reduce, w_excite, b_excite, w_project, cotangent
):
    raw, raw_grad, early, late, mail = block(
        w_expand.T,
        w_project,
        w_depth,
        w_reduce.T,
        w_excite,
        b_excite[None, :],
        b_reduce[None, :],
        features.swapaxes(2, 3),
        cotangent.swapaxes(2, 3),
    )
    (
        s_expand, s_depth, s_reduce, s_excite, s_bexcite, s_project, s_breduce, output, grad,
    ) = finish(early, late, mail, raw, raw_grad)
    return (
        output.swapaxes(2, 3),
        grad.swapaxes(2, 3),
        s_expand.T,
        s_depth,
        s_reduce.T,
        s_excite,
        s_bexcite[0],
        s_project,
        s_breduce[0],
    )


def solution(mesh):
    return jax.shard_map(
        on_device,
        mesh=mesh,
        in_specs=(
            P("dp", "space", None, None),
            P(None, "dp"),
            P(None, None, "dp"),
            P("dp", None),
            P(),
            P(None, "dp"),
            P("dp"),
            P("dp", None),
            P("dp", "space", None, None),
        ),
        out_specs=(
            P("dp", "space", None, None),
            P("dp", "space", None, None),
            P(None, "dp"),
            P(None, None, "dp"),
            P("dp", None),
            P(None, "dp"),
            P("dp"),
            P("dp", None),
            P(),
        ),
        check_vma=False,
    )
```

```python
import functools

import jax
import jax.numpy as jnp
from jax import lax
from jax.experimental import pallas as pl
from jax.experimental.pallas import tpu as pltpu
from jax.sharding import PartitionSpec as P

F32 = jnp.float32
BF16 = jnp.bfloat16
MESH = pl.DeviceIdType.MESH
HIGH = lax.Precision.HIGHEST

IMGS, ROWS, COLS, C, SE = 2, 12, 100, 176, 44
BLOCK, SUB = 13, 16
PIX = BLOCK * SUB
WIDE = BLOCK + 4
HROWS = ROWS + 4
PART, SLOT = 66, 72
CP = 16 * SLOT
TILES = CP // 128
AREA = 9600.0
NS, ND = 8, 16

VMEM = pl.BlockSpec(memory_space=pltpu.VMEM)
ANY = pl.BlockSpec(memory_space=pl.ANY)


def sigmoid(value):
    return 0.5 * jnp.tanh(0.5 * value) + 0.5


def swish(value):
    half = 0.5 * value
    return half + half * jnp.tanh(half)


def swish_grad(value):
    sig = sigmoid(value)
    act = value * sig
    return sig + act - act * sig


def twice_swish_grad(value):
    half = 0.5 * value
    twice = 1.0 + jnp.tanh(half)
    return twice * ((value - half * twice) + 1.0)


def dot_nt(left, right, precision=None):
    return lax.dot_general(
        left, right, (((1,), (1,)), ((), ())), precision=precision, preferred_element_type=F32
    )


def dot_tn(left, right, precision=None):
    return lax.dot_general(
        left, right, (((0,), (0,)), ((), ())), precision=precision, preferred_element_type=F32
    )


def dot_nn(left, right, precision=None):
    return lax.dot_general(
        left, right, (((1,), (0,)), ((), ())), precision=precision, preferred_element_type=F32
    )


def one_hot(img, transposed):
    shape = (COLS, PIX) if transposed else (PIX, COLS)
    place = lax.broadcasted_iota(jnp.int32, shape, 1 if transposed else 0)
    col = lax.broadcasted_iota(jnp.int32, shape, 0 if transposed else 1)
    wanted = (col % BLOCK) * SUB + img * 8 + col // BLOCK
    return jnp.where(place == wanted, 1.0, 0.0).astype(BF16)


def point_taps(taps):
    w0, w1, w2, w3, w4 = taps
    even, odd = w0 + w2 + w4, w1 + w3
    even2, odd2 = w0 + 4.0 * w2 + 16.0 * w4, 2.0 * w1 + 8.0 * w3
    even3, odd3 = w0 + 0.25 * w2 + 0.0625 * w4, 0.5 * w1 + 0.125 * w3
    return [
        w0,
        (even + odd) * (-2.0 / 9.0),
        (even - odd) * (-2.0 / 9.0),
        (even2 + odd2) * (1.0 / 360.0),
        (even2 - odd2) * (1.0 / 360.0),
        (even3 + odd3) * (32.0 / 45.0),
        (even3 - odd3) * (32.0 / 45.0),
        w4,
    ]


def taps_from_points(g):
    s1, d1 = (g[1] + g[2]) * (-2.0 / 9.0), (g[1] - g[2]) * (-2.0 / 9.0)
    s2, d2 = (g[3] + g[4]) * (1.0 / 360.0), (g[3] - g[4]) * (1.0 / 360.0)
    s3, d3 = (g[5] + g[6]) * (32.0 / 45.0), (g[5] - g[6]) * (32.0 / 45.0)
    return [
        g[0] + s1 + s2 + s3,
        d1 + 2.0 * d2 + 0.5 * d3,
        s1 + 4.0 * s2 + 0.25 * s3,
        d1 + 8.0 * d2 + 0.125 * d3,
        s1 + 16.0 * s2 + 0.0625 * s3 + g[7],
    ]


def to_points(x):
    x0, x1, x2, x3, x4, x5, x6, x7 = x
    f3, f4 = 5.0 * x3, 5.0 * x4
    e1, o1 = (x6 + x2) - 4.25 * x4, (x5 + x1) - 4.25 * x3
    e2, o2 = (x2 - f4) + 4.0 * x6, (x1 - f3) + 4.0 * x5
    e3, o3 = (4.0 * x2 - f4) + x6, (4.0 * x1 - f3) + x5
    o2, o3 = o2 + o2, 0.5 * o3
    return [
        (x0 - x6) + 5.25 * (x4 - x2),
        e1 + o1,
        e1 - o1,
        e2 + o2,
        e2 - o2,
        e3 + o3,
        e3 - o3,
        (x7 - x1) + 5.25 * (x3 - x5),
    ]


def from_points(m):
    s1, d1 = m[1] + m[2], m[1] - m[2]
    s2, d2 = m[3] + m[4], m[3] - m[4]
    s3, d3 = m[5] + m[6], m[5] - m[6]
    return [
        (m[0] + s1) + (s2 + s3),
        (d1 + 2.0 * d2) + 0.5 * d3,
        (s1 + 4.0 * s2) + 0.25 * s3,
        ((d1 + 8.0 * d2) + 0.125 * d3) + m[7],
    ]


def outputs_to_points(y):
    y0, y1, y2, y3 = y
    a, b = y0 + y2, y1 + y3
    c, d = y0 + 4.0 * y2, 2.0 * y1 + 8.0 * y3
    e, f = y0 + 0.25 * y2, 0.5 * y1 + 0.125 * y3
    return [y0, a + b, a - b, c + d, c - d, e + f, e - f, y3]


def dot_split(left, right, dims):
    high = left.astype(BF16)
    rest = left - high.astype(F32)
    middle = rest.astype(BF16)
    low = (rest - middle.astype(F32)).astype(BF16)
    parts = jnp.concatenate([high.astype(F32), middle.astype(F32), low.astype(F32)], axis=0)
    product = lax.dot_general(
        parts.astype(BF16), right.astype(BF16), (dims, ((), ())), preferred_element_type=F32
    )
    count = left.shape[0]
    return (product[2 * count :] + product[count : 2 * count]) + product[:count]


def spread_taps(taps, wide_taps, flip):
    for j in range(5):
        column = [taps[5 * i + j : 5 * i + j + 1, :] for i in range(5)]
        if flip:
            column = [0.5 * value for value in column[::-1]]
        place = 4 - j if flip else j
        for p, value in enumerate(point_taps(column)):
            wide_taps[5 * p + place] = jnp.broadcast_to(value, (8, 128))


def with_edges(value):
    block = lax.broadcasted_iota(jnp.int32, (2, 8, 128), 1)
    left = jnp.where(block > 0, pltpu.roll(value[BLOCK - 2 :], 1, 1), 0.0)
    right = jnp.where(block < 7, pltpu.roll(value[:2], 7, 1), 0.0)
    return jnp.concatenate([left, value, right], axis=0)


def conv_rows(ref, q, h, wide_taps):
    points = to_points([ref[4 * q + n, :, 8 * h : 8 * h + 8, :] for n in range(8)])
    totals = []
    for p in range(8):
        source = with_edges(points[p])
        total = source[0:BLOCK] * wide_taps[5 * p][None]
        for j in range(1, 5):
            total = total + source[j : j + BLOCK] * wide_taps[5 * p + j][None]
        totals.append(total)
    return from_points(totals)


def pad_mask():
    block = lax.broadcasted_iota(jnp.int32, (4, 8, 128), 1)
    return jnp.where(block < 7, 1.0, 0.0)


def gate_row(depth, dgated, gates, h, keep):
    gate = gates[h : h + 1, :][None]
    half_gate = gates[2 + h : 3 + h, :][None]
    half_pull = gates[4 + h : 5 + h, :][None]
    half = 0.5 * depth
    twice = 1.0 + jnp.tanh(half)
    act = half * twice
    gated = act * gate
    ddepth = (dgated * half_gate + half_pull) * (twice * ((depth - act) + 1.0))
    ddepth = jnp.concatenate([ddepth[:9], ddepth[9:] * keep], axis=0)
    return gated, ddepth


def unpermute(value, out, r):
    for img in range(2):
        out[img, r] = dot_tn(value, one_hot(img, False)).astype(BF16)


def all_channels_out(rows_in, weights, base, shift, out):
    def chunk(q, carry):
        block = rows_in[pl.ds(pl.multiple_of(4 * PIX * q, 4 * PIX), 4 * PIX), :]
        product = dot_nn(block, weights[...]).reshape(4, PIX, C)
        for n in range(4):
            value = product[n] + base[4 * q + n + shift].astype(F32)
            unpermute(value.astype(BF16), out, 4 * q + n)
        return carry

    lax.fori_loop(0, 3, chunk, 0)


def all_channels_grad(rows_in, turned, grad):
    def lanes(q, carry):
        span = pl.ds(pl.multiple_of(384 * q, 128), 384)
        grad[:, span] = dot_nn(turned[...], rows_in[:, span])
        return carry

    lax.fori_loop(0, 3, lanes, 0)


OFFSETS = sorted(
    ((x, y) for x in range(4) for y in range(4) if x or y),
    key=lambda at: -(min(at[0], 4 - at[0]) + min(at[1], 4 - at[1])),
)


def dp_peer(k, sign):
    me_d = lax.axis_index("dp")
    x, y = OFFSETS[k - 1]
    column = lax.rem(lax.div(me_d, 4) + (x if sign > 0 else 4 - x), 4)
    return 4 * column + lax.rem(lax.rem(me_d, 4) + (y if sign > 0 else 4 - y), 4)


def to_dp(src, dst, send, recv, by_sender=False):
    me_s, me_d = lax.axis_index("space"), lax.axis_index("dp")
    copies = []
    for k in range(1, ND):
        target = dp_peer(k, 1)
        copies.append(
            pltpu.make_async_remote_copy(
                src_ref=src.at[target],
                dst_ref=dst.at[me_d] if by_sender else dst.at[k],
                send_sem=send.at[k],
                recv_sem=recv.at[k],
                device_id=(me_s, target),
                device_id_type=MESH,
            )
        )
    return copies


def to_space(ref, send, recv):
    me_s, me_d = lax.axis_index("space"), lax.axis_index("dp")
    copies = []
    for k in (4, 5, 3, 6, 2, 7, 1):
        copies.append(
            pltpu.make_async_remote_copy(
                src_ref=ref.at[me_s],
                dst_ref=ref.at[me_s],
                send_sem=send.at[k],
                recv_sem=recv.at[k],
                device_id=(lax.rem(me_s + k, NS), me_d),
                device_id_type=MESH,
            )
        )
    return copies


def to_neighbours(down_src, down_dst, up_src, up_dst, send, recv):
    me_s, me_d = lax.axis_index("space"), lax.axis_index("dp")
    down = pltpu.make_async_remote_copy(
        src_ref=down_src,
        dst_ref=down_dst,
        send_sem=send[0],
        recv_sem=recv[0],
        device_id=(lax.rem(me_s + 1, NS), me_d),
        device_id_type=MESH,
    )
    up = pltpu.make_async_remote_copy(
        src_ref=up_src,
        dst_ref=up_dst,
        send_sem=send[1],
        recv_sem=recv[1],
        device_id=(lax.rem(me_s + NS - 1, NS), me_d),
        device_id_type=MESH,
    )
    return down, up


def dp_sum(copies, piece, got):
    total = piece[lax.axis_index("dp")].astype(F32)
    for k, copy in enumerate(copies):
        copy.wait()
        total = total + got[k + 1].astype(F32)
    return total


def space_sum(copies, ref):
    for copy in copies:
        copy.wait()
    total = ref[0].astype(F32)
    for s in range(1, NS):
        total = total + ref[s].astype(F32)
    return total


EARLY = C + 32


def block_kernel(
    wet, wpr, taps, wrt, wx_own, bex, bred, feats_in, cot_in,
    out_to, out_grad_to, early, late, mail_out,
    out, out_grad, feats, cot, stage, pack, full, top, bottom, flatw, fp, cp, fpt, cpt, we, wp, misc,
    wide_taps, ex, dgs, coming_pre, coming_dg, saved, depth, sums, packed, landed, lanes, vecs, gates, msgs, mail,
    edge, above, below, gated, dpre, acc, held, flat, flat_taps,
    epiece, egot, espace, lpiece, lgot, lspace, tpiece, tgot, tspace,
    wsend, wrecv, hsend, hrecv, csend, crecv, ssend, srecv, msend, mrecv,
    dsend, drecv, esend, erecv, fsend, frecv, lsend, lrecv, gsend, grecv,
    tsend, trecv, usend, urecv, insem,
):
    me_s, me_d = lax.axis_index("space"), lax.axis_index("dp")
    core = lax.rem(me_s, 2)
    barrier = pltpu.get_barrier_semaphore()
    for k in range(1, ND):
        pl.semaphore_signal(
            barrier, inc=1, device_id=(me_s, dp_peer(k, 1)), device_id_type=MESH
        )
    for k in range(1, NS):
        pl.semaphore_signal(
            barrier, inc=1, device_id=(lax.rem(me_s + k, NS), me_d), device_id_type=MESH
        )

    arrive = [
        pltpu.make_async_copy(feats_in, feats, insem.at[0]),
        pltpu.make_async_copy(cot_in, cot, insem.at[1]),
    ]
    for copy in arrive:
        copy.start()

    stage[...] = jnp.zeros_like(stage)
    stage[0, 0:PART, 0:C] = wet[...].astype(F32)
    stage[1, 0:PART, 0:C] = wpr[...].astype(F32)
    side = slice(C, C + PART)
    for i in range(5):
        stage[0, 5 * i : 5 * i + 5, side] = taps[i].astype(F32)
    stage[0, 32 : 32 + SE, side] = wrt[...].astype(F32)
    stage[1, 0:SE, side] = wx_own[...].astype(F32)
    stage[1, 48:49, side] = bex[...].astype(F32)
    pack[...] = stage[...].astype(BF16)
    pl.semaphore_wait(barrier, NS + ND - 2)
    copies = []
    for k in range(1, ND):
        copy = pltpu.make_async_remote_copy(
            src_ref=pack.at[core],
            dst_ref=full.at[core, me_d],
            send_sem=wsend.at[k],
            recv_sem=wrecv.at[k],
            device_id=(me_s, dp_peer(k, 1)),
            device_id_type=MESH,
        )
        copy.start()
        copies.append(copy)
    for copy in arrive:
        copy.wait()
    halo = to_neighbours(
        feats.at[:, pl.ds(ROWS - 2, 2)],
        top,
        feats.at[:, pl.ds(0, 2)],
        bottom,
        (hsend.at[0], hsend.at[1]),
        (hrecv.at[0], hrecv.at[1]),
    )
    for copy in halo:
        copy.start()
    full[0, me_d] = pack[0]
    full[1, me_d] = pack[1]
    spread = (one_hot(0, False), one_hot(1, False))
    gather_t = (one_hot(0, True), one_hot(1, True))

    def permute(r, carry):
        for src, dst, shift in ((feats, fp, 2), (cot, cp, 0)):
            a, b = src[0, r], src[1, r]
            dst[r + shift] = (dot_nt(spread[0], a) + dot_nt(spread[1], b)).astype(BF16)
        return carry

    lax.fori_loop(0, ROWS, permute, 0)
    for r in range(ROWS):
        for src, dst in ((feats, fpt), (cot, cpt)):
            value = dot_nn(src[0, r], gather_t[0]) + dot_nn(src[1, r], gather_t[1])
            dst[:, PIX * r : PIX * (r + 1)] = value.astype(BF16)
    shares = []
    for k, copy in enumerate(copies, 1):
        copy.wait_recv()
        sender = dp_peer(k, -1)
        share = pltpu.make_async_remote_copy(
            src_ref=full.at[core, sender],
            dst_ref=full.at[core, sender],
            send_sem=csend.at[k],
            recv_sem=crecv.at[k],
            device_id=(me_s + 1 - 2 * core, me_d),
            device_id_type=MESH,
        )
        share.start()
        shares.append(share)
    for copy in halo:
        copy.wait()
    has_top = jnp.where(me_s > 0, 1.0, 0.0)
    has_bottom = jnp.where(me_s < NS - 1, 1.0, 0.0)
    for r in range(2):
        value = dot_nt(spread[0], top[0, r]) + dot_nt(spread[1], top[1, r])
        fp[r] = (value * has_top).astype(BF16)
        value = dot_nt(spread[0], bottom[0, r]) + dot_nt(spread[1], bottom[1, r])
        fp[ROWS + 2 + r] = (value * has_bottom).astype(BF16)
    for copy in copies:
        copy.wait_send()
    for share in shares:
        share.wait()
    for half, whole in ((0, we), (1, wp)):
        for d in range(ND):
            part = full[half, d].astype(F32)
            flatw[d * SLOT : (d + 1) * SLOT, :] = part[0:SLOT, 0:C]
            span = slice(d * SLOT, (d + 1) * SLOT)
            if half == 0:
                misc[0:80, span] = part[:, C : C + SLOT]
            else:
                misc[80:136, span] = part[0:56, C : C + SLOT]
        whole[...] = flatw[...].astype(BF16)

    keep = pad_mask()

    def lane_of(t):
        return pl.ds(pl.multiple_of(128 * t, 128), 128)

    def pre_rows(t, start, count):
        product = dot_nt(fp[pl.ds(start, count)].reshape(count * PIX, C), we[lane_of(t), :])
        coming_pre[pl.ds(start, count)] = product.reshape(count, BLOCK, SUB, 128)

    def cot_rows(t, start, count):
        product = dot_nt(cp[pl.ds(start, count)].reshape(count * PIX, C), wp[lane_of(t), :])
        coming_dg[pl.ds(start, count)] = product.reshape(count, BLOCK, SUB, 128)

    def next_tile(t):
        return jnp.minimum(t + 1, TILES - 1)

    def take_dg():
        def row(r, carry):
            dgs[r] = coming_dg[r]
            return carry

        lax.fori_loop(0, ROWS, row, 0)

    def first(t, carry):
        spread_taps(misc[0:32, lane_of(t)], wide_taps, False)

        def expand(q, carry):
            for n in range(4):
                ex[4 * q + n] = swish(coming_pre[4 * q + n]).astype(BF16).astype(F32)
            return carry

        lax.fori_loop(0, HROWS // 4, expand, 0)
        take_dg()

        def conv(q, carry):
            pools, grads = list(carry[:2]), list(carry[2:])
            for h in range(2):
                rows = slice(8 * h, 8 * h + 8)
                for n, total in enumerate(conv_rows(ex, q, h, wide_taps)):
                    depth[t, 4 * q + n, :, rows, :] = total
                    act = swish(total)
                    grads[h] = grads[h] + jnp.sum(act * dgs[4 * q + n, :, rows, :], axis=0)
                    pools[h] = pools[h] + jnp.sum(act[:9], axis=0)
                    pools[h] = pools[h] + jnp.sum(act[9:] * keep, axis=0)
            for n in range(4):
                saved[t, 4 * q + n] = ex[4 * q + n].astype(BF16)
            pre_rows(next_tile(t), jnp.minimum(6 * q, HROWS - 6), 6)
            cot_rows(next_tile(t), 4 * q, 4)
            return (*pools, *grads)

        zero = jnp.zeros((8, 128), F32)
        parts = lax.fori_loop(0, ROWS // 4, conv, (zero,) * 4)
        for r in range(ROWS, HROWS):
            saved[t, r] = ex[r].astype(BF16)
        for k in range(4):
            sums[t, k : k + 1, :] = jnp.sum(parts[k], axis=0, keepdims=True)
        return carry

    def begin(q, carry):
        pre_rows(0, 8 * q, 8)
        cot_rows(0, 6 * q, 6)
        return carry

    lax.fori_loop(0, 2, begin, 0)
    lax.fori_loop(0, TILES, first, 0)

    packed[...] = jnp.zeros_like(packed)
    for t in range(TILES):
        packed[t // 2, 4 * (t % 2) : 4 * (t % 2) + 4, :] = sums[t, 0:4, :]
    landed[me_s] = packed[...]
    copies = to_space(landed, ssend, srecv)
    for copy in copies:
        copy.start()

    def begin_again(q, carry):
        cot_rows(0, 6 * q, 6)
        return carry

    lax.fori_loop(0, 2, begin_again, 0)
    total = space_sum(copies, landed)
    for t in range(TILES):
        lanes[0:4, 128 * t : 128 * (t + 1)] = total[t // 2, 4 * (t % 2) : 4 * (t % 2) + 4]
    lanes[:, CP:] = jnp.zeros((8, 128), F32)
    wr = misc[32 : 32 + SE, :]
    wx = misc[80 : 80 + SE, :]
    pooled = lanes[0:2, 0:CP] / AREA
    dgate = lanes[2:4, 0:CP]
    squeeze_pre = dot_split(pooled, wr, ((1,), (1,))) + bred[...].astype(F32)
    squeeze = swish(squeeze_pre)
    gate = sigmoid(dot_split(squeeze, wx, ((1,), (0,))) + misc[128:129, :])
    dlogit = dgate * gate * (1.0 - gate)
    dsq = dot_split(dlogit, wx, ((1,), (1,))) * swish_grad(squeeze_pre)
    dpooled = dot_split(dsq, wr, ((1,), (0,)))
    gates[0:2, :] = gate
    gates[2:4, :] = 0.5 * gate
    gates[4:6, :] = dpooled * (0.5 / AREA)
    gates[6:8, :] = jnp.zeros((2, CP), F32)
    lanes[0:2, 0:CP] = pooled
    lanes[2:4, 0:CP] = dlogit
    vecs[...] = jnp.zeros((8, 128), F32)
    vecs[4:6, 0:SE] = squeeze
    vecs[6:8, 0:SE] = dsq

    def edge_copies(t):
        return to_neighbours(
            edge.at[t, 1],
            above.at[t],
            edge.at[t, 0],
            below.at[t],
            (dsend.at[0, t], dsend.at[1, t]),
            (drecv.at[0, t], drecv.at[1, t]),
        )

    def second(t, carry):
        take_dg()

        def pointwise(q, carry):
            for n in range(4):
                r = 4 * q + n
                both = []
                for h in range(2):
                    rows = slice(8 * h, 8 * h + 8)
                    value, ddepth = gate_row(
                        depth[t, r, :, rows, :],
                        dgs[r, :, rows, :],
                        gates.at[:, lane_of(t)],
                        h,
                        keep,
                    )
                    depth[t, r, :, rows, :] = ddepth.astype(BF16).astype(F32)
                    both.append(value)
                gated[pl.ds(pl.multiple_of(r * PIX, PIX), PIX), lane_of(t)] = (
                    jnp.concatenate(both, axis=1).reshape(PIX, 128).astype(BF16)
                )
            cot_rows(next_tile(t), 4 * q, 4)
            return carry

        lax.fori_loop(0, ROWS // 4, pointwise, 0)
        for n in range(2):
            edge[t, 0, n] = depth[t, n].astype(BF16)
            edge[t, 1, n] = depth[t, ROWS - 2 + n].astype(BF16)
        for copy in edge_copies(t):
            copy.start()
        return carry

    lax.fori_loop(0, TILES, second, 0)

    def pieces_of(source, rows, piece):
        for d in range(ND):
            piece[d] = source[0:rows, SLOT * d : SLOT * d + 128].astype(BF16)

    flat[:, CP:] = jnp.zeros((C, 128), F32)
    flat_taps[...] = jnp.zeros_like(flat_taps)
    all_channels_grad(gated, cpt, flat)
    pieces_of(flat, C, epiece)
    for copy in to_dp(epiece, egot, esend, erecv):
        copy.start()

    def third(t, carry):
        spread_taps(misc[0:32, lane_of(t)], wide_taps, True)

        def middle(r, carry):
            ex[r + 2] = depth[t, r]
            return carry

        lax.fori_loop(0, ROWS, middle, 0)

        def slopes(q, carry):
            for n in range(4):
                dgs[4 * q + n] = twice_swish_grad(coming_pre[4 * q + n + 2])
            return carry

        lax.fori_loop(0, ROWS // 4, slopes, 0)
        for copy in edge_copies(t):
            copy.wait()
        for n in range(2):
            ex[n] = above[t, n].astype(F32) * has_top
            ex[ROWS + 2 + n] = below[t, n].astype(F32) * has_bottom

        def conv(q, carry):
            both = []
            for h in range(2):
                rows = slice(8 * h, 8 * h + 8)
                values = conv_rows(ex, q, h, wide_taps)
                both.append([value * dgs[4 * q + n, :, rows, :] for n, value in enumerate(values)])
            for n in range(4):
                value = jnp.concatenate([both[0][n], both[1][n]], axis=1)
                span = pl.ds(pl.multiple_of((4 * q + n) * PIX, PIX), PIX)
                dpre[span, lane_of(t)] = value.reshape(PIX, 128).astype(BF16)
            pre_rows(next_tile(t), 4 * q + 2, 4)
            return carry

        lax.fori_loop(0, ROWS // 4, conv, 0)

        @pl.when(t == TILES // 2)
        def _():
            total = dp_sum(to_dp(epiece, egot, esend, erecv), epiece, egot)
            espace[me_s] = total.astype(BF16)
            for copy in to_space(espace, fsend, frecv):
                copy.start()

        return carry

    def begin_third(q, carry):
        pre_rows(0, 6 * q + 2, 6)
        return carry

    lax.fori_loop(0, 2, begin_third, 0)
    lax.fori_loop(0, TILES, third, 0)

    all_channels_grad(dpre, fpt, flat)
    pieces_of(flat, C, lpiece)
    for copy in to_dp(lpiece, lgot, lsend, lrecv):
        copy.start()

    def tap_grads(t, carry):
        acc[...] = jnp.zeros_like(acc)

        def window(q, carry):
            for h in range(2):
                rows = slice(8 * h, 8 * h + 8)
                points = to_points([saved[t, 4 * q + n].astype(F32)[:, rows, :] for n in range(8)])
                for p in range(8):
                    held[p] = with_edges(points[p])
                mine = outputs_to_points([depth[t, 4 * q + n, :, rows, :] for n in range(4)])
                for p in range(8):
                    source = held[p]
                    for j in range(5):
                        k = 5 * p + j
                        acc[k] = acc[k] + jnp.sum(mine[p] * source[j : j + BLOCK], axis=0)
            return carry

        lax.fori_loop(0, ROWS // 4, window, 0)
        for j in range(5):
            sums_at = [jnp.sum(acc[5 * p + j], axis=0, keepdims=True) for p in range(8)]
            for i, value in enumerate(taps_from_points(sums_at)):
                flat_taps[5 * i + j : 5 * i + j + 1, lane_of(t)] = value

        @pl.when(t == TILES // 2)
        def _():
            total = dp_sum(to_dp(lpiece, lgot, lsend, lrecv), lpiece, lgot)
            lspace[me_s] = total.astype(BF16)
            for copy in to_space(lspace, gsend, grecv):
                copy.start()

        return carry

    lax.fori_loop(0, TILES, tap_grads, 0)
    pieces_of(flat_taps, 32, tpiece)
    copies = to_dp(tpiece, tgot, tsend, trecv)
    for copy in copies:
        copy.start()
    for d in range(ND):
        msgs[d, 0:4, :] = lanes[0:4, SLOT * d : SLOT * d + 128]
        msgs[d, 4:8, :] = vecs[4:8, :]
    mail[me_d] = msgs[me_d]
    small = to_dp(msgs, mail, msend, mrecv, True)
    for copy in small:
        copy.start()

    all_channels_out(dpre, we, cp, 0, out_grad)
    leave = pltpu.make_async_copy(out_grad, out_grad_to, insem.at[0])
    leave.start()
    tspace[me_s] = dp_sum(copies, tpiece, tgot).astype(BF16)
    copies = to_space(tspace, usend, urecv)
    for copy in copies:
        copy.start()
    all_channels_out(gated, wp, fp, 2, out)
    leave_too = pltpu.make_async_copy(out, out_to, insem.at[1])
    leave_too.start()
    for copy in small:
        copy.wait()
    mail_out[...] = mail[...]
    early[0:C] = space_sum(to_space(espace, fsend, frecv), espace)
    late[...] = space_sum(to_space(lspace, gsend, grecv), lspace)
    early[C:] = space_sum(copies, tspace)
    leave.wait()
    leave_too.wait()


def block(*args):
    def bf16(*shape):
        return pltpu.VMEM(shape, BF16)

    def f32(*shape):
        return pltpu.VMEM(shape, F32)

    def sems(*shape):
        return pltpu.SemaphoreType.DMA(shape)

    return pl.pallas_call(
        block_kernel,
        out_shape=(
            jax.ShapeDtypeStruct((IMGS, ROWS, C, COLS), BF16),
            jax.ShapeDtypeStruct((IMGS, ROWS, C, COLS), BF16),
            jax.ShapeDtypeStruct((EARLY, 128), F32),
            jax.ShapeDtypeStruct((C, 128), F32),
            jax.ShapeDtypeStruct((ND, 8, 128), F32),
        ),
        in_specs=[VMEM] * 7 + [ANY] * 2,
        out_specs=(ANY, ANY, VMEM, VMEM, VMEM),
        scratch_shapes=[
            bf16(IMGS, ROWS, C, COLS),
            bf16(IMGS, ROWS, C, COLS),
            bf16(IMGS, ROWS, C, COLS),
            bf16(IMGS, ROWS, C, COLS),
            f32(2, 80, 256),
            bf16(2, 80, 256),
            bf16(2, ND, 80, 256),
            bf16(IMGS, 2, C, COLS),
            bf16(IMGS, 2, C, COLS),
            f32(CP, C),
            bf16(HROWS, PIX, C),
            bf16(ROWS, PIX, C),
            bf16(C, ROWS * PIX),
            bf16(C, ROWS * PIX),
            bf16(CP, C),
            bf16(CP, C),
            f32(136, CP),
            f32(40, 8, 128),
            f32(HROWS, BLOCK, SUB, 128),
            f32(ROWS, BLOCK, SUB, 128),
            f32(HROWS, BLOCK, SUB, 128),
            f32(ROWS, BLOCK, SUB, 128),
            bf16(TILES, HROWS, BLOCK, SUB, 128),
            f32(TILES, ROWS, BLOCK, SUB, 128),
            f32(TILES, 8, 128),
            f32(5, 8, 128),
            f32(NS, 5, 8, 128),
            f32(8, CP + 128),
            f32(8, 128),
            f32(8, CP),
            f32(ND, 8, 128),
            f32(ND, 8, 128),
            bf16(TILES, 2, 2, BLOCK, SUB, 128),
            bf16(TILES, 2, BLOCK, SUB, 128),
            bf16(TILES, 2, BLOCK, SUB, 128),
            bf16(ROWS * PIX, CP),
            bf16(ROWS * PIX, CP),
            f32(40, 8, 128),
            f32(8, WIDE, 8, 128),
            f32(C, CP + 128),
            f32(32, CP + 128),
            bf16(ND, C, 128),
            bf16(ND, C, 128),
            bf16(NS, C, 128),
            bf16(ND, C, 128),
            bf16(ND, C, 128),
            bf16(NS, C, 128),
            bf16(ND, 32, 128),
            bf16(ND, 32, 128),
            bf16(NS, 32, 128),
            sems(ND),
            sems(ND),
            sems(2),
            sems(2),
            sems(ND),
            sems(ND),
            sems(NS),
            sems(NS),
            sems(ND),
            sems(ND),
            sems(2, TILES),
            sems(2, TILES),
            sems(ND),
            sems(ND),
            sems(NS),
            sems(NS),
            sems(ND),
            sems(ND),
            sems(NS),
            sems(NS),
            sems(ND),
            sems(ND),
            sems(NS),
            sems(NS),
            sems(2),
        ],
        compiler_params=pltpu.CompilerParams(
            collective_id=0, has_side_effects=True, vmem_limit_bytes=63 * 2**20
        ),
        name="block",
    )(*args)


def finish_kernel(
    early, late, mail, raw, raw_grad,
    gexp, gdepth, greduce, gexcite, gbex, gproj, gbred, out, out_grad,
):
    out[...] = raw[...]
    out_grad[...] = raw_grad[...]

    @pl.when(pl.program_id(0) == 0)
    def _():
        gexp[...] = late[...].T[0:PART]
        gproj[...] = early[0:C].T[0:PART]
        for i in range(5):
            gdepth[i] = early[C + 5 * i : C + 5 * i + 5, 0:PART]
        rows = [mail[d] for d in range(ND)]
        pool_all = jnp.concatenate([row[0:2] for row in rows], axis=0)
        dlog_all = jnp.concatenate([row[2:4] for row in rows], axis=0)
        sq_all = jnp.concatenate([row[4:6] for row in rows], axis=0)
        dsq_all = jnp.concatenate([row[6:8] for row in rows], axis=0)
        greduce[...] = dot_tn(dsq_all, pool_all, HIGH)[0:SE, 0:PART]
        gexcite[...] = dot_tn(sq_all, dlog_all, HIGH)[0:SE, 0:PART]
        gbex[...] = jnp.sum(dlog_all, axis=0, keepdims=True)[:, 0:PART]
        gbred[...] = jnp.sum(dsq_all, axis=0, keepdims=True)[:, 0:SE]


def finish(early, late, mail, raw, raw_grad):
    def whole(*shape):
        zeros = (0,) * len(shape)
        return pl.BlockSpec(shape, lambda n: zeros)

    part = pl.BlockSpec((IMGS, 6, C, COLS), lambda n: (0, n, 0, 0))
    shapes = ((PART, C), (5, 5, PART), (SE, PART), (SE, PART), (1, PART), (PART, C), (1, SE))
    return pl.pallas_call(
        finish_kernel,
        grid=(ROWS // 6,),
        out_shape=tuple(jax.ShapeDtypeStruct(shape, F32) for shape in shapes)
        + (jax.ShapeDtypeStruct((IMGS, ROWS, C, COLS), BF16),) * 2,
        in_specs=[whole(EARLY, 128), whole(C, 128), whole(ND, 8, 128), part, part],
        out_specs=tuple(whole(*shape) for shape in shapes) + (part, part),
        name="finish",
    )(early, late, mail, raw, raw_grad)


def on_device(
    features, w_expand, w_depth, w_reduce, b_reduce, w_excite, b_excite, w_project, cotangent
):
    raw, raw_grad, early, late, mail = block(
        w_expand.T,
        w_project,
        w_depth,
        w_reduce.T,
        w_excite,
        b_excite[None, :],
        b_reduce[None, :],
        features.swapaxes(2, 3),
        cotangent.swapaxes(2, 3),
    )
    (
        s_expand, s_depth, s_reduce, s_excite, s_bexcite, s_project, s_breduce, output, grad,
    ) = finish(early, late, mail, raw, raw_grad)
    return (
        output.swapaxes(2, 3),
        grad.swapaxes(2, 3),
        s_expand.T,
        s_depth,
        s_reduce.T,
        s_excite,
        s_bexcite[0],
        s_project,
        s_breduce[0],
    )


def solution(mesh):
    return jax.shard_map(
        on_device,
        mesh=mesh,
        in_specs=(
            P("dp", "space", None, None),
            P(None, "dp"),
            P(None, None, "dp"),
            P("dp", None),
            P(),
            P(None, "dp"),
            P("dp"),
            P("dp", None),
            P("dp", "space", None, None),
        ),
        out_specs=(
            P("dp", "space", None, None),
            P("dp", "space", None, None),
            P(None, "dp"),
            P(None, None, "dp"),
            P("dp", None),
            P(None, "dp"),
            P("dp"),
            P("dp", None),
            P(),
        ),
        check_vma=False,
    )
```
